128 devices in a mesh: seq: 4 (over x), grp: 16 (over y, z), exp: 2 (over core).
Axes of the slice: x: 4, y: 4, z: 4, core: 2. Of those that a mesh axis runs over, the one named last changes fastest.
Arguments:
- tokens: bfloat16 [16, 2048, 1024], P('grp', ('seq', 'exp')), may hold values from -6 to 6
- segments: int32 [16, 2048], P('grp', ('seq', 'exp')), may hold values from 0 to 3, never falling along the last dimension, each value on 1 to 1792 neighbouring positions
- routes: int32 [16, 2048, 8], P('grp', ('seq', 'exp')), may hold values from 0 to 31, all different within a row
- rank_order: int32 [16, 2048, 8], P('grp', ('seq', 'exp')), may hold values from 0 to 7, each once within a row
- attn_gain: float32 [1024], replicated, may hold values from 0.5 to 1.5
- w_query: bfloat16 [1024, 1024], replicated, may hold values from -0.75 to 0.75
- w_key: bfloat16 [1024, 512], replicated, may hold values from -0.75 to 0.75
- w_value: bfloat16 [1024, 512], replicated, may hold values from -0.1875 to 0.1875
- w_output: bfloat16 [1024, 1024], replicated, may hold values from -4 to 4
- ffn_gain: float32 [1024], replicated, may hold values from 0.5 to 1.5
- w_router: bfloat16 [1024, 32], replicated, may hold values from -0.09375 to 0.09375
- expert_in: bfloat16 [32, 1024, 1024], P(('grp', 'exp')), may hold values from -0.1875 to 0.1875
- expert_out: bfloat16 [32, 512, 1024], P(('grp', 'exp')), may hold values from -2 to 2
- cotangent: bfloat16 [16, 2048, 1024], P('grp', ('seq', 'exp')), may hold values from -6 to 6
Outputs:
- output: bfloat16 [16, 2048, 1024], P('grp', ('seq', 'exp'))
- input_grad: bfloat16 [16, 2048, 1024], P('grp', ('seq', 'exp'))
- attn_gain_grad: float32 [1024], replicated
- query_grad: float32 [1024, 1024], replicated
- key_grad: float32 [1024, 512], replicated
- value_grad: float32 [1024, 512], replicated
- output_w_grad: float32 [1024, 1024], replicated
- ffn_gain_grad: float32 [1024], replicated
- router_grad: float32 [1024, 32], replicated
- expert_in_grad: float32 [32, 1024, 1024], P(('grp', 'exp'))
- expert_out_grad: float32 [32, 512, 1024], P(('grp', 'exp'))
The draws below stay inside these ranges and needn't reach their ends.
Inputs may be any that keep to these rules, and one draw needn't show every extreme that they name: `segments`: document numbers never fall along a sequence; one document of each sequence has 1792 tokens. `routes`: each token names 8 different experts; every expert is named somewhere. `rank_order`: each token's row is a permutation of 0 to 7.
All inputs are finite; a program needn't handle non-finite values.
Results may differ from the reference program's by a relative error of at most 0.015.
The reference program's roundings to bfloat16 on the way count: a program that leaves them out, or rounds other values in their place, can miss the bound.
Values may be sent and summed in bfloat16 or wider, within the bound.
A program may use at most 256 MiB of HBM per device.

```python
import math
from functools import partial
import jax
import jax.numpy as jnp
import numpy as np
from jax import lax

D = 1024
HEADS = 16
KV_HEADS = 8
HEAD = 64
FF = 512
TOP = 8
WINDOW = 1024
TOK_DEV = 256
EXPERTS = 32
LEN = 2048
SEQS = 16
CAP = 80


def levels(rng, shape, shards, low, largest):
    factor_of = 1.0
    for position, parts in shards:
        heights = jax.random.uniform(jax.random.fold_in(jax.random.fold_in(rng, 6), position), (parts,), jnp.float32, low / len(shards), largest / len(shards))
        factor_of = factor_of * jnp.repeat(jnp.exp(heights), shape[position] // parts).reshape((-1,) + (1,) * (len(shape) - 1 - position))
    return factor_of


def choose_distinct(key, rows, count, top, lift):
    order = jax.random.permutation(jax.random.fold_in(key, 1), count)
    favour = order
    for power in range(3):
        favour = favour * favour // count
    favour = favour * lift // count
    chance = jax.random.randint(jax.random.fold_in(key, 2), (rows, count), 0, 4096) + favour
    sure = jax.random.permutation(jax.random.fold_in(key, 3), rows)[jnp.arange(count) % rows]
    chance = jnp.where(jnp.arange(rows)[:, None] == sure[None, :], 1 << 14, chance)
    merit = chance * count + jnp.arange(count)
    return lax.top_k(merit.astype(jnp.int32), top)[1].astype(jnp.int32)


def profile(number_of, total, bound, slope):
    loads = [(1 << 20) // math.isqrt(standing ** slope) + 1 for standing in range(2, number_of + 1)]
    spare, given = total - bound - (number_of - 1), [1] * (number_of - 1)
    while spare > 0:
        movable = [i for i in range(number_of - 1) if given[i] < bound]
        mass, budget = sum([loads[i] for i in movable]), spare
        for i in movable:
            extra = min(bound - given[i], max(1, budget * loads[i] // mass), spare)
            given[i] = given[i] + extra
            spare = spare - extra
    return np.array([bound] + given)


def ragged_sizes(stream_key, number_of, total, reach, lean):
    if number_of == 2:
        one = jax.random.randint(stream_key, (), max(1, total - reach), min(reach, total - 1) + 1)
        return jnp.stack([one, total - one])
    sizes = jnp.asarray(profile(number_of, total, reach, lean), jnp.int32)
    pairs = (number_of - 1) // 2
    giver, sink = sizes[1:1 + 2 * pairs:2], sizes[2:2 + 2 * pairs:2]
    room = jnp.minimum(giver - 1, reach - sink)
    moved = jax.random.randint(jax.random.fold_in(stream_key, 1), (pairs,), 0, 1 << 20) % (room + 1)
    sizes = sizes.at[1:1 + 2 * pairs:2].set(giver - moved).at[2:2 + 2 * pairs:2].set(sink + moved)
    return sizes[jax.random.permutation(jax.random.fold_in(stream_key, 2), number_of)]


def noise(stream_key, extent, width, limit, cuts=(), held_as=jnp.bfloat16):
    factor_of = levels(stream_key, extent, cuts, -0.22, 0.18) if cuts else 1.0
    values = jax.random.normal(stream_key, extent, jnp.float32) * width * factor_of
    return jnp.minimum(jnp.maximum(values, -limit), limit).astype(held_as)


def setup_inputs(seed: int = 0) -> dict:
    seeds = jax.random.split(jax.random.key(seed), 15)
    return {
        "tokens": noise(seeds[0], (SEQS, LEN, D), 1.0, 6.0, ((0, 16), (1, 8))),
        "segments": jax.vmap(lambda own: jnp.searchsorted(jnp.cumsum(ragged_sizes(own, 4, LEN, LEN - TOK_DEV, 0)), jnp.arange(LEN), side="right"))(jax.random.split(seeds[1], SEQS)).reshape((SEQS, LEN)).astype(jnp.int32),
        "routes": choose_distinct(seeds[2], SEQS * LEN, EXPERTS, TOP, 2048).reshape((SEQS, LEN, TOP)),
        "rank_order": jax.vmap(lambda own: jax.random.permutation(own, TOP))(jax.random.split(seeds[3], SEQS * LEN)).reshape((SEQS, LEN, TOP)).astype(jnp.int32),
        "attn_gain": jnp.clip(1.0 + 0.1 * jax.random.normal(seeds[4], (D,), jnp.float32), 0.5, 1.5),
        "w_query": noise(seeds[5], (D, D), (D // 16) ** -0.5, 0.75),
        "w_key": noise(seeds[6], (D, KV_HEADS * HEAD), (D // 16) ** -0.5, 0.75),
        "w_value": noise(seeds[7], (D, KV_HEADS * HEAD), D ** -0.5, 0.1875),
        "w_output": noise(seeds[8], (D, D), 2 ** -0.5, 4.0),
        "ffn_gain": jnp.clip(1.0 + 0.1 * jax.random.normal(seeds[9], (D,), jnp.float32), 0.5, 1.5),
        "w_router": noise(seeds[10], (D, EXPERTS), (4 * D) ** -0.5, 0.09375),
        "expert_in": noise(seeds[11], (EXPERTS, D, 2 * FF), D ** -0.5, 0.1875, ((0, 32),)),
        "expert_out": noise(seeds[12], (EXPERTS, FF, D), (max(FF // 64, 1)) ** -0.5, 2.0, ((0, 32),)),
        "cotangent": noise(seeds[13], (SEQS, LEN, D), 1.0, 6.0, ((0, 16), (1, 8))),
    }


@jax.custom_vjp
def lowered_scores(v):
    return lax.optimization_barrier(v.astype(jnp.bfloat16)).astype(jnp.float32)

@jax.custom_vjp
def lowered_backward(v):
    return v

def low_keep(v):
    return (lowered_scores(v), None)

def low_pass(kept, grad):
    return (grad,)

def back_keep(v):
    return (v, None)

def back_low(kept, grad):
    return (lowered_scores(grad),)
lowered_scores.defvjp(low_keep, low_pass)
lowered_backward.defvjp(back_keep, back_low)
EPSILON = 1e-06
ATTENTION_FACTOR = 0.015625
RESIDUAL_MULT = 0.22
ROPE_BASE = 10000.0
MASKED = -1e+30
MAXIMUM_PRECISE = lax.Precision.HIGHEST

def rms_norm(values, norm_gain):
    inverse = lax.rsqrt(lax.optimization_barrier(jnp.mean(values * values, axis=-1, keepdims=True)) + EPSILON)
    return values * inverse * norm_gain

def rotate(values, positions):
    half_dim = values.shape[-1] // 2
    frequency = jnp.exp(jnp.arange(half_dim, dtype=jnp.float32) * (-2.0 * math.log(ROPE_BASE) / values.shape[-1]))
    angles = positions.astype(jnp.float32)[:, None] * frequency[None, :]
    cosine = jnp.cos(angles)[:, None, :]
    sine_part = jnp.sin(angles)[:, None, :]
    first_half = values[..., :half_dim]
    second_half = values[..., half_dim:]
    return jnp.concatenate([first_half * cosine - second_half * sine_part, second_half * cosine + first_half * sine_part], axis=-1)

def place_pairs(route_ids, rank_ids, experts, capacity):
    tok_rows, top_count = route_ids.shape
    by_order = (rank_ids[:, :, None] == jnp.arange(top_count, dtype=jnp.int32)[None, None, :]).astype(jnp.int32)
    by_expert = (route_ids[:, :, None] == jnp.arange(experts, dtype=jnp.int32)[None, None, :]).astype(jnp.int32)
    counts = lax.optimization_barrier(jnp.sum(by_order[:, :, :, None] * by_expert[:, :, None, :], axis=1))
    before = (jnp.cumsum(counts, axis=0) - counts).reshape(tok_rows, top_count * experts)
    totals = lax.optimization_barrier(jnp.sum(counts, axis=0))
    offsets = (jnp.cumsum(totals, axis=0) - totals).reshape(top_count * experts)
    flat_index = rank_ids * experts + route_ids
    slot_place = jnp.take_along_axis(before, flat_index, axis=1) + offsets[flat_index]
    destination = jnp.where(slot_place < capacity, route_ids * capacity + slot_place, experts * capacity).astype(jnp.int32)
    source = jnp.full((experts * capacity + 1,), tok_rows * top_count, jnp.int32)
    source = source.at[destination.reshape(-1)].set(jnp.arange(tok_rows * top_count, dtype=jnp.int32))
    return (destination, source[:experts * capacity])

def attend(query_rows, key_rows, values_in, segment_ids):
    seq_len, q_heads, head_dim = query_rows.shape
    kv_heads = key_rows.shape[1]
    block_rows = min(512, seq_len)
    pad_keys = jnp.pad(key_rows, ((WINDOW, 0), (0, 0), (0, 0)))
    pad_values = jnp.pad(values_in, ((WINDOW, 0), (0, 0), (0, 0)))
    pad_segments = jnp.pad(segment_ids, (WINDOW, 0), constant_values=-1)

    def one_block(begin_row):
        query_tile_rows = lax.dynamic_slice_in_dim(query_rows, begin_row, block_rows, 0).reshape(block_rows, kv_heads, q_heads // kv_heads, head_dim)
        key_tile_rows = lax.dynamic_slice_in_dim(pad_keys, begin_row, block_rows + WINDOW, 0)
        value_tile_rows = lax.dynamic_slice_in_dim(pad_values, begin_row, block_rows + WINDOW, 0)
        key_segments = lax.dynamic_slice_in_dim(pad_segments, begin_row, block_rows + WINDOW, 0)
        query_segments = lax.dynamic_slice_in_dim(segment_ids, begin_row, block_rows, 0)
        query_pos = begin_row + jnp.arange(block_rows, dtype=jnp.int32)
        key_pos = begin_row - WINDOW + jnp.arange(block_rows + WINDOW, dtype=jnp.int32)
        distance = query_pos[:, None] - key_pos[None, :]
        allowed = (query_segments[:, None] == key_segments[None, :]) & (distance >= 0) & (distance < WINDOW)
        score_matrix = lowered_backward(ATTENTION_FACTOR * jnp.einsum('dklp,okp->kldo', query_tile_rows, key_tile_rows, precision=MAXIMUM_PRECISE))
        score_matrix = jnp.where(allowed[None, None], score_matrix, MASKED)
        probability_gathered = jax.nn.softmax(score_matrix, axis=-1)
        attended_values = jnp.einsum('uzjq,quk->juzk', lowered_scores(probability_gathered), value_tile_rows, precision=MAXIMUM_PRECISE)
        return attended_values.reshape(block_rows, q_heads * head_dim)
    starts = jnp.arange(seq_len // block_rows, dtype=jnp.int32) * block_rows
    return lax.map(jax.checkpoint(one_block), starts).reshape(seq_len, q_heads * head_dim)

def reference(tokens, segments, routes, rank_order, attn_gain, w_query, w_key, w_value, w_output, ffn_gain, w_router, expert_in, expert_out, cotangent):
    block_count = SEQS * LEN // TOK_DEV
    destination, source = jax.vmap(partial(place_pairs, experts=EXPERTS, capacity=CAP))(routes.reshape(block_count, TOK_DEV, TOP), rank_order.reshape(block_count, TOK_DEV, TOP))
    positions = jnp.arange(LEN, dtype=jnp.int32)

    def forward(inputs, gain_one, query_w, key_w, value_w, out_w, gain_two, router_w, up_w, down_w):
        normed = lowered_scores(rms_norm(inputs, gain_one)).reshape(SEQS * LEN, D)
        query_pre = lowered_backward(jnp.dot(normed, query_w, precision=MAXIMUM_PRECISE)).reshape(SEQS, LEN, HEADS, HEAD)
        key_pre = lowered_backward(jnp.dot(normed, key_w, precision=MAXIMUM_PRECISE)).reshape(SEQS, LEN, KV_HEADS, HEAD)
        value_gathered = lowered_backward(lowered_scores(jnp.dot(normed, value_w, precision=MAXIMUM_PRECISE))).reshape(SEQS, LEN, KV_HEADS, HEAD)
        query_rows = lowered_scores(rotate(query_pre, positions))
        key_rows = lowered_scores(rotate(key_pre, positions))

        def per_sequence(pieces):
            return attend(pieces[0], pieces[1], pieces[2], pieces[3])
        attended_values = lax.map(jax.checkpoint(per_sequence), (query_rows, key_rows, value_gathered, segments))
        heads_out = lowered_backward(lowered_scores(attended_values.reshape(SEQS * LEN, D)))
        branch = lowered_backward(jnp.dot(heads_out, out_w, precision=MAXIMUM_PRECISE))
        residual = inputs.reshape(SEQS * LEN, D) + RESIDUAL_MULT * branch
        routed_in = lowered_scores(rms_norm(residual, gain_two))
        logits = lowered_backward(jnp.dot(routed_in, router_w, precision=MAXIMUM_PRECISE))
        picked = jnp.take_along_axis(logits, routes.reshape(SEQS * LEN, TOP), axis=1)
        gate_weights = jax.nn.softmax(picked, axis=1)

        def per_block(pieces):
            block_in, block_gates, block_dest, block_source = pieces
            extended = jnp.concatenate([block_in, jnp.zeros((1, D), jnp.float32)], axis=0)
            slot_rows = lowered_backward(extended[block_source // TOP].reshape(EXPERTS, CAP, D))
            gate_up = lowered_backward(jnp.einsum('ecd,edf->ecf', slot_rows, up_w, precision=MAXIMUM_PRECISE))
            hidden = lowered_scores(jax.nn.silu(gate_up[..., :FF]) * gate_up[..., FF:])
            expert_res = lowered_backward(lowered_scores(jnp.einsum('ecf,efd->ecd', hidden, down_w, precision=MAXIMUM_PRECISE)))
            flat_res = jnp.concatenate([expert_res.reshape(EXPERTS * CAP, D), jnp.zeros((1, D), jnp.float32)], axis=0)
            gathered = flat_res[block_dest]
            return lax.optimization_barrier(jnp.sum(block_gates[:, :, None] * gathered, axis=1))
        moe_out = lax.map(jax.checkpoint(per_block), (routed_in.reshape(block_count, TOK_DEV, D), gate_weights.reshape(block_count, TOK_DEV, TOP), destination, source))
        result = residual + RESIDUAL_MULT * moe_out.reshape(SEQS * LEN, D)
        return result.reshape(SEQS, LEN, D)
    output, pullback = jax.vjp(forward, tokens.astype(jnp.float32), attn_gain.astype(jnp.float32), w_query.astype(jnp.float32), w_key.astype(jnp.float32), w_value.astype(jnp.float32), w_output.astype(jnp.float32), ffn_gain.astype(jnp.float32), w_router.astype(jnp.float32), expert_in.astype(jnp.float32), expert_out.astype(jnp.float32))
    gradients = pullback(cotangent.astype(jnp.float32))
    return (output.astype(jnp.bfloat16), gradients[0].astype(jnp.bfloat16), gradients[1], gradients[2], gradients[3], gradients[4], gradients[5], gradients[6], gradients[7], gradients[8], gradients[9])
```

```python
import functools
import math

import jax
import jax.numpy as jnp
from jax import lax
from jax.experimental import pallas as pl
from jax.experimental.pallas import tpu as pltpu
from jax.sharding import PartitionSpec as P

HEADS = 16
KV_HEADS = 8
HEAD = 64
WINDOW = 1024


EPSILON = 1e-06
ATTENTION_FACTOR = 0.015625
RESIDUAL_MULT = 0.22
ROPE_BASE = 10000.0
MASKED = -1e30


def from_behind(value, axis, steps):
    count = lax.axis_size(axis)
    initial, last = (max(0, -steps), min(count, count - steps))
    return lax.ppermute(value, axis, [(source, source + steps) for source in range(initial, last)])


def product(left_side, right_side):
    return jnp.dot(left_side, right_side, preferred_element_type=jnp.float32)


def inner_rows(left_side, right_side):
    return jnp.einsum("ta,tb->ab", left_side, right_side, preferred_element_type=jnp.float32)


def product_back(left_side, right_side):
    return jnp.einsum("tb,ab->ta", left_side, right_side, preferred_element_type=jnp.float32)


def rope_tables(positions, head_dim):
    half_dim = head_dim // 2
    frequency = jnp.exp(
        jnp.arange(half_dim, dtype=jnp.float32) * (-2.0 * math.log(ROPE_BASE) / head_dim)
    )
    angles = positions.astype(jnp.float32)[:, None] * frequency[None, :]
    return (jnp.cos(angles)[:, None, :], jnp.sin(angles)[:, None, :])


def rotate(values, cosine, sine_part):
    half_dim = values.shape[-1] // 2
    first_half = values[..., :half_dim]
    second_half = values[..., half_dim:]
    return jnp.concatenate(
        [
            first_half * cosine - second_half * sine_part,
            second_half * cosine + first_half * sine_part,
        ],
        axis=-1,
    )


def unrotate(values, cosine, sine_part):
    half_dim = values.shape[-1] // 2
    first_half = values[..., :half_dim]
    second_half = values[..., half_dim:]
    return jnp.concatenate(
        [
            first_half * cosine + second_half * sine_part,
            second_half * cosine - first_half * sine_part,
        ],
        axis=-1,
    )


MESH = pl.DeviceIdType.MESH
CAPACITY = 80
BLOCK = 256
HALF = 128
QUARTER = 64
WIDTH = 1024
INNER = 512
PLANE = 16
GROUP = 4
BF = jnp.bfloat16
F32 = jnp.float32


def mod4(value):
    return lax.rem(value + 8, 4)


def plane_id(part, first, second):
    return first * 4 + second if part == 0 else second * 4 + first


def plane_coords(part):
    index = lax.axis_index("grp")
    row, column = index // 4, lax.rem(index, 4)
    return (row, column) if part == 0 else (column, row)


def plane_copy(source, target, send_sem, recv_sem, index):
    return pltpu.make_async_remote_copy(
        src_ref=source,
        dst_ref=target,
        send_sem=send_sem,
        recv_sem=recv_sem,
        device_id={"grp": index},
        device_id_type=MESH,
    )


def greet_plane():
    row, column = plane_coords(0)
    barrier = pltpu.get_barrier_semaphore()
    for index in (
        mod4(row + 1) * 4 + column,
        mod4(row - 1) * 4 + column,
        row * 4 + mod4(column + 1),
        row * 4 + mod4(column - 1),
    ):
        pl.semaphore_signal(barrier, inc=1, device_id={"grp": index}, device_id_type=MESH)
    pl.semaphore_wait(barrier, 4)


class PlaneGather:
    order = {0: 0, -1: 1, 1: 2, 2: 3}

    def __init__(self, part, blocks, send_sems, recv_sems):
        self.part, self.blocks = part, blocks
        self.send_sems, self.recv_sems = send_sems, recv_sems
        self.first, self.second = plane_coords(part)
        self.started = []

    def ref(self, da, db, half=None):
        index = plane_id(self.part, mod4(self.first + da), mod4(self.second + db))
        begin = self.part * HALF
        if half is None:
            return self.blocks.at[index, pl.ds(begin, HALF)]
        return self.blocks.at[index, pl.ds(begin + half * QUARTER, QUARTER)]

    def copy(self, da, db, half, axis, step, slot):
        if axis == 0:
            to = plane_id(self.part, mod4(self.first + step), self.second)
        else:
            to = plane_id(self.part, self.first, mod4(self.second + step))
        ref, sem = self.ref(da, db, half), self.part * 20 + slot
        return plane_copy(ref, ref, self.send_sems.at[sem], self.recv_sems.at[sem], to)

    def send(self, *where):
        self.copy(*where).start()
        self.started.append(where)

    def wait(self, da, db, half, slot):
        ref, sem = self.ref(da, db, half), self.part * 20 + slot
        plane_copy(
            ref, ref, self.send_sems.at[sem], self.recv_sems.at[sem],
            plane_id(self.part, self.first, self.second),
        ).wait_recv()

    def begin(self):
        self.send(0, 0, None, 0, 1, 0)
        self.send(0, 0, None, 0, -1, 1)

    def spread(self, da):
        slot = 4 + 4 * self.order[da]
        self.send(da, 0, None, 1, 1, slot)
        self.send(da, 0, None, 1, -1, slot + 1)

    def forward_first(self):
        self.wait(-1, 0, None, 0)
        self.send(-1, 0, 0, 0, 1, 2)
        self.wait(1, 0, None, 1)
        self.send(1, 0, 1, 0, -1, 3)

    def forward_second(self, da):
        slot = 4 + 4 * self.order[da]
        self.wait(da, -1, None, slot)
        self.send(da, -1, 0, 1, 1, slot + 2)
        self.wait(da, 1, None, slot + 1)
        self.send(da, 1, 1, 1, -1, slot + 3)

    def wait_far_first(self):
        self.wait(2, 0, 0, 2)
        self.wait(2, 0, 1, 3)

    def wait_far_second(self, da):
        slot = 4 + 4 * self.order[da]
        self.wait(da, 2, 0, slot + 2)
        self.wait(da, 2, 1, slot + 3)

    def finish(self):
        for where in self.started:
            self.copy(*where).wait_send()


class PlaneReduce:
    order = {2: 0, 1: 1, -1: 2, 0: 3}

    def __init__(self, part, partial, buffers, send_sems, recv_sems, total):
        self.part, self.partial, self.total = part, partial, total
        self.far, self.near, self.summed, self.far_two, self.near_two = buffers
        self.send_sems, self.recv_sems = send_sems, recv_sems
        self.first, self.second = plane_coords(part)
        self.started = []

    def ref(self, da, db, half=None):
        index = plane_id(self.part, mod4(self.first + da), mod4(self.second + db))
        begin = self.part * HALF
        if half is None:
            return self.partial.at[index, pl.ds(begin, HALF)]
        return self.partial.at[index, pl.ds(begin + half * QUARTER, QUARTER)]

    def send(self, source, target, axis, step, slot):
        if axis == 0:
            to = plane_id(self.part, mod4(self.first + step), self.second)
        else:
            to = plane_id(self.part, self.first, mod4(self.second + step))
        sem = self.part * 20 + slot
        copy = plane_copy(source, target, self.send_sems.at[sem], self.recv_sems.at[sem], to)
        copy.start()
        self.started.append(copy)

    def wait(self, target, slot):
        sem = self.part * 20 + slot
        plane_copy(
            target, target, self.send_sems.at[sem], self.recv_sems.at[sem],
            plane_id(self.part, self.first, self.second),
        ).wait_recv()

    def add(self, target, source):
        target[...] = (target[...].astype(F32) + source[...].astype(F32)).astype(BF)

    def step_far(self, da):
        part, place = self.part, self.order[da]
        self.send(self.ref(da, 2, 0), self.far.at[part, place, 0], 1, 1, 4 * place)
        self.send(self.ref(da, 2, 1), self.far.at[part, place, 1], 1, -1, 4 * place + 1)

    def step_near(self, da):
        part, place = self.part, self.order[da]
        self.wait(self.far.at[part, place, 0], 4 * place)
        self.add(self.ref(da, 1, 0), self.far.at[part, place, 0])
        self.send(self.ref(da, 1), self.near.at[part, place, 0], 1, 1, 4 * place + 2)
        self.wait(self.far.at[part, place, 1], 4 * place + 1)
        self.add(self.ref(da, -1, 1), self.far.at[part, place, 1])
        self.send(self.ref(da, -1), self.near.at[part, place, 1], 1, -1, 4 * place + 3)

    def step_sum(self, da):
        part, place = self.part, self.order[da]
        self.wait(self.near.at[part, place, 0], 4 * place + 2)
        self.wait(self.near.at[part, place, 1], 4 * place + 3)
        value = (
            self.ref(da, 0)[...].astype(F32)
            + self.near[part, place, 0].astype(F32)
            + self.near[part, place, 1].astype(F32)
        )
        rows = pl.ds(part * HALF, HALF)
        if da == 0:
            self.total[rows] = value
            self.wait(self.near_two.at[part, 0], 18)
            self.wait(self.near_two.at[part, 1], 19)
            self.total[rows] += self.near_two[part, 0].astype(F32) + self.near_two[part, 1].astype(F32)
            return
        self.summed[part, place] = value.astype(BF)
        lower, upper = pl.ds(0, QUARTER), pl.ds(QUARTER, QUARTER)
        if da == 2:
            self.send(self.summed.at[part, 0, lower], self.far_two.at[part, 0], 0, 1, 16)
            self.send(self.summed.at[part, 0, upper], self.far_two.at[part, 1], 0, -1, 17)
        if da == 1:
            self.wait(self.far_two.at[part, 0], 16)
            self.add(self.summed.at[part, 1, lower], self.far_two.at[part, 0])
            self.send(self.summed.at[part, 1], self.near_two.at[part, 0], 0, 1, 18)
        if da == -1:
            self.wait(self.far_two.at[part, 1], 17)
            self.add(self.summed.at[part, 2, upper], self.far_two.at[part, 1])
            self.send(self.summed.at[part, 2], self.near_two.at[part, 1], 0, -1, 19)

    def finish(self):
        for copy in self.started:
            copy.wait_send()


def reduce_buffers():
    return [
        pltpu.VMEM((2, 4, 2, QUARTER, WIDTH), BF),
        pltpu.VMEM((2, 4, 2, HALF, WIDTH), BF),
        pltpu.VMEM((2, 3, HALF, WIDTH), BF),
        pltpu.VMEM((2, 2, QUARTER, WIDTH), BF),
        pltpu.VMEM((2, 2, HALF, WIDTH), BF),
    ]


def run_reduce(reducers):
    for da in (2, 1, -1, 0):
        for reducer in reducers:
            reducer.step_far(da)
    for da in (2, 1, -1, 0):
        for reducer in reducers:
            reducer.step_near(da)
    for da in (2, 1, -1, 0):
        for reducer in reducers:
            reducer.step_sum(da)
    for reducer in reducers:
        reducer.finish()


def gather_kernel(own_ref, out_ref, blocks, send_sems, recv_sems, local_sem):
    greet_plane()
    blocks[lax.axis_index("grp")] = own_ref[...]
    gathers = [PlaneGather(part, blocks, send_sems, recv_sems) for part in (0, 1)]
    for gather in gathers:
        gather.begin()
    for gather in gathers:
        gather.spread(0)
    for gather in gathers:
        gather.forward_first()
        gather.spread(-1)
        gather.spread(1)
    for gather in gathers:
        gather.forward_second(0)
    for gather in gathers:
        gather.wait_far_first()
        gather.spread(2)
    for da in (-1, 1, 2):
        for gather in gathers:
            gather.forward_second(da)
    for da in (0, -1, 1, 2):
        for gather in gathers:
            gather.wait_far_second(da)
    for gather in gathers:
        gather.finish()
    copy = pltpu.make_async_copy(blocks, out_ref, local_sem)
    copy.start()
    copy.wait()


def gather_plane(own):
    return pl.pallas_call(
        gather_kernel,
        out_shape=jax.ShapeDtypeStruct((PLANE, BLOCK, WIDTH), BF),
        in_specs=[pl.BlockSpec(memory_space=pltpu.VMEM)],
        out_specs=pl.BlockSpec(memory_space=pl.ANY),
        scratch_shapes=[
            pltpu.VMEM((PLANE, BLOCK, WIDTH), BF),
            pltpu.SemaphoreType.DMA((40,)),
            pltpu.SemaphoreType.DMA((40,)),
            pltpu.SemaphoreType.DMA,
        ],
        compiler_params=pltpu.CompilerParams(
            collective_id=0, has_side_effects=True, vmem_limit_bytes=58 << 20
        ),
    )(own)


def reduce_kernel(partial_ref, out_ref, partial, far, near, summed, far_two, near_two, send_sems, recv_sems, local_sem):
    copy = pltpu.make_async_copy(partial_ref, partial, local_sem)
    copy.start()
    greet_plane()
    copy.wait()
    buffers = (far, near, summed, far_two, near_two)
    run_reduce([PlaneReduce(part, partial, buffers, send_sems, recv_sems, out_ref) for part in (0, 1)])


def reduce_plane(partial):
    return pl.pallas_call(
        reduce_kernel,
        out_shape=jax.ShapeDtypeStruct((BLOCK, WIDTH), F32),
        in_specs=[pl.BlockSpec(memory_space=pl.ANY)],
        out_specs=pl.BlockSpec(memory_space=pltpu.VMEM),
        scratch_shapes=[pltpu.VMEM((PLANE, BLOCK, WIDTH), BF)]
        + reduce_buffers()
        + [
            pltpu.SemaphoreType.DMA((40,)),
            pltpu.SemaphoreType.DMA((40,)),
            pltpu.SemaphoreType.DMA,
        ],
        compiler_params=pltpu.CompilerParams(
            collective_id=1, has_side_effects=True, vmem_limit_bytes=58 << 20
        ),
    )(partial)


def dot_tn(left, right):
    return lax.dot_general(left, right, (((0,), (0,)), ((), ())), preferred_element_type=F32)


def dot_nt(left, right):
    return lax.dot_general(left, right, (((1,), (1,)), ((), ())), preferred_element_type=F32)


def dot_nn(left, right):
    return lax.dot_general(left, right, (((1,), (0,)), ((), ())), preferred_element_type=F32)


def expert_kernel(
    rows_ref,
    meta_ref,
    cot_ref,
    w_in_ref,
    w_out_ref,
    row_total_ref,
    score_out_ref,
    moe_ref,
    d_in_ref,
    d_out_ref,
    blocks,
    meta_in,
    score_send,
    cots,
    w_in,
    w_out,
    d_in,
    d_out,
    row_partial,
    moe_stage,
    picks,
    slot_rows,
    slot_cots,
    slot_grads,
    slot_res,
    slot_back,
    far,
    near,
    summed,
    far_two,
    near_two,
    send_sems,
    recv_sems,
    rsend_sems,
    rrecv_sems,
    meta_send,
    meta_recv,
    score_ssem,
    score_rsem,
    weight_send,
    weight_recv,
    local_sems,
    cot_sems,
    moe_sems,
):
    me = lax.axis_index("grp")
    core = lax.axis_index("exp")
    row, column = me // 4, lax.rem(me, 4)
    barrier = pltpu.get_barrier_semaphore()
    for step in range(1, PLANE):
        pl.semaphore_signal(
            barrier, inc=1, device_id={"grp": lax.rem(me + step, PLANE)}, device_id_type=MESH
        )
    pl.semaphore_signal(barrier, inc=1, device_id={"exp": 1 - core}, device_id_type=MESH)

    load_in = pltpu.make_async_copy(w_in_ref, w_in.at[core], local_sems.at[0])
    load_out = pltpu.make_async_copy(w_out_ref, w_out.at[core], local_sems.at[1])
    load_in.start()
    load_out.start()
    blocks[me] = rows_ref[...]
    meta_in[me] = meta_ref[me]
    d_in[...] = jnp.zeros_like(d_in)
    d_out[...] = jnp.zeros_like(d_out)

    def cot_copy(group, j):
        shift = group + group // 2 - 2 * (group // 3)
        index = mod4(row + j) * 4 + mod4(column + shift)
        return pltpu.make_async_copy(
            cot_ref.at[index], cots.at[lax.rem(group, 2), j], cot_sems.at[lax.rem(group, 2), j]
        )

    for j in range(GROUP):
        cot_copy(0, j).start()
    pl.semaphore_wait(barrier, PLANE)

    gathers = [PlaneGather(part, blocks, send_sems, recv_sems) for part in (0, 1)]
    for gather in gathers:
        gather.begin()
    for gather in gathers:
        gather.spread(0)
    meta_copies = []
    for step in range(1, PLANE):
        to = lax.rem(me + step, PLANE)
        copy = plane_copy(
            meta_ref.at[to], meta_in.at[me], meta_send.at[step], meta_recv.at[step], to
        )
        copy.start()
        meta_copies.append(copy)
    weight_copies = []
    for slot, (source, target) in enumerate(((w_in_ref, w_in), (w_out_ref, w_out))):
        copy = pltpu.make_async_remote_copy(
            src_ref=source,
            dst_ref=target.at[core],
            send_sem=weight_send.at[slot],
            recv_sem=weight_recv.at[slot],
            device_id={"exp": 1 - core},
            device_id_type=MESH,
        )
        copy.start()
        weight_copies.append(copy)
    load_in.wait()
    load_out.wait()
    for copy in weight_copies:
        copy.wait()
    for copy in meta_copies:
        copy.wait()
    for gather in gathers:
        gather.forward_first()
        gather.spread(-1)
        gather.spread(1)
    gathers[1].forward_second(0)
    for gather in gathers:
        gather.wait_far_first()
        gather.spread(2)
    gathers[1].wait_far_second(0)

    def moe_copy(j, index):
        return pltpu.make_async_copy(moe_stage.at[j], moe_ref.at[index], moe_sems.at[j])

    @pl.loop(0, 4)
    def _(group):
        shift = group + group // 2 - 2 * (group // 3)
        place = mod4(column + shift)
        parity = lax.rem(group, 2)

        @pl.when(group == 0)
        def _():
            gathers[0].forward_second(0)
            gathers[0].forward_second(-1)
            gathers[0].forward_second(1)
            gathers[0].forward_second(2)
            gathers[1].forward_second(-1)
            gathers[1].forward_second(1)

        @pl.when(group == 1)
        def _():
            gathers[1].wait_far_second(1)
            gathers[1].wait_far_second(-1)
            gathers[1].forward_second(2)

        @pl.when(group == 2)
        def _():
            for da in (0, -1, 1, 2):
                gathers[0].wait_far_second(da)
            gathers[1].wait_far_second(2)

        @pl.when(group < 3)
        def _():
            for j in range(GROUP):
                cot_copy(group + 1, j).start()

        for j in range(GROUP):
            cot_copy(group, j).wait()

        for expert in range(2):
            gates = []
            for j in range(GROUP):
                index = mod4(row + j) * 4 + place
                slots = meta_in[index, pl.ds(expert, 1), :]
                gate_row = meta_in[index, pl.ds(2 + expert, 1), :]
                slot_id = lax.broadcasted_iota(jnp.int32, (CAPACITY, BLOCK), 0).astype(F32)
                hit = slot_id == slots
                pick = jnp.where(hit, 1.0, 0.0).astype(BF)
                gate = jnp.sum(jnp.where(hit, gate_row, 0.0), axis=1, keepdims=True)
                gates.append(gate)
                here = pl.ds(j * CAPACITY, CAPACITY)
                picks[j, pl.ds(expert * CAPACITY, CAPACITY), :] = pick
                slot_rows[here, :] = dot_nn(pick, blocks[index]).astype(BF)
                cot_rows = dot_nn(pick, cots[parity, j])
                slot_cots[here, :] = cot_rows.astype(BF)
                slot_grads[here, :] = (gate * (RESIDUAL_MULT * cot_rows)).astype(BF)
            gate = jnp.concatenate(gates, axis=0)
            gate_up = dot_nn(slot_rows[...], w_in[expert])
            gate_half, up_half = gate_up[:, :INNER], gate_up[:, INNER:]
            sigmoid = jax.nn.sigmoid(gate_half)
            activated = gate_half * sigmoid
            hidden = (activated * up_half).astype(BF)
            result = dot_nn(hidden, w_out[expert]).astype(BF).astype(F32)
            scored = RESIDUAL_MULT * jnp.sum(
                slot_cots[...].astype(F32) * result, axis=1, keepdims=True
            )
            slot_res[expert] = (gate * result).astype(BF)
            hidden_grad = dot_nt(slot_grads[...], w_out[expert])
            gate_part = hidden_grad * up_half * sigmoid * (1.0 + gate_half * (1.0 - sigmoid))
            up_part = hidden_grad * activated
            pair_grad = jnp.concatenate([gate_part.astype(BF), up_part.astype(BF)], axis=1)
            slot_back[expert] = dot_nt(pair_grad, w_in[expert]).astype(BF)
            d_out[expert] += dot_tn(hidden, slot_grads[...])
            d_in[expert] += dot_tn(slot_rows[...], pair_grad)
            for j in range(GROUP):
                index = mod4(row + j) * 4 + place
                pick = picks[j, pl.ds(expert * CAPACITY, CAPACITY), :].astype(F32)
                spread = jnp.sum(
                    pick * scored[j * CAPACITY : (j + 1) * CAPACITY], axis=0, keepdims=True
                )
                score_send[index, pl.ds(expert, 1), :] = spread

        for j in range(GROUP):
            index = mod4(row + j) * 4 + place
            here = pl.ds(j * CAPACITY, CAPACITY)
            pick = picks[j]

            @pl.when(group > 0)
            def _():
                moe_copy(j, index).wait()

            values = jnp.concatenate([slot_res[0, here, :], slot_res[1, here, :]], axis=0)
            moe_stage[j] = dot_tn(pick, values).astype(BF)
            moe_copy(j, index).start()
            values = jnp.concatenate([slot_back[0, here, :], slot_back[1, here, :]], axis=0)
            row_partial[index] = dot_tn(pick, values).astype(BF)

    for gather in gathers:
        gather.finish()
    reducers = [
        PlaneReduce(
            part, row_partial, (far, near, summed, far_two, near_two), rsend_sems, rrecv_sems, row_total_ref
        )
        for part in (0, 1)
    ]
    for da in (2, 1, -1, 0):
        for reducer in reducers:
            reducer.step_far(da)
    score_out_ref[me] = score_send[me]
    score_copies = []
    for step in range(1, PLANE):
        to = lax.rem(me + step, PLANE)
        copy = plane_copy(
            score_send.at[to], score_out_ref.at[me], score_ssem.at[step], score_rsem.at[step], to
        )
        copy.start()
        score_copies.append(copy)
    store_in = pltpu.make_async_copy(d_in, d_in_ref, local_sems.at[0])
    store_out = pltpu.make_async_copy(d_out, d_out_ref, local_sems.at[1])
    store_in.start()
    store_out.start()
    for da in (2, 1, -1, 0):
        for reducer in reducers:
            reducer.step_near(da)
    for da in (2, 1, -1, 0):
        for reducer in reducers:
            reducer.step_sum(da)
    for reducer in reducers:
        reducer.finish()
    for copy in score_copies:
        copy.wait()
    for j in range(GROUP):
        moe_copy(j, j).wait()
    store_in.wait()
    store_out.wait()


def run_experts(rows, meta, cots, expert_in, expert_out):
    vmem = pl.BlockSpec(memory_space=pltpu.VMEM)
    hbm = pl.BlockSpec(memory_space=pl.ANY)
    dma = pltpu.SemaphoreType.DMA
    slots = GROUP * CAPACITY
    return pl.pallas_call(
        expert_kernel,
        out_shape=(
            jax.ShapeDtypeStruct((BLOCK, WIDTH), F32),
            jax.ShapeDtypeStruct((PLANE, 8, BLOCK), F32),
            jax.ShapeDtypeStruct((PLANE, BLOCK, WIDTH), BF),
            jax.ShapeDtypeStruct((2, WIDTH, 2 * INNER), F32),
            jax.ShapeDtypeStruct((2, INNER, WIDTH), F32),
        ),
        in_specs=[vmem, vmem, hbm, hbm, hbm],
        out_specs=(vmem, vmem, hbm, hbm, hbm),
        scratch_shapes=[
            pltpu.VMEM((PLANE, BLOCK, WIDTH), BF),
            pltpu.VMEM((PLANE, 8, BLOCK), F32),
            pltpu.VMEM((PLANE, 8, BLOCK), F32),
            pltpu.VMEM((2, GROUP, BLOCK, WIDTH), BF),
            pltpu.VMEM((2, WIDTH, 2 * INNER), BF),
            pltpu.VMEM((2, INNER, WIDTH), BF),
            pltpu.VMEM((2, WIDTH, 2 * INNER), F32),
            pltpu.VMEM((2, INNER, WIDTH), F32),
            pltpu.VMEM((PLANE, BLOCK, WIDTH), BF),
            pltpu.VMEM((GROUP, BLOCK, WIDTH), BF),
            pltpu.VMEM((GROUP, 2 * CAPACITY, BLOCK), BF),
            pltpu.VMEM((slots, WIDTH), BF),
            pltpu.VMEM((slots, WIDTH), BF),
            pltpu.VMEM((slots, WIDTH), BF),
            pltpu.VMEM((2, slots, WIDTH), BF),
            pltpu.VMEM((2, slots, WIDTH), BF),
        ]
        + reduce_buffers()
        + [dma((40,))] * 4
        + [dma((PLANE,))] * 4
        + [dma((2,))] * 3
        + [dma((2, GROUP)), dma((GROUP,))],
        compiler_params=pltpu.CompilerParams(
            collective_id=2, has_side_effects=True, vmem_limit_bytes=VMEM_LIMIT
        ),
    )(rows, meta, cots, expert_in, expert_out)


VMEM_LIMIT = 63 << 20


def place_slots(route_ids, rank_ids, experts):
    tok_rows, top_count = route_ids.shape
    hits = route_ids[:, :, None] == jnp.arange(experts, dtype=jnp.int32)
    rank_of = jnp.sum(jnp.where(hits, rank_ids[:, :, None] + 1, 0), axis=1) - 1
    chosen = rank_of >= 0
    ranks = jnp.arange(top_count, dtype=jnp.int32)
    counts = (rank_of[:, None, :] == ranks[None, :, None]).reshape(tok_rows, top_count * experts)
    lowered = counts.astype(BF)
    tok = jnp.arange(tok_rows, dtype=jnp.int32)
    earlier = (tok[:, None] > tok[None, :]).astype(BF)
    before = product(earlier, lowered)
    totals = jnp.sum(counts.astype(F32), axis=0).reshape(top_count, experts)
    offsets = (jnp.cumsum(totals, axis=0) - totals).reshape(1, top_count * experts)
    place = jnp.where(counts, before + offsets, 0.0).reshape(tok_rows, top_count, experts)
    return chosen, jnp.sum(place, axis=1)


def on_device(
    tokens,
    segments,
    routes,
    rank_order,
    attn_gain,
    w_query,
    w_key,
    w_value,
    w_output,
    ffn_gain,
    w_router,
    expert_in,
    expert_out,
    cotangent,
):
    tok_rows = tokens.shape[1]
    model_width = tokens.shape[2]
    experts = w_router.shape[1]
    kv_width = w_key.shape[1]
    kv_heads = KV_HEADS
    head_dim = HEAD
    q_heads = HEADS
    group_size = q_heads // kv_heads
    blocks = lax.axis_size(("seq", "exp"))
    block_id = lax.axis_index(("seq", "exp"))
    hop_count = min(-(-WINDOW // tok_rows), blocks - 1)
    key_span = (hop_count + 1) * tok_rows
    inputs = tokens[0].astype(jnp.float32)
    seg_ids = segments[0]
    route_ids = routes[0]
    rank_ids = rank_order[0]
    positions = block_id * tok_rows + jnp.arange(tok_rows, dtype=jnp.int32)
    cosine, sine_part = rope_tables(positions, head_dim)
    scale_one = lax.rsqrt(jnp.mean(inputs * inputs, axis=-1, keepdims=True) + EPSILON)
    normed = (inputs * scale_one * attn_gain).astype(jnp.bfloat16)
    query_pre = product(normed, w_query).reshape(tok_rows, q_heads, head_dim)
    key_pre = product(normed, w_key).reshape(tok_rows, kv_heads, head_dim)
    value_own = product(normed, w_value).astype(jnp.bfloat16)
    query_rows = (
        rotate(query_pre, cosine, sine_part)
        .astype(jnp.bfloat16)
        .reshape(tok_rows, kv_heads, group_size, head_dim)
    )
    key_own = rotate(key_pre, cosine, sine_part).astype(jnp.bfloat16).reshape(tok_rows, kv_width)
    key_parts = [key_own]
    value_parts = [value_own]
    seg_parts = [seg_ids]
    for hop_index in range(1, hop_count + 1):
        key_far, value_far, seg_far = from_behind(
            (key_own, value_own, seg_ids), ("seq", "exp"), hop_index
        )
        key_parts.insert(0, key_far)
        value_parts.insert(0, value_far)
        seg_parts.insert(0, seg_far)
    key_gathered = jnp.concatenate(key_parts, axis=0).reshape(key_span, kv_heads, head_dim)
    value_gathered = jnp.concatenate(value_parts, axis=0).reshape(key_span, kv_heads, head_dim)
    seg_all = jnp.concatenate(seg_parts, axis=0)
    key_pos = (block_id - hop_count) * tok_rows + jnp.arange(key_span, dtype=jnp.int32)
    distance = positions[:, None] - key_pos[None, :]
    allowed = (
        (seg_ids[:, None] == seg_all[None, :])
        & (distance >= 0)
        & (distance < WINDOW)
        & (key_pos[None, :] >= 0)
    )

    def scores_of():
        raw_scores = ATTENTION_FACTOR * jnp.einsum(
            "dklp,okp->kldo", query_rows, key_gathered, preferred_element_type=jnp.float32
        )
        return jnp.where(allowed[None, None], raw_scores, MASKED)

    score_matrix = scores_of()
    top_score = jnp.max(score_matrix, axis=-1, keepdims=True)
    expsum = jnp.sum(jnp.exp(score_matrix - top_score), axis=-1, keepdims=True)
    probability_lowered = (jnp.exp(score_matrix - top_score) / expsum).astype(jnp.bfloat16)
    heads_out = (
        jnp.einsum(
            "uzjq,quk->juzk",
            probability_lowered,
            value_gathered,
            preferred_element_type=jnp.float32,
        )
        .astype(jnp.bfloat16)
        .reshape(tok_rows, model_width)
    )
    branch = product(heads_out, w_output)
    residual = inputs + RESIDUAL_MULT * branch
    scale_two = lax.rsqrt(jnp.mean(residual * residual, axis=-1, keepdims=True) + EPSILON)
    routed_in = (residual * scale_two * ffn_gain).astype(jnp.bfloat16)
    logits = product(routed_in, w_router)
    chosen, slot_place = place_slots(route_ids, rank_ids, experts)
    gates = jax.nn.softmax(jnp.where(chosen, logits, MASKED), axis=1)
    gates = jnp.where(chosen, gates, 0.0)
    kept_place = jnp.where(chosen & (slot_place < CAPACITY), slot_place, -1.0)
    meta = jnp.concatenate(
        [
            kept_place.T.reshape(PLANE, 2, tok_rows),
            gates.T.reshape(PLANE, 2, tok_rows),
            jnp.zeros((PLANE, 4, tok_rows), jnp.float32),
        ],
        axis=1,
    )
    cots = gather_plane(cotangent[0])
    expert_row_sum, scores, moe_partial, d_in, d_out = run_experts(
        routed_in, meta, cots, expert_in[0], expert_out[0]
    )
    moe_out = reduce_plane(moe_partial)
    output = (residual + RESIDUAL_MULT * moe_out).astype(jnp.bfloat16)[None]
    upstream = cotangent[0].astype(jnp.float32)
    core = lax.axis_index("exp")

    def pair_sum(value):
        other = lax.dynamic_index_in_dim(value, 1 - core, 0, keepdims=True).astype(jnp.bfloat16)
        own = lax.dynamic_index_in_dim(value, core, 0, keepdims=True)
        return own + lax.ppermute(other, "exp", [(0, 1), (1, 0)]).astype(jnp.float32)

    up_w_grad, down_w_grad = pair_sum(d_in), pair_sum(d_out)
    gate_grad = scores[:, :2, :].reshape(experts, tok_rows).T
    choice_grad = gates * (gate_grad - jnp.sum(gates * gate_grad, axis=1, keepdims=True))
    logit_grad = choice_grad.astype(jnp.bfloat16)
    router_w_grad = inner_rows(routed_in, logit_grad)
    routed_grad = product_back(logit_grad, w_router) + expert_row_sum
    normal_two = residual * scale_two
    ffn_gain_grad = jnp.sum(routed_grad * normal_two, axis=0)
    weighted_two = routed_grad * ffn_gain
    residual_grad = (
        upstream
        + scale_two * weighted_two
        - residual * scale_two**3 * jnp.mean(weighted_two * residual, axis=-1, keepdims=True)
    )
    branch_grad = (RESIDUAL_MULT * residual_grad).astype(jnp.bfloat16)
    out_w_grad = inner_rows(heads_out, branch_grad)
    head_gradient = (
        product_back(branch_grad, w_output)
        .astype(jnp.bfloat16)
        .reshape(tok_rows, kv_heads, group_size, head_dim)
    )
    score_matrix = scores_of()
    probs_full = jnp.exp(score_matrix - top_score) / expsum
    probability_lowered = probs_full.astype(jnp.bfloat16)
    prob_grad = jnp.einsum(
        "dklp,okp->kldo", head_gradient, value_gathered, preferred_element_type=jnp.float32
    )
    score_gradient = (
        probs_full * (prob_grad - jnp.sum(probs_full * prob_grad, axis=-1, keepdims=True))
    ).astype(jnp.bfloat16)
    queries_grad = ATTENTION_FACTOR * jnp.einsum(
        "uzjq,quk->juzk", score_gradient, key_gathered, preferred_element_type=jnp.float32
    )
    keys_grad_all = (
        ATTENTION_FACTOR
        * jnp.einsum(
            "ykze,zykm->eym", score_gradient, query_rows, preferred_element_type=jnp.float32
        )
    ).reshape(key_span, kv_width)
    values_grad_all = jnp.einsum(
        "ykze,zykm->eym", probability_lowered, head_gradient, preferred_element_type=jnp.float32
    ).reshape(key_span, kv_width)
    keys_grad = keys_grad_all[hop_count * tok_rows :]
    values_grad = values_grad_all[hop_count * tok_rows :]
    for hop_index in range(1, hop_count + 1):
        first_row = (hop_count - hop_index) * tok_rows
        key_back, value_back = (
            from_behind(
                keys_grad_all[first_row : first_row + tok_rows].astype(jnp.bfloat16),
                ("seq", "exp"),
                -hop_index,
            ).astype(jnp.float32),
            from_behind(
                values_grad_all[first_row : first_row + tok_rows].astype(jnp.bfloat16),
                ("seq", "exp"),
                -hop_index,
            ).astype(jnp.float32),
        )
        keys_grad = keys_grad + key_back
        values_grad = values_grad + value_back
    query_pre_grad = (
        unrotate(queries_grad.reshape(tok_rows, q_heads, head_dim), cosine, sine_part)
        .astype(jnp.bfloat16)
        .reshape(tok_rows, model_width)
    )
    key_pre_grad = (
        unrotate(keys_grad.reshape(tok_rows, kv_heads, head_dim), cosine, sine_part)
        .astype(jnp.bfloat16)
        .reshape(tok_rows, kv_width)
    )
    value_pre_grad = values_grad.astype(jnp.bfloat16)
    query_w_grad = inner_rows(normed, query_pre_grad)
    key_w_grad = inner_rows(normed, key_pre_grad)
    value_w_grad = inner_rows(normed, value_pre_grad)
    normed_grad = (
        product_back(query_pre_grad, w_query)
        + product_back(key_pre_grad, w_key)
        + product_back(value_pre_grad, w_value)
    )
    attn_gain_grad = jnp.sum(normed_grad * inputs * scale_one, axis=0)
    weighted_one = normed_grad * attn_gain
    input_grad = (
        residual_grad
        + scale_one * weighted_one
        - inputs * scale_one**3 * jnp.mean(weighted_one * inputs, axis=-1, keepdims=True)
    )
    up_total, down_total = (
        lax.psum(up_w_grad.astype(jnp.bfloat16), "seq").astype(jnp.float32),
        lax.psum(down_w_grad.astype(jnp.bfloat16), "seq").astype(jnp.float32),
    )
    gain_one_total, query_total, key_total, value_total, out_total, gain_two_total, router_total = (
        lax.psum(
            (
                attn_gain_grad,
                query_w_grad,
                key_w_grad,
                value_w_grad,
                out_w_grad,
                ffn_gain_grad,
                router_w_grad,
            ),
            ("seq", "grp", "exp"),
        )
    )
    return (
        output,
        input_grad.astype(jnp.bfloat16)[None],
        gain_one_total,
        query_total,
        key_total,
        value_total,
        out_total,
        gain_two_total,
        router_total,
        up_total,
        down_total,
    )


def solution(mesh):
    placed = (
        P("grp", ("seq", "exp"), None),
        P("grp", ("seq", "exp")),
        P("grp", ("seq", "exp"), None),
        P("grp", ("seq", "exp"), None),
        P(),
        P(),
        P(),
        P(),
        P(),
        P(),
        P(),
        P(("grp", "exp"), None, None),
        P(("grp", "exp"), None, None),
        P("grp", ("seq", "exp"), None),
    )
    return jax.shard_map(
        on_device,
        mesh=mesh,
        in_specs=placed,
        out_specs=(
            P("grp", ("seq", "exp"), None),
            P("grp", ("seq", "exp"), None),
            P(),
            P(),
            P(),
            P(),
            P(),
            P(),
            P(),
            P(("grp", "exp"), None, None),
            P(("grp", "exp"), None, None),
        ),
        check_vma=False,
    )
```

```python
import functools
import math

import jax
import jax.numpy as jnp
from jax import lax
from jax.experimental import pallas as pl
from jax.experimental.pallas import tpu as pltpu
from jax.sharding import PartitionSpec as P

HEADS = 16
KV_HEADS = 8
HEAD = 64
WINDOW = 1024


EPSILON = 1e-06
ATTENTION_FACTOR = 0.015625
RESIDUAL_MULT = 0.22
ROPE_BASE = 10000.0
MASKED = -1e30


def from_behind(value, axis, steps):
    count = lax.axis_size(axis)
    initial, last = (max(0, -steps), min(count, count - steps))
    return lax.ppermute(value, axis, [(source, source + steps) for source in range(initial, last)])


def product(left_side, right_side):
    return jnp.dot(left_side, right_side, preferred_element_type=jnp.float32)


def inner_rows(left_side, right_side):
    return jnp.einsum("ta,tb->ab", left_side, right_side, preferred_element_type=jnp.float32)


def product_back(left_side, right_side):
    return jnp.einsum("tb,ab->ta", left_side, right_side, preferred_element_type=jnp.float32)


def rope_tables(positions, head_dim):
    half_dim = head_dim // 2
    frequency = jnp.exp(
        jnp.arange(half_dim, dtype=jnp.float32) * (-2.0 * math.log(ROPE_BASE) / head_dim)
    )
    angles = positions.astype(jnp.float32)[:, None] * frequency[None, :]
    return (jnp.cos(angles)[:, None, :], jnp.sin(angles)[:, None, :])


def rotate(values, cosine, sine_part):
    half_dim = values.shape[-1] // 2
    first_half = values[..., :half_dim]
    second_half = values[..., half_dim:]
    return jnp.concatenate(
        [
            first_half * cosine - second_half * sine_part,
            second_half * cosine + first_half * sine_part,
        ],
        axis=-1,
    )


def unrotate(values, cosine, sine_part):
    half_dim = values.shape[-1] // 2
    first_half = values[..., :half_dim]
    second_half = values[..., half_dim:]
    return jnp.concatenate(
        [
            first_half * cosine + second_half * sine_part,
            second_half * cosine - first_half * sine_part,
        ],
        axis=-1,
    )


MESH = pl.DeviceIdType.MESH
CAPACITY = 80
BLOCK = 256
HALF = 128
QUARTER = 64
WIDTH = 1024
INNER = 512
PLANE = 16
GROUP = 4
BF = jnp.bfloat16
F32 = jnp.float32


def mod4(value):
    return lax.rem(value + 8, 4)


def plane_id(part, first, second):
    return first * 4 + second if part == 0 else second * 4 + first


def plane_coords(part):
    index = lax.axis_index("grp")
    row, column = index // 4, lax.rem(index, 4)
    return (row, column) if part == 0 else (column, row)


def plane_copy(source, target, send_sem, recv_sem, index):
    return pltpu.make_async_remote_copy(
        src_ref=source,
        dst_ref=target,
        send_sem=send_sem,
        recv_sem=recv_sem,
        device_id={"grp": index},
        device_id_type=MESH,
    )


def greet_plane():
    row, column = plane_coords(0)
    barrier = pltpu.get_barrier_semaphore()
    for index in (
        mod4(row + 1) * 4 + column,
        mod4(row - 1) * 4 + column,
        row * 4 + mod4(column + 1),
        row * 4 + mod4(column - 1),
    ):
        pl.semaphore_signal(barrier, inc=1, device_id={"grp": index}, device_id_type=MESH)
    pl.semaphore_wait(barrier, 4)


class PlaneGather:
    order = {0: 0, -1: 1, 1: 2, 2: 3}

    def __init__(self, part, blocks, send_sems, recv_sems):
        self.part, self.blocks = part, blocks
        self.send_sems, self.recv_sems = send_sems, recv_sems
        self.first, self.second = plane_coords(part)
        self.started = []

    def ref(self, da, db, half=None):
        index = plane_id(self.part, mod4(self.first + da), mod4(self.second + db))
        begin = self.part * HALF
        if half is None:
            return self.blocks.at[index, pl.ds(begin, HALF)]
        return self.blocks.at[index, pl.ds(begin + half * QUARTER, QUARTER)]

    def copy(self, da, db, half, axis, step, slot):
        if axis == 0:
            to = plane_id(self.part, mod4(self.first + step), self.second)
        else:
            to = plane_id(self.part, self.first, mod4(self.second + step))
        ref, sem = self.ref(da, db, half), self.part * 20 + slot
        return plane_copy(ref, ref, self.send_sems.at[sem], self.recv_sems.at[sem], to)

    def send(self, *where):
        self.copy(*where).start()
        self.started.append(where)

    def wait(self, da, db, half, slot):
        ref, sem = self.ref(da, db, half), self.part * 20 + slot
        plane_copy(
            ref, ref, self.send_sems.at[sem], self.recv_sems.at[sem],
            plane_id(self.part, self.first, self.second),
        ).wait_recv()

    def begin(self):
        self.send(0, 0, None, 0, 1, 0)
        self.send(0, 0, None, 0, -1, 1)

    def spread(self, da):
        slot = 4 + 4 * self.order[da]
        self.send(da, 0, None, 1, 1, slot)
        self.send(da, 0, None, 1, -1, slot + 1)

    def forward_first(self):
        self.wait(-1, 0, None, 0)
        self.send(-1, 0, 0, 0, 1, 2)
        self.wait(1, 0, None, 1)
        self.send(1, 0, 1, 0, -1, 3)

    def forward_second(self, da):
        slot = 4 + 4 * self.order[da]
        self.wait(da, -1, None, slot)
        self.send(da, -1, 0, 1, 1, slot + 2)
        self.wait(da, 1, None, slot + 1)
        self.send(da, 1, 1, 1, -1, slot + 3)

    def wait_far_first(self):
        self.wait(2, 0, 0, 2)
        self.wait(2, 0, 1, 3)

    def wait_far_second(self, da):
        slot = 4 + 4 * self.order[da]
        self.wait(da, 2, 0, slot + 2)
        self.wait(da, 2, 1, slot + 3)

    def finish(self):
        for where in self.started:
            self.copy(*where).wait_send()


class PlaneReduce:
    order = {2: 0, 1: 1, -1: 2, 0: 3}

    def __init__(self, part, partial, buffers, send_sems, recv_sems, total):
        self.part, self.partial, self.total = part, partial, total
        self.far, self.near, self.summed, self.far_two, self.near_two = buffers
        self.send_sems, self.recv_sems = send_sems, recv_sems
        self.first, self.second = plane_coords(part)
        self.started = []

    def ref(self, da, db, half=None):
        index = plane_id(self.part, mod4(self.first + da), mod4(self.second + db))
        begin = self.part * HALF
        if half is None:
            return self.partial.at[index, pl.ds(begin, HALF)]
        return self.partial.at[index, pl.ds(begin + half * QUARTER, QUARTER)]

    def send(self, source, target, axis, step, slot):
        if axis == 0:
            to = plane_id(self.part, mod4(self.first + step), self.second)
        else:
            to = plane_id(self.part, self.first, mod4(self.second + step))
        sem = self.part * 20 + slot
        copy = plane_copy(source, target, self.send_sems.at[sem], self.recv_sems.at[sem], to)
        copy.start()
        self.started.append(copy)

    def wait(self, target, slot):
        sem = self.part * 20 + slot
        plane_copy(
            target, target, self.send_sems.at[sem], self.recv_sems.at[sem],
            plane_id(self.part, self.first, self.second),
        ).wait_recv()

    def add(self, target, source):
        target[...] = (target[...].astype(F32) + source[...].astype(F32)).astype(BF)

    def step_far(self, da):
        part, place = self.part, self.order[da]
        self.send(self.ref(da, 2, 0), self.far.at[part, place, 0], 1, 1, 4 * place)
        self.send(self.ref(da, 2, 1), self.far.at[part, place, 1], 1, -1, 4 * place + 1)

    def step_near(self, da):
        part, place = self.part, self.order[da]
        self.wait(self.far.at[part, place, 0], 4 * place)
        self.add(self.ref(da, 1, 0), self.far.at[part, place, 0])
        self.send(self.ref(da, 1), self.near.at[part, place, 0], 1, 1, 4 * place + 2)
        self.wait(self.far.at[part, place, 1], 4 * place + 1)
        self.add(self.ref(da, -1, 1), self.far.at[part, place, 1])
        self.send(self.ref(da, -1), self.near.at[part, place, 1], 1, -1, 4 * place + 3)

    def step_sum(self, da):
        part, place = self.part, self.order[da]
        self.wait(self.near.at[part, place, 0], 4 * place + 2)
        self.wait(self.near.at[part, place, 1], 4 * place + 3)
        value = (
            self.ref(da, 0)[...].astype(F32)
            + self.near[part, place, 0].astype(F32)
            + self.near[part, place, 1].astype(F32)
        )
        rows = pl.ds(part * HALF, HALF)
        if da == 0:
            self.total[rows] = value
            self.wait(self.near_two.at[part, 0], 18)
            self.wait(self.near_two.at[part, 1], 19)
            self.total[rows] += self.near_two[part, 0].astype(F32) + self.near_two[part, 1].astype(F32)
            return
        self.summed[part, place] = value.astype(BF)
        lower, upper = pl.ds(0, QUARTER), pl.ds(QUARTER, QUARTER)
        if da == 2:
            self.send(self.summed.at[part, 0, lower], self.far_two.at[part, 0], 0, 1, 16)
            self.send(self.summed.at[part, 0, upper], self.far_two.at[part, 1], 0, -1, 17)
        if da == 1:
            self.wait(self.far_two.at[part, 0], 16)
            self.add(self.summed.at[part, 1, lower], self.far_two.at[part, 0])
            self.send(self.summed.at[part, 1], self.near_two.at[part, 0], 0, 1, 18)
        if da == -1:
            self.wait(self.far_two.at[part, 1], 17)
            self.add(self.summed.at[part, 2, upper], self.far_two.at[part, 1])
            self.send(self.summed.at[part, 2], self.near_two.at[part, 1], 0, -1, 19)

    def finish(self):
        for copy in self.started:
            copy.wait_send()


def reduce_buffers():
    return [
        pltpu.VMEM((2, 4, 2, QUARTER, WIDTH), BF),
        pltpu.VMEM((2, 4, 2, HALF, WIDTH), BF),
        pltpu.VMEM((2, 3, HALF, WIDTH), BF),
        pltpu.VMEM((2, 2, QUARTER, WIDTH), BF),
        pltpu.VMEM((2, 2, HALF, WIDTH), BF),
    ]


def run_reduce(reducers):
    for da in (2, 1, -1, 0):
        for reducer in reducers:
            reducer.step_far(da)
    for da in (2, 1, -1, 0):
        for reducer in reducers:
            reducer.step_near(da)
    for da in (2, 1, -1, 0):
        for reducer in reducers:
            reducer.step_sum(da)
    for reducer in reducers:
        reducer.finish()


def gather_kernel(own_ref, out_ref, blocks, send_sems, recv_sems, local_sem):
    greet_plane()
    blocks[lax.axis_index("grp")] = own_ref[...]
    gathers = [PlaneGather(part, blocks, send_sems, recv_sems) for part in (0, 1)]
    for gather in gathers:
        gather.begin()
    for gather in gathers:
        gather.spread(0)
    for gather in gathers:
        gather.forward_first()
        gather.spread(-1)
        gather.spread(1)
    for gather in gathers:
        gather.forward_second(0)
    for gather in gathers:
        gather.wait_far_first()
        gather.spread(2)
    for da in (-1, 1, 2):
        for gather in gathers:
            gather.forward_second(da)
    for da in (0, -1, 1, 2):
        for gather in gathers:
            gather.wait_far_second(da)
    for gather in gathers:
        gather.finish()
    copy = pltpu.make_async_copy(blocks, out_ref, local_sem)
    copy.start()
    copy.wait()


def gather_plane(own):
    return pl.pallas_call(
        gather_kernel,
        out_shape=jax.ShapeDtypeStruct((PLANE, BLOCK, WIDTH), BF),
        in_specs=[pl.BlockSpec(memory_space=pltpu.VMEM)],
        out_specs=pl.BlockSpec(memory_space=pl.ANY),
        scratch_shapes=[
            pltpu.VMEM((PLANE, BLOCK, WIDTH), BF),
            pltpu.SemaphoreType.DMA((40,)),
            pltpu.SemaphoreType.DMA((40,)),
            pltpu.SemaphoreType.DMA,
        ],
        compiler_params=pltpu.CompilerParams(
            collective_id=0, has_side_effects=True, vmem_limit_bytes=58 << 20
        ),
    )(own)


class RowRing:
    def __init__(self, summed, total, far, near, send_sems, recv_sems):
        self.summed, self.total, self.far, self.near = summed, total, far, near
        self.send_sems, self.recv_sems = send_sems, recv_sems
        self.me = lax.axis_index("seq")
        self.rows = summed.shape[0] // 4
        self.started = []

    def piece(self, ref, shift, half=None):
        begin = mod4(self.me + shift) * self.rows
        if half is None:
            return ref.at[pl.ds(begin, self.rows)]
        return ref.at[pl.ds(begin + half * (self.rows // 2), self.rows // 2)]

    def send(self, source, target, step, slot):
        copy = pltpu.make_async_remote_copy(
            src_ref=source,
            dst_ref=target,
            send_sem=self.send_sems.at[slot],
            recv_sem=self.recv_sems.at[slot],
            device_id={"seq": mod4(self.me + step)},
            device_id_type=MESH,
        )
        copy.start()
        self.started.append(copy)

    def wait(self, target, slot):
        pltpu.make_async_remote_copy(
            src_ref=target,
            dst_ref=target,
            send_sem=self.send_sems.at[slot],
            recv_sem=self.recv_sems.at[slot],
            device_id={"seq": self.me},
            device_id_type=MESH,
        ).wait_recv()

    def add(self, target, source):
        target[...] = (target[...].astype(F32) + source[...].astype(F32)).astype(BF)

    def step_far(self):
        self.send(self.piece(self.summed, 2, 0), self.far.at[0], 1, 0)
        self.send(self.piece(self.summed, 2, 1), self.far.at[1], -1, 1)

    def step_near(self):
        self.wait(self.far.at[0], 0)
        self.add(self.piece(self.summed, 1, 0), self.far.at[0])
        self.send(self.piece(self.summed, 1), self.near.at[0], 1, 2)
        self.wait(self.far.at[1], 1)
        self.add(self.piece(self.summed, -1, 1), self.far.at[1])
        self.send(self.piece(self.summed, -1), self.near.at[1], -1, 3)

    def step_sum(self):
        self.wait(self.near.at[0], 2)
        self.wait(self.near.at[1], 3)
        self.piece(self.total, 0)[...] = (
            self.piece(self.summed, 0)[...].astype(F32)
            + self.near[0].astype(F32)
            + self.near[1].astype(F32)
        ).astype(BF)
        own = self.piece(self.total, 0)
        self.send(own, own, 1, 4)
        self.send(own, own, -1, 5)

    def step_forward(self):
        self.wait(self.piece(self.total, -1), 4)
        half = self.piece(self.total, -1, 0)
        self.send(half, half, 1, 6)
        self.wait(self.piece(self.total, 1), 5)
        half = self.piece(self.total, 1, 1)
        self.send(half, half, -1, 7)

    def finish(self):
        self.wait(self.piece(self.total, 2, 0), 6)
        self.wait(self.piece(self.total, 2, 1), 7)
        for copy in self.started:
            copy.wait_send()


def return_kernel(
    partial_ref,
    grad_ref,
    out_ref,
    grad_total_ref,
    partial,
    far,
    near,
    summed,
    far_two,
    near_two,
    grads,
    grad_far,
    grad_near,
    send_sems,
    recv_sems,
    ring_send,
    ring_recv,
    local_sems,
):
    load_grads = pltpu.make_async_copy(grad_ref, grads, local_sems.at[0])
    load = pltpu.make_async_copy(partial_ref, partial, local_sems.at[1])
    load_grads.start()
    load.start()
    row, column = plane_coords(0)
    line = lax.axis_index("seq")
    barrier = pltpu.get_barrier_semaphore()
    for index in (
        mod4(row + 1) * 4 + column,
        mod4(row - 1) * 4 + column,
        row * 4 + mod4(column + 1),
        row * 4 + mod4(column - 1),
    ):
        pl.semaphore_signal(barrier, inc=1, device_id={"grp": index}, device_id_type=MESH)
    for step in (1, -1):
        pl.semaphore_signal(
            barrier, inc=1, device_id={"seq": mod4(line + step)}, device_id_type=MESH
        )
    pl.semaphore_wait(barrier, 6)
    buffers = (far, near, summed, far_two, near_two)
    reducers = [
        PlaneReduce(part, partial, buffers, send_sems, recv_sems, out_ref) for part in (0, 1)
    ]
    ring = RowRing(grads, grad_total_ref, grad_far, grad_near, ring_send, ring_recv)
    load_grads.wait()
    ring.step_far()
    load.wait()
    for da in (2, 1, -1, 0):
        for reducer in reducers:
            reducer.step_far(da)
    ring.step_near()
    for da in (2, 1, -1, 0):
        for reducer in reducers:
            reducer.step_near(da)
    ring.step_sum()
    for da in (2, 1, -1, 0):
        for reducer in reducers:
            reducer.step_sum(da)
    ring.step_forward()
    for reducer in reducers:
        reducer.finish()
    ring.finish()


def return_plane(partial, grads):
    dma = pltpu.SemaphoreType.DMA
    rows = grads.shape[0]
    vmem = pl.BlockSpec(memory_space=pltpu.VMEM)
    hbm = pl.BlockSpec(memory_space=pl.ANY)
    return pl.pallas_call(
        return_kernel,
        out_shape=(
            jax.ShapeDtypeStruct((BLOCK, WIDTH), F32),
            jax.ShapeDtypeStruct(grads.shape, BF),
        ),
        in_specs=[hbm, hbm],
        out_specs=(vmem, vmem),
        scratch_shapes=[pltpu.VMEM((PLANE, BLOCK, WIDTH), BF)]
        + reduce_buffers()
        + [
            pltpu.VMEM(grads.shape, BF),
            pltpu.VMEM((2, rows // 8, WIDTH), BF),
            pltpu.VMEM((2, rows // 4, WIDTH), BF),
            dma((40,)),
            dma((40,)),
            dma((8,)),
            dma((8,)),
            dma((2,)),
        ],
        compiler_params=pltpu.CompilerParams(
            collective_id=1, has_side_effects=True, vmem_limit_bytes=58 << 20
        ),
    )(partial, grads)


class CubeSum:
    def __init__(self, part, matrix, out, far, near, mid, low, send_sems, recv_sems):
        self.part, self.matrix, self.out = part, matrix, out
        self.far, self.near, self.mid, self.low = far, near, mid, low
        self.send_sems, self.recv_sems = send_sems, recv_sems
        line, plane = lax.axis_index("seq"), lax.axis_index("grp")
        coords = (line, plane // 4, lax.rem(plane, 4))
        self.coords = coords
        self.place = [coords[(part + level) % 3] for level in range(3)]
        self.started = []

    def device(self, level, step):
        axis = (self.part + level) % 3
        there = mod4(self.coords[axis] + step)
        if axis == 0:
            return {"seq": there}
        if axis == 1:
            return {"grp": there * 4 + self.coords[2]}
        return {"grp": self.coords[1] * 4 + there}

    def rows(self, level, shift):
        begin = 0
        for upper in range(level):
            begin = begin + self.place[upper] * (256 // 4**upper)
        return begin + mod4(self.place[level] + shift) * (256 // 4**level)

    def copy(self, source, target, level, step, slot):
        return pltpu.make_async_remote_copy(
            src_ref=source,
            dst_ref=target,
            send_sem=self.send_sems.at[self.part, slot],
            recv_sem=self.recv_sems.at[self.part, slot],
            device_id=self.device(level, step),
            device_id_type=MESH,
        )

    def send(self, source, target, level, step, slot):
        copy = self.copy(source, target, level, step, slot)
        copy.start()
        self.started.append(copy)

    def wait(self, target, slot):
        self.copy(target, target, 0, 0, slot).wait_recv()

    def add(self, target, *sources):
        value = target[...].astype(F32)
        for source in sources:
            value = value + source[...].astype(F32)
        target[...] = value.astype(BF)

    def step_far(self):
        begin = self.rows(0, 2)
        self.send(self.matrix.at[pl.ds(begin, 128)], self.far.at[0], 0, 1, 0)
        self.send(self.matrix.at[pl.ds(begin + 128, 128)], self.far.at[1], 0, -1, 1)

    def step_near(self):
        begin = self.rows(0, 1)
        self.wait(self.far.at[0], 0)
        self.add(self.matrix.at[pl.ds(begin, 128)], self.far.at[0])
        self.send(self.matrix.at[pl.ds(begin, 256)], self.near.at[0], 0, 1, 2)
        begin = self.rows(0, -1)
        self.wait(self.far.at[1], 1)
        self.add(self.matrix.at[pl.ds(begin + 128, 128)], self.far.at[1])
        self.send(self.matrix.at[pl.ds(begin, 256)], self.near.at[1], 0, -1, 3)

    def step_mid(self):
        self.wait(self.near.at[0], 2)
        self.wait(self.near.at[1], 3)
        self.add(self.matrix.at[pl.ds(self.rows(0, 0), 256)], self.near.at[0], self.near.at[1])
        for step in (1, 2, 3):
            self.send(
                self.matrix.at[pl.ds(self.rows(1, step), 64)], self.mid.at[step - 1], 1, step, 3 + step
            )

    def step_low(self):
        for step in (1, 2, 3):
            self.wait(self.mid.at[step - 1], 3 + step)
        self.add(
            self.matrix.at[pl.ds(self.rows(1, 0), 64)], self.mid.at[0], self.mid.at[1], self.mid.at[2]
        )
        for step in (1, 2, 3):
            self.send(
                self.matrix.at[pl.ds(self.rows(2, step), 16)], self.low.at[step - 1], 2, step, 6 + step
            )

    def step_done(self):
        for step in (1, 2, 3):
            self.wait(self.low.at[step - 1], 6 + step)
        own = self.rows(2, 0)
        value = self.matrix[pl.ds(own, 16), :].astype(F32)
        for step in (1, 2, 3):
            value = value + self.low[step - 1].astype(F32)
        self.out[pl.ds(own, 16), :] = value.astype(BF)
        ref = self.out.at[pl.ds(own, 16)]
        for step in (1, 2, 3):
            self.send(ref, ref, 2, step, 9 + step)

    def back_mid(self):
        for step in (1, 2, 3):
            self.wait(self.out.at[pl.ds(self.rows(2, -step), 16)], 9 + step)
        ref = self.out.at[pl.ds(self.rows(1, 0), 64)]
        for step in (1, 2, 3):
            self.send(ref, ref, 1, step, 12 + step)

    def back_near(self):
        for step in (1, 2, 3):
            self.wait(self.out.at[pl.ds(self.rows(1, -step), 64)], 12 + step)
        ref = self.out.at[pl.ds(self.rows(0, 0), 256)]
        self.send(ref, ref, 0, 1, 16)
        self.send(ref, ref, 0, -1, 17)
        self.share(0, 20)

    def back_far(self):
        begin = self.rows(0, -1)
        self.wait(self.out.at[pl.ds(begin, 256)], 16)
        ref = self.out.at[pl.ds(begin, 128)]
        self.send(ref, ref, 0, 1, 18)
        self.share(-1, 21)
        begin = self.rows(0, 1)
        self.wait(self.out.at[pl.ds(begin, 256)], 17)
        ref = self.out.at[pl.ds(begin + 128, 128)]
        self.send(ref, ref, 0, -1, 19)
        self.share(1, 22)

    def back_last(self):
        begin = self.rows(0, 2)
        self.wait(self.out.at[pl.ds(begin, 128)], 18)
        self.wait(self.out.at[pl.ds(begin + 128, 128)], 19)
        self.share(2, 23)

    def share_copy(self, shift, slot):
        ref = self.out.at[pl.ds(self.rows(0, shift), 256)]
        return pltpu.make_async_remote_copy(
            src_ref=ref,
            dst_ref=ref,
            send_sem=self.send_sems.at[self.part, slot],
            recv_sem=self.recv_sems.at[self.part, slot],
            device_id={"exp": 1 - lax.axis_index("exp")},
            device_id_type=MESH,
        )

    def share(self, shift, slot):
        copy = self.share_copy(shift, slot)
        copy.start()
        self.started.append(copy)

    def finish(self, other_out):
        for shift, slot in ((0, 20), (-1, 21), (1, 22), (2, 23)):
            ref = other_out.at[pl.ds(self.rows(0, shift), 256)]
            pltpu.make_async_remote_copy(
                src_ref=ref,
                dst_ref=ref,
                send_sem=self.send_sems.at[self.part, slot],
                recv_sem=self.recv_sems.at[self.part, slot],
                device_id={"exp": 1 - lax.axis_index("exp")},
                device_id_type=MESH,
            ).wait_recv()
        for copy in self.started:
            copy.wait_send()


SMALL_ROWS = 40


def total_kernel(
    mats_ref,
    small_ref,
    out_ref,
    small_out_ref,
    matrix,
    far,
    near,
    mid,
    low,
    arrived,
    small,
    small_first,
    send_sems,
    recv_sems,
    core_send,
    core_recv,
    small_send,
    small_recv,
):
    line, plane, core = lax.axis_index("seq"), lax.axis_index("grp"), lax.axis_index("exp")
    row, column = plane // 4, lax.rem(plane, 4)
    other = 1 - core
    places = (line, row, column)

    def neighbour(axis, step):
        if axis == 0:
            return {"seq": mod4(line + step)}
        if axis == 1:
            return {"grp": mod4(row + step) * 4 + column}
        return {"grp": row * 4 + mod4(column + step)}

    barrier = pltpu.get_barrier_semaphore()
    for axis in range(3):
        for step in (1, 2, 3):
            pl.semaphore_signal(
                barrier, inc=1, device_id=neighbour(axis, step), device_id_type=MESH
            )
    pl.semaphore_signal(barrier, inc=1, device_id={"exp": other}, device_id_type=MESH)
    pl.semaphore_wait(barrier, 10)

    def to_core(source, target, slot):
        return pltpu.make_async_remote_copy(
            src_ref=source,
            dst_ref=target,
            send_sem=core_send.at[slot],
            recv_sem=core_recv.at[slot],
            device_id={"exp": other},
            device_id_type=MESH,
        )

    own_small = pl.ds(core * SMALL_ROWS, SMALL_ROWS)
    core_copies = [to_core(mats_ref.at[other * 3 + part], arrived.at[part], part) for part in range(3)]
    core_copies.append(
        to_core(small_ref.at[pl.ds(other * SMALL_ROWS, SMALL_ROWS)], small_first, 3)
    )
    for copy in core_copies:
        copy.start()
    sums = [
        CubeSum(
            part,
            matrix.at[part],
            out_ref.at[core * 3 + part],
            far.at[part],
            near.at[part],
            mid.at[part],
            low.at[part],
            send_sems,
            recv_sems,
        )
        for part in range(3)
    ]
    for part in range(3):
        core_copies[part].wait()
        matrix[part] = (
            mats_ref[core * 3 + part].astype(F32) + arrived[part].astype(F32)
        ).astype(BF)
        sums[part].step_far()
    small_copies = []

    def small_step(axis):
        for step in (1, 2, 3):
            copy = pltpu.make_async_remote_copy(
                src_ref=small.at[axis, places[axis]],
                dst_ref=small.at[axis, places[axis]],
                send_sem=small_send.at[axis, step],
                recv_sem=small_recv.at[axis, step],
                device_id=neighbour(axis, step),
                device_id_type=MESH,
            )
            copy.start()
            small_copies.append(copy)

    def small_sum(axis):
        for step in (1, 2, 3):
            ref = small.at[axis, mod4(places[axis] - step)]
            pltpu.make_async_remote_copy(
                src_ref=ref,
                dst_ref=ref,
                send_sem=small_send.at[axis, step],
                recv_sem=small_recv.at[axis, step],
                device_id=neighbour(axis, step),
                device_id_type=MESH,
            ).wait_recv()
        return (small[axis, 0] + small[axis, 1]) + (small[axis, 2] + small[axis, 3])

    core_copies[3].wait()
    small[0, line] = small_ref[own_small, :] + small_first[...]
    small_step(0)
    for cube in sums:
        cube.step_near()
    small[1, row] = small_sum(0)
    small_step(1)
    for cube in sums:
        cube.step_mid()
    small[2, column] = small_sum(1)
    small_step(2)
    for cube in sums:
        cube.step_low()
    small_out_ref[own_small, :] = small_sum(2)
    small_last = to_core(small_out_ref.at[own_small], small_out_ref.at[own_small], 4)
    small_last.start()
    for cube in sums:
        cube.step_done()
    for cube in sums:
        cube.back_mid()
    for cube in sums:
        cube.back_near()
    for cube in sums:
        cube.back_far()
    for cube in sums:
        cube.back_last()
    for part in range(3):
        sums[part].finish(out_ref.at[other * 3 + part])
    small_last.wait_send()
    theirs = small_out_ref.at[pl.ds(other * SMALL_ROWS, SMALL_ROWS)]
    to_core(theirs, theirs, 4).wait_recv()
    for copy in small_copies:
        copy.wait_send()


def total_all(mats, small):
    dma = pltpu.SemaphoreType.DMA
    vmem = pl.BlockSpec(memory_space=pltpu.VMEM)
    return pl.pallas_call(
        total_kernel,
        out_shape=(
            jax.ShapeDtypeStruct((6, 1024, 512), BF),
            jax.ShapeDtypeStruct((2 * SMALL_ROWS, 512), F32),
        ),
        in_specs=[vmem, vmem],
        out_specs=(vmem, vmem),
        scratch_shapes=[
            pltpu.VMEM((3, 1024, 512), BF),
            pltpu.VMEM((3, 2, 128, 512), BF),
            pltpu.VMEM((3, 2, 256, 512), BF),
            pltpu.VMEM((3, 3, 64, 512), BF),
            pltpu.VMEM((3, 3, 16, 512), BF),
            pltpu.VMEM((3, 1024, 512), BF),
            pltpu.VMEM((3, 4, SMALL_ROWS, 512), F32),
            pltpu.VMEM((SMALL_ROWS, 512), F32),
            dma((3, 24)),
            dma((3, 24)),
            dma((5,)),
            dma((5,)),
            dma((3, 4)),
            dma((3, 4)),
        ],
        compiler_params=pltpu.CompilerParams(
            collective_id=3, has_side_effects=True, vmem_limit_bytes=40 << 20
        ),
    )(mats, small)


def dot_tn(left, right):
    return lax.dot_general(left, right, (((0,), (0,)), ((), ())), preferred_element_type=F32)


def dot_nt(left, right):
    return lax.dot_general(left, right, (((1,), (1,)), ((), ())), preferred_element_type=F32)


def dot_nn(left, right):
    return lax.dot_general(left, right, (((1,), (0,)), ((), ())), preferred_element_type=F32)


def expert_kernel(
    rows_ref,
    meta_ref,
    cot_ref,
    w_in_ref,
    w_out_ref,
    row_total_ref,
    score_out_ref,
    moe_ref,
    grad_ref,
    blocks,
    meta_in,
    score_send,
    cots,
    w_in,
    w_out,
    d_in,
    d_out,
    row_partial,
    moe_stage,
    picks,
    slot_rows,
    slot_cots,
    slot_grads,
    slot_res,
    slot_back,
    far,
    near,
    summed,
    far_two,
    near_two,
    send_sems,
    recv_sems,
    rsend_sems,
    rrecv_sems,
    meta_send,
    meta_recv,
    score_ssem,
    score_rsem,
    weight_send,
    weight_recv,
    local_sems,
    cot_sems,
    moe_sems,
    pair_send,
    pair_recv,
    pair_ready,
):
    me = lax.axis_index("grp")
    core = lax.axis_index("exp")
    row, column = me // 4, lax.rem(me, 4)
    barrier = pltpu.get_barrier_semaphore()
    for step in range(1, PLANE):
        pl.semaphore_signal(
            barrier, inc=1, device_id={"grp": lax.rem(me + step, PLANE)}, device_id_type=MESH
        )
    pl.semaphore_signal(barrier, inc=1, device_id={"exp": 1 - core}, device_id_type=MESH)

    load_in = pltpu.make_async_copy(w_in_ref, w_in.at[core], local_sems.at[0])
    load_out = pltpu.make_async_copy(w_out_ref, w_out.at[core], local_sems.at[1])
    load_in.start()
    load_out.start()
    blocks[me] = rows_ref[...]
    meta_in[me] = meta_ref[me]
    d_in[...] = jnp.zeros_like(d_in)
    d_out[...] = jnp.zeros_like(d_out)

    def cot_copy(group, j):
        shift = group + group // 2 - 2 * (group // 3)
        index = mod4(row + j) * 4 + mod4(column + shift)
        return pltpu.make_async_copy(
            cot_ref.at[index], cots.at[lax.rem(group, 2), j], cot_sems.at[lax.rem(group, 2), j]
        )

    for j in range(GROUP):
        cot_copy(0, j).start()
    pl.semaphore_wait(barrier, PLANE)

    gathers = [PlaneGather(part, blocks, send_sems, recv_sems) for part in (0, 1)]
    for gather in gathers:
        gather.begin()
    for gather in gathers:
        gather.spread(0)
    meta_copies = []
    for step in range(1, PLANE):
        to = lax.rem(me + step, PLANE)
        copy = plane_copy(
            meta_ref.at[to], meta_in.at[me], meta_send.at[step], meta_recv.at[step], to
        )
        copy.start()
        meta_copies.append(copy)
    weight_copies = []
    for slot, (source, target) in enumerate(((w_in_ref, w_in), (w_out_ref, w_out))):
        copy = pltpu.make_async_remote_copy(
            src_ref=source,
            dst_ref=target.at[core],
            send_sem=weight_send.at[slot],
            recv_sem=weight_recv.at[slot],
            device_id={"exp": 1 - core},
            device_id_type=MESH,
        )
        copy.start()
        weight_copies.append(copy)
    load_in.wait()
    load_out.wait()
    for copy in weight_copies:
        copy.wait()
    for copy in meta_copies:
        copy.wait()
    for gather in gathers:
        gather.forward_first()
        gather.spread(-1)
        gather.spread(1)
    gathers[1].forward_second(0)
    for gather in gathers:
        gather.wait_far_first()
        gather.spread(2)
    gathers[1].wait_far_second(0)

    def moe_copy(j, index):
        return pltpu.make_async_copy(moe_stage.at[j], moe_ref.at[index], moe_sems.at[j])

    @pl.loop(0, 4)
    def _(group):
        shift = group + group // 2 - 2 * (group // 3)
        place = mod4(column + shift)
        parity = lax.rem(group, 2)

        @pl.when(group == 0)
        def _():
            gathers[0].forward_second(0)
            gathers[0].forward_second(-1)
            gathers[0].forward_second(1)
            gathers[0].forward_second(2)
            gathers[1].forward_second(-1)
            gathers[1].forward_second(1)

        @pl.when(group == 1)
        def _():
            gathers[1].wait_far_second(1)
            gathers[1].wait_far_second(-1)
            gathers[1].forward_second(2)

        @pl.when(group == 2)
        def _():
            for da in (0, -1, 1, 2):
                gathers[0].wait_far_second(da)
            gathers[1].wait_far_second(2)

        @pl.when(group < 3)
        def _():
            for j in range(GROUP):
                cot_copy(group + 1, j).start()

        for j in range(GROUP):
            cot_copy(group, j).wait()

        for expert in range(2):
            gates = []
            for j in range(GROUP):
                index = mod4(row + j) * 4 + place
                slots = meta_in[index, pl.ds(expert, 1), :]
                gate_row = meta_in[index, pl.ds(2 + expert, 1), :]
                slot_id = lax.broadcasted_iota(jnp.int32, (CAPACITY, BLOCK), 0).astype(F32)
                hit = slot_id == slots
                pick = jnp.where(hit, 1.0, 0.0).astype(BF)
                gate = jnp.sum(jnp.where(hit, gate_row, 0.0), axis=1, keepdims=True)
                gates.append(gate)
                here = pl.ds(j * CAPACITY, CAPACITY)
                picks[j, pl.ds(expert * CAPACITY, CAPACITY), :] = pick
                slot_rows[here, :] = dot_nn(pick, blocks[index]).astype(BF)
                cot_rows = dot_nn(pick, cots[parity, j])
                slot_cots[here, :] = cot_rows.astype(BF)
                slot_grads[here, :] = (gate * (RESIDUAL_MULT * cot_rows)).astype(BF)
            gate = jnp.concatenate(gates, axis=0)
            gate_up = dot_nn(slot_rows[...], w_in[expert])
            gate_half, up_half = gate_up[:, :INNER], gate_up[:, INNER:]
            sigmoid = jax.nn.sigmoid(gate_half)
            activated = gate_half * sigmoid
            hidden = (activated * up_half).astype(BF)
            result = dot_nn(hidden, w_out[expert]).astype(BF).astype(F32)
            scored = RESIDUAL_MULT * jnp.sum(
                slot_cots[...].astype(F32) * result, axis=1, keepdims=True
            )
            slot_res[expert] = (gate * result).astype(BF)
            hidden_grad = dot_nt(slot_grads[...], w_out[expert])
            gate_part = hidden_grad * up_half * sigmoid * (1.0 + gate_half * (1.0 - sigmoid))
            up_part = hidden_grad * activated
            pair_grad = jnp.concatenate([gate_part.astype(BF), up_part.astype(BF)], axis=1)
            slot_back[expert] = dot_nt(pair_grad, w_in[expert]).astype(BF)
            d_out[expert] += dot_tn(hidden, slot_grads[...])
            d_in[expert] += dot_tn(slot_rows[...], pair_grad)
            for j in range(GROUP):
                index = mod4(row + j) * 4 + place
                pick = picks[j, pl.ds(expert * CAPACITY, CAPACITY), :].astype(F32)
                spread = jnp.sum(
                    pick * scored[j * CAPACITY : (j + 1) * CAPACITY], axis=0, keepdims=True
                )
                score_send[index, pl.ds(expert, 1), :] = spread

        for j in range(GROUP):
            index = mod4(row + j) * 4 + place
            here = pl.ds(j * CAPACITY, CAPACITY)
            pick = picks[j]

            @pl.when(group > 0)
            def _():
                moe_copy(j, index).wait()

            values = jnp.concatenate([slot_res[0, here, :], slot_res[1, here, :]], axis=0)
            moe_stage[j] = dot_tn(pick, values).astype(BF)
            moe_copy(j, index).start()
            values = jnp.concatenate([slot_back[0, here, :], slot_back[1, here, :]], axis=0)
            row_partial[index] = dot_tn(pick, values).astype(BF)

    for gather in gathers:
        gather.finish()
    reducers = [
        PlaneReduce(
            part, row_partial, (far, near, summed, far_two, near_two), rsend_sems, rrecv_sems, row_total_ref
        )
        for part in (0, 1)
    ]
    for da in (2, 1, -1, 0):
        for reducer in reducers:
            reducer.step_far(da)
    score_out_ref[me] = score_send[me]
    score_copies = []
    for step in range(1, PLANE):
        to = lax.rem(me + step, PLANE)
        copy = plane_copy(
            score_send.at[to], score_out_ref.at[me], score_ssem.at[step], score_rsem.at[step], to
        )
        copy.start()
        score_copies.append(copy)
    other = 1 - core
    for j in range(4):
        cots[0, j] = d_in[other, pl.ds(j * BLOCK, BLOCK), :].astype(BF)
    for j in range(2):
        cots[1, j] = d_out[other, pl.ds(j * BLOCK, BLOCK), :].astype(BF)
    pl.semaphore_signal(pair_ready, inc=1, device_id={"exp": other}, device_id_type=MESH)
    pl.semaphore_wait(pair_ready, 1)
    pair_copies = []
    for j in range(6):
        copy = pltpu.make_async_remote_copy(
            src_ref=cots.at[j // 4, j % 4],
            dst_ref=blocks.at[j],
            send_sem=pair_send.at[j],
            recv_sem=pair_recv.at[j],
            device_id={"exp": other},
            device_id_type=MESH,
        )
        copy.start()
        pair_copies.append(copy)
    for da in (2, 1, -1, 0):
        for reducer in reducers:
            reducer.step_near(da)
    for j in range(6):
        pair_copies[j].wait()
        here = pl.ds((j % 4) * BLOCK, BLOCK)
        if j < 4:
            w_in[0, here, :] = (d_in[core, here, :] + blocks[j].astype(F32)).astype(BF)
        else:
            w_out[0, here, :] = (d_out[core, here, :] + blocks[j].astype(F32)).astype(BF)
    store_in = pltpu.make_async_copy(w_in.at[0], grad_ref.at[pl.ds(0, WIDTH)], local_sems.at[0])
    store_out = pltpu.make_async_copy(
        w_out.at[0], grad_ref.at[pl.ds(WIDTH, INNER)], local_sems.at[1]
    )
    store_in.start()
    store_out.start()
    for da in (2, 1, -1, 0):
        for reducer in reducers:
            reducer.step_sum(da)
    for reducer in reducers:
        reducer.finish()
    for copy in score_copies:
        copy.wait()
    for j in range(GROUP):
        moe_copy(j, j).wait()
    store_in.wait()
    store_out.wait()


def run_experts(rows, meta, cots, expert_in, expert_out):
    vmem = pl.BlockSpec(memory_space=pltpu.VMEM)
    hbm = pl.BlockSpec(memory_space=pl.ANY)
    dma = pltpu.SemaphoreType.DMA
    slots = GROUP * CAPACITY
    return pl.pallas_call(
        expert_kernel,
        out_shape=(
            jax.ShapeDtypeStruct((BLOCK, WIDTH), F32),
            jax.ShapeDtypeStruct((PLANE, 8, BLOCK), F32),
            jax.ShapeDtypeStruct((PLANE, BLOCK, WIDTH), BF),
            jax.ShapeDtypeStruct((WIDTH + INNER, WIDTH), BF),
        ),
        in_specs=[vmem, vmem, hbm, hbm, hbm],
        out_specs=(vmem, vmem, hbm, hbm),
        scratch_shapes=[
            pltpu.VMEM((PLANE, BLOCK, WIDTH), BF),
            pltpu.VMEM((PLANE, 8, BLOCK), F32),
            pltpu.VMEM((PLANE, 8, BLOCK), F32),
            pltpu.VMEM((2, GROUP, BLOCK, WIDTH), BF),
            pltpu.VMEM((2, WIDTH, 2 * INNER), BF),
            pltpu.VMEM((2, INNER, WIDTH), BF),
            pltpu.VMEM((2, WIDTH, 2 * INNER), F32),
            pltpu.VMEM((2, INNER, WIDTH), F32),
            pltpu.VMEM((PLANE, BLOCK, WIDTH), BF),
            pltpu.VMEM((GROUP, BLOCK, WIDTH), BF),
            pltpu.VMEM((GROUP, 2 * CAPACITY, BLOCK), BF),
            pltpu.VMEM((slots, WIDTH), BF),
            pltpu.VMEM((slots, WIDTH), BF),
            pltpu.VMEM((slots, WIDTH), BF),
            pltpu.VMEM((2, slots, WIDTH), BF),
            pltpu.VMEM((2, slots, WIDTH), BF),
        ]
        + reduce_buffers()
        + [dma((40,))] * 4
        + [dma((PLANE,))] * 4
        + [dma((2,))] * 3
        + [dma((2, GROUP)), dma((GROUP,))]
        + [dma((6,))] * 2
        + [pltpu.SemaphoreType.REGULAR],
        compiler_params=pltpu.CompilerParams(
            collective_id=2, has_side_effects=True, vmem_limit_bytes=VMEM_LIMIT
        ),
    )(rows, meta, cots, expert_in, expert_out)


VMEM_LIMIT = 63 << 20


def place_slots(route_ids, rank_ids, experts):
    tok_rows, top_count = route_ids.shape
    hits = route_ids[:, :, None] == jnp.arange(experts, dtype=jnp.int32)
    rank_of = jnp.sum(jnp.where(hits, rank_ids[:, :, None] + 1, 0), axis=1) - 1
    chosen = rank_of >= 0
    ranks = jnp.arange(top_count, dtype=jnp.int32)
    counts = (rank_of[:, None, :] == ranks[None, :, None]).reshape(tok_rows, top_count * experts)
    lowered = counts.astype(BF)
    tok = jnp.arange(tok_rows, dtype=jnp.int32)
    earlier = (tok[:, None] > tok[None, :]).astype(BF)
    before = product(earlier, lowered)
    totals = jnp.sum(counts.astype(F32), axis=0).reshape(top_count, experts)
    offsets = (jnp.cumsum(totals, axis=0) - totals).reshape(1, top_count * experts)
    place = jnp.where(counts, before + offsets, 0.0).reshape(tok_rows, top_count, experts)
    return chosen, jnp.sum(place, axis=1)


def on_device(
    tokens,
    segments,
    routes,
    rank_order,
    attn_gain,
    w_query,
    w_key,
    w_value,
    w_output,
    ffn_gain,
    w_router,
    expert_in,
    expert_out,
    cotangent,
):
    tok_rows = tokens.shape[1]
    model_width = tokens.shape[2]
    experts = w_router.shape[1]
    kv_width = w_key.shape[1]
    kv_heads = KV_HEADS
    head_dim = HEAD
    q_heads = HEADS
    group_size = q_heads // kv_heads
    blocks = lax.axis_size(("seq", "exp"))
    block_id = lax.axis_index(("seq", "exp"))
    hop_count = min(-(-WINDOW // tok_rows), blocks - 1)
    key_span = (hop_count + 1) * tok_rows
    inputs = tokens[0].astype(jnp.float32)
    seg_ids = segments[0]
    route_ids = routes[0]
    rank_ids = rank_order[0]
    positions = block_id * tok_rows + jnp.arange(tok_rows, dtype=jnp.int32)
    cosine, sine_part = rope_tables(positions, head_dim)
    scale_one = lax.rsqrt(jnp.mean(inputs * inputs, axis=-1, keepdims=True) + EPSILON)
    normed = (inputs * scale_one * attn_gain).astype(jnp.bfloat16)
    query_pre = product(normed, w_query).reshape(tok_rows, q_heads, head_dim)
    key_pre = product(normed, w_key).reshape(tok_rows, kv_heads, head_dim)
    value_own = product(normed, w_value).astype(jnp.bfloat16)
    query_rows = (
        rotate(query_pre, cosine, sine_part)
        .astype(jnp.bfloat16)
        .reshape(tok_rows, kv_heads, group_size, head_dim)
    )
    key_own = rotate(key_pre, cosine, sine_part).astype(jnp.bfloat16).reshape(tok_rows, kv_width)
    key_parts = [key_own]
    value_parts = [value_own]
    seg_parts = [seg_ids]
    for hop_index in range(1, hop_count + 1):
        key_far, value_far, seg_far = from_behind(
            (key_own, value_own, seg_ids), ("seq", "exp"), hop_index
        )
        key_parts.insert(0, key_far)
        value_parts.insert(0, value_far)
        seg_parts.insert(0, seg_far)
    key_gathered = jnp.concatenate(key_parts, axis=0).reshape(key_span, kv_heads, head_dim)
    value_gathered = jnp.concatenate(value_parts, axis=0).reshape(key_span, kv_heads, head_dim)
    seg_all = jnp.concatenate(seg_parts, axis=0)
    key_pos = (block_id - hop_count) * tok_rows + jnp.arange(key_span, dtype=jnp.int32)
    distance = positions[:, None] - key_pos[None, :]
    allowed = (
        (seg_ids[:, None] == seg_all[None, :])
        & (distance >= 0)
        & (distance < WINDOW)
        & (key_pos[None, :] >= 0)
    )

    def scores_of():
        raw_scores = ATTENTION_FACTOR * jnp.einsum(
            "dklp,okp->kldo", query_rows, key_gathered, preferred_element_type=jnp.float32
        )
        return jnp.where(allowed[None, None], raw_scores, MASKED)

    score_matrix = scores_of()
    top_score = jnp.max(score_matrix, axis=-1, keepdims=True)
    expsum = jnp.sum(jnp.exp(score_matrix - top_score), axis=-1, keepdims=True)
    probability_lowered = (jnp.exp(score_matrix - top_score) / expsum).astype(jnp.bfloat16)
    heads_out = (
        jnp.einsum(
            "uzjq,quk->juzk",
            probability_lowered,
            value_gathered,
            preferred_element_type=jnp.float32,
        )
        .astype(jnp.bfloat16)
        .reshape(tok_rows, model_width)
    )
    branch = product(heads_out, w_output)
    residual = inputs + RESIDUAL_MULT * branch
    scale_two = lax.rsqrt(jnp.mean(residual * residual, axis=-1, keepdims=True) + EPSILON)
    routed_in = (residual * scale_two * ffn_gain).astype(jnp.bfloat16)
    logits = product(routed_in, w_router)
    chosen, slot_place = place_slots(route_ids, rank_ids, experts)
    gates = jax.nn.softmax(jnp.where(chosen, logits, MASKED), axis=1)
    gates = jnp.where(chosen, gates, 0.0)
    kept_place = jnp.where(chosen & (slot_place < CAPACITY), slot_place, -1.0)
    meta = jnp.concatenate(
        [
            kept_place.T.reshape(PLANE, 2, tok_rows),
            gates.T.reshape(PLANE, 2, tok_rows),
            jnp.zeros((PLANE, 4, tok_rows), jnp.float32),
        ],
        axis=1,
    )
    cots = gather_plane(cotangent[0])
    expert_row_sum, scores, moe_partial, expert_grads = run_experts(
        routed_in, meta, cots, expert_in[0], expert_out[0]
    )
    moe_out, expert_total = return_plane(moe_partial, expert_grads)
    output = (residual + RESIDUAL_MULT * moe_out).astype(jnp.bfloat16)[None]
    upstream = cotangent[0].astype(jnp.float32)
    gate_grad = scores[:, :2, :].reshape(experts, tok_rows).T
    choice_grad = gates * (gate_grad - jnp.sum(gates * gate_grad, axis=1, keepdims=True))
    logit_grad = choice_grad.astype(jnp.bfloat16)
    router_w_grad = inner_rows(routed_in, logit_grad)
    routed_grad = product_back(logit_grad, w_router) + expert_row_sum
    normal_two = residual * scale_two
    ffn_gain_grad = jnp.sum(routed_grad * normal_two, axis=0)
    weighted_two = routed_grad * ffn_gain
    residual_grad = (
        upstream
        + scale_two * weighted_two
        - residual * scale_two**3 * jnp.mean(weighted_two * residual, axis=-1, keepdims=True)
    )
    branch_grad = (RESIDUAL_MULT * residual_grad).astype(jnp.bfloat16)
    head_gradient = (
        product_back(branch_grad, w_output)
        .astype(jnp.bfloat16)
        .reshape(tok_rows, kv_heads, group_size, head_dim)
    )
    score_matrix = scores_of()
    probs_full = jnp.exp(score_matrix - top_score) / expsum
    probability_lowered = probs_full.astype(jnp.bfloat16)
    prob_grad = jnp.einsum(
        "dklp,okp->kldo", head_gradient, value_gathered, preferred_element_type=jnp.float32
    )
    score_gradient = (
        probs_full * (prob_grad - jnp.sum(probs_full * prob_grad, axis=-1, keepdims=True))
    ).astype(jnp.bfloat16)
    queries_grad = ATTENTION_FACTOR * jnp.einsum(
        "uzjq,quk->juzk", score_gradient, key_gathered, preferred_element_type=jnp.float32
    )
    keys_grad_all = (
        ATTENTION_FACTOR
        * jnp.einsum(
            "ykze,zykm->eym", score_gradient, query_rows, preferred_element_type=jnp.float32
        )
    ).reshape(key_span, kv_width)
    values_grad_all = jnp.einsum(
        "ykze,zykm->eym", probability_lowered, head_gradient, preferred_element_type=jnp.float32
    ).reshape(key_span, kv_width)
    keys_grad = keys_grad_all[hop_count * tok_rows :]
    values_grad = values_grad_all[hop_count * tok_rows :]
    for hop_index in range(1, hop_count + 1):
        first_row = (hop_count - hop_index) * tok_rows
        key_back, value_back = (
            from_behind(
                keys_grad_all[first_row : first_row + tok_rows].astype(jnp.bfloat16),
                ("seq", "exp"),
                -hop_index,
            ).astype(jnp.float32),
            from_behind(
                values_grad_all[first_row : first_row + tok_rows].astype(jnp.bfloat16),
                ("seq", "exp"),
                -hop_index,
            ).astype(jnp.float32),
        )
        keys_grad = keys_grad + key_back
        values_grad = values_grad + value_back
    query_pre_grad = (
        unrotate(queries_grad.reshape(tok_rows, q_heads, head_dim), cosine, sine_part)
        .astype(jnp.bfloat16)
        .reshape(tok_rows, model_width)
    )
    key_pre_grad = (
        unrotate(keys_grad.reshape(tok_rows, kv_heads, head_dim), cosine, sine_part)
        .astype(jnp.bfloat16)
        .reshape(tok_rows, kv_width)
    )
    value_pre_grad = values_grad.astype(jnp.bfloat16)
    normed_grad = (
        product_back(query_pre_grad, w_query)
        + product_back(key_pre_grad, w_key)
        + product_back(value_pre_grad, w_value)
    )
    attn_gain_grad = jnp.sum(normed_grad * inputs * scale_one, axis=0)
    weighted_one = normed_grad * attn_gain
    input_grad = (
        residual_grad
        + scale_one * weighted_one
        - inputs * scale_one**3 * jnp.mean(weighted_one * inputs, axis=-1, keepdims=True)
    )
    up_total = expert_total[None, :model_width].astype(jnp.float32)
    down_total = expert_total[None, model_width:].astype(jnp.float32)
    half = model_width // 2
    mats = jnp.stack(
        [
            inner_rows(normed, query_pre_grad[:, :half]),
            inner_rows(normed, query_pre_grad[:, half:]),
            inner_rows(normed, key_pre_grad),
            inner_rows(normed, value_pre_grad),
            inner_rows(heads_out, branch_grad[:, :half]),
            inner_rows(heads_out, branch_grad[:, half:]),
        ]
    ).astype(jnp.bfloat16)
    small = jnp.concatenate(
        [
            router_w_grad.reshape(64, 512),
            attn_gain_grad.reshape(2, 512),
            ffn_gain_grad.reshape(2, 512),
            jnp.zeros((2 * SMALL_ROWS - 68, 512), jnp.float32),
        ],
        axis=0,
    )
    mats_total, small_total = total_all(mats, small)
    query_total = jnp.concatenate([mats_total[0], mats_total[1]], axis=1).astype(jnp.float32)
    key_total = mats_total[2].astype(jnp.float32)
    value_total = mats_total[3].astype(jnp.float32)
    out_total = jnp.concatenate([mats_total[4], mats_total[5]], axis=1).astype(jnp.float32)
    router_total = small_total[:64].reshape(router_w_grad.shape)
    gain_one_total = small_total[64:66].reshape(model_width)
    gain_two_total = small_total[66:68].reshape(model_width)
    return (
        output,
        input_grad.astype(jnp.bfloat16)[None],
        gain_one_total,
        query_total,
        key_total,
        value_total,
        out_total,
        gain_two_total,
        router_total,
        up_total,
        down_total,
    )


def solution(mesh):
    placed = (
        P("grp", ("seq", "exp"), None),
        P("grp", ("seq", "exp")),
        P("grp", ("seq", "exp"), None),
        P("grp", ("seq", "exp"), None),
        P(),
        P(),
        P(),
        P(),
        P(),
        P(),
        P(),
        P(("grp", "exp"), None, None),
        P(("grp", "exp"), None, None),
        P("grp", ("seq", "exp"), None),
    )
    return jax.shard_map(
        on_device,
        mesh=mesh,
        in_specs=placed,
        out_specs=(
            P("grp", ("seq", "exp"), None),
            P("grp", ("seq", "exp"), None),
            P(),
            P(),
            P(),
            P(),
            P(),
            P(),
            P(),
            P(("grp", "exp"), None, None),
            P(("grp", "exp"), None, None),
        ),
        check_vma=False,
    )
```

```python
import functools
import math

import jax
import jax.numpy as jnp
from jax import lax
from jax.experimental import pallas as pl
from jax.experimental.pallas import tpu as pltpu
from jax.sharding import PartitionSpec as P

HEADS = 16
KV_HEADS = 8
HEAD = 64
WINDOW = 1024


EPSILON = 1e-06
ATTENTION_FACTOR = 0.015625
RESIDUAL_MULT = 0.22
ROPE_BASE = 10000.0
MASKED = -1e30


def from_behind(value, axis, steps):
    count = lax.axis_size(axis)
    initial, last = (max(0, -steps), min(count, count - steps))
    return lax.ppermute(value, axis, [(source, source + steps) for source in range(initial, last)])


def product(left_side, right_side):
    return jnp.dot(left_side, right_side, preferred_element_type=jnp.float32)


def inner_rows(left_side, right_side):
    return jnp.einsum("ta,tb->ab", left_side, right_side, preferred_element_type=jnp.float32)


def product_back(left_side, right_side):
    return jnp.einsum("tb,ab->ta", left_side, right_side, preferred_element_type=jnp.float32)


def rope_tables(positions, head_dim):
    half_dim = head_dim // 2
    frequency = jnp.exp(
        jnp.arange(half_dim, dtype=jnp.float32) * (-2.0 * math.log(ROPE_BASE) / head_dim)
    )
    angles = positions.astype(jnp.float32)[:, None] * frequency[None, :]
    return (jnp.cos(angles)[:, None, :], jnp.sin(angles)[:, None, :])


def rotate(values, cosine, sine_part):
    half_dim = values.shape[-1] // 2
    first_half = values[..., :half_dim]
    second_half = values[..., half_dim:]
    return jnp.concatenate(
        [
            first_half * cosine - second_half * sine_part,
            second_half * cosine + first_half * sine_part,
        ],
        axis=-1,
    )


def unrotate(values, cosine, sine_part):
    half_dim = values.shape[-1] // 2
    first_half = values[..., :half_dim]
    second_half = values[..., half_dim:]
    return jnp.concatenate(
        [
            first_half * cosine + second_half * sine_part,
            second_half * cosine - first_half * sine_part,
        ],
        axis=-1,
    )


MESH = pl.DeviceIdType.MESH
CAPACITY = 80
BLOCK = 256
HALF = 128
QUARTER = 64
WIDTH = 1024
INNER = 512
PLANE = 16
GROUP = 4
BF = jnp.bfloat16
F32 = jnp.float32


def mod4(value):
    return lax.rem(value + 8, 4)


def plane_id(part, first, second):
    return first * 4 + second if part == 0 else second * 4 + first


def plane_coords(part):
    index = lax.axis_index("grp")
    row, column = index // 4, lax.rem(index, 4)
    return (row, column) if part == 0 else (column, row)


def plane_copy(source, target, send_sem, recv_sem, index):
    return pltpu.make_async_remote_copy(
        src_ref=source,
        dst_ref=target,
        send_sem=send_sem,
        recv_sem=recv_sem,
        device_id={"grp": index},
        device_id_type=MESH,
    )


def greet_plane():
    row, column = plane_coords(0)
    barrier = pltpu.get_barrier_semaphore()
    for index in (
        mod4(row + 1) * 4 + column,
        mod4(row - 1) * 4 + column,
        row * 4 + mod4(column + 1),
        row * 4 + mod4(column - 1),
    ):
        pl.semaphore_signal(barrier, inc=1, device_id={"grp": index}, device_id_type=MESH)
    pl.semaphore_wait(barrier, 4)


class PlaneGather:
    order = {0: 0, -1: 1, 1: 2, 2: 3}

    def __init__(self, part, blocks, send_sems, recv_sems):
        self.part, self.blocks = part, blocks
        self.send_sems, self.recv_sems = send_sems, recv_sems
        self.first, self.second = plane_coords(part)
        self.started = []

    def ref(self, da, db, half=None):
        index = plane_id(self.part, mod4(self.first + da), mod4(self.second + db))
        begin = self.part * HALF
        if half is None:
            return self.blocks.at[index, pl.ds(begin, HALF)]
        return self.blocks.at[index, pl.ds(begin + half * QUARTER, QUARTER)]

    def copy(self, da, db, half, axis, step, slot):
        if axis == 0:
            to = plane_id(self.part, mod4(self.first + step), self.second)
        else:
            to = plane_id(self.part, self.first, mod4(self.second + step))
        ref, sem = self.ref(da, db, half), self.part * 20 + slot
        return plane_copy(ref, ref, self.send_sems.at[sem], self.recv_sems.at[sem], to)

    def send(self, *where):
        self.copy(*where).start()
        self.started.append(where)

    def wait(self, da, db, half, slot):
        ref, sem = self.ref(da, db, half), self.part * 20 + slot
        plane_copy(
            ref, ref, self.send_sems.at[sem], self.recv_sems.at[sem],
            plane_id(self.part, self.first, self.second),
        ).wait_recv()

    def begin(self):
        self.send(0, 0, None, 0, 1, 0)
        self.send(0, 0, None, 0, -1, 1)

    def spread(self, da):
        slot = 4 + 4 * self.order[da]
        self.send(da, 0, None, 1, 1, slot)
        self.send(da, 0, None, 1, -1, slot + 1)

    def forward_first(self):
        self.wait(-1, 0, None, 0)
        self.send(-1, 0, 0, 0, 1, 2)
        self.wait(1, 0, None, 1)
        self.send(1, 0, 1, 0, -1, 3)

    def forward_second(self, da):
        slot = 4 + 4 * self.order[da]
        self.wait(da, -1, None, slot)
        self.send(da, -1, 0, 1, 1, slot + 2)
        self.wait(da, 1, None, slot + 1)
        self.send(da, 1, 1, 1, -1, slot + 3)

    def wait_far_first(self):
        self.wait(2, 0, 0, 2)
        self.wait(2, 0, 1, 3)

    def wait_far_second(self, da):
        slot = 4 + 4 * self.order[da]
        self.wait(da, 2, 0, slot + 2)
        self.wait(da, 2, 1, slot + 3)

    def finish(self):
        for where in self.started:
            self.copy(*where).wait_send()


class PlaneReduce:
    order = {2: 0, 1: 1, -1: 2, 0: 3}

    def __init__(self, part, partial, buffers, send_sems, recv_sems, total):
        self.part, self.partial, self.total = part, partial, total
        self.far, self.near, self.summed, self.far_two, self.near_two = buffers
        self.send_sems, self.recv_sems = send_sems, recv_sems
        self.first, self.second = plane_coords(part)
        self.started = []

    def ref(self, da, db, half=None):
        index = plane_id(self.part, mod4(self.first + da), mod4(self.second + db))
        begin = self.part * HALF
        if half is None:
            return self.partial.at[index, pl.ds(begin, HALF)]
        return self.partial.at[index, pl.ds(begin + half * QUARTER, QUARTER)]

    def send(self, source, target, axis, step, slot):
        if axis == 0:
            to = plane_id(self.part, mod4(self.first + step), self.second)
        else:
            to = plane_id(self.part, self.first, mod4(self.second + step))
        sem = self.part * 20 + slot
        copy = plane_copy(source, target, self.send_sems.at[sem], self.recv_sems.at[sem], to)
        copy.start()
        self.started.append(copy)

    def wait(self, target, slot):
        sem = self.part * 20 + slot
        plane_copy(
            target, target, self.send_sems.at[sem], self.recv_sems.at[sem],
            plane_id(self.part, self.first, self.second),
        ).wait_recv()

    def add(self, target, source):
        target[...] = (target[...].astype(F32) + source[...].astype(F32)).astype(BF)

    def step_far(self, da):
        part, place = self.part, self.order[da]
        self.send(self.ref(da, 2, 0), self.far.at[part, place, 0], 1, 1, 4 * place)
        self.send(self.ref(da, 2, 1), self.far.at[part, place, 1], 1, -1, 4 * place + 1)

    def step_near(self, da):
        part, place = self.part, self.order[da]
        self.wait(self.far.at[part, place, 0], 4 * place)
        self.add(self.ref(da, 1, 0), self.far.at[part, place, 0])
        self.send(self.ref(da, 1), self.near.at[part, place, 0], 1, 1, 4 * place + 2)
        self.wait(self.far.at[part, place, 1], 4 * place + 1)
        self.add(self.ref(da, -1, 1), self.far.at[part, place, 1])
        self.send(self.ref(da, -1), self.near.at[part, place, 1], 1, -1, 4 * place + 3)

    def step_sum(self, da):
        part, place = self.part, self.order[da]
        self.wait(self.near.at[part, place, 0], 4 * place + 2)
        self.wait(self.near.at[part, place, 1], 4 * place + 3)
        value = (
            self.ref(da, 0)[...].astype(F32)
            + self.near[part, place, 0].astype(F32)
            + self.near[part, place, 1].astype(F32)
        )
        rows = pl.ds(part * HALF, HALF)
        if da == 0:
            self.total[rows] = value
            self.wait(self.near_two.at[part, 0], 18)
            self.wait(self.near_two.at[part, 1], 19)
            self.total[rows] += self.near_two[part, 0].astype(F32) + self.near_two[part, 1].astype(F32)
            return
        self.summed[part, place] = value.astype(BF)
        lower, upper = pl.ds(0, QUARTER), pl.ds(QUARTER, QUARTER)
        if da == 2:
            self.send(self.summed.at[part, 0, lower], self.far_two.at[part, 0], 0, 1, 16)
            self.send(self.summed.at[part, 0, upper], self.far_two.at[part, 1], 0, -1, 17)
        if da == 1:
            self.wait(self.far_two.at[part, 0], 16)
            self.add(self.summed.at[part, 1, lower], self.far_two.at[part, 0])
            self.send(self.summed.at[part, 1], self.near_two.at[part, 0], 0, 1, 18)
        if da == -1:
            self.wait(self.far_two.at[part, 1], 17)
            self.add(self.summed.at[part, 2, upper], self.far_two.at[part, 1])
            self.send(self.summed.at[part, 2], self.near_two.at[part, 1], 0, -1, 19)

    def finish(self):
        for copy in self.started:
            copy.wait_send()


def reduce_buffers():
    return [
        pltpu.VMEM((2, 4, 2, QUARTER, WIDTH), BF),
        pltpu.VMEM((2, 4, 2, HALF, WIDTH), BF),
        pltpu.VMEM((2, 3, HALF, WIDTH), BF),
        pltpu.VMEM((2, 2, QUARTER, WIDTH), BF),
        pltpu.VMEM((2, 2, HALF, WIDTH), BF),
    ]


def run_reduce(reducers):
    for da in (2, 1, -1, 0):
        for reducer in reducers:
            reducer.step_far(da)
    for da in (2, 1, -1, 0):
        for reducer in reducers:
            reducer.step_near(da)
    for da in (2, 1, -1, 0):
        for reducer in reducers:
            reducer.step_sum(da)
    for reducer in reducers:
        reducer.finish()


class RowRing:
    def __init__(self, summed, total, far, near, send_sems, recv_sems):
        self.summed, self.total, self.far, self.near = summed, total, far, near
        self.send_sems, self.recv_sems = send_sems, recv_sems
        self.me = lax.axis_index("seq")
        self.rows = summed.shape[0] // 4
        self.started = []

    def piece(self, ref, shift, half=None):
        begin = mod4(self.me + shift) * self.rows
        if half is None:
            return ref.at[pl.ds(begin, self.rows)]
        return ref.at[pl.ds(begin + half * (self.rows // 2), self.rows // 2)]

    def send(self, source, target, step, slot):
        copy = pltpu.make_async_remote_copy(
            src_ref=source,
            dst_ref=target,
            send_sem=self.send_sems.at[slot],
            recv_sem=self.recv_sems.at[slot],
            device_id={"seq": mod4(self.me + step)},
            device_id_type=MESH,
        )
        copy.start()
        self.started.append(copy)

    def wait(self, target, slot):
        pltpu.make_async_remote_copy(
            src_ref=target,
            dst_ref=target,
            send_sem=self.send_sems.at[slot],
            recv_sem=self.recv_sems.at[slot],
            device_id={"seq": self.me},
            device_id_type=MESH,
        ).wait_recv()

    def add(self, target, source):
        target[...] = (target[...].astype(F32) + source[...].astype(F32)).astype(BF)

    def step_far(self):
        self.send(self.piece(self.summed, 2, 0), self.far.at[0], 1, 0)
        self.send(self.piece(self.summed, 2, 1), self.far.at[1], -1, 1)

    def step_near(self):
        self.wait(self.far.at[0], 0)
        self.add(self.piece(self.summed, 1, 0), self.far.at[0])
        self.send(self.piece(self.summed, 1), self.near.at[0], 1, 2)
        self.wait(self.far.at[1], 1)
        self.add(self.piece(self.summed, -1, 1), self.far.at[1])
        self.send(self.piece(self.summed, -1), self.near.at[1], -1, 3)

    def step_sum(self):
        self.wait(self.near.at[0], 2)
        self.wait(self.near.at[1], 3)
        self.piece(self.total, 0)[...] = (
            self.piece(self.summed, 0)[...].astype(F32)
            + self.near[0].astype(F32)
            + self.near[1].astype(F32)
        ).astype(BF)
        own = self.piece(self.total, 0)
        self.send(own, own, 1, 4)
        self.send(own, own, -1, 5)

    def step_forward(self):
        self.wait(self.piece(self.total, -1), 4)
        half = self.piece(self.total, -1, 0)
        self.send(half, half, 1, 6)
        self.wait(self.piece(self.total, 1), 5)
        half = self.piece(self.total, 1, 1)
        self.send(half, half, -1, 7)

    def finish(self):
        self.wait(self.piece(self.total, 2, 0), 6)
        self.wait(self.piece(self.total, 2, 1), 7)
        for copy in self.started:
            copy.wait_send()


def return_kernel(
    partial_ref,
    grad_ref,
    out_ref,
    grad_total_ref,
    partial,
    far,
    near,
    summed,
    far_two,
    near_two,
    grads,
    grad_far,
    grad_near,
    send_sems,
    recv_sems,
    ring_send,
    ring_recv,
    local_sems,
):
    load_grads = pltpu.make_async_copy(grad_ref, grads, local_sems.at[0])
    load = pltpu.make_async_copy(partial_ref, partial, local_sems.at[1])
    load_grads.start()
    load.start()
    row, column = plane_coords(0)
    line = lax.axis_index("seq")
    barrier = pltpu.get_barrier_semaphore()
    for index in (
        mod4(row + 1) * 4 + column,
        mod4(row - 1) * 4 + column,
        row * 4 + mod4(column + 1),
        row * 4 + mod4(column - 1),
    ):
        pl.semaphore_signal(barrier, inc=1, device_id={"grp": index}, device_id_type=MESH)
    for step in (1, -1):
        pl.semaphore_signal(
            barrier, inc=1, device_id={"seq": mod4(line + step)}, device_id_type=MESH
        )
    pl.semaphore_wait(barrier, 6)
    buffers = (far, near, summed, far_two, near_two)
    reducers = [
        PlaneReduce(part, partial, buffers, send_sems, recv_sems, out_ref) for part in (0, 1)
    ]
    ring = RowRing(grads, grad_total_ref, grad_far, grad_near, ring_send, ring_recv)
    load_grads.wait()
    ring.step_far()
    load.wait()
    for da in (2, 1, -1, 0):
        for reducer in reducers:
            reducer.step_far(da)
    ring.step_near()
    for da in (2, 1, -1, 0):
        for reducer in reducers:
            reducer.step_near(da)
    ring.step_sum()
    for da in (2, 1, -1, 0):
        for reducer in reducers:
            reducer.step_sum(da)
    ring.step_forward()
    for reducer in reducers:
        reducer.finish()
    ring.finish()


def return_plane(partial, grads):
    dma = pltpu.SemaphoreType.DMA
    rows = grads.shape[0]
    vmem = pl.BlockSpec(memory_space=pltpu.VMEM)
    hbm = pl.BlockSpec(memory_space=pl.ANY)
    return pl.pallas_call(
        return_kernel,
        out_shape=(
            jax.ShapeDtypeStruct((BLOCK, WIDTH), F32),
            jax.ShapeDtypeStruct(grads.shape, BF),
        ),
        in_specs=[hbm, hbm],
        out_specs=(vmem, vmem),
        scratch_shapes=[pltpu.VMEM((PLANE, BLOCK, WIDTH), BF)]
        + reduce_buffers()
        + [
            pltpu.VMEM(grads.shape, BF),
            pltpu.VMEM((2, rows // 8, WIDTH), BF),
            pltpu.VMEM((2, rows // 4, WIDTH), BF),
            dma((40,)),
            dma((40,)),
            dma((8,)),
            dma((8,)),
            dma((2,)),
        ],
        compiler_params=pltpu.CompilerParams(
            collective_id=1, has_side_effects=True, vmem_limit_bytes=58 << 20
        ),
    )(partial, grads)


class CubeSum:
    def __init__(self, part, matrix, out, far, near, mid, low, send_sems, recv_sems):
        self.part, self.matrix, self.out = part, matrix, out
        self.far, self.near, self.mid, self.low = far, near, mid, low
        self.send_sems, self.recv_sems = send_sems, recv_sems
        line, plane = lax.axis_index("seq"), lax.axis_index("grp")
        coords = (line, plane // 4, lax.rem(plane, 4))
        self.coords = coords
        self.place = [coords[(part + level) % 3] for level in range(3)]
        self.started = []

    def device(self, level, step):
        axis = (self.part + level) % 3
        there = mod4(self.coords[axis] + step)
        if axis == 0:
            return {"seq": there}
        if axis == 1:
            return {"grp": there * 4 + self.coords[2]}
        return {"grp": self.coords[1] * 4 + there}

    def rows(self, level, shift):
        begin = 0
        for upper in range(level):
            begin = begin + self.place[upper] * (256 // 4**upper)
        return begin + mod4(self.place[level] + shift) * (256 // 4**level)

    def copy(self, source, target, level, step, slot):
        return pltpu.make_async_remote_copy(
            src_ref=source,
            dst_ref=target,
            send_sem=self.send_sems.at[self.part, slot],
            recv_sem=self.recv_sems.at[self.part, slot],
            device_id=self.device(level, step),
            device_id_type=MESH,
        )

    def send(self, source, target, level, step, slot):
        copy = self.copy(source, target, level, step, slot)
        copy.start()
        self.started.append(copy)

    def wait(self, target, slot):
        self.copy(target, target, 0, 0, slot).wait_recv()

    def add(self, target, *sources):
        value = target[...].astype(F32)
        for source in sources:
            value = value + source[...].astype(F32)
        target[...] = value.astype(BF)

    def step_far(self):
        begin = self.rows(0, 2)
        self.send(self.matrix.at[pl.ds(begin, 128)], self.far.at[0], 0, 1, 0)
        self.send(self.matrix.at[pl.ds(begin + 128, 128)], self.far.at[1], 0, -1, 1)

    def step_near(self):
        begin = self.rows(0, 1)
        self.wait(self.far.at[0], 0)
        self.add(self.matrix.at[pl.ds(begin, 128)], self.far.at[0])
        self.send(self.matrix.at[pl.ds(begin, 256)], self.near.at[0], 0, 1, 2)
        begin = self.rows(0, -1)
        self.wait(self.far.at[1], 1)
        self.add(self.matrix.at[pl.ds(begin + 128, 128)], self.far.at[1])
        self.send(self.matrix.at[pl.ds(begin, 256)], self.near.at[1], 0, -1, 3)

    def step_mid(self):
        self.wait(self.near.at[0], 2)
        self.wait(self.near.at[1], 3)
        self.add(self.matrix.at[pl.ds(self.rows(0, 0), 256)], self.near.at[0], self.near.at[1])
        for step in (1, 2, 3):
            self.send(
                self.matrix.at[pl.ds(self.rows(1, step), 64)], self.mid.at[step - 1], 1, step, 3 + step
            )

    def step_low(self):
        for step in (1, 2, 3):
            self.wait(self.mid.at[step - 1], 3 + step)
        self.add(
            self.matrix.at[pl.ds(self.rows(1, 0), 64)], self.mid.at[0], self.mid.at[1], self.mid.at[2]
        )
        for step in (1, 2, 3):
            self.send(
                self.matrix.at[pl.ds(self.rows(2, step), 16)], self.low.at[step - 1], 2, step, 6 + step
            )

    def step_done(self):
        for step in (1, 2, 3):
            self.wait(self.low.at[step - 1], 6 + step)
        own = self.rows(2, 0)
        value = self.matrix[pl.ds(own, 16), :].astype(F32)
        for step in (1, 2, 3):
            value = value + self.low[step - 1].astype(F32)
        self.out[pl.ds(own, 16), :] = value.astype(BF)
        ref = self.out.at[pl.ds(own, 16)]
        for step in (1, 2, 3):
            self.send(ref, ref, 2, step, 9 + step)

    def back_mid(self):
        for step in (1, 2, 3):
            self.wait(self.out.at[pl.ds(self.rows(2, -step), 16)], 9 + step)
        ref = self.out.at[pl.ds(self.rows(1, 0), 64)]
        for step in (1, 2, 3):
            self.send(ref, ref, 1, step, 12 + step)

    def back_near(self):
        for step in (1, 2, 3):
            self.wait(self.out.at[pl.ds(self.rows(1, -step), 64)], 12 + step)
        ref = self.out.at[pl.ds(self.rows(0, 0), 256)]
        self.send(ref, ref, 0, 1, 16)
        self.send(ref, ref, 0, -1, 17)
        self.share(0, 20)

    def back_far(self):
        begin = self.rows(0, -1)
        self.wait(self.out.at[pl.ds(begin, 256)], 16)
        ref = self.out.at[pl.ds(begin, 128)]
        self.send(ref, ref, 0, 1, 18)
        self.share(-1, 21)
        begin = self.rows(0, 1)
        self.wait(self.out.at[pl.ds(begin, 256)], 17)
        ref = self.out.at[pl.ds(begin + 128, 128)]
        self.send(ref, ref, 0, -1, 19)
        self.share(1, 22)

    def back_last(self):
        begin = self.rows(0, 2)
        self.wait(self.out.at[pl.ds(begin, 128)], 18)
        self.wait(self.out.at[pl.ds(begin + 128, 128)], 19)
        self.share(2, 23)

    def share_copy(self, shift, slot):
        ref = self.out.at[pl.ds(self.rows(0, shift), 256)]
        return pltpu.make_async_remote_copy(
            src_ref=ref,
            dst_ref=ref,
            send_sem=self.send_sems.at[self.part, slot],
            recv_sem=self.recv_sems.at[self.part, slot],
            device_id={"exp": 1 - lax.axis_index("exp")},
            device_id_type=MESH,
        )

    def share(self, shift, slot):
        copy = self.share_copy(shift, slot)
        copy.start()
        self.started.append(copy)

    def finish(self, other_out):
        for shift, slot in ((0, 20), (-1, 21), (1, 22), (2, 23)):
            ref = other_out.at[pl.ds(self.rows(0, shift), 256)]
            pltpu.make_async_remote_copy(
                src_ref=ref,
                dst_ref=ref,
                send_sem=self.send_sems.at[self.part, slot],
                recv_sem=self.recv_sems.at[self.part, slot],
                device_id={"exp": 1 - lax.axis_index("exp")},
                device_id_type=MESH,
            ).wait_recv()
        for copy in self.started:
            copy.wait_send()


SMALL_ROWS = 40


def total_kernel(
    mats_ref,
    small_ref,
    out_ref,
    small_out_ref,
    matrix,
    far,
    near,
    mid,
    low,
    arrived,
    small,
    small_first,
    send_sems,
    recv_sems,
    core_send,
    core_recv,
    small_send,
    small_recv,
):
    line, plane, core = lax.axis_index("seq"), lax.axis_index("grp"), lax.axis_index("exp")
    row, column = plane // 4, lax.rem(plane, 4)
    other = 1 - core
    places = (line, row, column)

    def neighbour(axis, step):
        if axis == 0:
            return {"seq": mod4(line + step)}
        if axis == 1:
            return {"grp": mod4(row + step) * 4 + column}
        return {"grp": row * 4 + mod4(column + step)}

    barrier = pltpu.get_barrier_semaphore()
    for axis in range(3):
        for step in (1, 2, 3):
            pl.semaphore_signal(
                barrier, inc=1, device_id=neighbour(axis, step), device_id_type=MESH
            )
    pl.semaphore_signal(barrier, inc=1, device_id={"exp": other}, device_id_type=MESH)
    pl.semaphore_wait(barrier, 10)

    def to_core(source, target, slot):
        return pltpu.make_async_remote_copy(
            src_ref=source,
            dst_ref=target,
            send_sem=core_send.at[slot],
            recv_sem=core_recv.at[slot],
            device_id={"exp": other},
            device_id_type=MESH,
        )

    own_small = pl.ds(core * SMALL_ROWS, SMALL_ROWS)
    core_copies = [to_core(mats_ref.at[other * 3 + part], arrived.at[part], part) for part in range(3)]
    core_copies.append(
        to_core(small_ref.at[pl.ds(other * SMALL_ROWS, SMALL_ROWS)], small_first, 3)
    )
    for copy in core_copies:
        copy.start()
    sums = [
        CubeSum(
            part,
            matrix.at[part],
            out_ref.at[core * 3 + part],
            far.at[part],
            near.at[part],
            mid.at[part],
            low.at[part],
            send_sems,
            recv_sems,
        )
        for part in range(3)
    ]
    for part in range(3):
        core_copies[part].wait()
        matrix[part] = (
            mats_ref[core * 3 + part].astype(F32) + arrived[part].astype(F32)
        ).astype(BF)
        sums[part].step_far()
    small_copies = []

    def small_step(axis):
        for step in (1, 2, 3):
            copy = pltpu.make_async_remote_copy(
                src_ref=small.at[axis, places[axis]],
                dst_ref=small.at[axis, places[axis]],
                send_sem=small_send.at[axis, step],
                recv_sem=small_recv.at[axis, step],
                device_id=neighbour(axis, step),
                device_id_type=MESH,
            )
            copy.start()
            small_copies.append(copy)

    def small_sum(axis):
        for step in (1, 2, 3):
            ref = small.at[axis, mod4(places[axis] - step)]
            pltpu.make_async_remote_copy(
                src_ref=ref,
                dst_ref=ref,
                send_sem=small_send.at[axis, step],
                recv_sem=small_recv.at[axis, step],
                device_id=neighbour(axis, step),
                device_id_type=MESH,
            ).wait_recv()
        return (small[axis, 0] + small[axis, 1]) + (small[axis, 2] + small[axis, 3])

    core_copies[3].wait()
    small[0, line] = small_ref[own_small, :] + small_first[...]
    small_step(0)
    for cube in sums:
        cube.step_near()
    small[1, row] = small_sum(0)
    small_step(1)
    for cube in sums:
        cube.step_mid()
    small[2, column] = small_sum(1)
    small_step(2)
    for cube in sums:
        cube.step_low()
    small_out_ref[own_small, :] = small_sum(2)
    small_last = to_core(small_out_ref.at[own_small], small_out_ref.at[own_small], 4)
    small_last.start()
    for cube in sums:
        cube.step_done()
    for cube in sums:
        cube.back_mid()
    for cube in sums:
        cube.back_near()
    for cube in sums:
        cube.back_far()
    for cube in sums:
        cube.back_last()
    for part in range(3):
        sums[part].finish(out_ref.at[other * 3 + part])
    small_last.wait_send()
    theirs = small_out_ref.at[pl.ds(other * SMALL_ROWS, SMALL_ROWS)]
    to_core(theirs, theirs, 4).wait_recv()
    for copy in small_copies:
        copy.wait_send()


def total_all(mats, small):
    dma = pltpu.SemaphoreType.DMA
    vmem = pl.BlockSpec(memory_space=pltpu.VMEM)
    return pl.pallas_call(
        total_kernel,
        out_shape=(
            jax.ShapeDtypeStruct((6, 1024, 512), BF),
            jax.ShapeDtypeStruct((2 * SMALL_ROWS, 512), F32),
        ),
        in_specs=[vmem, vmem],
        out_specs=(vmem, vmem),
        scratch_shapes=[
            pltpu.VMEM((3, 1024, 512), BF),
            pltpu.VMEM((3, 2, 128, 512), BF),
            pltpu.VMEM((3, 2, 256, 512), BF),
            pltpu.VMEM((3, 3, 64, 512), BF),
            pltpu.VMEM((3, 3, 16, 512), BF),
            pltpu.VMEM((3, 1024, 512), BF),
            pltpu.VMEM((3, 4, SMALL_ROWS, 512), F32),
            pltpu.VMEM((SMALL_ROWS, 512), F32),
            dma((3, 24)),
            dma((3, 24)),
            dma((5,)),
            dma((5,)),
            dma((3, 4)),
            dma((3, 4)),
        ],
        compiler_params=pltpu.CompilerParams(
            collective_id=3, has_side_effects=True, vmem_limit_bytes=40 << 20
        ),
    )(mats, small)


def dot_tn(left, right):
    return lax.dot_general(left, right, (((0,), (0,)), ((), ())), preferred_element_type=F32)


def dot_nt(left, right):
    return lax.dot_general(left, right, (((1,), (1,)), ((), ())), preferred_element_type=F32)


def dot_nn(left, right):
    return lax.dot_general(left, right, (((1,), (0,)), ((), ())), preferred_element_type=F32)


def expert_kernel(
    rows_ref,
    meta_ref,
    cot_ref,
    w_in_ref,
    w_out_ref,
    sib_in_ref,
    sib_out_ref,
    row_total_ref,
    score_out_ref,
    moe_ref,
    grad_ref,
    blocks,
    meta_in,
    score_send,
    cots,
    w_in,
    w_out,
    d_in,
    d_out,
    row_partial,
    moe_stage,
    picks,
    slot_rows,
    slot_cots,
    slot_grads,
    slot_res,
    slot_back,
    far,
    near,
    summed,
    far_two,
    near_two,
    send_sems,
    recv_sems,
    rsend_sems,
    rrecv_sems,
    meta_send,
    meta_recv,
    score_ssem,
    score_rsem,
    local_sems,
    cot_sems,
    moe_sems,
    pair_send,
    pair_recv,
    pair_ready,
):
    me = lax.axis_index("grp")
    core = lax.axis_index("exp")
    row, column = me // 4, lax.rem(me, 4)
    barrier = pltpu.get_barrier_semaphore()
    for step in range(1, PLANE):
        pl.semaphore_signal(
            barrier, inc=1, device_id={"grp": lax.rem(me + step, PLANE)}, device_id_type=MESH
        )
    pl.semaphore_signal(barrier, inc=1, device_id={"exp": 1 - core}, device_id_type=MESH)

    loads = [
        pltpu.make_async_copy(source, target, local_sems.at[slot])
        for slot, (source, target) in enumerate(
            (
                (w_in_ref, w_in.at[core]),
                (w_out_ref, w_out.at[core]),
                (sib_in_ref, w_in.at[1 - core]),
                (sib_out_ref, w_out.at[1 - core]),
            )
        )
    ]
    for load in loads:
        load.start()
    blocks[me] = rows_ref[...]
    meta_in[me] = meta_ref[me]
    d_in[...] = jnp.zeros_like(d_in)
    d_out[...] = jnp.zeros_like(d_out)

    def cot_copy(group, j):
        shift = group + group // 2 - 2 * (group // 3)
        index = mod4(row + j) * 4 + mod4(column + shift)
        return pltpu.make_async_copy(
            cot_ref.at[index], cots.at[lax.rem(group, 2), j], cot_sems.at[lax.rem(group, 2), j]
        )

    for j in range(GROUP):
        cot_copy(0, j).start()
    pl.semaphore_wait(barrier, PLANE)

    gathers = [PlaneGather(part, blocks, send_sems, recv_sems) for part in (0, 1)]
    for gather in gathers:
        gather.begin()
    for gather in gathers:
        gather.spread(0)
    meta_copies = []
    for step in range(1, PLANE):
        to = lax.rem(me + step, PLANE)
        copy = plane_copy(
            meta_ref.at[to], meta_in.at[me], meta_send.at[step], meta_recv.at[step], to
        )
        copy.start()
        meta_copies.append(copy)
    for load in loads:
        load.wait()
    for copy in meta_copies:
        copy.wait()
    for gather in gathers:
        gather.forward_first()
        gather.spread(-1)
        gather.spread(1)
    gathers[1].forward_second(0)
    for gather in gathers:
        gather.wait_far_first()
        gather.spread(2)
    gathers[1].wait_far_second(0)

    def moe_copy(j, index):
        return pltpu.make_async_copy(moe_stage.at[j], moe_ref.at[index], moe_sems.at[j])

    @pl.loop(0, 4)
    def _(group):
        shift = group + group // 2 - 2 * (group // 3)
        place = mod4(column + shift)
        parity = lax.rem(group, 2)

        @pl.when(group == 0)
        def _():
            gathers[0].forward_second(0)
            gathers[0].forward_second(-1)
            gathers[0].forward_second(1)
            gathers[0].forward_second(2)
            gathers[1].forward_second(-1)
            gathers[1].forward_second(1)

        @pl.when(group == 1)
        def _():
            gathers[1].wait_far_second(1)
            gathers[1].wait_far_second(-1)
            gathers[1].forward_second(2)

        @pl.when(group == 2)
        def _():
            for da in (0, -1, 1, 2):
                gathers[0].wait_far_second(da)
            gathers[1].wait_far_second(2)

        @pl.when(group < 3)
        def _():
            for j in range(GROUP):
                cot_copy(group + 1, j).start()

        for j in range(GROUP):
            cot_copy(group, j).wait()

        for expert in range(2):
            gates = []
            for j in range(GROUP):
                index = mod4(row + j) * 4 + place
                slots = meta_in[index, pl.ds(expert, 1), :]
                gate_row = meta_in[index, pl.ds(2 + expert, 1), :]
                slot_id = lax.broadcasted_iota(jnp.int32, (CAPACITY, BLOCK), 0).astype(F32)
                hit = slot_id == slots
                pick = jnp.where(hit, 1.0, 0.0).astype(BF)
                gate = jnp.sum(jnp.where(hit, gate_row, 0.0), axis=1, keepdims=True)
                gates.append(gate)
                here = pl.ds(j * CAPACITY, CAPACITY)
                picks[j, pl.ds(expert * CAPACITY, CAPACITY), :] = pick
                slot_rows[here, :] = dot_nn(pick, blocks[index]).astype(BF)
                cot_rows = dot_nn(pick, cots[parity, j])
                slot_cots[here, :] = cot_rows.astype(BF)
                slot_grads[here, :] = (gate * (RESIDUAL_MULT * cot_rows)).astype(BF)
            gate = jnp.concatenate(gates, axis=0)
            gate_up = dot_nn(slot_rows[...], w_in[expert])
            gate_half, up_half = gate_up[:, :INNER], gate_up[:, INNER:]
            sigmoid = jax.nn.sigmoid(gate_half)
            activated = gate_half * sigmoid
            hidden = (activated * up_half).astype(BF)
            result = dot_nn(hidden, w_out[expert]).astype(BF).astype(F32)
            scored = RESIDUAL_MULT * jnp.sum(
                slot_cots[...].astype(F32) * result, axis=1, keepdims=True
            )
            slot_res[expert] = (gate * result).astype(BF)
            hidden_grad = dot_nt(slot_grads[...], w_out[expert])
            gate_part = hidden_grad * up_half * sigmoid * (1.0 + gate_half * (1.0 - sigmoid))
            up_part = hidden_grad * activated
            pair_grad = jnp.concatenate([gate_part.astype(BF), up_part.astype(BF)], axis=1)
            slot_back[expert] = dot_nt(pair_grad, w_in[expert]).astype(BF)
            d_out[expert] += dot_tn(hidden, slot_grads[...])
            d_in[expert] += dot_tn(slot_rows[...], pair_grad)
            for j in range(GROUP):
                index = mod4(row + j) * 4 + place
                pick = picks[j, pl.ds(expert * CAPACITY, CAPACITY), :].astype(F32)
                spread = jnp.sum(
                    pick * scored[j * CAPACITY : (j + 1) * CAPACITY], axis=0, keepdims=True
                )
                score_send[index, pl.ds(expert, 1), :] = spread

        for j in range(GROUP):
            index = mod4(row + j) * 4 + place
            here = pl.ds(j * CAPACITY, CAPACITY)
            pick = picks[j]

            @pl.when(group > 0)
            def _():
                moe_copy(j, index).wait()

            values = jnp.concatenate([slot_res[0, here, :], slot_res[1, here, :]], axis=0)
            moe_stage[j] = dot_tn(pick, values).astype(BF)
            moe_copy(j, index).start()
            values = jnp.concatenate([slot_back[0, here, :], slot_back[1, here, :]], axis=0)
            row_partial[index] = dot_tn(pick, values).astype(BF)

    for gather in gathers:
        gather.finish()
    reducers = [
        PlaneReduce(
            part, row_partial, (far, near, summed, far_two, near_two), rsend_sems, rrecv_sems, row_total_ref
        )
        for part in (0, 1)
    ]
    for da in (2, 1, -1, 0):
        for reducer in reducers:
            reducer.step_far(da)
    score_out_ref[me] = score_send[me]
    score_copies = []
    for step in range(1, PLANE):
        to = lax.rem(me + step, PLANE)
        copy = plane_copy(
            score_send.at[to], score_out_ref.at[me], score_ssem.at[step], score_rsem.at[step], to
        )
        copy.start()
        score_copies.append(copy)
    other = 1 - core
    for j in range(4):
        cots[0, j] = d_in[other, pl.ds(j * BLOCK, BLOCK), :].astype(BF)
    for j in range(2):
        cots[1, j] = d_out[other, pl.ds(j * BLOCK, BLOCK), :].astype(BF)
    pl.semaphore_signal(pair_ready, inc=1, device_id={"exp": other}, device_id_type=MESH)
    pl.semaphore_wait(pair_ready, 1)
    pair_copies = []
    for j in range(6):
        copy = pltpu.make_async_remote_copy(
            src_ref=cots.at[j // 4, j % 4],
            dst_ref=blocks.at[j],
            send_sem=pair_send.at[j],
            recv_sem=pair_recv.at[j],
            device_id={"exp": other},
            device_id_type=MESH,
        )
        copy.start()
        pair_copies.append(copy)
    for da in (2, 1, -1, 0):
        for reducer in reducers:
            reducer.step_near(da)
    for j in range(6):
        pair_copies[j].wait()
        here = pl.ds((j % 4) * BLOCK, BLOCK)
        if j < 4:
            w_in[0, here, :] = (d_in[core, here, :] + blocks[j].astype(F32)).astype(BF)
        else:
            w_out[0, here, :] = (d_out[core, here, :] + blocks[j].astype(F32)).astype(BF)
    store_in = pltpu.make_async_copy(w_in.at[0], grad_ref.at[pl.ds(0, WIDTH)], local_sems.at[0])
    store_out = pltpu.make_async_copy(
        w_out.at[0], grad_ref.at[pl.ds(WIDTH, INNER)], local_sems.at[1]
    )
    store_in.start()
    store_out.start()
    for da in (2, 1, -1, 0):
        for reducer in reducers:
            reducer.step_sum(da)
    for reducer in reducers:
        reducer.finish()
    for copy in score_copies:
        copy.wait()
    for j in range(GROUP):
        moe_copy(j, j).wait()
    store_in.wait()
    store_out.wait()


def run_experts(rows, meta, cots, expert_in, expert_out, sib_in, sib_out):
    vmem = pl.BlockSpec(memory_space=pltpu.VMEM)
    hbm = pl.BlockSpec(memory_space=pl.ANY)
    dma = pltpu.SemaphoreType.DMA
    slots = GROUP * CAPACITY
    return pl.pallas_call(
        expert_kernel,
        out_shape=(
            jax.ShapeDtypeStruct((BLOCK, WIDTH), F32),
            jax.ShapeDtypeStruct((PLANE, 8, BLOCK), F32),
            jax.ShapeDtypeStruct((PLANE, BLOCK, WIDTH), BF),
            jax.ShapeDtypeStruct((WIDTH + INNER, WIDTH), BF),
        ),
        in_specs=[vmem, vmem, hbm, hbm, hbm, hbm, hbm],
        out_specs=(vmem, vmem, hbm, hbm),
        scratch_shapes=[
            pltpu.VMEM((PLANE, BLOCK, WIDTH), BF),
            pltpu.VMEM((PLANE, 8, BLOCK), F32),
            pltpu.VMEM((PLANE, 8, BLOCK), F32),
            pltpu.VMEM((2, GROUP, BLOCK, WIDTH), BF),
            pltpu.VMEM((2, WIDTH, 2 * INNER), BF),
            pltpu.VMEM((2, INNER, WIDTH), BF),
            pltpu.VMEM((2, WIDTH, 2 * INNER), F32),
            pltpu.VMEM((2, INNER, WIDTH), F32),
            pltpu.VMEM((PLANE, BLOCK, WIDTH), BF),
            pltpu.VMEM((GROUP, BLOCK, WIDTH), BF),
            pltpu.VMEM((GROUP, 2 * CAPACITY, BLOCK), BF),
            pltpu.VMEM((slots, WIDTH), BF),
            pltpu.VMEM((slots, WIDTH), BF),
            pltpu.VMEM((slots, WIDTH), BF),
            pltpu.VMEM((2, slots, WIDTH), BF),
            pltpu.VMEM((2, slots, WIDTH), BF),
        ]
        + reduce_buffers()
        + [dma((40,))] * 4
        + [dma((PLANE,))] * 4
        + [dma((4,))]
        + [dma((2, GROUP)), dma((GROUP,))]
        + [dma((6,))] * 2
        + [pltpu.SemaphoreType.REGULAR],
        compiler_params=pltpu.CompilerParams(
            collective_id=2, has_side_effects=True, vmem_limit_bytes=VMEM_LIMIT
        ),
    )(rows, meta, cots, expert_in, expert_out, sib_in, sib_out)


VMEM_LIMIT = 63 << 20


def rope_lanes(values, cosine, sine):
    lane = lax.broadcasted_iota(jnp.int32, (1, 128), 1)
    lower = lax.rem(lane, 64) < 32
    chunks = []
    for begin in range(0, values.shape[1], 128):
        chunk = values[:, begin : begin + 128]
        partner = jnp.where(lower, pltpu.roll(chunk, 96, 1), pltpu.roll(chunk, 32, 1))
        chunks.append(chunk * cosine + partner * sine)
    return chunks


def norm_scale(values):
    return lax.rsqrt(jnp.mean(values * values, axis=1, keepdims=True) + EPSILON)


def slot_table(routes, ranks):
    expert = lax.broadcasted_iota(jnp.int32, (BLOCK, 32), 1)
    rank_of = jnp.zeros((BLOCK, 32), jnp.int32)
    for k in range(8):
        rank_of = rank_of + jnp.where(routes[:, k : k + 1] == expert, ranks[:, k : k + 1] + 1, 0)
    chosen = rank_of > 0
    row = lax.broadcasted_iota(jnp.int32, (BLOCK, BLOCK), 0)
    lane = lax.broadcasted_iota(jnp.int32, (BLOCK, BLOCK), 1)
    source = lax.broadcasted_iota(jnp.int32, (32, BLOCK), 0)
    target = lax.broadcasted_iota(jnp.int32, (32, BLOCK), 1)
    repeat = jnp.where(lax.rem(target, 32) == source, 1.0, 0.0).astype(BF)
    rank_wide = dot_nn(rank_of.astype(F32).astype(BF), repeat)
    hit = rank_wide == (lane // 32 + 1).astype(F32)
    counts = jnp.where(hit, 1.0, 0.0)
    earlier = jnp.where(row > lane, 1.0, 0.0).astype(BF)
    before = dot_nn(earlier, counts.astype(BF))
    totals = jnp.sum(counts, axis=0, keepdims=True)
    lower = (lax.rem(row, 32) == lax.rem(lane, 32)) & (row // 32 < lane // 32)
    offsets = dot_nn(totals.astype(BF), jnp.where(lower, 1.0, 0.0).astype(BF))
    place = jnp.where(hit, before + offsets, 0.0)
    place = place[:, :128] + place[:, 128:]
    place = place + pltpu.roll(place, 64, 1)
    place = place + pltpu.roll(place, 32, 1)
    place = place[:, :32]
    return chosen, jnp.where(chosen & (place < CAPACITY), place, -1.0)


def attend_kernel(
    tokens_ref,
    seg_ref,
    routes_ref,
    ranks_ref,
    gain_one_ref,
    w_query_ref,
    w_key_ref,
    w_value_ref,
    w_output_ref,
    gain_two_ref,
    w_router_ref,
    cosine_ref,
    sine_ref,
    cot_ref,
    w_in_ref,
    w_out_ref,
    routed_ref,
    residual_ref,
    heads_ref,
    normed_ref,
    query_ref,
    kv_ref,
    lse_ref,
    bias_ref,
    gates_ref,
    meta_ref,
    cots_ref,
    sib_in_ref,
    sib_out_ref,
    segs,
    top,
    expsum,
    acc,
    send_sems,
    recv_sems,
    kv_send,
    kv_recv,
    seg_send,
    seg_recv,
    weight_send,
    weight_recv,
    local_sem,
):
    line, plane, core = lax.axis_index("seq"), lax.axis_index("grp"), lax.axis_index("exp")
    block = 2 * line + core
    row, column = plane // 4, lax.rem(plane, 4)
    barrier = pltpu.get_barrier_semaphore()
    for index in (
        mod4(row + 1) * 4 + column,
        mod4(row - 1) * 4 + column,
        row * 4 + mod4(column + 1),
        row * 4 + mod4(column - 1),
    ):
        pl.semaphore_signal(barrier, inc=1, device_id={"grp": index}, device_id_type=MESH)
    for step in (1, 2, 3):
        pl.semaphore_signal(
            barrier, inc=1, device_id={"seq": mod4(line + step)}, device_id_type=MESH
        )
    pl.semaphore_signal(barrier, inc=1, device_id={"exp": 1 - core}, device_id_type=MESH)
    own_cot = pltpu.make_async_copy(cot_ref, cots_ref.at[plane], local_sem)
    own_cot.start()

    tokens = tokens_ref[...].astype(F32)
    normed = (tokens * norm_scale(tokens) * gain_one_ref[...]).astype(BF)
    normed_ref[...] = normed
    cosine, sine = cosine_ref[...], sine_ref[...]
    keys = dot_nn(normed, w_key_ref[...])
    values = dot_nn(normed, w_value_ref[...]).astype(BF)
    key_chunks = rope_lanes(keys, cosine, sine)
    for head in range(KV_HEADS):
        chunk = key_chunks[head // 2].astype(BF)
        key = chunk[:, (head % 2) * 64 : (head % 2) * 64 + 64]
        kv_ref[0, head] = jnp.concatenate([key, values[:, head * 64 : head * 64 + 64]], axis=1)
    segs[0] = seg_ref[...]
    own_cot.wait()
    pl.semaphore_wait(barrier, 8)

    def kv_copies(source, target, device, slot):
        return [
            pltpu.make_async_remote_copy(
                src_ref=ref.at[source],
                dst_ref=ref.at[target],
                send_sem=sends.at[slot],
                recv_sem=recvs.at[target],
                device_id=device,
                device_id_type=MESH,
            )
            for ref, sends, recvs in ((kv_ref, kv_send, kv_recv), (segs, seg_send, seg_recv))
        ]

    sibling = {"exp": 1 - core}
    to_near = kv_copies(0, 2, {"seq": mod4(line + 1)}, 1)
    to_far = kv_copies(0, 4, {"seq": mod4(line + 2)}, 2)
    to_sibling = kv_copies(0, 1, sibling, 0)
    forward_near = kv_copies(2, 3 - 2 * core, sibling, 3)
    forward_far = kv_copies(4, 3, sibling, 4)

    def begin(copies):
        for copy in copies:
            copy.start()

    def sent(copies):
        for copy in copies:
            copy.wait_send()

    @pl.when(line < 3)
    def _():
        begin(to_near)

    @pl.when(core == 0)
    def _():
        begin(to_sibling)

    @pl.when(line < 2)
    def _():
        begin(to_far)

    gathers = [PlaneGather(part, cots_ref, send_sems, recv_sems) for part in (0, 1)]
    for gather in gathers:
        gather.begin()
    for gather in gathers:
        gather.spread(0)
    weight_copies = [
        pltpu.make_async_remote_copy(
            src_ref=source,
            dst_ref=target,
            send_sem=weight_send.at[slot],
            recv_sem=weight_recv.at[slot],
            device_id=sibling,
            device_id_type=MESH,
        )
        for slot, (source, target) in enumerate(((w_in_ref, sib_in_ref), (w_out_ref, sib_out_ref)))
    ]
    begin(weight_copies)

    lane = lax.broadcasted_iota(jnp.int32, (1, 128), 1)
    queries = dot_nn(normed, w_query_ref[...])
    for head, chunk in enumerate(rope_lanes(queries, cosine, sine)):
        chunk = (chunk.astype(BF).astype(F32) * ATTENTION_FACTOR)
        query_ref[head, :BLOCK, :] = jnp.where(lane < 64, chunk, 0.0).astype(BF)
        query_ref[head, BLOCK:, :] = jnp.where(lane < 64, pltpu.roll(chunk, 64, 1), 0.0).astype(BF)
    top[...] = jnp.full(top.shape, MASKED, F32)
    expsum[...] = jnp.zeros(expsum.shape, F32)
    acc[...] = jnp.zeros(acc.shape, F32)
    seg_column = seg_ref[...].T[:, :1]

    def attend(slot):
        i = lax.broadcasted_iota(jnp.int32, (BLOCK, BLOCK), 0)
        j = lax.broadcasted_iota(jnp.int32, (BLOCK, BLOCK), 1)
        distance = slot * BLOCK + i - j
        allowed = (seg_column == segs[slot, 0:1, :]) & (distance >= 0) & (distance < WINDOW)
        bias = jnp.where(allowed, 0.0, MASKED)
        bias_ref[slot] = bias

        @pl.loop(0, KV_HEADS)
        def _(head):
            pair = kv_ref[slot, head]
            one = bias_ref[slot]
            score = dot_nt(query_ref[head], pair)
            score = score + jnp.concatenate([one, one], axis=0)
            old = top[head][:, :1]
            new = jnp.maximum(old, jnp.max(score, axis=1, keepdims=True))
            weight = jnp.exp(score - new)
            fade = jnp.exp(old - new)
            expsum[head] = expsum[head] * fade + jnp.sum(weight, axis=1, keepdims=True)
            acc[head] = acc[head] * fade + dot_nn(weight.astype(BF), pair)
            top[head] = jnp.broadcast_to(new, (2 * BLOCK, 128))

    def wait_block(slot):
        for ref, sends, recvs in ((kv_ref, kv_send, kv_recv), (segs, seg_send, seg_recv)):
            pltpu.make_async_remote_copy(
                src_ref=ref.at[slot],
                dst_ref=ref.at[slot],
                send_sem=sends.at[0],
                recv_sem=recvs.at[slot],
                device_id=sibling,
                device_id_type=MESH,
            ).wait_recv()

    attend(0)
    for gather in gathers:
        gather.forward_first()
        gather.spread(-1)
        gather.spread(1)

    chosen, kept = slot_table(routes_ref[...], ranks_ref[...])
    kept_rows = jnp.concatenate([kept, jnp.zeros((BLOCK, 96), F32)], axis=1).T
    for index in range(PLANE):
        meta_ref[index, 0:2, :] = kept_rows[2 * index : 2 * index + 2]
        meta_ref[index, 4:8, :] = jnp.zeros((4, BLOCK), F32)

    first = 2 - core

    @pl.when(block >= first)
    def _():
        wait_block(first)

        @pl.when(core == 0)
        def _():
            begin(forward_near)

        attend(first)

    for gather in gathers:
        gather.forward_second(0)
    for gather in gathers:
        gather.wait_far_first()
        gather.spread(2)
    second = 1 + core

    @pl.when(block >= second)
    def _():
        wait_block(second)

        @pl.when(core == 1)
        def _():
            begin(forward_near)

        attend(second)

    for da in (-1, 1):
        for gather in gathers:
            gather.forward_second(da)
    third = 4 - core

    @pl.when(block >= third)
    def _():
        wait_block(third)
        attend(third)

    for gather in gathers:
        gather.forward_second(2)
    fourth = 3 + core

    @pl.when(block >= fourth)
    def _():
        wait_block(fourth)

        @pl.when(core == 1)
        def _():
            begin(forward_far)

        attend(fourth)

    for head in range(KV_HEADS):
        inverse = 1.0 / expsum[head][:, :1]
        pair = acc[head] * inverse
        heads_ref[:, head * 128 : head * 128 + 128] = jnp.where(
            lane < 64, pltpu.roll(pair[:BLOCK], 64, 1), pair[BLOCK:]
        ).astype(BF)
        lse_ref[head] = top[head] + jnp.log(expsum[head])
    branch = dot_nn(heads_ref[...], w_output_ref[...])
    residual = tokens_ref[...].astype(F32) + RESIDUAL_MULT * branch
    residual_ref[...] = residual
    routed = (residual * norm_scale(residual) * gain_two_ref[...]).astype(BF)
    routed_ref[...] = routed
    logits = dot_nn(routed, w_router_ref[...])
    logits = jnp.where(chosen, logits, MASKED)
    powers = jnp.exp(logits - jnp.max(logits, axis=1, keepdims=True))
    gates = jnp.where(chosen, powers / jnp.sum(powers, axis=1, keepdims=True), 0.0)
    gates_ref[...] = gates
    gate_rows = jnp.concatenate([gates, jnp.zeros((BLOCK, 96), F32)], axis=1).T
    for index in range(PLANE):
        meta_ref[index, 2:4, :] = gate_rows[2 * index : 2 * index + 2]

    for da in (0, -1, 1, 2):
        for gather in gathers:
            gather.wait_far_second(da)
    for gather in gathers:
        gather.finish()
    for copy in weight_copies:
        copy.wait()

    @pl.when(line < 3)
    def _():
        sent(to_near)

    @pl.when(core == 0)
    def _():
        sent(to_sibling)

    @pl.when(line < 2)
    def _():
        sent(to_far)

    @pl.when(line >= 1)
    def _():
        sent(forward_near)

    @pl.when((line >= 2) & (core == 1))
    def _():
        sent(forward_far)


def run_attention(
    tokens, seg_tile, routes, ranks, gain_one, w_query, w_key, w_value, w_output, gain_two,
    w_router, cosine, sine, cot, expert_in, expert_out,
):
    vmem = pl.BlockSpec(memory_space=pltpu.VMEM)
    hbm = pl.BlockSpec(memory_space=pl.ANY)
    dma = pltpu.SemaphoreType.DMA
    shape = jax.ShapeDtypeStruct
    return pl.pallas_call(
        attend_kernel,
        out_shape=(
            shape((BLOCK, WIDTH), BF),
            shape((BLOCK, WIDTH), F32),
            shape((BLOCK, WIDTH), BF),
            shape((BLOCK, WIDTH), BF),
            shape((KV_HEADS, 2 * BLOCK, 128), BF),
            shape((5, KV_HEADS, BLOCK, 128), BF),
            shape((KV_HEADS, 2 * BLOCK, 128), F32),
            shape((5, BLOCK, BLOCK), F32),
            shape((BLOCK, 32), F32),
            shape((PLANE, 8, BLOCK), F32),
            shape((PLANE, BLOCK, WIDTH), BF),
            shape((WIDTH, 2 * INNER), BF),
            shape((INNER, WIDTH), BF),
        ),
        in_specs=[vmem] * 13 + [hbm] * 3,
        out_specs=(vmem,) * 10 + (hbm,) * 3,
        scratch_shapes=[
            pltpu.VMEM((5, 8, BLOCK), F32),
            pltpu.VMEM((KV_HEADS, 2 * BLOCK, 128), F32),
            pltpu.VMEM((KV_HEADS, 2 * BLOCK, 128), F32),
            pltpu.VMEM((KV_HEADS, 2 * BLOCK, 128), F32),
            dma((40,)),
            dma((40,)),
            dma((5,)),
            dma((5,)),
            dma((5,)),
            dma((5,)),
            dma((2,)),
            dma((2,)),
            dma,
        ],
        compiler_params=pltpu.CompilerParams(
            collective_id=0, has_side_effects=True, vmem_limit_bytes=58 << 20
        ),
    )(
        tokens, seg_tile, routes, ranks, gain_one, w_query, w_key, w_value, w_output, gain_two,
        w_router, cosine, sine, cot, expert_in, expert_out,
    )


def on_device(
    tokens,
    segments,
    routes,
    rank_order,
    attn_gain,
    w_query,
    w_key,
    w_value,
    w_output,
    ffn_gain,
    w_router,
    expert_in,
    expert_out,
    cotangent,
):
    tok_rows = tokens.shape[1]
    model_width = tokens.shape[2]
    experts = w_router.shape[1]
    kv_width = w_key.shape[1]
    kv_heads = KV_HEADS
    head_dim = HEAD
    q_heads = HEADS
    group_size = q_heads // kv_heads
    blocks = lax.axis_size(("seq", "exp"))
    block_id = lax.axis_index(("seq", "exp"))
    hop_count = min(-(-WINDOW // tok_rows), blocks - 1)
    key_span = (hop_count + 1) * tok_rows
    inputs = tokens[0].astype(jnp.float32)
    positions = block_id * tok_rows + jnp.arange(tok_rows, dtype=jnp.int32)
    cosine, sine_part = rope_tables(positions, head_dim)
    cosine_lanes = jnp.tile(cosine[:, 0], (1, 4))
    sine_lanes = jnp.tile(jnp.concatenate([-sine_part[:, 0], sine_part[:, 0]], axis=1), (1, 2))
    seg_tile = jnp.broadcast_to(segments.astype(jnp.float32), (8, tok_rows))
    (
        routed_in, residual, heads_out, normed, query_heads, kv_heads_all, lse, bias, gates, meta,
        cots, sib_in, sib_out,
    ) = run_attention(
        tokens[0], seg_tile, routes[0], rank_order[0], attn_gain[None], w_query, w_key, w_value,
        w_output, ffn_gain[None], w_router, cosine_lanes, sine_lanes, cotangent[0], expert_in[0],
        expert_out[0],
    )
    scale_one = lax.rsqrt(jnp.mean(inputs * inputs, axis=-1, keepdims=True) + EPSILON)
    scale_two = lax.rsqrt(jnp.mean(residual * residual, axis=-1, keepdims=True) + EPSILON)
    expert_row_sum, scores, moe_partial, expert_grads = run_experts(
        routed_in, meta, cots, expert_in[0], expert_out[0], sib_in, sib_out
    )
    moe_out, expert_total = return_plane(moe_partial, expert_grads)
    output = (residual + RESIDUAL_MULT * moe_out).astype(jnp.bfloat16)[None]
    upstream = cotangent[0].astype(jnp.float32)
    gate_grad = scores[:, :2, :].reshape(experts, tok_rows).T
    choice_grad = gates * (gate_grad - jnp.sum(gates * gate_grad, axis=1, keepdims=True))
    logit_grad = choice_grad.astype(jnp.bfloat16)
    router_w_grad = inner_rows(routed_in, logit_grad)
    routed_grad = product_back(logit_grad, w_router) + expert_row_sum
    normal_two = residual * scale_two
    ffn_gain_grad = jnp.sum(routed_grad * normal_two, axis=0)
    weighted_two = routed_grad * ffn_gain
    residual_grad = (
        upstream
        + scale_two * weighted_two
        - residual * scale_two**3 * jnp.mean(weighted_two * residual, axis=-1, keepdims=True)
    )
    branch_grad = (RESIDUAL_MULT * residual_grad).astype(jnp.bfloat16)
    head_gradient = (
        product_back(branch_grad, w_output)
        .astype(jnp.bfloat16)
        .reshape(tok_rows, kv_heads, group_size, head_dim)
    )
    kv_cat = jnp.flip(kv_heads_all, 0).transpose(0, 2, 1, 3).reshape(key_span, kv_heads, 128)
    key_gathered, value_gathered = kv_cat[..., :64], kv_cat[..., 64:]
    valid = (block_id - jnp.arange(hop_count, -1, -1) >= 0).repeat(tok_rows)
    key_gathered = jnp.where(valid[:, None, None], key_gathered, 0)
    value_gathered = jnp.where(valid[:, None, None], value_gathered, 0)
    query_rows = (
        (query_heads[..., :64].astype(jnp.float32) * 64).astype(jnp.bfloat16)
        .reshape(kv_heads, 2, tok_rows, head_dim).transpose(2, 0, 1, 3)
    )
    bias_all = jnp.where(
        valid[None], jnp.flip(bias, 0).transpose(1, 0, 2).reshape(tok_rows, key_span), MASKED
    )
    raw_scores = ATTENTION_FACTOR * jnp.einsum(
        "dklp,okp->kldo", query_rows, key_gathered, preferred_element_type=jnp.float32
    )
    lse_rows = lse[:, :, 0].reshape(kv_heads, 2, tok_rows, 1)
    probs_full = jnp.exp(jnp.where(bias_all == 0, raw_scores, MASKED) - lse_rows)
    probability_lowered = probs_full.astype(jnp.bfloat16)
    prob_grad = jnp.einsum(
        "dklp,okp->kldo", head_gradient, value_gathered, preferred_element_type=jnp.float32
    )
    score_gradient = (
        probs_full * (prob_grad - jnp.sum(probs_full * prob_grad, axis=-1, keepdims=True))
    ).astype(jnp.bfloat16)
    queries_grad = ATTENTION_FACTOR * jnp.einsum(
        "uzjq,quk->juzk", score_gradient, key_gathered, preferred_element_type=jnp.float32
    )
    keys_grad_all = (
        ATTENTION_FACTOR
        * jnp.einsum(
            "ykze,zykm->eym", score_gradient, query_rows, preferred_element_type=jnp.float32
        )
    ).reshape(key_span, kv_width)
    values_grad_all = jnp.einsum(
        "ykze,zykm->eym", probability_lowered, head_gradient, preferred_element_type=jnp.float32
    ).reshape(key_span, kv_width)
    keys_grad = keys_grad_all[hop_count * tok_rows :]
    values_grad = values_grad_all[hop_count * tok_rows :]
    for hop_index in range(1, hop_count + 1):
        first_row = (hop_count - hop_index) * tok_rows
        key_back, value_back = (
            from_behind(
                keys_grad_all[first_row : first_row + tok_rows].astype(jnp.bfloat16),
                ("seq", "exp"),
                -hop_index,
            ).astype(jnp.float32),
            from_behind(
                values_grad_all[first_row : first_row + tok_rows].astype(jnp.bfloat16),
                ("seq", "exp"),
                -hop_index,
            ).astype(jnp.float32),
        )
        keys_grad = keys_grad + key_back
        values_grad = values_grad + value_back
    query_pre_grad = (
        unrotate(queries_grad.reshape(tok_rows, q_heads, head_dim), cosine, sine_part)
        .astype(jnp.bfloat16)
        .reshape(tok_rows, model_width)
    )
    key_pre_grad = (
        unrotate(keys_grad.reshape(tok_rows, kv_heads, head_dim), cosine, sine_part)
        .astype(jnp.bfloat16)
        .reshape(tok_rows, kv_width)
    )
    value_pre_grad = values_grad.astype(jnp.bfloat16)
    normed_grad = (
        product_back(query_pre_grad, w_query)
        + product_back(key_pre_grad, w_key)
        + product_back(value_pre_grad, w_value)
    )
    attn_gain_grad = jnp.sum(normed_grad * inputs * scale_one, axis=0)
    weighted_one = normed_grad * attn_gain
    input_grad = (
        residual_grad
        + scale_one * weighted_one
        - inputs * scale_one**3 * jnp.mean(weighted_one * inputs, axis=-1, keepdims=True)
    )
    up_total = expert_total[None, :model_width].astype(jnp.float32)
    down_total = expert_total[None, model_width:].astype(jnp.float32)
    half = model_width // 2
    mats = jnp.stack(
        [
            inner_rows(normed, query_pre_grad[:, :half]),
            inner_rows(normed, query_pre_grad[:, half:]),
            inner_rows(normed, key_pre_grad),
            inner_rows(normed, value_pre_grad),
            inner_rows(heads_out, branch_grad[:, :half]),
            inner_rows(heads_out, branch_grad[:, half:]),
        ]
    ).astype(jnp.bfloat16)
    small = jnp.concatenate(
        [
            router_w_grad.reshape(64, 512),
            attn_gain_grad.reshape(2, 512),
            ffn_gain_grad.reshape(2, 512),
            jnp.zeros((2 * SMALL_ROWS - 68, 512), jnp.float32),
        ],
        axis=0,
    )
    mats_total, small_total = total_all(mats, small)
    query_total = jnp.concatenate([mats_total[0], mats_total[1]], axis=1).astype(jnp.float32)
    key_total = mats_total[2].astype(jnp.float32)
    value_total = mats_total[3].astype(jnp.float32)
    out_total = jnp.concatenate([mats_total[4], mats_total[5]], axis=1).astype(jnp.float32)
    router_total = small_total[:64].reshape(router_w_grad.shape)
    gain_one_total = small_total[64:66].reshape(model_width)
    gain_two_total = small_total[66:68].reshape(model_width)
    return (
        output,
        input_grad.astype(jnp.bfloat16)[None],
        gain_one_total,
        query_total,
        key_total,
        value_total,
        out_total,
        gain_two_total,
        router_total,
        up_total,
        down_total,
    )


def solution(mesh):
    placed = (
        P("grp", ("seq", "exp"), None),
        P("grp", ("seq", "exp")),
        P("grp", ("seq", "exp"), None),
        P("grp", ("seq", "exp"), None),
        P(),
        P(),
        P(),
        P(),
        P(),
        P(),
        P(),
        P(("grp", "exp"), None, None),
        P(("grp", "exp"), None, None),
        P("grp", ("seq", "exp"), None),
    )
    return jax.shard_map(
        on_device,
        mesh=mesh,
        in_specs=placed,
        out_specs=(
            P("grp", ("seq", "exp"), None),
            P("grp", ("seq", "exp"), None),
            P(),
            P(),
            P(),
            P(),
            P(),
            P(),
            P(),
            P(("grp", "exp"), None, None),
            P(("grp", "exp"), None, None),
        ),
        check_vma=False,
    )
```

```python
import math

import jax
import jax.numpy as jnp
from jax import lax
from jax.experimental import pallas as pl
from jax.experimental.pallas import tpu as pltpu
from jax.sharding import PartitionSpec as P

HEADS = 16
KV_HEADS = 8
HEAD = 64
WINDOW = 1024


EPSILON = 1e-06
ATTENTION_FACTOR = 0.015625
RESIDUAL_MULT = 0.22
ROPE_BASE = 10000.0
MASKED = -1e30


def rope_tables(positions, head_dim):
    half_dim = head_dim // 2
    frequency = jnp.exp(
        jnp.arange(half_dim, dtype=jnp.float32) * (-2.0 * math.log(ROPE_BASE) / head_dim)
    )
    angles = positions.astype(jnp.float32)[:, None] * frequency[None, :]
    return (jnp.cos(angles)[:, None, :], jnp.sin(angles)[:, None, :])


MESH = pl.DeviceIdType.MESH
CAPACITY = 80
BLOCK = 256
HALF = 128
QUARTER = 64
WIDTH = 1024
INNER = 512
PLANE = 16
GROUP = 4
BF = jnp.bfloat16
F32 = jnp.float32


def mod4(value):
    return lax.rem(value + 8, 4)


def plane_id(part, first, second):
    return first * 4 + second if part == 0 else second * 4 + first


def plane_coords(part):
    index = lax.axis_index("grp")
    row, column = index // 4, lax.rem(index, 4)
    return (row, column) if part == 0 else (column, row)


def plane_copy(source, target, send_sem, recv_sem, index):
    return pltpu.make_async_remote_copy(
        src_ref=source,
        dst_ref=target,
        send_sem=send_sem,
        recv_sem=recv_sem,
        device_id={"grp": index},
        device_id_type=MESH,
    )


def greet_plane():
    row, column = plane_coords(0)
    barrier = pltpu.get_barrier_semaphore()
    for index in (
        mod4(row + 1) * 4 + column,
        mod4(row - 1) * 4 + column,
        row * 4 + mod4(column + 1),
        row * 4 + mod4(column - 1),
    ):
        pl.semaphore_signal(barrier, inc=1, device_id={"grp": index}, device_id_type=MESH)
    pl.semaphore_wait(barrier, 4)


class PlaneGather:
    order = {0: 0, -1: 1, 1: 2, 2: 3}

    def __init__(self, part, blocks, send_sems, recv_sems):
        self.part, self.blocks = part, blocks
        self.send_sems, self.recv_sems = send_sems, recv_sems
        self.first, self.second = plane_coords(part)
        self.started = []

    def ref(self, da, db, half=None):
        index = plane_id(self.part, mod4(self.first + da), mod4(self.second + db))
        begin = self.part * HALF
        if half is None:
            return self.blocks.at[index, pl.ds(begin, HALF)]
        return self.blocks.at[index, pl.ds(begin + half * QUARTER, QUARTER)]

    def copy(self, da, db, half, axis, step, slot):
        if axis == 0:
            to = plane_id(self.part, mod4(self.first + step), self.second)
        else:
            to = plane_id(self.part, self.first, mod4(self.second + step))
        ref, sem = self.ref(da, db, half), self.part * 20 + slot
        return plane_copy(ref, ref, self.send_sems.at[sem], self.recv_sems.at[sem], to)

    def send(self, *where):
        self.copy(*where).start()
        self.started.append(where)

    def wait(self, da, db, half, slot):
        ref, sem = self.ref(da, db, half), self.part * 20 + slot
        plane_copy(
            ref, ref, self.send_sems.at[sem], self.recv_sems.at[sem],
            plane_id(self.part, self.first, self.second),
        ).wait_recv()

    def begin(self):
        self.send(0, 0, None, 0, 1, 0)
        self.send(0, 0, None, 0, -1, 1)

    def spread(self, da):
        slot = 4 + 4 * self.order[da]
        self.send(da, 0, None, 1, 1, slot)
        self.send(da, 0, None, 1, -1, slot + 1)

    def forward_first(self):
        self.wait(-1, 0, None, 0)
        self.send(-1, 0, 0, 0, 1, 2)
        self.wait(1, 0, None, 1)
        self.send(1, 0, 1, 0, -1, 3)

    def forward_second(self, da):
        slot = 4 + 4 * self.order[da]
        self.wait(da, -1, None, slot)
        self.send(da, -1, 0, 1, 1, slot + 2)
        self.wait(da, 1, None, slot + 1)
        self.send(da, 1, 1, 1, -1, slot + 3)

    def wait_far_first(self):
        self.wait(2, 0, 0, 2)
        self.wait(2, 0, 1, 3)

    def wait_far_second(self, da):
        slot = 4 + 4 * self.order[da]
        self.wait(da, 2, 0, slot + 2)
        self.wait(da, 2, 1, slot + 3)

    def finish(self):
        for where in self.started:
            self.copy(*where).wait_send()


class PlaneReduce:
    order = {2: 0, 1: 1, -1: 2, 0: 3}

    def __init__(self, part, partial, buffers, send_sems, recv_sems, total):
        self.part, self.partial, self.total = part, partial, total
        self.far, self.near, self.summed, self.far_two, self.near_two = buffers
        self.send_sems, self.recv_sems = send_sems, recv_sems
        self.first, self.second = plane_coords(part)
        self.started = []

    def ref(self, da, db, half=None):
        index = plane_id(self.part, mod4(self.first + da), mod4(self.second + db))
        begin = self.part * HALF
        if half is None:
            return self.partial.at[index, pl.ds(begin, HALF)]
        return self.partial.at[index, pl.ds(begin + half * QUARTER, QUARTER)]

    def send(self, source, target, axis, step, slot):
        if axis == 0:
            to = plane_id(self.part, mod4(self.first + step), self.second)
        else:
            to = plane_id(self.part, self.first, mod4(self.second + step))
        sem = self.part * 20 + slot
        copy = plane_copy(source, target, self.send_sems.at[sem], self.recv_sems.at[sem], to)
        copy.start()
        self.started.append(copy)

    def wait(self, target, slot):
        sem = self.part * 20 + slot
        plane_copy(
            target, target, self.send_sems.at[sem], self.recv_sems.at[sem],
            plane_id(self.part, self.first, self.second),
        ).wait_recv()

    def add(self, target, source):
        target[...] = (target[...].astype(F32) + source[...].astype(F32)).astype(BF)

    def step_far(self, da):
        part, place = self.part, self.order[da]
        self.send(self.ref(da, 2, 0), self.far.at[part, place, 0], 1, 1, 4 * place)
        self.send(self.ref(da, 2, 1), self.far.at[part, place, 1], 1, -1, 4 * place + 1)

    def step_near(self, da):
        part, place = self.part, self.order[da]
        self.wait(self.far.at[part, place, 0], 4 * place)
        self.add(self.ref(da, 1, 0), self.far.at[part, place, 0])
        self.send(self.ref(da, 1), self.near.at[part, place, 0], 1, 1, 4 * place + 2)
        self.wait(self.far.at[part, place, 1], 4 * place + 1)
        self.add(self.ref(da, -1, 1), self.far.at[part, place, 1])
        self.send(self.ref(da, -1), self.near.at[part, place, 1], 1, -1, 4 * place + 3)

    def step_sum(self, da):
        part, place = self.part, self.order[da]
        self.wait(self.near.at[part, place, 0], 4 * place + 2)
        self.wait(self.near.at[part, place, 1], 4 * place + 3)
        value = (
            self.ref(da, 0)[...].astype(F32)
            + self.near[part, place, 0].astype(F32)
            + self.near[part, place, 1].astype(F32)
        )
        rows = pl.ds(part * HALF, HALF)
        if da == 0:
            self.total[rows] = value
            self.wait(self.near_two.at[part, 0], 18)
            self.wait(self.near_two.at[part, 1], 19)
            self.total[rows] += self.near_two[part, 0].astype(F32) + self.near_two[part, 1].astype(F32)
            return
        self.summed[part, place] = value.astype(BF)
        lower, upper = pl.ds(0, QUARTER), pl.ds(QUARTER, QUARTER)
        if da == 2:
            self.send(self.summed.at[part, 0, lower], self.far_two.at[part, 0], 0, 1, 16)
            self.send(self.summed.at[part, 0, upper], self.far_two.at[part, 1], 0, -1, 17)
        if da == 1:
            self.wait(self.far_two.at[part, 0], 16)
            self.add(self.summed.at[part, 1, lower], self.far_two.at[part, 0])
            self.send(self.summed.at[part, 1], self.near_two.at[part, 0], 0, 1, 18)
        if da == -1:
            self.wait(self.far_two.at[part, 1], 17)
            self.add(self.summed.at[part, 2, upper], self.far_two.at[part, 1])
            self.send(self.summed.at[part, 2], self.near_two.at[part, 1], 0, -1, 19)

    def finish(self):
        for copy in self.started:
            copy.wait_send()


def reduce_buffers():
    return [
        pltpu.VMEM((2, 4, 2, QUARTER, WIDTH), BF),
        pltpu.VMEM((2, 4, 2, HALF, WIDTH), BF),
        pltpu.VMEM((2, 3, HALF, WIDTH), BF),
        pltpu.VMEM((2, 2, QUARTER, WIDTH), BF),
        pltpu.VMEM((2, 2, HALF, WIDTH), BF),
    ]


def run_reduce(reducers):
    for da in (2, 1, -1, 0):
        for reducer in reducers:
            reducer.step_far(da)
    for da in (2, 1, -1, 0):
        for reducer in reducers:
            reducer.step_near(da)
    for da in (2, 1, -1, 0):
        for reducer in reducers:
            reducer.step_sum(da)
    for reducer in reducers:
        reducer.finish()


class RowRing:
    def __init__(self, summed, total, far, near, send_sems, recv_sems, local_sems):
        self.summed, self.total, self.far, self.near = summed, total, far, near
        self.local_sem = local_sems.at[3]
        self.send_sems, self.recv_sems = send_sems, recv_sems
        self.me = lax.axis_index("seq")
        self.rows = summed.shape[0] // 4
        self.started = []

    def piece(self, ref, shift, half=None):
        begin = mod4(self.me + shift) * self.rows
        if half is None:
            return ref.at[pl.ds(begin, self.rows)]
        return ref.at[pl.ds(begin + half * (self.rows // 2), self.rows // 2)]

    def send(self, source, target, step, slot):
        copy = pltpu.make_async_remote_copy(
            src_ref=source,
            dst_ref=target,
            send_sem=self.send_sems.at[slot],
            recv_sem=self.recv_sems.at[slot],
            device_id={"seq": mod4(self.me + step)},
            device_id_type=MESH,
        )
        copy.start()
        self.started.append(copy)

    def wait(self, target, slot):
        pltpu.make_async_remote_copy(
            src_ref=target,
            dst_ref=target,
            send_sem=self.send_sems.at[slot],
            recv_sem=self.recv_sems.at[slot],
            device_id={"seq": self.me},
            device_id_type=MESH,
        ).wait_recv()

    def add(self, target, source):
        target[...] = (target[...].astype(F32) + source[...].astype(F32)).astype(BF)

    def step_far(self):
        self.send(self.piece(self.summed, 2, 0), self.far.at[0], 1, 0)
        self.send(self.piece(self.summed, 2, 1), self.far.at[1], -1, 1)

    def step_near(self):
        self.wait(self.far.at[0], 0)
        self.add(self.piece(self.summed, 1, 0), self.far.at[0])
        self.send(self.piece(self.summed, 1), self.near.at[0], 1, 2)
        self.wait(self.far.at[1], 1)
        self.add(self.piece(self.summed, -1, 1), self.far.at[1])
        self.send(self.piece(self.summed, -1), self.near.at[1], -1, 3)

    def step_sum(self):
        self.wait(self.near.at[0], 2)
        self.wait(self.near.at[1], 3)
        own = self.piece(self.summed, 0)
        own[...] = (
            own[...].astype(F32) + self.near[0].astype(F32) + self.near[1].astype(F32)
        ).astype(BF)
        target = self.piece(self.total, 0)
        self.send(own, target, 1, 4)
        self.send(own, target, -1, 5)
        pltpu.make_async_copy(own, target, self.local_sem).start()

    def step_forward(self):
        self.wait(self.piece(self.total, -1), 4)
        half = self.piece(self.total, -1, 0)
        self.send(half, half, 1, 6)
        self.wait(self.piece(self.total, 1), 5)
        half = self.piece(self.total, 1, 1)
        self.send(half, half, -1, 7)

    def finish(self):
        self.wait(self.piece(self.total, 2, 0), 6)
        self.wait(self.piece(self.total, 2, 1), 7)
        pltpu.make_async_copy(
            self.piece(self.summed, 0), self.piece(self.total, 0), self.local_sem
        ).wait()
        for copy in self.started:
            copy.wait_send()


class CubeSum:
    def __init__(self, part, matrix, out, far, near, mid, low, send_sems, recv_sems):
        self.part, self.matrix, self.out = part, matrix, out
        self.far, self.near, self.mid, self.low = far, near, mid, low
        self.send_sems, self.recv_sems = send_sems, recv_sems
        line, plane = lax.axis_index("seq"), lax.axis_index("grp")
        coords = (line, plane // 4, lax.rem(plane, 4))
        self.coords = coords
        self.place = [coords[(part + level) % 3] for level in range(3)]
        self.started = []

    def device(self, level, step):
        axis = (self.part + level) % 3
        there = mod4(self.coords[axis] + step)
        if axis == 0:
            return {"seq": there}
        if axis == 1:
            return {"grp": there * 4 + self.coords[2]}
        return {"grp": self.coords[1] * 4 + there}

    def rows(self, level, shift):
        begin = 0
        for upper in range(level):
            begin = begin + self.place[upper] * (256 // 4**upper)
        return begin + mod4(self.place[level] + shift) * (256 // 4**level)

    def copy(self, source, target, level, step, slot):
        return pltpu.make_async_remote_copy(
            src_ref=source,
            dst_ref=target,
            send_sem=self.send_sems.at[self.part, slot],
            recv_sem=self.recv_sems.at[self.part, slot],
            device_id=self.device(level, step),
            device_id_type=MESH,
        )

    def send(self, source, target, level, step, slot):
        copy = self.copy(source, target, level, step, slot)
        copy.start()
        self.started.append(copy)

    def wait(self, target, slot):
        self.copy(target, target, 0, 0, slot).wait_recv()

    def add(self, target, *sources):
        value = target[...].astype(F32)
        for source in sources:
            value = value + source[...].astype(F32)
        target[...] = value.astype(BF)

    def step_far(self):
        begin = self.rows(0, 2)
        self.send(self.matrix.at[pl.ds(begin, 128)], self.far.at[0], 0, 1, 0)
        self.send(self.matrix.at[pl.ds(begin + 128, 128)], self.far.at[1], 0, -1, 1)

    def step_near(self):
        begin = self.rows(0, 1)
        self.wait(self.far.at[0], 0)
        self.add(self.matrix.at[pl.ds(begin, 128)], self.far.at[0])
        self.send(self.matrix.at[pl.ds(begin, 256)], self.near.at[0], 0, 1, 2)
        begin = self.rows(0, -1)
        self.wait(self.far.at[1], 1)
        self.add(self.matrix.at[pl.ds(begin + 128, 128)], self.far.at[1])
        self.send(self.matrix.at[pl.ds(begin, 256)], self.near.at[1], 0, -1, 3)

    def step_mid(self):
        self.wait(self.near.at[0], 2)
        self.wait(self.near.at[1], 3)
        self.add(self.matrix.at[pl.ds(self.rows(0, 0), 256)], self.near.at[0], self.near.at[1])
        for step in (1, 2, 3):
            self.send(
                self.matrix.at[pl.ds(self.rows(1, step), 64)], self.mid.at[step - 1], 1, step, 3 + step
            )

    def step_low(self):
        for step in (1, 2, 3):
            self.wait(self.mid.at[step - 1], 3 + step)
        self.add(
            self.matrix.at[pl.ds(self.rows(1, 0), 64)], self.mid.at[0], self.mid.at[1], self.mid.at[2]
        )
        for step in (1, 2, 3):
            self.send(
                self.matrix.at[pl.ds(self.rows(2, step), 16)], self.low.at[step - 1], 2, step, 6 + step
            )

    def step_done(self):
        for step in (1, 2, 3):
            self.wait(self.low.at[step - 1], 6 + step)
        own = self.rows(2, 0)
        value = self.matrix[pl.ds(own, 16), :].astype(F32)
        for step in (1, 2, 3):
            value = value + self.low[step - 1].astype(F32)
        self.out[pl.ds(own, 16), :] = value.astype(BF)
        ref = self.out.at[pl.ds(own, 16)]
        for step in (1, 2, 3):
            self.send(ref, ref, 2, step, 9 + step)

    def back_mid(self):
        for step in (1, 2, 3):
            self.wait(self.out.at[pl.ds(self.rows(2, -step), 16)], 9 + step)
        ref = self.out.at[pl.ds(self.rows(1, 0), 64)]
        for step in (1, 2, 3):
            self.send(ref, ref, 1, step, 12 + step)

    def back_near(self):
        for step in (1, 2, 3):
            self.wait(self.out.at[pl.ds(self.rows(1, -step), 64)], 12 + step)
        ref = self.out.at[pl.ds(self.rows(0, 0), 256)]
        self.send(ref, ref, 0, 1, 16)
        self.send(ref, ref, 0, -1, 17)
        self.share(0, 20)

    def back_far(self):
        begin = self.rows(0, -1)
        self.wait(self.out.at[pl.ds(begin, 256)], 16)
        ref = self.out.at[pl.ds(begin, 128)]
        self.send(ref, ref, 0, 1, 18)
        self.share(-1, 21)
        begin = self.rows(0, 1)
        self.wait(self.out.at[pl.ds(begin, 256)], 17)
        ref = self.out.at[pl.ds(begin + 128, 128)]
        self.send(ref, ref, 0, -1, 19)
        self.share(1, 22)

    def back_last(self):
        begin = self.rows(0, 2)
        self.wait(self.out.at[pl.ds(begin, 128)], 18)
        self.wait(self.out.at[pl.ds(begin + 128, 128)], 19)
        self.share(2, 23)

    def share_copy(self, shift, slot):
        ref = self.out.at[pl.ds(self.rows(0, shift), 256)]
        return pltpu.make_async_remote_copy(
            src_ref=ref,
            dst_ref=ref,
            send_sem=self.send_sems.at[self.part, slot],
            recv_sem=self.recv_sems.at[self.part, slot],
            device_id={"exp": 1 - lax.axis_index("exp")},
            device_id_type=MESH,
        )

    def share(self, shift, slot):
        copy = self.share_copy(shift, slot)
        copy.start()
        self.started.append(copy)

    def finish(self, other_out):
        for shift, slot in ((0, 20), (-1, 21), (1, 22), (2, 23)):
            ref = other_out.at[pl.ds(self.rows(0, shift), 256)]
            pltpu.make_async_remote_copy(
                src_ref=ref,
                dst_ref=ref,
                send_sem=self.send_sems.at[self.part, slot],
                recv_sem=self.recv_sems.at[self.part, slot],
                device_id={"exp": 1 - lax.axis_index("exp")},
                device_id_type=MESH,
            ).wait_recv()
        for copy in self.started:
            copy.wait_send()


SMALL_ROWS = 24


def total_kernel(
    mats_ref,
    small_ref,
    out_ref,
    small_out_ref,
    matrix,
    far,
    near,
    mid,
    low,
    arrived,
    small,
    small_first,
    send_sems,
    recv_sems,
    core_send,
    core_recv,
    small_send,
    small_recv,
):
    line, plane, core = lax.axis_index("seq"), lax.axis_index("grp"), lax.axis_index("exp")
    row, column = plane // 4, lax.rem(plane, 4)
    other = 1 - core
    places = (line, row, column)

    def neighbour(axis, step):
        if axis == 0:
            return {"seq": mod4(line + step)}
        if axis == 1:
            return {"grp": mod4(row + step) * 4 + column}
        return {"grp": row * 4 + mod4(column + step)}

    barrier = pltpu.get_barrier_semaphore()
    for axis in range(3):
        for step in (1, 2, 3):
            pl.semaphore_signal(
                barrier, inc=1, device_id=neighbour(axis, step), device_id_type=MESH
            )
    pl.semaphore_signal(barrier, inc=1, device_id={"exp": other}, device_id_type=MESH)
    pl.semaphore_wait(barrier, 10)

    def to_core(source, target, slot):
        return pltpu.make_async_remote_copy(
            src_ref=source,
            dst_ref=target,
            send_sem=core_send.at[slot],
            recv_sem=core_recv.at[slot],
            device_id={"exp": other},
            device_id_type=MESH,
        )

    own_small = pl.ds(core * SMALL_ROWS, SMALL_ROWS)
    core_copies = [to_core(mats_ref.at[other * 3 + part], arrived.at[part], part) for part in range(3)]
    core_copies.append(
        to_core(small_ref.at[pl.ds(other * SMALL_ROWS, SMALL_ROWS)], small_first, 3)
    )
    for copy in core_copies:
        copy.start()
    sums = [
        CubeSum(
            part,
            matrix.at[part],
            out_ref.at[core * 3 + part],
            far.at[part],
            near.at[part],
            mid.at[part],
            low.at[part],
            send_sems,
            recv_sems,
        )
        for part in range(3)
    ]
    for part in range(3):
        core_copies[part].wait()
        matrix[part] = (
            mats_ref[core * 3 + part].astype(F32) + arrived[part].astype(F32)
        ).astype(BF)
        sums[part].step_far()
    small_copies = []

    def small_step(axis):
        for step in (1, 2, 3):
            copy = pltpu.make_async_remote_copy(
                src_ref=small.at[axis, places[axis]],
                dst_ref=small.at[axis, places[axis]],
                send_sem=small_send.at[axis, step],
                recv_sem=small_recv.at[axis, step],
                device_id=neighbour(axis, step),
                device_id_type=MESH,
            )
            copy.start()
            small_copies.append(copy)

    def small_sum(axis):
        for step in (1, 2, 3):
            ref = small.at[axis, mod4(places[axis] - step)]
            pltpu.make_async_remote_copy(
                src_ref=ref,
                dst_ref=ref,
                send_sem=small_send.at[axis, step],
                recv_sem=small_recv.at[axis, step],
                device_id=neighbour(axis, step),
                device_id_type=MESH,
            ).wait_recv()
        return (small[axis, 0] + small[axis, 1]) + (small[axis, 2] + small[axis, 3])

    core_copies[3].wait()
    small[0, line] = small_ref[own_small, :] + small_first[...]
    small_step(0)
    for cube in sums:
        cube.step_near()
    small[1, row] = small_sum(0)
    small_step(1)
    for cube in sums:
        cube.step_mid()
    small[2, column] = small_sum(1)
    small_step(2)
    for cube in sums:
        cube.step_low()
    small_out_ref[own_small, :] = small_sum(2)
    small_last = to_core(small_out_ref.at[own_small], small_out_ref.at[own_small], 4)
    small_last.start()
    for cube in sums:
        cube.step_done()
    for cube in sums:
        cube.back_mid()
    for cube in sums:
        cube.back_near()
    for cube in sums:
        cube.back_far()
    for cube in sums:
        cube.back_last()
    for part in range(3):
        sums[part].finish(out_ref.at[other * 3 + part])
    small_last.wait_send()
    theirs = small_out_ref.at[pl.ds(other * SMALL_ROWS, SMALL_ROWS)]
    to_core(theirs, theirs, 4).wait_recv()
    for copy in small_copies:
        copy.wait_send()


def total_all(mats, small):
    dma = pltpu.SemaphoreType.DMA
    vmem = pl.BlockSpec(memory_space=pltpu.VMEM)
    return pl.pallas_call(
        total_kernel,
        out_shape=(
            jax.ShapeDtypeStruct((6, 1024, 512), BF),
            jax.ShapeDtypeStruct((2 * SMALL_ROWS, WIDTH), F32),
        ),
        in_specs=[vmem, vmem],
        out_specs=(vmem, vmem),
        scratch_shapes=[
            pltpu.VMEM((3, 1024, 512), BF),
            pltpu.VMEM((3, 2, 128, 512), BF),
            pltpu.VMEM((3, 2, 256, 512), BF),
            pltpu.VMEM((3, 3, 64, 512), BF),
            pltpu.VMEM((3, 3, 16, 512), BF),
            pltpu.VMEM((3, 1024, 512), BF),
            pltpu.VMEM((3, 4, SMALL_ROWS, WIDTH), F32),
            pltpu.VMEM((SMALL_ROWS, WIDTH), F32),
            dma((3, 24)),
            dma((3, 24)),
            dma((5,)),
            dma((5,)),
            dma((3, 4)),
            dma((3, 4)),
        ],
        compiler_params=pltpu.CompilerParams(
            collective_id=3, has_side_effects=True, vmem_limit_bytes=40 << 20
        ),
    )(mats, small)


def dot_tn(left, right):
    return lax.dot_general(left, right, (((0,), (0,)), ((), ())), preferred_element_type=F32)


def dot_nt(left, right):
    return lax.dot_general(left, right, (((1,), (1,)), ((), ())), preferred_element_type=F32)


def dot_nn(left, right):
    return lax.dot_general(left, right, (((1,), (0,)), ((), ())), preferred_element_type=F32)


def expert_kernel(
    rows_ref,
    meta_ref,
    cot_ref,
    w_in_ref,
    w_out_ref,
    sib_in_ref,
    sib_out_ref,
    row_total_ref,
    score_out_ref,
    moe_ref,
    grad_ref,
    blocks,
    meta_in,
    score_send,
    cots,
    w_in,
    w_out,
    d_in,
    d_out,
    row_partial,
    moe_stage,
    picks,
    slot_rows,
    slot_cots,
    slot_grads,
    slot_res,
    slot_back,
    far,
    near,
    summed,
    far_two,
    near_two,
    send_sems,
    recv_sems,
    rsend_sems,
    rrecv_sems,
    meta_send,
    meta_recv,
    score_ssem,
    score_rsem,
    local_sems,
    cot_sems,
    moe_sems,
    pair_send,
    pair_recv,
    pair_ready,
):
    me = lax.axis_index("grp")
    core = lax.axis_index("exp")
    row, column = me // 4, lax.rem(me, 4)
    barrier = pltpu.get_barrier_semaphore()
    for step in range(1, PLANE):
        pl.semaphore_signal(
            barrier, inc=1, device_id={"grp": lax.rem(me + step, PLANE)}, device_id_type=MESH
        )
    pl.semaphore_signal(barrier, inc=1, device_id={"exp": 1 - core}, device_id_type=MESH)

    loads = [
        pltpu.make_async_copy(source, target, local_sems.at[slot])
        for slot, (source, target) in enumerate(
            (
                (w_in_ref, w_in.at[core]),
                (w_out_ref, w_out.at[core]),
                (sib_in_ref, w_in.at[1 - core]),
                (sib_out_ref, w_out.at[1 - core]),
            )
        )
    ]
    for load in loads:
        load.start()
    blocks[me] = rows_ref[...]
    meta_in[me] = meta_ref[me]
    d_in[...] = jnp.zeros_like(d_in)
    d_out[...] = jnp.zeros_like(d_out)

    def cot_copy(group, j):
        shift = group + group // 2 - 2 * (group // 3)
        index = mod4(row + j) * 4 + mod4(column + shift)
        return pltpu.make_async_copy(
            cot_ref.at[index], cots.at[lax.rem(group, 2), j], cot_sems.at[lax.rem(group, 2), j]
        )

    for j in range(GROUP):
        cot_copy(0, j).start()
    pl.semaphore_wait(barrier, PLANE)

    gathers = [PlaneGather(part, blocks, send_sems, recv_sems) for part in (0, 1)]
    for gather in gathers:
        gather.begin()
    for gather in gathers:
        gather.spread(0)
    meta_copies = []
    for step in range(1, PLANE):
        to = lax.rem(me + step, PLANE)
        copy = plane_copy(
            meta_ref.at[to], meta_in.at[me], meta_send.at[step], meta_recv.at[step], to
        )
        copy.start()
        meta_copies.append(copy)
    for load in loads:
        load.wait()
    for copy in meta_copies:
        copy.wait()
    for gather in gathers:
        gather.forward_first()
        gather.spread(-1)
        gather.spread(1)
    gathers[1].forward_second(0)
    for gather in gathers:
        gather.wait_far_first()
        gather.spread(2)
    gathers[1].wait_far_second(0)

    def moe_copy(j, index):
        return pltpu.make_async_copy(moe_stage.at[j], moe_ref.at[index], moe_sems.at[j])

    @pl.loop(0, 4)
    def _(group):
        shift = group + group // 2 - 2 * (group // 3)
        place = mod4(column + shift)
        parity = lax.rem(group, 2)

        @pl.when(group == 0)
        def _():
            gathers[0].forward_second(0)
            gathers[0].forward_second(-1)
            gathers[0].forward_second(1)
            gathers[0].forward_second(2)
            gathers[1].forward_second(-1)
            gathers[1].forward_second(1)

        @pl.when(group == 1)
        def _():
            gathers[1].wait_far_second(1)
            gathers[1].wait_far_second(-1)
            gathers[1].forward_second(2)

        @pl.when(group == 2)
        def _():
            for da in (0, -1, 1, 2):
                gathers[0].wait_far_second(da)
            gathers[1].wait_far_second(2)

        @pl.when(group < 3)
        def _():
            for j in range(GROUP):
                cot_copy(group + 1, j).start()

        for j in range(GROUP):
            cot_copy(group, j).wait()

        for expert in range(2):
            gates = []
            for j in range(GROUP):
                index = mod4(row + j) * 4 + place
                slots = meta_in[index, pl.ds(expert, 1), :]
                gate_row = meta_in[index, pl.ds(2 + expert, 1), :]
                slot_id = lax.broadcasted_iota(jnp.int32, (CAPACITY, BLOCK), 0).astype(F32)
                hit = slot_id == slots
                pick = jnp.where(hit, 1.0, 0.0).astype(BF)
                gate = jnp.sum(jnp.where(hit, gate_row, 0.0), axis=1, keepdims=True)
                gates.append(gate)
                here = pl.ds(j * CAPACITY, CAPACITY)
                picks[j, pl.ds(expert * CAPACITY, CAPACITY), :] = pick
                slot_rows[here, :] = dot_nn(pick, blocks[index]).astype(BF)
                cot_rows = dot_nn(pick, cots[parity, j])
                slot_cots[here, :] = cot_rows.astype(BF)
                slot_grads[here, :] = (gate * (RESIDUAL_MULT * cot_rows)).astype(BF)
            gate = jnp.concatenate(gates, axis=0)
            gate_up = dot_nn(slot_rows[...], w_in[expert])
            gate_half, up_half = gate_up[:, :INNER], gate_up[:, INNER:]
            sigmoid = jax.nn.sigmoid(gate_half)
            activated = gate_half * sigmoid
            hidden = (activated * up_half).astype(BF)
            result = dot_nn(hidden, w_out[expert]).astype(BF).astype(F32)
            scored = RESIDUAL_MULT * jnp.sum(
                slot_cots[...].astype(F32) * result, axis=1, keepdims=True
            )
            slot_res[expert] = (gate * result).astype(BF)
            hidden_grad = dot_nt(slot_grads[...], w_out[expert])
            gate_part = hidden_grad * up_half * sigmoid * (1.0 + gate_half * (1.0 - sigmoid))
            up_part = hidden_grad * activated
            pair_grad = jnp.concatenate([gate_part.astype(BF), up_part.astype(BF)], axis=1)
            slot_back[expert] = dot_nt(pair_grad, w_in[expert]).astype(BF)
            d_out[expert] += dot_tn(hidden, slot_grads[...])
            d_in[expert] += dot_tn(slot_rows[...], pair_grad)
            for j in range(GROUP):
                index = mod4(row + j) * 4 + place
                pick = picks[j, pl.ds(expert * CAPACITY, CAPACITY), :].astype(F32)
                spread = jnp.sum(
                    pick * scored[j * CAPACITY : (j + 1) * CAPACITY], axis=0, keepdims=True
                )
                score_send[index, pl.ds(expert, 1), :] = spread

        for j in range(GROUP):
            index = mod4(row + j) * 4 + place
            here = pl.ds(j * CAPACITY, CAPACITY)
            pick = picks[j]

            @pl.when(group > 0)
            def _():
                moe_copy(j, index).wait()

            values = jnp.concatenate([slot_res[0, here, :], slot_res[1, here, :]], axis=0)
            moe_stage[j] = dot_tn(pick, values).astype(BF)
            moe_copy(j, index).start()
            values = jnp.concatenate([slot_back[0, here, :], slot_back[1, here, :]], axis=0)
            row_partial[index] = dot_tn(pick, values).astype(BF)

    for gather in gathers:
        gather.finish()
    reducers = [
        PlaneReduce(
            part, row_partial, (far, near, summed, far_two, near_two), rsend_sems, rrecv_sems, row_total_ref
        )
        for part in (0, 1)
    ]
    for da in (2, 1, -1, 0):
        for reducer in reducers:
            reducer.step_far(da)
    score_out_ref[me] = score_send[me]
    score_copies = []
    for step in range(1, PLANE):
        to = lax.rem(me + step, PLANE)
        copy = plane_copy(
            score_send.at[to], score_out_ref.at[me], score_ssem.at[step], score_rsem.at[step], to
        )
        copy.start()
        score_copies.append(copy)
    other = 1 - core
    for j in range(4):
        cots[0, j] = d_in[other, pl.ds(j * BLOCK, BLOCK), :].astype(BF)
    for j in range(2):
        cots[1, j] = d_out[other, pl.ds(j * BLOCK, BLOCK), :].astype(BF)
    pl.semaphore_signal(pair_ready, inc=1, device_id={"exp": other}, device_id_type=MESH)
    pl.semaphore_wait(pair_ready, 1)
    pair_copies = []
    for j in range(6):
        copy = pltpu.make_async_remote_copy(
            src_ref=cots.at[j // 4, j % 4],
            dst_ref=blocks.at[j],
            send_sem=pair_send.at[j],
            recv_sem=pair_recv.at[j],
            device_id={"exp": other},
            device_id_type=MESH,
        )
        copy.start()
        pair_copies.append(copy)
    for da in (2, 1, -1, 0):
        for reducer in reducers:
            reducer.step_near(da)
    for j in range(6):
        pair_copies[j].wait()
        here = pl.ds((j % 4) * BLOCK, BLOCK)
        if j < 4:
            w_in[0, here, :] = (d_in[core, here, :] + blocks[j].astype(F32)).astype(BF)
        else:
            w_out[0, here, :] = (d_out[core, here, :] + blocks[j].astype(F32)).astype(BF)
    store_in = pltpu.make_async_copy(w_in.at[0], grad_ref.at[pl.ds(0, WIDTH)], local_sems.at[0])
    store_out = pltpu.make_async_copy(
        w_out.at[0], grad_ref.at[pl.ds(WIDTH, INNER)], local_sems.at[1]
    )
    store_in.start()
    store_out.start()
    for da in (2, 1, -1, 0):
        for reducer in reducers:
            reducer.step_sum(da)
    for reducer in reducers:
        reducer.finish()
    for copy in score_copies:
        copy.wait()
    for j in range(GROUP):
        moe_copy(j, j).wait()
    store_in.wait()
    store_out.wait()


def run_experts(rows, meta, cots, expert_in, expert_out, sib_in, sib_out):
    vmem = pl.BlockSpec(memory_space=pltpu.VMEM)
    hbm = pl.BlockSpec(memory_space=pl.ANY)
    dma = pltpu.SemaphoreType.DMA
    slots = GROUP * CAPACITY
    return pl.pallas_call(
        expert_kernel,
        out_shape=(
            jax.ShapeDtypeStruct((BLOCK, WIDTH), F32),
            jax.ShapeDtypeStruct((PLANE, 8, BLOCK), F32),
            jax.ShapeDtypeStruct((PLANE, BLOCK, WIDTH), BF),
            jax.ShapeDtypeStruct((WIDTH + INNER, WIDTH), BF),
        ),
        in_specs=[vmem, vmem, hbm, hbm, hbm, hbm, hbm],
        out_specs=(vmem, vmem, hbm, hbm),
        scratch_shapes=[
            pltpu.VMEM((PLANE, BLOCK, WIDTH), BF),
            pltpu.VMEM((PLANE, 8, BLOCK), F32),
            pltpu.VMEM((PLANE, 8, BLOCK), F32),
            pltpu.VMEM((2, GROUP, BLOCK, WIDTH), BF),
            pltpu.VMEM((2, WIDTH, 2 * INNER), BF),
            pltpu.VMEM((2, INNER, WIDTH), BF),
            pltpu.VMEM((2, WIDTH, 2 * INNER), F32),
            pltpu.VMEM((2, INNER, WIDTH), F32),
            pltpu.VMEM((PLANE, BLOCK, WIDTH), BF),
            pltpu.VMEM((GROUP, BLOCK, WIDTH), BF),
            pltpu.VMEM((GROUP, 2 * CAPACITY, BLOCK), BF),
            pltpu.VMEM((slots, WIDTH), BF),
            pltpu.VMEM((slots, WIDTH), BF),
            pltpu.VMEM((slots, WIDTH), BF),
            pltpu.VMEM((2, slots, WIDTH), BF),
            pltpu.VMEM((2, slots, WIDTH), BF),
        ]
        + reduce_buffers()
        + [dma((40,))] * 4
        + [dma((PLANE,))] * 4
        + [dma((4,))]
        + [dma((2, GROUP)), dma((GROUP,))]
        + [dma((6,))] * 2
        + [pltpu.SemaphoreType.REGULAR],
        compiler_params=pltpu.CompilerParams(
            collective_id=2, has_side_effects=True, vmem_limit_bytes=VMEM_LIMIT
        ),
    )(rows, meta, cots, expert_in, expert_out, sib_in, sib_out)


VMEM_LIMIT = 63 << 20


def rope_lanes(values, cosine, sine):
    lane = lax.broadcasted_iota(jnp.int32, (1, 128), 1)
    lower = lax.rem(lane, 64) < 32
    chunks = []
    for begin in range(0, values.shape[1], 128):
        chunk = values[:, begin : begin + 128]
        partner = jnp.where(lower, pltpu.roll(chunk, 96, 1), pltpu.roll(chunk, 32, 1))
        chunks.append(chunk * cosine + partner * sine)
    return chunks


def norm_scale(values):
    return lax.rsqrt(jnp.mean(values * values, axis=1, keepdims=True) + EPSILON)


def slot_table(routes, ranks):
    expert = lax.broadcasted_iota(jnp.int32, (BLOCK, 32), 1)
    rank_of = jnp.zeros((BLOCK, 32), jnp.int32)
    for k in range(8):
        rank_of = rank_of + jnp.where(routes[:, k : k + 1] == expert, ranks[:, k : k + 1] + 1, 0)
    chosen = rank_of > 0
    row = lax.broadcasted_iota(jnp.int32, (BLOCK, BLOCK), 0)
    lane = lax.broadcasted_iota(jnp.int32, (BLOCK, BLOCK), 1)
    source = lax.broadcasted_iota(jnp.int32, (32, BLOCK), 0)
    target = lax.broadcasted_iota(jnp.int32, (32, BLOCK), 1)
    repeat = jnp.where(lax.rem(target, 32) == source, 1.0, 0.0).astype(BF)
    rank_wide = dot_nn(rank_of.astype(F32).astype(BF), repeat)
    hit = rank_wide == (lane // 32 + 1).astype(F32)
    counts = jnp.where(hit, 1.0, 0.0)
    earlier = jnp.where(row > lane, 1.0, 0.0).astype(BF)
    before = dot_nn(earlier, counts.astype(BF))
    totals = jnp.sum(counts, axis=0, keepdims=True)
    lower = (lax.rem(row, 32) == lax.rem(lane, 32)) & (row // 32 < lane // 32)
    offsets = dot_nn(totals.astype(BF), jnp.where(lower, 1.0, 0.0).astype(BF))
    place = jnp.where(hit, before + offsets, 0.0)
    place = place[:, :128] + place[:, 128:]
    place = place + pltpu.roll(place, 64, 1)
    place = place + pltpu.roll(place, 32, 1)
    place = place[:, :32]
    return chosen, jnp.where(chosen & (place < CAPACITY), place, -1.0)


def attend_kernel(
    tokens_ref,
    seg_ref,
    routes_ref,
    ranks_ref,
    gain_one_ref,
    w_query_ref,
    w_key_ref,
    w_value_ref,
    w_output_ref,
    gain_two_ref,
    w_router_ref,
    cosine_ref,
    sine_ref,
    cot_ref,
    w_in_ref,
    w_out_ref,
    routed_ref,
    residual_ref,
    heads_ref,
    normed_ref,
    query_ref,
    kv_ref,
    lse_ref,
    bias_ref,
    gates_ref,
    meta_ref,
    cots_ref,
    sib_in_ref,
    sib_out_ref,
    segs,
    top,
    expsum,
    acc,
    send_sems,
    recv_sems,
    kv_send,
    kv_recv,
    seg_send,
    seg_recv,
    weight_send,
    weight_recv,
    local_sem,
):
    line, plane, core = lax.axis_index("seq"), lax.axis_index("grp"), lax.axis_index("exp")
    block = 2 * line + core
    row, column = plane // 4, lax.rem(plane, 4)
    barrier = pltpu.get_barrier_semaphore()
    for index in (
        mod4(row + 1) * 4 + column,
        mod4(row - 1) * 4 + column,
        row * 4 + mod4(column + 1),
        row * 4 + mod4(column - 1),
    ):
        pl.semaphore_signal(barrier, inc=1, device_id={"grp": index}, device_id_type=MESH)
    for step in (1, 2, 3):
        pl.semaphore_signal(
            barrier, inc=1, device_id={"seq": mod4(line + step)}, device_id_type=MESH
        )
    pl.semaphore_signal(barrier, inc=1, device_id={"exp": 1 - core}, device_id_type=MESH)
    own_cot = pltpu.make_async_copy(cot_ref, cots_ref.at[plane], local_sem)
    own_cot.start()

    tokens = tokens_ref[...].astype(F32)
    normed = (tokens * norm_scale(tokens) * gain_one_ref[...]).astype(BF)
    normed_ref[...] = normed
    cosine, sine = cosine_ref[...], sine_ref[...]
    keys = dot_nn(normed, w_key_ref[...])
    values = dot_nn(normed, w_value_ref[...]).astype(BF)
    key_chunks = rope_lanes(keys, cosine, sine)
    for head in range(KV_HEADS):
        chunk = key_chunks[head // 2].astype(BF)
        key = chunk[:, (head % 2) * 64 : (head % 2) * 64 + 64]
        kv_ref[0, head] = jnp.concatenate([key, values[:, head * 64 : head * 64 + 64]], axis=1)
    segs[0] = seg_ref[...]
    own_cot.wait()
    pl.semaphore_wait(barrier, 8)

    def kv_copies(source, target, device, slot):
        return [
            pltpu.make_async_remote_copy(
                src_ref=ref.at[source],
                dst_ref=ref.at[target],
                send_sem=sends.at[slot],
                recv_sem=recvs.at[target],
                device_id=device,
                device_id_type=MESH,
            )
            for ref, sends, recvs in ((kv_ref, kv_send, kv_recv), (segs, seg_send, seg_recv))
        ]

    sibling = {"exp": 1 - core}
    to_near = kv_copies(0, 2, {"seq": mod4(line + 1)}, 1)
    to_far = kv_copies(0, 4, {"seq": mod4(line + 2)}, 2)
    to_sibling = kv_copies(0, 1, sibling, 0)
    forward_near = kv_copies(2, 3 - 2 * core, sibling, 3)
    forward_far = kv_copies(4, 3, sibling, 4)

    def begin(copies):
        for copy in copies:
            copy.start()

    def sent(copies):
        for copy in copies:
            copy.wait_send()

    @pl.when(line < 3)
    def _():
        begin(to_near)

    @pl.when(core == 0)
    def _():
        begin(to_sibling)

    @pl.when(line < 2)
    def _():
        begin(to_far)

    gathers = [PlaneGather(part, cots_ref, send_sems, recv_sems) for part in (0, 1)]
    for gather in gathers:
        gather.begin()
    for gather in gathers:
        gather.spread(0)
    weight_copies = [
        pltpu.make_async_remote_copy(
            src_ref=source,
            dst_ref=target,
            send_sem=weight_send.at[slot],
            recv_sem=weight_recv.at[slot],
            device_id=sibling,
            device_id_type=MESH,
        )
        for slot, (source, target) in enumerate(((w_in_ref, sib_in_ref), (w_out_ref, sib_out_ref)))
    ]
    begin(weight_copies)

    lane = lax.broadcasted_iota(jnp.int32, (1, 128), 1)
    queries = dot_nn(normed, w_query_ref[...])
    for head, chunk in enumerate(rope_lanes(queries, cosine, sine)):
        chunk = (chunk.astype(BF).astype(F32) * ATTENTION_FACTOR)
        query_ref[head, :BLOCK, :] = jnp.where(lane < 64, chunk, 0.0).astype(BF)
        query_ref[head, BLOCK:, :] = jnp.where(lane < 64, pltpu.roll(chunk, 64, 1), 0.0).astype(BF)
    top[...] = jnp.full(top.shape, MASKED, F32)
    expsum[...] = jnp.zeros(expsum.shape, F32)
    acc[...] = jnp.zeros(acc.shape, F32)
    seg_column = seg_ref[...].T[:, :1]

    def attend(slot):
        i = lax.broadcasted_iota(jnp.int32, (BLOCK, BLOCK), 0)
        j = lax.broadcasted_iota(jnp.int32, (BLOCK, BLOCK), 1)
        distance = slot * BLOCK + i - j
        allowed = (seg_column == segs[slot, 0:1, :]) & (distance >= 0) & (distance < WINDOW)
        bias = jnp.where(allowed, 0.0, MASKED)
        bias_ref[slot] = bias

        @pl.loop(0, KV_HEADS)
        def _(head):
            pair = kv_ref[slot, head]
            one = bias_ref[slot]
            score = dot_nt(query_ref[head], pair)
            score = score + jnp.concatenate([one, one], axis=0)
            old = top[head][:, :1]
            new = jnp.maximum(old, jnp.max(score, axis=1, keepdims=True))
            weight = jnp.exp(score - new)
            fade = jnp.exp(old - new)
            expsum[head] = expsum[head] * fade + jnp.sum(weight, axis=1, keepdims=True)
            acc[head] = acc[head] * fade + dot_nn(weight.astype(BF), pair)
            top[head] = jnp.broadcast_to(new, (2 * BLOCK, 128))

    def wait_block(slot):
        for ref, sends, recvs in ((kv_ref, kv_send, kv_recv), (segs, seg_send, seg_recv)):
            pltpu.make_async_remote_copy(
                src_ref=ref.at[slot],
                dst_ref=ref.at[slot],
                send_sem=sends.at[0],
                recv_sem=recvs.at[slot],
                device_id=sibling,
                device_id_type=MESH,
            ).wait_recv()

    attend(0)
    for gather in gathers:
        gather.forward_first()
        gather.spread(-1)
        gather.spread(1)

    chosen, kept = slot_table(routes_ref[...], ranks_ref[...])
    kept_rows = jnp.concatenate([kept, jnp.zeros((BLOCK, 96), F32)], axis=1).T
    for index in range(PLANE):
        meta_ref[index, 0:2, :] = kept_rows[2 * index : 2 * index + 2]
        meta_ref[index, 4:8, :] = jnp.zeros((4, BLOCK), F32)

    first = 2 - core

    @pl.when(block >= first)
    def _():
        wait_block(first)

        @pl.when(core == 0)
        def _():
            begin(forward_near)

        attend(first)

    for gather in gathers:
        gather.forward_second(0)
    for gather in gathers:
        gather.wait_far_first()
        gather.spread(2)
    second = 1 + core

    @pl.when(block >= second)
    def _():
        wait_block(second)

        @pl.when(core == 1)
        def _():
            begin(forward_near)

        attend(second)

    for da in (-1, 1):
        for gather in gathers:
            gather.forward_second(da)
    third = 4 - core

    @pl.when(block >= third)
    def _():
        wait_block(third)
        attend(third)

    for gather in gathers:
        gather.forward_second(2)
    fourth = 3 + core

    @pl.when(block >= fourth)
    def _():
        wait_block(fourth)

        @pl.when(core == 1)
        def _():
            begin(forward_far)

        attend(fourth)

    for head in range(KV_HEADS):
        inverse = 1.0 / expsum[head][:, :1]
        pair = acc[head] * inverse
        heads_ref[:, head * 128 : head * 128 + 128] = jnp.where(
            lane < 64, pltpu.roll(pair[:BLOCK], 64, 1), pair[BLOCK:]
        ).astype(BF)
        lse_ref[head] = top[head] + jnp.log(expsum[head])
    branch = dot_nn(heads_ref[...], w_output_ref[...])
    residual = tokens_ref[...].astype(F32) + RESIDUAL_MULT * branch
    residual_ref[...] = residual
    routed = (residual * norm_scale(residual) * gain_two_ref[...]).astype(BF)
    routed_ref[...] = routed
    logits = dot_nn(routed, w_router_ref[...])
    logits = jnp.where(chosen, logits, MASKED)
    powers = jnp.exp(logits - jnp.max(logits, axis=1, keepdims=True))
    gates = jnp.where(chosen, powers / jnp.sum(powers, axis=1, keepdims=True), 0.0)
    gates_ref[...] = gates
    gate_rows = jnp.concatenate([gates, jnp.zeros((BLOCK, 96), F32)], axis=1).T
    for index in range(PLANE):
        meta_ref[index, 2:4, :] = gate_rows[2 * index : 2 * index + 2]

    for da in (0, -1, 1, 2):
        for gather in gathers:
            gather.wait_far_second(da)
    for gather in gathers:
        gather.finish()
    for copy in weight_copies:
        copy.wait()

    @pl.when(line < 3)
    def _():
        sent(to_near)

    @pl.when(core == 0)
    def _():
        sent(to_sibling)

    @pl.when(line < 2)
    def _():
        sent(to_far)

    @pl.when(line >= 1)
    def _():
        sent(forward_near)

    @pl.when((line >= 2) & (core == 1))
    def _():
        sent(forward_far)


def run_attention(
    tokens, seg_tile, routes, ranks, gain_one, w_query, w_key, w_value, w_output, gain_two,
    w_router, cosine, sine, cot, expert_in, expert_out,
):
    vmem = pl.BlockSpec(memory_space=pltpu.VMEM)
    hbm = pl.BlockSpec(memory_space=pl.ANY)
    dma = pltpu.SemaphoreType.DMA
    shape = jax.ShapeDtypeStruct
    return pl.pallas_call(
        attend_kernel,
        out_shape=(
            shape((BLOCK, WIDTH), BF),
            shape((BLOCK, WIDTH), F32),
            shape((BLOCK, WIDTH), BF),
            shape((BLOCK, WIDTH), BF),
            shape((KV_HEADS, 2 * BLOCK, 128), BF),
            shape((5, KV_HEADS, BLOCK, 128), BF),
            shape((KV_HEADS, 2 * BLOCK, 128), F32),
            shape((5, BLOCK, BLOCK), F32),
            shape((BLOCK, 32), F32),
            shape((PLANE, 8, BLOCK), F32),
            shape((PLANE, BLOCK, WIDTH), BF),
            shape((WIDTH, 2 * INNER), BF),
            shape((INNER, WIDTH), BF),
        ),
        in_specs=[vmem] * 13 + [hbm] * 3,
        out_specs=(vmem,) * 10 + (hbm,) * 3,
        scratch_shapes=[
            pltpu.VMEM((5, 8, BLOCK), F32),
            pltpu.VMEM((KV_HEADS, 2 * BLOCK, 128), F32),
            pltpu.VMEM((KV_HEADS, 2 * BLOCK, 128), F32),
            pltpu.VMEM((KV_HEADS, 2 * BLOCK, 128), F32),
            dma((40,)),
            dma((40,)),
            dma((5,)),
            dma((5,)),
            dma((5,)),
            dma((5,)),
            dma((2,)),
            dma((2,)),
            dma,
        ],
        compiler_params=pltpu.CompilerParams(
            collective_id=0, has_side_effects=True, vmem_limit_bytes=58 << 20
        ),
    )(
        tokens, seg_tile, routes, ranks, gain_one, w_query, w_key, w_value, w_output, gain_two,
        w_router, cosine, sine, cot, expert_in, expert_out,
    )


def backward_kernel(
    tokens_ref,
    cot_ref,
    residual_ref,
    row_total_ref,
    scores_ref,
    gates_ref,
    routed_ref,
    heads_ref,
    normed_ref,
    query_ref,
    kv_ref,
    bias_ref,
    w_query_ref,
    w_key_ref,
    w_value_ref,
    w_output_ref,
    w_router_ref,
    gain_one_ref,
    gain_two_ref,
    cosine_ref,
    sine_ref,
    lse_ref,
    partial_ref,
    grad_ref,
    output_ref,
    input_grad_ref,
    small_ref,
    mats_ref,
    grad_total_ref,
    partial,
    far,
    near,
    summed,
    far_two,
    near_two,
    grads,
    grad_far,
    grad_near,
    moe_total,
    stats,
    head_grads,
    query_grads,
    own_grads,
    stage,
    from_pair,
    from_near,
    from_far,
    residual_grad,
    mats,
    send_sems,
    recv_sems,
    ring_send,
    ring_recv,
    kv_send,
    kv_recv,
    local_sems,
    mats_sems,
):
    line, plane, core = lax.axis_index("seq"), lax.axis_index("grp"), lax.axis_index("exp")
    block = 2 * line + core
    row, column = plane // 4, lax.rem(plane, 4)
    load_grads = pltpu.make_async_copy(grad_ref, grads, local_sems.at[0])
    load = pltpu.make_async_copy(partial_ref, partial, local_sems.at[1])
    load_lse = pltpu.make_async_copy(lse_ref, stats, local_sems.at[2])
    load_grads.start()
    load.start()
    load_lse.start()
    barrier = pltpu.get_barrier_semaphore()
    for index in (
        mod4(row + 1) * 4 + column,
        mod4(row - 1) * 4 + column,
        row * 4 + mod4(column + 1),
        row * 4 + mod4(column - 1),
    ):
        pl.semaphore_signal(barrier, inc=1, device_id={"grp": index}, device_id_type=MESH)
    for step in (1, 2, 3):
        pl.semaphore_signal(
            barrier, inc=1, device_id={"seq": mod4(line + step)}, device_id_type=MESH
        )
    pl.semaphore_signal(barrier, inc=1, device_id={"exp": 1 - core}, device_id_type=MESH)
    pl.semaphore_wait(barrier, 8)
    buffers = (far, near, summed, far_two, near_two)
    reducers = [
        PlaneReduce(part, partial, buffers, send_sems, recv_sems, moe_total) for part in (0, 1)
    ]
    ring = RowRing(grads, grad_total_ref, grad_far, grad_near, ring_send, ring_recv, local_sems)
    load_grads.wait()
    ring.step_far()
    load.wait()
    for da in (2, 1, -1, 0):
        for reducer in reducers:
            reducer.step_far(da)

    lane = lax.broadcasted_iota(jnp.int32, (1, 128), 1)
    lower = lane < 64
    gate_grad = jnp.concatenate(
        [scores_ref[index, 0:2, :] for index in range(PLANE)] + [jnp.zeros((96, BLOCK), F32)], axis=0
    ).T[:, :32]
    gates = gates_ref[...]
    choice_grad = gates * (gate_grad - jnp.sum(gates * gate_grad, axis=1, keepdims=True))
    logit_grad = choice_grad.astype(BF)
    small_ref[0:32, :] = dot_tn(logit_grad, routed_ref[...])
    routed_grad = dot_nt(logit_grad, w_router_ref[...]) + row_total_ref[...]
    residual = residual_ref[...]
    scale_two = norm_scale(residual)
    small_ref[33:34, :] = jnp.sum(routed_grad * residual * scale_two, axis=0, keepdims=True)
    small_ref[34:48, :] = jnp.zeros((14, WIDTH), F32)
    weighted = routed_grad * gain_two_ref[...]
    shared = scale_two * scale_two * scale_two * jnp.mean(weighted * residual, axis=1, keepdims=True)
    grown = cot_ref[...].astype(F32) + scale_two * weighted - residual * shared
    residual_grad[...] = grown
    branch_grad = (RESIDUAL_MULT * grown).astype(BF)
    head_grad = dot_nt(branch_grad, w_output_ref[...]).astype(BF)
    load_lse.wait()
    for head in range(KV_HEADS):
        chunk = head_grad[:, head * 128 : head * 128 + 128].astype(F32)
        other = heads_ref[:, head * 128 : head * 128 + 128].astype(F32)
        head_grads[head, :BLOCK, :] = jnp.where(lower, 0.0, pltpu.roll(chunk, 64, 1)).astype(BF)
        head_grads[head, BLOCK:, :] = jnp.where(lower, 0.0, chunk).astype(BF)
        both = chunk * other
        one = jnp.sum(jnp.where(lower, both, 0.0), axis=1, keepdims=True)
        two = jnp.sum(jnp.where(lower, 0.0, both), axis=1, keepdims=True)
        stats[head, :BLOCK, :] = jnp.where(lower, stats[head, :BLOCK, :], one)
        stats[head, BLOCK:, :] = jnp.where(lower, stats[head, BLOCK:, :], two)
    query_grads[...] = jnp.zeros(query_grads.shape, F32)

    def store_mats(slot, index):
        return pltpu.make_async_copy(mats.at[slot], mats_ref.at[index], mats_sems.at[slot])

    for slot in range(2):
        mats[slot] = dot_tn(heads_ref[...], branch_grad[:, slot * 512 : slot * 512 + 512]).astype(BF)
        store_mats(slot, 4 + slot).start()

    def attend_back(slot):
        @pl.loop(0, KV_HEADS)
        def _(head):
            pair, query, out_grad = kv_ref[slot, head], query_ref[head], head_grads[head]
            one = bias_ref[slot]
            score = dot_nt(query, pair) + jnp.concatenate([one, one], axis=0)
            prob = jnp.exp(score - stats[head][:, :1])
            prob_grad = dot_nt(out_grad, pair)
            score_grad = (prob * (prob_grad - stats[head][:, 64:65])).astype(BF)
            query_grads[head] += dot_nn(score_grad, pair)
            own_grads[head] = dot_tn(score_grad, query) + dot_tn(prob.astype(BF), out_grad)
            stage[slot, head] = own_grads[head].astype(BF)

    sibling = {"exp": 1 - core}

    def kv_copy(source, target, device, slot):
        return pltpu.make_async_remote_copy(
            src_ref=source,
            dst_ref=target,
            send_sem=kv_send.at[slot],
            recv_sem=kv_recv.at[slot],
            device_id=device,
            device_id_type=MESH,
        )

    pair_three = kv_copy(stage.at[3], from_pair.at[core], sibling, 0)
    pair_one = kv_copy(stage.at[1], from_pair.at[2 + core], sibling, 1)
    to_near = kv_copy(stage.at[2], from_near, {"seq": mod4(line - 1)}, 2)
    to_far = kv_copy(stage.at[4], from_far, {"seq": mod4(line - 2)}, 3)

    def take_pair(three, slot):
        source = from_pair.at[(0 if three else 2) + 1 - core]
        kv_copy(source, source, sibling, 0 if three else 1).wait_recv()
        for head in range(KV_HEADS):
            stage[slot, head] = (
                stage[slot, head].astype(F32) + source[head].astype(F32)
            ).astype(BF)

    first, second, third, fourth = 3 + core, 4 - core, 1 + core, 2 - core

    @pl.when(block >= first)
    def _():
        attend_back(first)

    @pl.when((core == 0) & (line >= 2))
    def _():
        pair_three.start()

    ring.step_near()
    for reducer in reducers:
        reducer.step_near(2)
        reducer.step_near(1)

    @pl.when((core == 1) & (line >= 2))
    def _():
        take_pair(True, 4)
        to_far.start()

    @pl.when(block >= second)
    def _():
        attend_back(second)

    @pl.when((core == 1) & (line >= 1))
    def _():
        pair_three.start()

    @pl.when((core == 0) & (line >= 2))
    def _():
        to_far.start()

    for reducer in reducers:
        reducer.step_near(-1)
        reducer.step_near(0)

    @pl.when(block >= third)
    def _():
        attend_back(third)

    @pl.when((core == 0) & (line >= 1))
    def _():
        pair_one.start()

    ring.step_sum()
    for reducer in reducers:
        reducer.step_sum(2)

    @pl.when((core == 1) & (line >= 1))
    def _():
        take_pair(False, 2)
        to_near.start()

    @pl.when(block >= fourth)
    def _():
        attend_back(fourth)

    @pl.when(core == 1)
    def _():
        pair_one.start()

    @pl.when((core == 0) & (line >= 1))
    def _():
        take_pair(True, 2)
        to_near.start()

    for reducer in reducers:
        reducer.step_sum(1)
        reducer.step_sum(-1)
    attend_back(0)

    cosine, sine = cosine_ref[...], sine_ref[...]
    normed = normed_ref[...]
    query_chunks = []
    for head in range(KV_HEADS):
        chunk = jnp.where(
            lower, query_grads[head, :BLOCK, :], pltpu.roll(query_grads[head, BLOCK:, :], 64, 1)
        )
        query_chunks.append(chunk * ATTENTION_FACTOR)
    query_pre_grad = jnp.concatenate(
        rope_lanes(jnp.concatenate(query_chunks, axis=1), cosine, -sine), axis=1
    ).astype(BF)
    normed_grad = dot_nt(query_pre_grad, w_query_ref[...])
    for slot in range(2):
        store_mats(slot, 4 + slot).wait()
        mats[slot] = dot_tn(normed, query_pre_grad[:, slot * 512 : slot * 512 + 512]).astype(BF)
        store_mats(slot, slot).start()
    ring.step_forward()

    @pl.when(core == 0)
    def _():
        source = from_pair.at[3]
        kv_copy(source, source, sibling, 1).wait_recv()
        for head in range(KV_HEADS):
            own_grads[head] += source[head].astype(F32)

    @pl.when(line < 3)
    def _():
        kv_copy(from_near, from_near, sibling, 2).wait_recv()
        for head in range(KV_HEADS):
            own_grads[head] += from_near[head].astype(F32)

    @pl.when(line < 2)
    def _():
        kv_copy(from_far, from_far, sibling, 3).wait_recv()
        for head in range(KV_HEADS):
            own_grads[head] += from_far[head].astype(F32)

    key_chunks, value_chunks = [], []
    for head in range(0, KV_HEADS, 2):
        one, two = own_grads[head], own_grads[head + 1]
        key_chunks.append(jnp.where(lower, one, pltpu.roll(two, 64, 1)))
        value_chunks.append(jnp.where(lower, pltpu.roll(one, 64, 1), two))
    key_pre_grad = jnp.concatenate(
        rope_lanes(jnp.concatenate(key_chunks, axis=1), cosine, -sine), axis=1
    ).astype(BF)
    value_pre_grad = jnp.concatenate(value_chunks, axis=1).astype(BF)
    for slot, grad in enumerate((key_pre_grad, value_pre_grad)):
        store_mats(slot, slot).wait()
        mats[slot] = dot_tn(normed, grad).astype(BF)
        store_mats(slot, 2 + slot).start()
    normed_grad = (
        normed_grad
        + dot_nt(key_pre_grad, w_key_ref[...])
        + dot_nt(value_pre_grad, w_value_ref[...])
    )
    tokens = tokens_ref[...].astype(F32)
    scale_one = norm_scale(tokens)
    small_ref[32:33, :] = jnp.sum(normed_grad * tokens * scale_one, axis=0, keepdims=True)
    weighted = normed_grad * gain_one_ref[...]
    shared = scale_one * scale_one * scale_one * jnp.mean(weighted * tokens, axis=1, keepdims=True)
    input_grad_ref[...] = (residual_grad[...] + scale_one * weighted - tokens * shared).astype(BF)

    for reducer in reducers:
        reducer.step_sum(0)
    output_ref[...] = (residual_ref[...] + RESIDUAL_MULT * moe_total[...]).astype(BF)
    for reducer in reducers:
        reducer.finish()
    ring.finish()
    for slot in range(2):
        store_mats(slot, 2 + slot).wait()

    @pl.when(line >= 1 + (1 - core))
    def _():
        pair_three.wait_send()

    @pl.when((line >= 1) | (core == 1))
    def _():
        pair_one.wait_send()

    @pl.when(line >= 1)
    def _():
        to_near.wait_send()

    @pl.when(line >= 2)
    def _():
        to_far.wait_send()


def run_backward(*args):
    dma = pltpu.SemaphoreType.DMA
    rows = WIDTH + INNER
    vmem = pl.BlockSpec(memory_space=pltpu.VMEM)
    hbm = pl.BlockSpec(memory_space=pl.ANY)
    heads = (KV_HEADS, BLOCK, 128)
    shape = jax.ShapeDtypeStruct
    return pl.pallas_call(
        backward_kernel,
        out_shape=(
            shape((BLOCK, WIDTH), BF),
            shape((BLOCK, WIDTH), BF),
            shape((2 * SMALL_ROWS, WIDTH), F32),
            shape((6, WIDTH, 512), BF),
            shape((rows, WIDTH), BF),
        ),
        in_specs=[vmem] * 21 + [hbm] * 3,
        out_specs=(vmem, vmem, vmem, hbm, hbm),
        scratch_shapes=[pltpu.VMEM((PLANE, BLOCK, WIDTH), BF)]
        + reduce_buffers()
        + [
            pltpu.VMEM((rows, WIDTH), BF),
            pltpu.VMEM((2, rows // 8, WIDTH), BF),
            pltpu.VMEM((2, rows // 4, WIDTH), BF),
            pltpu.VMEM((BLOCK, WIDTH), F32),
            pltpu.VMEM((KV_HEADS, 2 * BLOCK, 128), F32),
            pltpu.VMEM((KV_HEADS, 2 * BLOCK, 128), BF),
            pltpu.VMEM((KV_HEADS, 2 * BLOCK, 128), F32),
            pltpu.VMEM(heads, F32),
            pltpu.VMEM((5,) + heads, BF),
            pltpu.VMEM((4,) + heads, BF),
            pltpu.VMEM(heads, BF),
            pltpu.VMEM(heads, BF),
            pltpu.VMEM((BLOCK, WIDTH), F32),
            pltpu.VMEM((2, WIDTH, 512), BF),
            dma((40,)),
            dma((40,)),
            dma((8,)),
            dma((8,)),
            dma((4,)),
            dma((4,)),
            dma((4,)),
            dma((2,)),
        ],
        compiler_params=pltpu.CompilerParams(
            collective_id=1, has_side_effects=True, vmem_limit_bytes=VMEM_LIMIT
        ),
    )(*args)


def on_device(
    tokens,
    segments,
    routes,
    rank_order,
    attn_gain,
    w_query,
    w_key,
    w_value,
    w_output,
    ffn_gain,
    w_router,
    expert_in,
    expert_out,
    cotangent,
):
    tok_rows = tokens.shape[1]
    model_width = tokens.shape[2]
    head_dim = HEAD
    block_id = lax.axis_index(("seq", "exp"))
    positions = block_id * tok_rows + jnp.arange(tok_rows, dtype=jnp.int32)
    cosine, sine_part = rope_tables(positions, head_dim)
    cosine_lanes = jnp.tile(cosine[:, 0], (1, 4))
    sine_lanes = jnp.tile(jnp.concatenate([-sine_part[:, 0], sine_part[:, 0]], axis=1), (1, 2))
    seg_tile = jnp.broadcast_to(segments.astype(jnp.float32), (8, tok_rows))
    (
        routed_in, residual, heads_out, normed, query_heads, kv_heads_all, lse, bias, gates, meta,
        cots, sib_in, sib_out,
    ) = run_attention(
        tokens[0], seg_tile, routes[0], rank_order[0], attn_gain[None], w_query, w_key, w_value,
        w_output, ffn_gain[None], w_router, cosine_lanes, sine_lanes, cotangent[0], expert_in[0],
        expert_out[0],
    )
    expert_row_sum, scores, moe_partial, expert_grads = run_experts(
        routed_in, meta, cots, expert_in[0], expert_out[0], sib_in, sib_out
    )
    output, input_grad, small, mats, expert_total = run_backward(
        tokens[0], cotangent[0], residual, expert_row_sum, scores, gates, routed_in, heads_out,
        normed, query_heads, kv_heads_all, bias, w_query, w_key, w_value, w_output, w_router,
        attn_gain[None], ffn_gain[None], cosine_lanes, sine_lanes, lse, moe_partial, expert_grads,
    )
    up_total = expert_total[None, :model_width].astype(jnp.float32)
    down_total = expert_total[None, model_width:].astype(jnp.float32)
    mats_total, small_total = total_all(mats, small)
    query_total = jnp.concatenate([mats_total[0], mats_total[1]], axis=1).astype(jnp.float32)
    key_total = mats_total[2].astype(jnp.float32)
    value_total = mats_total[3].astype(jnp.float32)
    out_total = jnp.concatenate([mats_total[4], mats_total[5]], axis=1).astype(jnp.float32)
    router_total = small_total[:32].T
    gain_one_total = small_total[32]
    gain_two_total = small_total[33]
    return (
        output[None],
        input_grad[None],
        gain_one_total,
        query_total,
        key_total,
        value_total,
        out_total,
        gain_two_total,
        router_total,
        up_total,
        down_total,
    )


def solution(mesh):
    placed = (
        P("grp", ("seq", "exp"), None),
        P("grp", ("seq", "exp")),
        P("grp", ("seq", "exp"), None),
        P("grp", ("seq", "exp"), None),
        P(),
        P(),
        P(),
        P(),
        P(),
        P(),
        P(),
        P(("grp", "exp"), None, None),
        P(("grp", "exp"), None, None),
        P("grp", ("seq", "exp"), None),
    )
    return jax.shard_map(
        on_device,
        mesh=mesh,
        in_specs=placed,
        out_specs=(
            P("grp", ("seq", "exp"), None),
            P("grp", ("seq", "exp"), None),
            P(),
            P(),
            P(),
            P(),
            P(),
            P(),
            P(),
            P(("grp", "exp"), None, None),
            P(("grp", "exp"), None, None),
        ),
        check_vma=False,
    )
```

```python
import math

import jax
import jax.numpy as jnp
from jax import lax
from jax.experimental import pallas as pl
from jax.experimental.pallas import tpu as pltpu
from jax.sharding import PartitionSpec as P

HEADS = 16
KV_HEADS = 8
HEAD = 64
WINDOW = 1024


EPSILON = 1e-06
ATTENTION_FACTOR = 0.015625
RESIDUAL_MULT = 0.22
ROPE_BASE = 10000.0
MASKED = -1e30


def rope_tables(positions, head_dim):
    half_dim = head_dim // 2
    frequency = jnp.exp(
        jnp.arange(half_dim, dtype=jnp.float32) * (-2.0 * math.log(ROPE_BASE) / head_dim)
    )
    angles = positions.astype(jnp.float32)[:, None] * frequency[None, :]
    return (jnp.cos(angles)[:, None, :], jnp.sin(angles)[:, None, :])


MESH = pl.DeviceIdType.MESH
CAPACITY = 80
BLOCK = 256
HALF = 128
QUARTER = 64
WIDTH = 1024
INNER = 512
PLANE = 16
GROUP = 3
BF = jnp.bfloat16
F32 = jnp.float32


def mod4(value):
    return lax.rem(value + 8, 4)


def plane_id(part, first, second):
    return first * 4 + second if part == 0 else second * 4 + first


def plane_coords(part):
    index = lax.axis_index("grp")
    row, column = index // 4, lax.rem(index, 4)
    return (row, column) if part == 0 else (column, row)


def plane_copy(source, target, send_sem, recv_sem, index):
    return pltpu.make_async_remote_copy(
        src_ref=source,
        dst_ref=target,
        send_sem=send_sem,
        recv_sem=recv_sem,
        device_id={"grp": index},
        device_id_type=MESH,
    )


def greet_plane():
    row, column = plane_coords(0)
    barrier = pltpu.get_barrier_semaphore()
    for index in (
        mod4(row + 1) * 4 + column,
        mod4(row - 1) * 4 + column,
        row * 4 + mod4(column + 1),
        row * 4 + mod4(column - 1),
    ):
        pl.semaphore_signal(barrier, inc=1, device_id={"grp": index}, device_id_type=MESH)
    pl.semaphore_wait(barrier, 4)


class PlaneGather:
    order = {0: 0, -1: 1, 1: 2, 2: 3}

    def __init__(self, part, blocks, send_sems, recv_sems):
        self.part, self.blocks = part, blocks
        self.send_sems, self.recv_sems = send_sems, recv_sems
        self.first, self.second = plane_coords(part)
        self.started = []

    def ref(self, da, db, half=None):
        index = plane_id(self.part, mod4(self.first + da), mod4(self.second + db))
        begin = pl.multiple_of(index * BLOCK + self.part * HALF, HALF)
        if half is None:
            return self.blocks.at[pl.ds(begin, HALF)]
        return self.blocks.at[pl.ds(pl.multiple_of(begin + half * QUARTER, QUARTER), QUARTER)]

    def copy(self, da, db, half, axis, step, slot):
        if axis == 0:
            to = plane_id(self.part, mod4(self.first + step), self.second)
        else:
            to = plane_id(self.part, self.first, mod4(self.second + step))
        ref, sem = self.ref(da, db, half), self.part * 20 + slot
        return plane_copy(ref, ref, self.send_sems.at[sem], self.recv_sems.at[sem], to)

    def send(self, *where):
        self.copy(*where).start()
        self.started.append(where)

    def wait(self, da, db, half, slot):
        ref, sem = self.ref(da, db, half), self.part * 20 + slot
        plane_copy(
            ref, ref, self.send_sems.at[sem], self.recv_sems.at[sem],
            plane_id(self.part, self.first, self.second),
        ).wait_recv()

    def begin(self):
        self.send(0, 0, None, 0, 1, 0)
        self.send(0, 0, None, 0, -1, 1)

    def spread(self, da):
        slot = 4 + 4 * self.order[da]
        self.send(da, 0, None, 1, 1, slot)
        self.send(da, 0, None, 1, -1, slot + 1)

    def forward_first(self):
        self.wait(-1, 0, None, 0)
        self.send(-1, 0, 0, 0, 1, 2)
        self.wait(1, 0, None, 1)
        self.send(1, 0, 1, 0, -1, 3)

    def forward_second(self, da):
        slot = 4 + 4 * self.order[da]
        self.wait(da, -1, None, slot)
        self.send(da, -1, 0, 1, 1, slot + 2)
        self.wait(da, 1, None, slot + 1)
        self.send(da, 1, 1, 1, -1, slot + 3)

    def wait_far_first(self):
        self.wait(2, 0, 0, 2)
        self.wait(2, 0, 1, 3)

    def wait_far_second(self, da):
        slot = 4 + 4 * self.order[da]
        self.wait(da, 2, 0, slot + 2)
        self.wait(da, 2, 1, slot + 3)

    def finish(self):
        for where in self.started:
            self.copy(*where).wait_send()


class PlaneReduce:
    order = {2: 0, 1: 1, -1: 2, 0: 3}

    def __init__(self, part, partial, buffers, send_sems, recv_sems, total):
        self.part, self.partial, self.total = part, partial, total
        self.far, self.near, self.summed, self.far_two, self.near_two = buffers
        self.send_sems, self.recv_sems = send_sems, recv_sems
        self.first, self.second = plane_coords(part)
        self.started = []

    def ref(self, da, db, half=None):
        index = plane_id(self.part, mod4(self.first + da), mod4(self.second + db))
        begin = self.part * HALF
        if half is None:
            return self.partial.at[index, pl.ds(begin, HALF)]
        return self.partial.at[index, pl.ds(begin + half * QUARTER, QUARTER)]

    def send(self, source, target, axis, step, slot):
        if axis == 0:
            to = plane_id(self.part, mod4(self.first + step), self.second)
        else:
            to = plane_id(self.part, self.first, mod4(self.second + step))
        sem = self.part * 20 + slot
        copy = plane_copy(source, target, self.send_sems.at[sem], self.recv_sems.at[sem], to)
        copy.start()
        self.started.append(copy)

    def wait(self, target, slot):
        sem = self.part * 20 + slot
        plane_copy(
            target, target, self.send_sems.at[sem], self.recv_sems.at[sem],
            plane_id(self.part, self.first, self.second),
        ).wait_recv()

    def add(self, target, source):
        target[...] = (target[...].astype(F32) + source[...].astype(F32)).astype(BF)

    def step_far(self, da):
        part, place = self.part, self.order[da]
        self.send(self.ref(da, 2, 0), self.far.at[part, place, 0], 1, 1, 4 * place)
        self.send(self.ref(da, 2, 1), self.far.at[part, place, 1], 1, -1, 4 * place + 1)

    def step_near(self, da):
        part, place = self.part, self.order[da]
        self.wait(self.far.at[part, place, 0], 4 * place)
        self.add(self.ref(da, 1, 0), self.far.at[part, place, 0])
        self.send(self.ref(da, 1), self.near.at[part, place, 0], 1, 1, 4 * place + 2)
        self.wait(self.far.at[part, place, 1], 4 * place + 1)
        self.add(self.ref(da, -1, 1), self.far.at[part, place, 1])
        self.send(self.ref(da, -1), self.near.at[part, place, 1], 1, -1, 4 * place + 3)

    def step_sum(self, da):
        part, place = self.part, self.order[da]
        self.wait(self.near.at[part, place, 0], 4 * place + 2)
        self.wait(self.near.at[part, place, 1], 4 * place + 3)
        value = (
            self.ref(da, 0)[...].astype(F32)
            + self.near[part, place, 0].astype(F32)
            + self.near[part, place, 1].astype(F32)
        )
        rows = pl.ds(part * HALF, HALF)
        if da == 0:
            self.total[rows] = value
            self.wait(self.near_two.at[part, 0], 18)
            self.wait(self.near_two.at[part, 1], 19)
            self.total[rows] += self.near_two[part, 0].astype(F32) + self.near_two[part, 1].astype(F32)
            return
        self.summed[part, place] = value.astype(BF)
        lower, upper = pl.ds(0, QUARTER), pl.ds(QUARTER, QUARTER)
        if da == 2:
            self.send(self.summed.at[part, 0, lower], self.far_two.at[part, 0], 0, 1, 16)
            self.send(self.summed.at[part, 0, upper], self.far_two.at[part, 1], 0, -1, 17)
        if da == 1:
            self.wait(self.far_two.at[part, 0], 16)
            self.add(self.summed.at[part, 1, lower], self.far_two.at[part, 0])
            self.send(self.summed.at[part, 1], self.near_two.at[part, 0], 0, 1, 18)
        if da == -1:
            self.wait(self.far_two.at[part, 1], 17)
            self.add(self.summed.at[part, 2, upper], self.far_two.at[part, 1])
            self.send(self.summed.at[part, 2], self.near_two.at[part, 1], 0, -1, 19)

    def finish(self):
        for copy in self.started:
            copy.wait_send()


def reduce_buffers():
    return [
        pltpu.VMEM((2, 4, 2, QUARTER, WIDTH), BF),
        pltpu.VMEM((2, 4, 2, HALF, WIDTH), BF),
        pltpu.VMEM((2, 3, HALF, WIDTH), BF),
        pltpu.VMEM((2, 2, QUARTER, WIDTH), BF),
        pltpu.VMEM((2, 2, HALF, WIDTH), BF),
    ]


def run_reduce(reducers):
    for da in (2, 1, -1, 0):
        for reducer in reducers:
            reducer.step_far(da)
    for da in (2, 1, -1, 0):
        for reducer in reducers:
            reducer.step_near(da)
    for da in (2, 1, -1, 0):
        for reducer in reducers:
            reducer.step_sum(da)
    for reducer in reducers:
        reducer.finish()


class FlatRows:
    def __init__(self, ref, begin, lead, rows):
        self.ref, self.begin, self.lead, self.rows = ref, begin, lead, rows

    def slice(self, index):
        flat = 0
        for extent, place in zip(self.lead, index if isinstance(index, tuple) else (index,)):
            flat = flat * extent + place
        return pl.ds(self.begin + flat * self.rows, self.rows)

    @property
    def at(self):
        return FlatView(self)

    def __getitem__(self, index):
        return self.ref[self.slice(index), :]


class FlatView:
    def __init__(self, flat):
        self.flat = flat

    def __getitem__(self, index):
        return self.flat.ref.at[self.flat.slice(index)]


class RowRing:
    def __init__(self, summed, far, near, send_sems, recv_sems):
        self.summed, self.far, self.near = summed, far, near
        self.send_sems, self.recv_sems = send_sems, recv_sems
        self.me = lax.axis_index("seq")
        self.rows = (WIDTH + INNER) // 4
        self.started = []

    def piece(self, ref, shift, half=None):
        begin = mod4(self.me + shift) * self.rows
        if half is None:
            return ref.at[pl.ds(pl.multiple_of(begin, 16), self.rows)]
        return ref.at[pl.ds(pl.multiple_of(begin + half * (self.rows // 2), 16), self.rows // 2)]

    def copy(self, source, target, step, slot):
        return pltpu.make_async_remote_copy(
            src_ref=source,
            dst_ref=target,
            send_sem=self.send_sems.at[slot],
            recv_sem=self.recv_sems.at[slot],
            device_id={"seq": mod4(self.me + step)},
            device_id_type=MESH,
        )

    def send(self, source, target, step, slot):
        copy = self.copy(source, target, step, slot)
        copy.start()
        self.started.append(copy)

    def wait(self, target, slot):
        self.copy(target, target, 1, slot).wait_recv()

    def add(self, target, source):
        target[...] = (target[...].astype(F32) + source[...].astype(F32)).astype(BF)

    def step_far(self):
        self.send(self.piece(self.summed, 2, 0), self.far.at[0], 1, 0)
        self.send(self.piece(self.summed, 2, 1), self.far.at[1], -1, 1)

    def step_near(self):
        self.wait(self.far.at[0], 0)
        self.add(self.piece(self.summed, 1, 0), self.far.at[0])
        self.send(self.piece(self.summed, 1), self.near.at[0], 1, 2)
        self.wait(self.far.at[1], 1)
        self.add(self.piece(self.summed, -1, 1), self.far.at[1])
        self.send(self.piece(self.summed, -1), self.near.at[1], -1, 3)

    def step_sum(self):
        self.wait(self.near.at[0], 2)
        self.wait(self.near.at[1], 3)
        own = self.piece(self.summed, 0)
        own[...] = (
            own[...].astype(F32) + self.near[0].astype(F32) + self.near[1].astype(F32)
        ).astype(BF)

    def finish(self):
        for copy in self.started:
            copy.wait_send()


class RowSpread(RowRing):
    def __init__(self, own, total, send_sems, recv_sems, local_sem):
        super().__init__(total, None, None, send_sems, recv_sems)
        self.own, self.local_sem = own, local_sem

    def begin(self):
        target = self.piece(self.summed, 0)
        self.send(self.own, target, 1, 0)
        self.send(self.own, target, -1, 1)
        pltpu.make_async_copy(self.own, target, self.local_sem).start()

    def forward(self):
        self.wait(self.piece(self.summed, -1), 0)
        half = self.piece(self.summed, -1, 0)
        self.send(half, half, 1, 2)
        self.wait(self.piece(self.summed, 1), 1)
        half = self.piece(self.summed, 1, 1)
        self.send(half, half, -1, 3)

    def finish(self):
        self.wait(self.piece(self.summed, 2, 0), 2)
        self.wait(self.piece(self.summed, 2, 1), 3)
        pltpu.make_async_copy(self.own, self.piece(self.summed, 0), self.local_sem).wait()
        super().finish()


class CubeSum:
    def __init__(self, part, matrix, out, far, near, mid, low, send_sems, recv_sems):
        self.part, self.matrix, self.out = part, matrix, out
        self.far, self.near, self.mid, self.low = far, near, mid, low
        self.send_sems, self.recv_sems = send_sems, recv_sems
        line, plane = lax.axis_index("seq"), lax.axis_index("grp")
        coords = (line, plane // 4, lax.rem(plane, 4))
        self.coords = coords
        self.place = [coords[(part + level) % 3] for level in range(3)]
        self.started = []

    def device(self, level, step):
        axis = (self.part + level) % 3
        there = mod4(self.coords[axis] + step)
        if axis == 0:
            return {"seq": there}
        if axis == 1:
            return {"grp": there * 4 + self.coords[2]}
        return {"grp": self.coords[1] * 4 + there}

    def rows(self, level, shift):
        begin = 0
        for upper in range(level):
            begin = begin + self.place[upper] * (256 // 4**upper)
        return begin + mod4(self.place[level] + shift) * (256 // 4**level)

    def copy(self, source, target, level, step, slot):
        return pltpu.make_async_remote_copy(
            src_ref=source,
            dst_ref=target,
            send_sem=self.send_sems.at[self.part, slot],
            recv_sem=self.recv_sems.at[self.part, slot],
            device_id=self.device(level, step),
            device_id_type=MESH,
        )

    def send(self, source, target, level, step, slot):
        copy = self.copy(source, target, level, step, slot)
        copy.start()
        self.started.append(copy)

    def wait(self, target, slot):
        self.copy(target, target, 0, 0, slot).wait_recv()

    def add(self, target, *sources):
        value = target[...].astype(F32)
        for source in sources:
            value = value + source[...].astype(F32)
        target[...] = value.astype(BF)

    def step_far(self):
        begin = self.rows(0, 2)
        self.send(self.matrix.at[pl.ds(begin, 128)], self.far.at[0], 0, 1, 0)
        self.send(self.matrix.at[pl.ds(begin + 128, 128)], self.far.at[1], 0, -1, 1)

    def step_near(self):
        begin = self.rows(0, 1)
        self.wait(self.far.at[0], 0)
        self.add(self.matrix.at[pl.ds(begin, 128)], self.far.at[0])
        self.send(self.matrix.at[pl.ds(begin, 256)], self.near.at[0], 0, 1, 2)
        begin = self.rows(0, -1)
        self.wait(self.far.at[1], 1)
        self.add(self.matrix.at[pl.ds(begin + 128, 128)], self.far.at[1])
        self.send(self.matrix.at[pl.ds(begin, 256)], self.near.at[1], 0, -1, 3)

    def step_mid(self):
        self.wait(self.near.at[0], 2)
        self.wait(self.near.at[1], 3)
        self.add(self.matrix.at[pl.ds(self.rows(0, 0), 256)], self.near.at[0], self.near.at[1])
        for step in (1, 2, 3):
            self.send(
                self.matrix.at[pl.ds(self.rows(1, step), 64)], self.mid.at[step - 1], 1, step, 3 + step
            )

    def step_low(self):
        for step in (1, 2, 3):
            self.wait(self.mid.at[step - 1], 3 + step)
        self.add(
            self.matrix.at[pl.ds(self.rows(1, 0), 64)], self.mid.at[0], self.mid.at[1], self.mid.at[2]
        )
        for step in (1, 2, 3):
            self.send(
                self.matrix.at[pl.ds(self.rows(2, step), 16)], self.low.at[step - 1], 2, step, 6 + step
            )

    def step_done(self):
        for step in (1, 2, 3):
            self.wait(self.low.at[step - 1], 6 + step)
        own = self.rows(2, 0)
        value = self.matrix[pl.ds(own, 16), :].astype(F32)
        for step in (1, 2, 3):
            value = value + self.low[step - 1].astype(F32)
        self.out[pl.ds(own, 16), :] = value.astype(BF)
        ref = self.out.at[pl.ds(own, 16)]
        for step in (1, 2, 3):
            self.send(ref, ref, 2, step, 9 + step)

    def back_mid(self):
        for step in (1, 2, 3):
            self.wait(self.out.at[pl.ds(self.rows(2, -step), 16)], 9 + step)
        ref = self.out.at[pl.ds(self.rows(1, 0), 64)]
        for step in (1, 2, 3):
            self.send(ref, ref, 1, step, 12 + step)

    def back_near(self):
        for step in (1, 2, 3):
            self.wait(self.out.at[pl.ds(self.rows(1, -step), 64)], 12 + step)
        ref = self.out.at[pl.ds(self.rows(0, 0), 256)]
        self.send(ref, ref, 0, 1, 16)
        self.send(ref, ref, 0, -1, 17)
        self.share(0, 20)

    def back_far(self):
        begin = self.rows(0, -1)
        self.wait(self.out.at[pl.ds(begin, 256)], 16)
        ref = self.out.at[pl.ds(begin, 128)]
        self.send(ref, ref, 0, 1, 18)
        self.share(-1, 21)
        begin = self.rows(0, 1)
        self.wait(self.out.at[pl.ds(begin, 256)], 17)
        ref = self.out.at[pl.ds(begin + 128, 128)]
        self.send(ref, ref, 0, -1, 19)
        self.share(1, 22)

    def back_last(self):
        begin = self.rows(0, 2)
        self.wait(self.out.at[pl.ds(begin, 128)], 18)
        self.wait(self.out.at[pl.ds(begin + 128, 128)], 19)
        self.share(2, 23)

    def share_copy(self, shift, slot):
        ref = self.out.at[pl.ds(self.rows(0, shift), 256)]
        return pltpu.make_async_remote_copy(
            src_ref=ref,
            dst_ref=ref,
            send_sem=self.send_sems.at[self.part, slot],
            recv_sem=self.recv_sems.at[self.part, slot],
            device_id={"exp": 1 - lax.axis_index("exp")},
            device_id_type=MESH,
        )

    def share(self, shift, slot):
        copy = self.share_copy(shift, slot)
        copy.start()
        self.started.append(copy)

    def finish(self, other_out):
        for shift, slot in ((0, 20), (-1, 21), (1, 22), (2, 23)):
            ref = other_out.at[pl.ds(self.rows(0, shift), 256)]
            pltpu.make_async_remote_copy(
                src_ref=ref,
                dst_ref=ref,
                send_sem=self.send_sems.at[self.part, slot],
                recv_sem=self.recv_sems.at[self.part, slot],
                device_id={"exp": 1 - lax.axis_index("exp")},
                device_id_type=MESH,
            ).wait_recv()
        for copy in self.started:
            copy.wait_send()


SMALL_ROWS = 24


def total_kernel(
    mats_ref,
    small_ref,
    out_ref,
    small_out_ref,
    matrix,
    far,
    near,
    mid,
    low,
    arrived,
    small,
    small_first,
    send_sems,
    recv_sems,
    core_send,
    core_recv,
    small_send,
    small_recv,
):
    line, plane, core = lax.axis_index("seq"), lax.axis_index("grp"), lax.axis_index("exp")
    row, column = plane // 4, lax.rem(plane, 4)
    other = 1 - core
    places = (line, row, column)

    def neighbour(axis, step):
        if axis == 0:
            return {"seq": mod4(line + step)}
        if axis == 1:
            return {"grp": mod4(row + step) * 4 + column}
        return {"grp": row * 4 + mod4(column + step)}

    barrier = pltpu.get_barrier_semaphore()
    for axis in range(3):
        for step in (1, 2, 3):
            pl.semaphore_signal(
                barrier, inc=1, device_id=neighbour(axis, step), device_id_type=MESH
            )
    pl.semaphore_signal(barrier, inc=1, device_id={"exp": other}, device_id_type=MESH)
    pl.semaphore_wait(barrier, 10)

    def to_core(source, target, slot):
        return pltpu.make_async_remote_copy(
            src_ref=source,
            dst_ref=target,
            send_sem=core_send.at[slot],
            recv_sem=core_recv.at[slot],
            device_id={"exp": other},
            device_id_type=MESH,
        )

    own_small = pl.ds(core * SMALL_ROWS, SMALL_ROWS)
    core_copies = [to_core(mats_ref.at[other * 3 + part], arrived.at[part], part) for part in range(3)]
    core_copies.append(
        to_core(small_ref.at[pl.ds(other * SMALL_ROWS, SMALL_ROWS)], small_first, 3)
    )
    for copy in core_copies:
        copy.start()
    sums = [
        CubeSum(
            part,
            matrix.at[part],
            out_ref.at[core * 3 + part],
            far.at[part],
            near.at[part],
            mid.at[part],
            low.at[part],
            send_sems,
            recv_sems,
        )
        for part in range(3)
    ]
    for part in range(3):
        core_copies[part].wait()
        matrix[part] = (
            mats_ref[core * 3 + part].astype(F32) + arrived[part].astype(F32)
        ).astype(BF)
        sums[part].step_far()
    small_copies = []

    def small_step(axis):
        for step in (1, 2, 3):
            copy = pltpu.make_async_remote_copy(
                src_ref=small.at[axis, places[axis]],
                dst_ref=small.at[axis, places[axis]],
                send_sem=small_send.at[axis, step],
                recv_sem=small_recv.at[axis, step],
                device_id=neighbour(axis, step),
                device_id_type=MESH,
            )
            copy.start()
            small_copies.append(copy)

    def small_sum(axis):
        for step in (1, 2, 3):
            ref = small.at[axis, mod4(places[axis] - step)]
            pltpu.make_async_remote_copy(
                src_ref=ref,
                dst_ref=ref,
                send_sem=small_send.at[axis, step],
                recv_sem=small_recv.at[axis, step],
                device_id=neighbour(axis, step),
                device_id_type=MESH,
            ).wait_recv()
        return (small[axis, 0] + small[axis, 1]) + (small[axis, 2] + small[axis, 3])

    core_copies[3].wait()
    small[0, line] = small_ref[own_small, :] + small_first[...]
    small_step(0)
    for cube in sums:
        cube.step_near()
    small[1, row] = small_sum(0)
    small_step(1)
    for cube in sums:
        cube.step_mid()
    small[2, column] = small_sum(1)
    small_step(2)
    for cube in sums:
        cube.step_low()
    small_out_ref[own_small, :] = small_sum(2)
    small_last = to_core(small_out_ref.at[own_small], small_out_ref.at[own_small], 4)
    small_last.start()
    for cube in sums:
        cube.step_done()
    for cube in sums:
        cube.back_mid()
    for cube in sums:
        cube.back_near()
    for cube in sums:
        cube.back_far()
    for cube in sums:
        cube.back_last()
    for part in range(3):
        sums[part].finish(out_ref.at[other * 3 + part])
    small_last.wait_send()
    theirs = small_out_ref.at[pl.ds(other * SMALL_ROWS, SMALL_ROWS)]
    to_core(theirs, theirs, 4).wait_recv()
    for copy in small_copies:
        copy.wait_send()


def total_all(mats, small):
    dma = pltpu.SemaphoreType.DMA
    vmem = pl.BlockSpec(memory_space=pltpu.VMEM)
    return pl.pallas_call(
        total_kernel,
        out_shape=(
            jax.ShapeDtypeStruct((6, 1024, 512), BF),
            jax.ShapeDtypeStruct((2 * SMALL_ROWS, WIDTH), F32),
        ),
        in_specs=[vmem, vmem],
        out_specs=(vmem, vmem),
        scratch_shapes=[
            pltpu.VMEM((3, 1024, 512), BF),
            pltpu.VMEM((3, 2, 128, 512), BF),
            pltpu.VMEM((3, 2, 256, 512), BF),
            pltpu.VMEM((3, 3, 64, 512), BF),
            pltpu.VMEM((3, 3, 16, 512), BF),
            pltpu.VMEM((3, 1024, 512), BF),
            pltpu.VMEM((3, 4, SMALL_ROWS, WIDTH), F32),
            pltpu.VMEM((SMALL_ROWS, WIDTH), F32),
            dma((3, 24)),
            dma((3, 24)),
            dma((5,)),
            dma((5,)),
            dma((3, 4)),
            dma((3, 4)),
        ],
        compiler_params=pltpu.CompilerParams(
            collective_id=3, has_side_effects=True, vmem_limit_bytes=40 << 20
        ),
    )(mats, small)


def dot_tn(left, right):
    return lax.dot_general(left, right, (((0,), (0,)), ((), ())), preferred_element_type=F32)


def dot_nt(left, right):
    return lax.dot_general(left, right, (((1,), (1,)), ((), ())), preferred_element_type=F32)


def dot_nn(left, right):
    return lax.dot_general(left, right, (((1,), (0,)), ((), ())), preferred_element_type=F32)


def expert_kernel(
    rows_ref,
    meta_ref,
    cot_ref,
    w_in_ref,
    w_out_ref,
    sib_in_ref,
    sib_out_ref,
    row_total_ref,
    score_out_ref,
    moe_ref,
    grad_ref,
    blocks,
    meta_in,
    score_send,
    cots,
    weights,
    kept_rows,
    kept_grads,
    kept_hidden,
    kept_pairs,
    row_partial,
    moe_stage,
    picks,
    slot_cots,
    slot_res,
    slot_back,
    summed,
    from_pair,
    send_sems,
    recv_sems,
    rsend_sems,
    rrecv_sems,
    meta_send,
    meta_recv,
    score_ssem,
    score_rsem,
    local_sems,
    cot_sems,
    moe_sems,
    pair_send,
    pair_recv,
    ring_send,
    ring_recv,
    plane_ready,
    line_ready,
):
    me = lax.axis_index("grp")
    core = lax.axis_index("exp")
    line = lax.axis_index("seq")
    other = 1 - core
    row, column = me // 4, lax.rem(me, 4)
    barrier = pltpu.get_barrier_semaphore()
    for step in range(1, PLANE):
        pl.semaphore_signal(
            barrier, inc=1, device_id={"grp": lax.rem(me + step, PLANE)}, device_id_type=MESH
        )
    pl.semaphore_signal(barrier, inc=1, device_id={"exp": other}, device_id_type=MESH)
    for step in (1, -1):
        pl.semaphore_signal(
            barrier, inc=1, device_id={"seq": mod4(line + step)}, device_id_type=MESH
        )

    def weight_in(expert):
        return weights.at[pl.ds(expert * WIDTH, WIDTH)]

    def weight_out(expert):
        return weights.at[pl.ds(2 * WIDTH + expert * INNER, INNER)]

    loads = [
        pltpu.make_async_copy(source, target, local_sems.at[slot])
        for slot, (source, target) in enumerate(
            (
                (w_in_ref, weight_in(core)),
                (w_out_ref, weight_out(core)),
                (sib_in_ref, weight_in(other)),
                (sib_out_ref, weight_out(other)),
            )
        )
    ]
    for load in loads:
        load.start()
    blocks[pl.ds(pl.multiple_of(me * BLOCK, BLOCK), BLOCK), :] = rows_ref[...]
    meta_in[me] = meta_ref[me]

    def place_of(power, j):
        step = power * 4**j
        return (
            mod4(row + lax.rem(ROW_STEPS // step, 4)) * 4
            + mod4(column + lax.rem(COLUMN_STEPS // step, 4))
        )

    def cot_copy(index, parity, j):
        return pltpu.make_async_copy(cot_ref.at[index], cots.at[parity, j], cot_sems.at[parity, j])

    def moe_copy(j, index):
        return pltpu.make_async_copy(moe_stage.at[j], moe_ref.at[index], moe_sems.at[j])

    cot_copy(me, 1, 0).start()
    for j in range(GROUP):
        cot_copy(place_of(1, j), 0, j).start()
    pl.semaphore_wait(barrier, PLANE + 2)

    gathers = [PlaneGather(part, blocks, send_sems, recv_sems) for part in (0, 1)]
    for gather in gathers:
        gather.begin()
    for gather in gathers:
        gather.spread(0)
    meta_copies = []
    for step in range(1, PLANE):
        to = lax.rem(me + step, PLANE)
        copy = plane_copy(
            meta_ref.at[to], meta_in.at[me], meta_send.at[step], meta_recv.at[step], to
        )
        copy.start()
        meta_copies.append(copy)

    def process(indices, parity, base, first_wait):
        count = len(indices)
        slots = count * CAPACITY
        gates = ([], [])
        for j, index in enumerate(indices):
            slot_id = lax.broadcasted_iota(jnp.int32, (CAPACITY, BLOCK), 0).astype(F32)
            hits = [slot_id == meta_in[index, expert : expert + 1, :] for expert in range(2)]
            for expert in range(2):
                gate_row = meta_in[index, 2 + expert : 3 + expert, :]
                gates[expert].append(
                    jnp.sum(jnp.where(hits[expert], gate_row, 0.0), axis=1, keepdims=True)
                )
            pick = jnp.concatenate(
                [jnp.where(hit, 1.0, 0.0).astype(BF) for hit in hits], axis=0
            )
            picks[j] = pick
            rows = dot_nn(pick, blocks[pl.ds(pl.multiple_of(index * BLOCK, BLOCK), BLOCK), :])
            cot_rows = dot_nn(pick, cots[parity, j])
            for expert in range(2):
                here = pl.ds(pl.multiple_of(base + j * CAPACITY, 16), CAPACITY)
                part = slice(expert * CAPACITY, expert * CAPACITY + CAPACITY)
                kept_rows[expert, here, :] = rows[part].astype(BF)
                slot_cots[expert, pl.ds(j * CAPACITY, CAPACITY), :] = cot_rows[part].astype(BF)
                kept_grads[expert, here, :] = (
                    gates[expert][j] * (RESIDUAL_MULT * cot_rows[part])
                ).astype(BF)
        here = pl.ds(pl.multiple_of(base, 16), slots)
        local = pl.ds(0, slots)
        for expert in range(2):
            gate = jnp.concatenate(gates[expert], axis=0) if count > 1 else gates[expert][0]
            gate_up = dot_nn(kept_rows[expert, here, :], weight_in(expert)[...])
            gate_half, up_half = gate_up[:, :INNER], gate_up[:, INNER:]
            sigmoid = jax.nn.sigmoid(gate_half)
            activated = gate_half * sigmoid
            hidden = (activated * up_half).astype(BF)
            kept_hidden[expert, here, :] = hidden
            result = dot_nn(hidden, weight_out(expert)[...]).astype(BF).astype(F32)
            scored = RESIDUAL_MULT * jnp.sum(
                slot_cots[expert, local, :].astype(F32) * result, axis=1, keepdims=True
            )
            slot_res[expert, local, :] = (gate * result).astype(BF)
            hidden_grad = dot_nt(kept_grads[expert, here, :], weight_out(expert)[...])
            gate_part = hidden_grad * up_half * sigmoid * (1.0 + gate_half * (1.0 - sigmoid))
            up_part = hidden_grad * activated
            pair_grad = jnp.concatenate([gate_part.astype(BF), up_part.astype(BF)], axis=1)
            kept_pairs[expert, here, :] = pair_grad
            slot_back[expert, local, :] = dot_nt(pair_grad, weight_in(expert)[...]).astype(BF)
            for j, index in enumerate(indices):
                pick = picks[j, pl.ds(expert * CAPACITY, CAPACITY), :].astype(F32)
                score_send[index, expert : expert + 1, :] = jnp.sum(
                    pick * scored[j * CAPACITY : (j + 1) * CAPACITY], axis=0, keepdims=True
                )
        for j, index in enumerate(indices):
            local = pl.ds(j * CAPACITY, CAPACITY)
            pick = picks[j]
            first_wait(j, index)
            values = jnp.concatenate([slot_res[0, local, :], slot_res[1, local, :]], axis=0)
            moe_stage[j] = dot_tn(pick, values).astype(BF)
            moe_copy(j, index).start()
            values = jnp.concatenate([slot_back[0, local, :], slot_back[1, local, :]], axis=0)
            row_partial[index] = dot_tn(pick, values).astype(BF)

    for load in loads:
        load.wait()
    cot_copy(me, 1, 0).wait()
    process([me], 1, 0, lambda j, index: None)
    for gather in gathers:
        gather.forward_first()
        gather.spread(-1)
        gather.spread(1)
    for gather in gathers:
        gather.forward_second(0)
    for copy in meta_copies:
        copy.wait()

    def one_group(group, power):
        parity = lax.rem(group, 2)

        @pl.when(group == 1)
        def _():
            for gather in gathers:
                gather.wait_far_first()
                gather.spread(2)
            for gather in gathers:
                gather.wait_far_second(0)

        @pl.when(group == 2)
        def _():
            for gather in gathers:
                gather.forward_second(1)
                gather.forward_second(-1)

        @pl.when(group == 3)
        def _():
            for gather in gathers:
                gather.forward_second(2)
            for gather in gathers:
                gather.wait_far_second(1)
                gather.wait_far_second(-1)

        @pl.when(group == 4)
        def _():
            for gather in gathers:
                gather.wait_far_second(2)

        indices = [place_of(power, j) for j in range(GROUP)]

        @pl.when(group < 4)
        def _():
            for j in range(GROUP):
                cot_copy(place_of(power * 4**GROUP, j), 1 - parity, j).start()

        for j in range(GROUP):
            cot_copy(indices[j], parity, j).wait()

        def first_wait(j, index):
            if j == 0:
                moe_copy(j, index).wait()
            else:

                @pl.when(group > 0)
                def _():
                    moe_copy(j, index).wait()

        process(indices, parity, CAPACITY + group * (GROUP * CAPACITY), first_wait)
        return lax.select(group < 4, power * 4**GROUP, power)

    lax.fori_loop(0, 5, one_group, jnp.int32(1))

    for gather in gathers:
        gather.finish()
    for index in (
        mod4(row + 1) * 4 + column,
        mod4(row - 1) * 4 + column,
        row * 4 + mod4(column + 1),
        row * 4 + mod4(column - 1),
    ):
        pl.semaphore_signal(plane_ready, inc=1, device_id={"grp": index}, device_id_type=MESH)
    for step in (1, -1):
        pl.semaphore_signal(
            line_ready, inc=1, device_id={"seq": mod4(line + step)}, device_id_type=MESH
        )
    buffers = (
        FlatRows(blocks, 0, (2, 4, 2), QUARTER),
        FlatRows(blocks, 1024, (2, 4, 2), HALF),
        summed,
        FlatRows(blocks, 3072, (2, 2), QUARTER),
        FlatRows(blocks, 3328, (2, 2), HALF),
    )
    reducers = [
        PlaneReduce(part, row_partial, buffers, rsend_sems, rrecv_sems, row_total_ref)
        for part in (0, 1)
    ]
    pl.semaphore_wait(plane_ready, 4)
    for da in (2, 1, -1, 0):
        for reducer in reducers:
            reducer.step_far(da)
    score_out_ref[me] = score_send[me]
    score_copies = []
    for step in range(1, PLANE):
        to = lax.rem(me + step, PLANE)
        copy = plane_copy(
            score_send.at[to], score_out_ref.at[me], score_ssem.at[step], score_rsem.at[step], to
        )
        copy.start()
        score_copies.append(copy)

    def grad_tile(expert, tile):
        columns = pl.ds((tile % 4) * BLOCK, BLOCK)
        if tile < 4:
            return dot_tn(kept_rows[expert, :, columns], kept_pairs[expert])
        return dot_tn(kept_hidden[expert, :, columns], kept_grads[expert])

    def pair_copy(tile):
        return pltpu.make_async_remote_copy(
            src_ref=cots.at[tile // GROUP, tile % GROUP],
            dst_ref=from_pair.at[tile],
            send_sem=pair_send.at[tile],
            recv_sem=pair_recv.at[tile],
            device_id={"exp": other},
            device_id_type=MESH,
        )

    for tile in range(6):
        cots[tile // GROUP, tile % GROUP] = grad_tile(other, tile).astype(BF)
        pair_copy(tile).start()
        if tile == 3:
            for reducer in reducers:
                reducer.step_near(2)
    for reducer in reducers:
        reducer.step_near(1)
    for tile in range(6):
        value = grad_tile(core, tile)
        pair_copy(tile).wait()
        weights[pl.ds(tile * BLOCK, BLOCK), :] = (value + from_pair[tile].astype(F32)).astype(BF)
        if tile == 2:
            for reducer in reducers:
                reducer.step_near(-1)
    pl.semaphore_wait(line_ready, 2)
    ring = RowRing(
        weights.at[pl.ds(0, WIDTH + INNER)],
        FlatRows(weights, 1536, (2,), 192),
        FlatRows(weights, 1920, (2,), 384),
        ring_send,
        ring_recv,
    )
    ring.step_far()
    for reducer in reducers:
        reducer.step_near(0)
    for reducer in reducers:
        reducer.step_sum(2)
    ring.step_near()
    for da in (1, -1):
        for reducer in reducers:
            reducer.step_sum(da)
    ring.step_sum()
    store = pltpu.make_async_copy(ring.piece(ring.summed, 0), grad_ref, local_sems.at[0])
    store.start()
    for reducer in reducers:
        reducer.step_sum(0)
    for reducer in reducers:
        reducer.finish()
    for copy in score_copies:
        copy.wait()
    for j in range(GROUP):
        moe_copy(j, j).wait()
    ring.finish()
    store.wait()


def step_table(steps):
    return sum(step * 4**i for i, step in enumerate(steps))


ROW_STEPS = step_table((1, 3, 0, 0, 2, 0, 1, 1, 3, 3, 2, 2, 1, 3, 2))
COLUMN_STEPS = step_table((0, 0, 1, 3, 0, 2, 1, 3, 1, 3, 1, 3, 2, 2, 2))


def run_experts(rows, meta, cots, expert_in, expert_out, sib_in, sib_out):
    vmem = pl.BlockSpec(memory_space=pltpu.VMEM)
    hbm = pl.BlockSpec(memory_space=pl.ANY)
    dma = pltpu.SemaphoreType.DMA
    slots = GROUP * CAPACITY
    every = PLANE * CAPACITY
    return pl.pallas_call(
        expert_kernel,
        out_shape=(
            jax.ShapeDtypeStruct((BLOCK, WIDTH), F32),
            jax.ShapeDtypeStruct((PLANE, 8, BLOCK), F32),
            jax.ShapeDtypeStruct((PLANE, BLOCK, WIDTH), BF),
            jax.ShapeDtypeStruct(((WIDTH + INNER) // 4, WIDTH), BF),
        ),
        in_specs=[vmem, vmem, hbm, hbm, hbm, hbm, hbm],
        out_specs=(vmem, vmem, hbm, hbm),
        scratch_shapes=[
            pltpu.VMEM((PLANE * BLOCK, WIDTH), BF),
            pltpu.VMEM((PLANE, 8, BLOCK), F32),
            pltpu.VMEM((PLANE, 8, BLOCK), F32),
            pltpu.VMEM((2, GROUP, BLOCK, WIDTH), BF),
            pltpu.VMEM((2 * (WIDTH + INNER), WIDTH), BF),
            pltpu.VMEM((2, every, WIDTH), BF),
            pltpu.VMEM((2, every, WIDTH), BF),
            pltpu.VMEM((2, every, INNER), BF),
            pltpu.VMEM((2, every, 2 * INNER), BF),
            pltpu.VMEM((PLANE, BLOCK, WIDTH), BF),
            pltpu.VMEM((GROUP, BLOCK, WIDTH), BF),
            pltpu.VMEM((GROUP, 2 * CAPACITY, BLOCK), BF),
            pltpu.VMEM((2, slots, WIDTH), BF),
            pltpu.VMEM((2, slots, WIDTH), BF),
            pltpu.VMEM((2, slots, WIDTH), BF),
            pltpu.VMEM((2, 3, HALF, WIDTH), BF),
            pltpu.VMEM((6, BLOCK, WIDTH), BF),
        ]
        + [dma((40,))] * 4
        + [dma((PLANE,))] * 4
        + [dma((4,)), dma((2, GROUP)), dma((GROUP,))]
        + [dma((6,))] * 2
        + [dma((4,))] * 2
        + [pltpu.SemaphoreType.REGULAR] * 2,
        compiler_params=pltpu.CompilerParams(
            collective_id=2, has_side_effects=True, vmem_limit_bytes=VMEM_LIMIT
        ),
    )(rows, meta, cots, expert_in, expert_out, sib_in, sib_out)


VMEM_LIMIT = 63 << 20


def rope_lanes(values, cosine, sine):
    lane = lax.broadcasted_iota(jnp.int32, (1, 128), 1)
    lower = lax.rem(lane, 64) < 32
    chunks = []
    for begin in range(0, values.shape[1], 128):
        chunk = values[:, begin : begin + 128]
        partner = jnp.where(lower, pltpu.roll(chunk, 96, 1), pltpu.roll(chunk, 32, 1))
        chunks.append(chunk * cosine + partner * sine)
    return chunks


def norm_scale(values):
    return lax.rsqrt(jnp.mean(values * values, axis=1, keepdims=True) + EPSILON)


def slot_table(routes, ranks):
    expert = lax.broadcasted_iota(jnp.int32, (BLOCK, 32), 1)
    rank_of = jnp.zeros((BLOCK, 32), jnp.int32)
    for k in range(8):
        rank_of = rank_of + jnp.where(routes[:, k : k + 1] == expert, ranks[:, k : k + 1] + 1, 0)
    chosen = rank_of > 0
    row = lax.broadcasted_iota(jnp.int32, (BLOCK, BLOCK), 0)
    lane = lax.broadcasted_iota(jnp.int32, (BLOCK, BLOCK), 1)
    source = lax.broadcasted_iota(jnp.int32, (32, BLOCK), 0)
    target = lax.broadcasted_iota(jnp.int32, (32, BLOCK), 1)
    repeat = jnp.where(lax.rem(target, 32) == source, 1.0, 0.0).astype(BF)
    rank_wide = dot_nn(rank_of.astype(F32).astype(BF), repeat)
    hit = rank_wide == (lane // 32 + 1).astype(F32)
    counts = jnp.where(hit, 1.0, 0.0)
    earlier = jnp.where(row > lane, 1.0, 0.0).astype(BF)
    before = dot_nn(earlier, counts.astype(BF))
    totals = jnp.sum(counts, axis=0, keepdims=True)
    lower = (lax.rem(row, 32) == lax.rem(lane, 32)) & (row // 32 < lane // 32)
    offsets = dot_nn(totals.astype(BF), jnp.where(lower, 1.0, 0.0).astype(BF))
    place = jnp.where(hit, before + offsets, 0.0)
    place = place[:, :128] + place[:, 128:]
    place = place + pltpu.roll(place, 64, 1)
    place = place + pltpu.roll(place, 32, 1)
    place = place[:, :32]
    return chosen, jnp.where(chosen & (place < CAPACITY), place, -1.0)


def attend_kernel(
    tokens_ref,
    seg_ref,
    routes_ref,
    ranks_ref,
    gain_one_ref,
    w_query_ref,
    w_key_ref,
    w_value_ref,
    w_output_ref,
    gain_two_ref,
    w_router_ref,
    cosine_ref,
    sine_ref,
    cot_ref,
    w_in_ref,
    w_out_ref,
    routed_ref,
    residual_ref,
    heads_ref,
    normed_ref,
    query_ref,
    kv_ref,
    lse_ref,
    bias_ref,
    gates_ref,
    meta_ref,
    cots_ref,
    sib_in_ref,
    sib_out_ref,
    segs,
    top,
    expsum,
    acc,
    send_sems,
    recv_sems,
    kv_send,
    kv_recv,
    seg_send,
    seg_recv,
    weight_send,
    weight_recv,
    local_sem,
):
    line, plane, core = lax.axis_index("seq"), lax.axis_index("grp"), lax.axis_index("exp")
    block = 2 * line + core
    row, column = plane // 4, lax.rem(plane, 4)
    barrier = pltpu.get_barrier_semaphore()
    for index in (
        mod4(row + 1) * 4 + column,
        mod4(row - 1) * 4 + column,
        row * 4 + mod4(column + 1),
        row * 4 + mod4(column - 1),
    ):
        pl.semaphore_signal(barrier, inc=1, device_id={"grp": index}, device_id_type=MESH)
    for step in (1, 2, 3):
        pl.semaphore_signal(
            barrier, inc=1, device_id={"seq": mod4(line + step)}, device_id_type=MESH
        )
    pl.semaphore_signal(barrier, inc=1, device_id={"exp": 1 - core}, device_id_type=MESH)
    own_cot = pltpu.make_async_copy(
        cot_ref, cots_ref.at[pl.ds(pl.multiple_of(plane * BLOCK, BLOCK), BLOCK)], local_sem
    )
    own_cot.start()

    tokens = tokens_ref[...].astype(F32)
    normed = (tokens * norm_scale(tokens) * gain_one_ref[...]).astype(BF)
    normed_ref[...] = normed
    cosine, sine = cosine_ref[...], sine_ref[...]
    keys = dot_nn(normed, w_key_ref[...])
    values = dot_nn(normed, w_value_ref[...]).astype(BF)
    key_chunks = rope_lanes(keys, cosine, sine)
    for head in range(KV_HEADS):
        chunk = key_chunks[head // 2].astype(BF)
        key = chunk[:, (head % 2) * 64 : (head % 2) * 64 + 64]
        kv_ref[0, head] = jnp.concatenate([key, values[:, head * 64 : head * 64 + 64]], axis=1)
    segs[0] = seg_ref[...]
    own_cot.wait()
    pl.semaphore_wait(barrier, 8)

    def kv_copies(source, target, device, slot):
        return [
            pltpu.make_async_remote_copy(
                src_ref=ref.at[source],
                dst_ref=ref.at[target],
                send_sem=sends.at[slot],
                recv_sem=recvs.at[target],
                device_id=device,
                device_id_type=MESH,
            )
            for ref, sends, recvs in ((kv_ref, kv_send, kv_recv), (segs, seg_send, seg_recv))
        ]

    sibling = {"exp": 1 - core}
    to_near = kv_copies(0, 2, {"seq": mod4(line + 1)}, 1)
    to_far = kv_copies(0, 4, {"seq": mod4(line + 2)}, 2)
    to_sibling = kv_copies(0, 1, sibling, 0)
    forward_near = kv_copies(2, 3 - 2 * core, sibling, 3)
    forward_far = kv_copies(4, 3, sibling, 4)

    def begin(copies):
        for copy in copies:
            copy.start()

    def sent(copies):
        for copy in copies:
            copy.wait_send()

    @pl.when(line < 3)
    def _():
        begin(to_near)

    @pl.when(core == 0)
    def _():
        begin(to_sibling)

    @pl.when(line < 2)
    def _():
        begin(to_far)

    gathers = [PlaneGather(part, cots_ref, send_sems, recv_sems) for part in (0, 1)]
    for gather in gathers:
        gather.begin()
    for gather in gathers:
        gather.spread(0)
    weight_copies = [
        pltpu.make_async_remote_copy(
            src_ref=source,
            dst_ref=target,
            send_sem=weight_send.at[slot],
            recv_sem=weight_recv.at[slot],
            device_id=sibling,
            device_id_type=MESH,
        )
        for slot, (source, target) in enumerate(((w_in_ref, sib_in_ref), (w_out_ref, sib_out_ref)))
    ]
    begin(weight_copies)

    lane = lax.broadcasted_iota(jnp.int32, (1, 128), 1)
    queries = dot_nn(normed, w_query_ref[...])
    for head, chunk in enumerate(rope_lanes(queries, cosine, sine)):
        chunk = (chunk.astype(BF).astype(F32) * ATTENTION_FACTOR)
        query_ref[head, :BLOCK, :] = jnp.where(lane < 64, chunk, 0.0).astype(BF)
        query_ref[head, BLOCK:, :] = jnp.where(lane < 64, pltpu.roll(chunk, 64, 1), 0.0).astype(BF)
    top[...] = jnp.full(top.shape, MASKED, F32)
    expsum[...] = jnp.zeros(expsum.shape, F32)
    acc[...] = jnp.zeros(acc.shape, F32)
    seg_column = seg_ref[...].T[:, :1]

    def attend(slot):
        i = lax.broadcasted_iota(jnp.int32, (BLOCK, BLOCK), 0)
        j = lax.broadcasted_iota(jnp.int32, (BLOCK, BLOCK), 1)
        distance = slot * BLOCK + i - j
        allowed = (seg_column == segs[slot, 0:1, :]) & (distance >= 0) & (distance < WINDOW)
        bias = jnp.where(allowed, 0.0, MASKED)
        bias_ref[slot] = bias

        @pl.loop(0, KV_HEADS)
        def _(head):
            pair = kv_ref[slot, head]
            one = bias_ref[slot]
            score = dot_nt(query_ref[head], pair)
            score = score + jnp.concatenate([one, one], axis=0)
            old = top[head][:, :1]
            new = jnp.maximum(old, jnp.max(score, axis=1, keepdims=True))
            weight = jnp.exp(score - new)
            fade = jnp.exp(old - new)
            expsum[head] = expsum[head] * fade + jnp.sum(weight, axis=1, keepdims=True)
            acc[head] = acc[head] * fade + dot_nn(weight.astype(BF), pair)
            top[head] = jnp.broadcast_to(new, (2 * BLOCK, 128))

    def wait_block(slot):
        for ref, sends, recvs in ((kv_ref, kv_send, kv_recv), (segs, seg_send, seg_recv)):
            pltpu.make_async_remote_copy(
                src_ref=ref.at[slot],
                dst_ref=ref.at[slot],
                send_sem=sends.at[0],
                recv_sem=recvs.at[slot],
                device_id=sibling,
                device_id_type=MESH,
            ).wait_recv()

    attend(0)
    for gather in gathers:
        gather.forward_first()
        gather.spread(-1)
        gather.spread(1)

    chosen, kept = slot_table(routes_ref[...], ranks_ref[...])
    kept_rows = jnp.concatenate([kept, jnp.zeros((BLOCK, 96), F32)], axis=1).T
    for index in range(PLANE):
        meta_ref[index, 0:2, :] = kept_rows[2 * index : 2 * index + 2]
        meta_ref[index, 4:8, :] = jnp.zeros((4, BLOCK), F32)

    first = 2 - core

    @pl.when(block >= first)
    def _():
        wait_block(first)

        @pl.when(core == 0)
        def _():
            begin(forward_near)

        attend(first)

    for gather in gathers:
        gather.forward_second(0)
    for gather in gathers:
        gather.wait_far_first()
        gather.spread(2)
    second = 1 + core

    @pl.when(block >= second)
    def _():
        wait_block(second)

        @pl.when(core == 1)
        def _():
            begin(forward_near)

        attend(second)

    for da in (-1, 1):
        for gather in gathers:
            gather.forward_second(da)
    third = 4 - core

    @pl.when(block >= third)
    def _():
        wait_block(third)
        attend(third)

    for gather in gathers:
        gather.forward_second(2)
    fourth = 3 + core

    @pl.when(block >= fourth)
    def _():
        wait_block(fourth)

        @pl.when(core == 1)
        def _():
            begin(forward_far)

        attend(fourth)

    for head in range(KV_HEADS):
        inverse = 1.0 / expsum[head][:, :1]
        pair = acc[head] * inverse
        heads_ref[:, head * 128 : head * 128 + 128] = jnp.where(
            lane < 64, pltpu.roll(pair[:BLOCK], 64, 1), pair[BLOCK:]
        ).astype(BF)
        lse_ref[head] = top[head] + jnp.log(expsum[head])
    branch = dot_nn(heads_ref[...], w_output_ref[...])
    residual = tokens_ref[...].astype(F32) + RESIDUAL_MULT * branch
    residual_ref[...] = residual
    routed = (residual * norm_scale(residual) * gain_two_ref[...]).astype(BF)
    routed_ref[...] = routed
    logits = dot_nn(routed, w_router_ref[...])
    logits = jnp.where(chosen, logits, MASKED)
    powers = jnp.exp(logits - jnp.max(logits, axis=1, keepdims=True))
    gates = jnp.where(chosen, powers / jnp.sum(powers, axis=1, keepdims=True), 0.0)
    gates_ref[...] = gates
    gate_rows = jnp.concatenate([gates, jnp.zeros((BLOCK, 96), F32)], axis=1).T
    for index in range(PLANE):
        meta_ref[index, 2:4, :] = gate_rows[2 * index : 2 * index + 2]

    for da in (0, -1, 1, 2):
        for gather in gathers:
            gather.wait_far_second(da)
    for gather in gathers:
        gather.finish()
    for copy in weight_copies:
        copy.wait()

    @pl.when(line < 3)
    def _():
        sent(to_near)

    @pl.when(core == 0)
    def _():
        sent(to_sibling)

    @pl.when(line < 2)
    def _():
        sent(to_far)

    @pl.when(line >= 1)
    def _():
        sent(forward_near)

    @pl.when((line >= 2) & (core == 1))
    def _():
        sent(forward_far)


def run_attention(
    tokens, seg_tile, routes, ranks, gain_one, w_query, w_key, w_value, w_output, gain_two,
    w_router, cosine, sine, cot, expert_in, expert_out,
):
    vmem = pl.BlockSpec(memory_space=pltpu.VMEM)
    hbm = pl.BlockSpec(memory_space=pl.ANY)
    dma = pltpu.SemaphoreType.DMA
    shape = jax.ShapeDtypeStruct
    return pl.pallas_call(
        attend_kernel,
        out_shape=(
            shape((BLOCK, WIDTH), BF),
            shape((BLOCK, WIDTH), F32),
            shape((BLOCK, WIDTH), BF),
            shape((BLOCK, WIDTH), BF),
            shape((KV_HEADS, 2 * BLOCK, 128), BF),
            shape((5, KV_HEADS, BLOCK, 128), BF),
            shape((KV_HEADS, 2 * BLOCK, 128), F32),
            shape((5, BLOCK, BLOCK), F32),
            shape((BLOCK, 32), F32),
            shape((PLANE, 8, BLOCK), F32),
            shape((PLANE * BLOCK, WIDTH), BF),
            shape((WIDTH, 2 * INNER), BF),
            shape((INNER, WIDTH), BF),
        ),
        in_specs=[vmem] * 13 + [hbm] * 3,
        out_specs=(vmem,) * 10 + (hbm,) * 3,
        scratch_shapes=[
            pltpu.VMEM((5, 8, BLOCK), F32),
            pltpu.VMEM((KV_HEADS, 2 * BLOCK, 128), F32),
            pltpu.VMEM((KV_HEADS, 2 * BLOCK, 128), F32),
            pltpu.VMEM((KV_HEADS, 2 * BLOCK, 128), F32),
            dma((40,)),
            dma((40,)),
            dma((5,)),
            dma((5,)),
            dma((5,)),
            dma((5,)),
            dma((2,)),
            dma((2,)),
            dma,
        ],
        compiler_params=pltpu.CompilerParams(
            collective_id=0, has_side_effects=True, vmem_limit_bytes=58 << 20
        ),
    )(
        tokens, seg_tile, routes, ranks, gain_one, w_query, w_key, w_value, w_output, gain_two,
        w_router, cosine, sine, cot, expert_in, expert_out,
    )


def backward_kernel(
    tokens_ref,
    cot_ref,
    residual_ref,
    row_total_ref,
    scores_ref,
    gates_ref,
    routed_ref,
    heads_ref,
    normed_ref,
    query_ref,
    kv_ref,
    bias_ref,
    w_query_ref,
    w_key_ref,
    w_value_ref,
    w_output_ref,
    w_router_ref,
    gain_one_ref,
    gain_two_ref,
    cosine_ref,
    sine_ref,
    lse_ref,
    partial_ref,
    grad_ref,
    output_ref,
    input_grad_ref,
    small_ref,
    mats_ref,
    grad_total_ref,
    partial,
    far,
    near,
    summed,
    far_two,
    near_two,
    moe_total,
    stats,
    head_grads,
    query_grads,
    own_grads,
    stage,
    from_pair,
    from_near,
    from_far,
    residual_grad,
    mats,
    send_sems,
    recv_sems,
    ring_send,
    ring_recv,
    kv_send,
    kv_recv,
    local_sems,
    mats_sems,
):
    line, plane, core = lax.axis_index("seq"), lax.axis_index("grp"), lax.axis_index("exp")
    block = 2 * line + core
    row, column = plane // 4, lax.rem(plane, 4)
    load = pltpu.make_async_copy(partial_ref, partial, local_sems.at[1])
    load_lse = pltpu.make_async_copy(lse_ref, stats, local_sems.at[2])
    load.start()
    load_lse.start()
    barrier = pltpu.get_barrier_semaphore()
    for index in (
        mod4(row + 1) * 4 + column,
        mod4(row - 1) * 4 + column,
        row * 4 + mod4(column + 1),
        row * 4 + mod4(column - 1),
    ):
        pl.semaphore_signal(barrier, inc=1, device_id={"grp": index}, device_id_type=MESH)
    for step in (1, 2, 3):
        pl.semaphore_signal(
            barrier, inc=1, device_id={"seq": mod4(line + step)}, device_id_type=MESH
        )
    pl.semaphore_signal(barrier, inc=1, device_id={"exp": 1 - core}, device_id_type=MESH)
    pl.semaphore_wait(barrier, 8)
    buffers = (far, near, summed, far_two, near_two)
    reducers = [
        PlaneReduce(part, partial, buffers, send_sems, recv_sems, moe_total) for part in (0, 1)
    ]
    spread = RowSpread(grad_ref, grad_total_ref, ring_send, ring_recv, local_sems.at[0])
    spread.begin()
    load.wait()
    for da in (2, 1, -1, 0):
        for reducer in reducers:
            reducer.step_far(da)

    lane = lax.broadcasted_iota(jnp.int32, (1, 128), 1)
    lower = lane < 64
    gate_grad = jnp.concatenate(
        [scores_ref[index, 0:2, :] for index in range(PLANE)] + [jnp.zeros((96, BLOCK), F32)], axis=0
    ).T[:, :32]
    gates = gates_ref[...]
    choice_grad = gates * (gate_grad - jnp.sum(gates * gate_grad, axis=1, keepdims=True))
    logit_grad = choice_grad.astype(BF)
    small_ref[0:32, :] = dot_tn(logit_grad, routed_ref[...])
    routed_grad = dot_nt(logit_grad, w_router_ref[...]) + row_total_ref[...]
    residual = residual_ref[...]
    scale_two = norm_scale(residual)
    small_ref[33:34, :] = jnp.sum(routed_grad * residual * scale_two, axis=0, keepdims=True)
    small_ref[34:48, :] = jnp.zeros((14, WIDTH), F32)
    weighted = routed_grad * gain_two_ref[...]
    shared = scale_two * scale_two * scale_two * jnp.mean(weighted * residual, axis=1, keepdims=True)
    grown = cot_ref[...].astype(F32) + scale_two * weighted - residual * shared
    residual_grad[...] = grown
    branch_grad = (RESIDUAL_MULT * grown).astype(BF)
    head_grad = dot_nt(branch_grad, w_output_ref[...]).astype(BF)
    load_lse.wait()
    for head in range(KV_HEADS):
        chunk = head_grad[:, head * 128 : head * 128 + 128].astype(F32)
        other = heads_ref[:, head * 128 : head * 128 + 128].astype(F32)
        head_grads[head, :BLOCK, :] = jnp.where(lower, 0.0, pltpu.roll(chunk, 64, 1)).astype(BF)
        head_grads[head, BLOCK:, :] = jnp.where(lower, 0.0, chunk).astype(BF)
        both = chunk * other
        one = jnp.sum(jnp.where(lower, both, 0.0), axis=1, keepdims=True)
        two = jnp.sum(jnp.where(lower, 0.0, both), axis=1, keepdims=True)
        stats[head, :BLOCK, :] = jnp.where(lower, stats[head, :BLOCK, :], one)
        stats[head, BLOCK:, :] = jnp.where(lower, stats[head, BLOCK:, :], two)
    query_grads[...] = jnp.zeros(query_grads.shape, F32)

    def store_mats(slot, index):
        return pltpu.make_async_copy(mats.at[slot], mats_ref.at[index], mats_sems.at[slot])

    for slot in range(2):
        mats[slot] = dot_tn(heads_ref[...], branch_grad[:, slot * 512 : slot * 512 + 512]).astype(BF)
        store_mats(slot, 4 + slot).start()

    def attend_back(slot):
        @pl.loop(0, KV_HEADS)
        def _(head):
            pair, query, out_grad = kv_ref[slot, head], query_ref[head], head_grads[head]
            one = bias_ref[slot]
            score = dot_nt(query, pair) + jnp.concatenate([one, one], axis=0)
            prob = jnp.exp(score - stats[head][:, :1])
            prob_grad = dot_nt(out_grad, pair)
            score_grad = (prob * (prob_grad - stats[head][:, 64:65])).astype(BF)
            query_grads[head] += dot_nn(score_grad, pair)
            own_grads[head] = dot_tn(score_grad, query) + dot_tn(prob.astype(BF), out_grad)
            stage[slot, head] = own_grads[head].astype(BF)

    sibling = {"exp": 1 - core}

    def kv_copy(source, target, device, slot):
        return pltpu.make_async_remote_copy(
            src_ref=source,
            dst_ref=target,
            send_sem=kv_send.at[slot],
            recv_sem=kv_recv.at[slot],
            device_id=device,
            device_id_type=MESH,
        )

    pair_three = kv_copy(stage.at[3], from_pair.at[core], sibling, 0)
    pair_one = kv_copy(stage.at[1], from_pair.at[2 + core], sibling, 1)
    to_near = kv_copy(stage.at[2], from_near, {"seq": mod4(line - 1)}, 2)
    to_far = kv_copy(stage.at[4], from_far, {"seq": mod4(line - 2)}, 3)

    def take_pair(three, slot):
        source = from_pair.at[(0 if three else 2) + 1 - core]
        kv_copy(source, source, sibling, 0 if three else 1).wait_recv()
        for head in range(KV_HEADS):
            stage[slot, head] = (
                stage[slot, head].astype(F32) + source[head].astype(F32)
            ).astype(BF)

    first, second, third, fourth = 3 + core, 4 - core, 1 + core, 2 - core

    @pl.when(block >= first)
    def _():
        attend_back(first)

    @pl.when((core == 0) & (line >= 2))
    def _():
        pair_three.start()

    for reducer in reducers:
        reducer.step_near(2)
        reducer.step_near(1)

    @pl.when((core == 1) & (line >= 2))
    def _():
        take_pair(True, 4)
        to_far.start()

    @pl.when(block >= second)
    def _():
        attend_back(second)

    @pl.when((core == 1) & (line >= 1))
    def _():
        pair_three.start()

    @pl.when((core == 0) & (line >= 2))
    def _():
        to_far.start()

    spread.forward()

    for reducer in reducers:
        reducer.step_near(-1)
        reducer.step_near(0)

    @pl.when(block >= third)
    def _():
        attend_back(third)

    @pl.when((core == 0) & (line >= 1))
    def _():
        pair_one.start()

    for reducer in reducers:
        reducer.step_sum(2)

    @pl.when((core == 1) & (line >= 1))
    def _():
        take_pair(False, 2)
        to_near.start()

    @pl.when(block >= fourth)
    def _():
        attend_back(fourth)

    @pl.when(core == 1)
    def _():
        pair_one.start()

    @pl.when((core == 0) & (line >= 1))
    def _():
        take_pair(True, 2)
        to_near.start()

    for reducer in reducers:
        reducer.step_sum(1)
        reducer.step_sum(-1)
    attend_back(0)

    cosine, sine = cosine_ref[...], sine_ref[...]
    normed = normed_ref[...]
    query_chunks = []
    for head in range(KV_HEADS):
        chunk = jnp.where(
            lower, query_grads[head, :BLOCK, :], pltpu.roll(query_grads[head, BLOCK:, :], 64, 1)
        )
        query_chunks.append(chunk * ATTENTION_FACTOR)
    query_pre_grad = jnp.concatenate(
        rope_lanes(jnp.concatenate(query_chunks, axis=1), cosine, -sine), axis=1
    ).astype(BF)
    normed_grad = dot_nt(query_pre_grad, w_query_ref[...])
    for slot in range(2):
        store_mats(slot, 4 + slot).wait()
        mats[slot] = dot_tn(normed, query_pre_grad[:, slot * 512 : slot * 512 + 512]).astype(BF)
        store_mats(slot, slot).start()

    @pl.when(core == 0)
    def _():
        source = from_pair.at[3]
        kv_copy(source, source, sibling, 1).wait_recv()
        for head in range(KV_HEADS):
            own_grads[head] += source[head].astype(F32)

    @pl.when(line < 3)
    def _():
        kv_copy(from_near, from_near, sibling, 2).wait_recv()
        for head in range(KV_HEADS):
            own_grads[head] += from_near[head].astype(F32)

    @pl.when(line < 2)
    def _():
        kv_copy(from_far, from_far, sibling, 3).wait_recv()
        for head in range(KV_HEADS):
            own_grads[head] += from_far[head].astype(F32)

    key_chunks, value_chunks = [], []
    for head in range(0, KV_HEADS, 2):
        one, two = own_grads[head], own_grads[head + 1]
        key_chunks.append(jnp.where(lower, one, pltpu.roll(two, 64, 1)))
        value_chunks.append(jnp.where(lower, pltpu.roll(one, 64, 1), two))
    key_pre_grad = jnp.concatenate(
        rope_lanes(jnp.concatenate(key_chunks, axis=1), cosine, -sine), axis=1
    ).astype(BF)
    value_pre_grad = jnp.concatenate(value_chunks, axis=1).astype(BF)
    for slot, grad in enumerate((key_pre_grad, value_pre_grad)):
        store_mats(slot, slot).wait()
        mats[slot] = dot_tn(normed, grad).astype(BF)
        store_mats(slot, 2 + slot).start()
    normed_grad = (
        normed_grad
        + dot_nt(key_pre_grad, w_key_ref[...])
        + dot_nt(value_pre_grad, w_value_ref[...])
    )
    tokens = tokens_ref[...].astype(F32)
    scale_one = norm_scale(tokens)
    small_ref[32:33, :] = jnp.sum(normed_grad * tokens * scale_one, axis=0, keepdims=True)
    weighted = normed_grad * gain_one_ref[...]
    shared = scale_one * scale_one * scale_one * jnp.mean(weighted * tokens, axis=1, keepdims=True)
    input_grad_ref[...] = (residual_grad[...] + scale_one * weighted - tokens * shared).astype(BF)

    for reducer in reducers:
        reducer.step_sum(0)
    output_ref[...] = (residual_ref[...] + RESIDUAL_MULT * moe_total[...]).astype(BF)
    for reducer in reducers:
        reducer.finish()
    spread.finish()
    for slot in range(2):
        store_mats(slot, 2 + slot).wait()

    @pl.when(line >= 1 + (1 - core))
    def _():
        pair_three.wait_send()

    @pl.when((line >= 1) | (core == 1))
    def _():
        pair_one.wait_send()

    @pl.when(line >= 1)
    def _():
        to_near.wait_send()

    @pl.when(line >= 2)
    def _():
        to_far.wait_send()


def run_backward(*args):
    dma = pltpu.SemaphoreType.DMA
    rows = WIDTH + INNER
    vmem = pl.BlockSpec(memory_space=pltpu.VMEM)
    hbm = pl.BlockSpec(memory_space=pl.ANY)
    heads = (KV_HEADS, BLOCK, 128)
    shape = jax.ShapeDtypeStruct
    return pl.pallas_call(
        backward_kernel,
        out_shape=(
            shape((BLOCK, WIDTH), BF),
            shape((BLOCK, WIDTH), BF),
            shape((2 * SMALL_ROWS, WIDTH), F32),
            shape((6, WIDTH, 512), BF),
            shape((rows, WIDTH), BF),
        ),
        in_specs=[vmem] * 21 + [hbm] * 3,
        out_specs=(vmem, vmem, vmem, hbm, hbm),
        scratch_shapes=[pltpu.VMEM((PLANE, BLOCK, WIDTH), BF)]
        + reduce_buffers()
        + [
            pltpu.VMEM((BLOCK, WIDTH), F32),
            pltpu.VMEM((KV_HEADS, 2 * BLOCK, 128), F32),
            pltpu.VMEM((KV_HEADS, 2 * BLOCK, 128), BF),
            pltpu.VMEM((KV_HEADS, 2 * BLOCK, 128), F32),
            pltpu.VMEM(heads, F32),
            pltpu.VMEM((5,) + heads, BF),
            pltpu.VMEM((4,) + heads, BF),
            pltpu.VMEM(heads, BF),
            pltpu.VMEM(heads, BF),
            pltpu.VMEM((BLOCK, WIDTH), F32),
            pltpu.VMEM((2, WIDTH, 512), BF),
            dma((40,)),
            dma((40,)),
            dma((4,)),
            dma((4,)),
            dma((4,)),
            dma((4,)),
            dma((3,)),
            dma((2,)),
        ],
        compiler_params=pltpu.CompilerParams(
            collective_id=1, has_side_effects=True, vmem_limit_bytes=VMEM_LIMIT
        ),
    )(*args)


def on_device(
    tokens,
    segments,
    routes,
    rank_order,
    attn_gain,
    w_query,
    w_key,
    w_value,
    w_output,
    ffn_gain,
    w_router,
    expert_in,
    expert_out,
    cotangent,
):
    tok_rows = tokens.shape[1]
    model_width = tokens.shape[2]
    head_dim = HEAD
    block_id = lax.axis_index(("seq", "exp"))
    positions = block_id * tok_rows + jnp.arange(tok_rows, dtype=jnp.int32)
    cosine, sine_part = rope_tables(positions, head_dim)
    cosine_lanes = jnp.tile(cosine[:, 0], (1, 4))
    sine_lanes = jnp.tile(jnp.concatenate([-sine_part[:, 0], sine_part[:, 0]], axis=1), (1, 2))
    seg_tile = jnp.broadcast_to(segments.astype(jnp.float32), (8, tok_rows))
    (
        routed_in, residual, heads_out, normed, query_heads, kv_heads_all, lse, bias, gates, meta,
        cots, sib_in, sib_out,
    ) = run_attention(
        tokens[0], seg_tile, routes[0], rank_order[0], attn_gain[None], w_query, w_key, w_value,
        w_output, ffn_gain[None], w_router, cosine_lanes, sine_lanes, cotangent[0], expert_in[0],
        expert_out[0],
    )
    expert_row_sum, scores, moe_partial, expert_grads = run_experts(
        routed_in, meta, cots.reshape(PLANE, BLOCK, WIDTH), expert_in[0], expert_out[0], sib_in, sib_out,
    )
    output, input_grad, small, mats, expert_total = run_backward(
        tokens[0], cotangent[0], residual, expert_row_sum, scores, gates, routed_in, heads_out,
        normed, query_heads, kv_heads_all, bias, w_query, w_key, w_value, w_output, w_router,
        attn_gain[None], ffn_gain[None], cosine_lanes, sine_lanes, lse, moe_partial, expert_grads,
    )
    up_total = expert_total[None, :model_width].astype(jnp.float32)
    down_total = expert_total[None, model_width:].astype(jnp.float32)
    mats_total, small_total = total_all(mats, small)
    query_total = jnp.concatenate([mats_total[0], mats_total[1]], axis=1).astype(jnp.float32)
    key_total = mats_total[2].astype(jnp.float32)
    value_total = mats_total[3].astype(jnp.float32)
    out_total = jnp.concatenate([mats_total[4], mats_total[5]], axis=1).astype(jnp.float32)
    router_total = small_total[:32].T
    gain_one_total = small_total[32]
    gain_two_total = small_total[33]
    return (
        output[None],
        input_grad[None],
        gain_one_total,
        query_total,
        key_total,
        value_total,
        out_total,
        gain_two_total,
        router_total,
        up_total,
        down_total,
    )


def solution(mesh):
    placed = (
        P("grp", ("seq", "exp"), None),
        P("grp", ("seq", "exp")),
        P("grp", ("seq", "exp"), None),
        P("grp", ("seq", "exp"), None),
        P(),
        P(),
        P(),
        P(),
        P(),
        P(),
        P(),
        P(("grp", "exp"), None, None),
        P(("grp", "exp"), None, None),
        P("grp", ("seq", "exp"), None),
    )
    return jax.shard_map(
        on_device,
        mesh=mesh,
        in_specs=placed,
        out_specs=(
            P("grp", ("seq", "exp"), None),
            P("grp", ("seq", "exp"), None),
            P(),
            P(),
            P(),
            P(),
            P(),
            P(),
            P(),
            P(("grp", "exp"), None, None),
            P(("grp", "exp"), None, None),
        ),
        check_vma=False,
    )
```

```python
import math

import jax
import jax.numpy as jnp
import numpy as np
from jax import lax
from jax.experimental import pallas as pl
from jax.experimental.pallas import tpu as pltpu
from jax.sharding import PartitionSpec as P

HEADS = 16
KV_HEADS = 8
HEAD = 64
WINDOW = 1024


EPSILON = 1e-06
ATTENTION_FACTOR = 0.015625
RESIDUAL_MULT = 0.22
ROPE_BASE = 10000.0
MASKED = -1e30


def rope_lane_table(length):
    half_dim = HEAD // 2
    frequency = np.exp(
        np.arange(half_dim, dtype=np.float32) * np.float32(-2.0 * math.log(ROPE_BASE) / HEAD)
    ).astype(np.float32)
    angles = np.arange(length, dtype=np.float32)[:, None] * frequency[None, :]
    cosine, sine = np.cos(angles), np.sin(angles)
    tables = (np.tile(cosine, (1, 4)), np.tile(np.concatenate([-sine, sine], axis=1), (1, 2)))
    return np.stack([table.reshape(-1, BLOCK, 128) for table in tables], axis=1).astype(np.float32)


MESH = pl.DeviceIdType.MESH
CAPACITY = 80
BLOCK = 256
HALF = 128
QUARTER = 64
WIDTH = 1024
INNER = 512
PLANE = 16
GROUP = 3
BF = jnp.bfloat16
F32 = jnp.float32


def mod4(value):
    return lax.rem(value + 8, 4)


def plane_id(part, first, second):
    return first * 4 + second if part == 0 else second * 4 + first


def plane_coords(part):
    index = lax.axis_index("grp")
    row, column = index // 4, lax.rem(index, 4)
    return (row, column) if part == 0 else (column, row)


def plane_copy(source, target, send_sem, recv_sem, index):
    return pltpu.make_async_remote_copy(
        src_ref=source,
        dst_ref=target,
        send_sem=send_sem,
        recv_sem=recv_sem,
        device_id={"grp": index},
        device_id_type=MESH,
    )


class PlaneGather:
    order = {0: 0, -1: 1, 1: 2, 2: 3}

    def __init__(self, part, blocks, send_sems, recv_sems):
        self.part, self.blocks = part, blocks
        self.send_sems, self.recv_sems = send_sems, recv_sems
        self.first, self.second = plane_coords(part)
        self.started = []

    def ref(self, da, db, half=None):
        index = plane_id(self.part, mod4(self.first + da), mod4(self.second + db))
        begin = pl.multiple_of(index * BLOCK + self.part * HALF, HALF)
        if half is None:
            return self.blocks.at[pl.ds(begin, HALF)]
        return self.blocks.at[pl.ds(pl.multiple_of(begin + half * QUARTER, QUARTER), QUARTER)]

    def copy(self, da, db, half, axis, step, slot):
        if axis == 0:
            to = plane_id(self.part, mod4(self.first + step), self.second)
        else:
            to = plane_id(self.part, self.first, mod4(self.second + step))
        ref, sem = self.ref(da, db, half), self.part * 20 + slot
        return plane_copy(ref, ref, self.send_sems.at[sem], self.recv_sems.at[sem], to)

    def send(self, *where):
        self.copy(*where).start()
        self.started.append(where)

    def wait(self, da, db, half, slot):
        ref, sem = self.ref(da, db, half), self.part * 20 + slot
        plane_copy(
            ref, ref, self.send_sems.at[sem], self.recv_sems.at[sem],
            plane_id(self.part, self.first, self.second),
        ).wait_recv()

    def begin(self):
        self.send(0, 0, None, 0, 1, 0)
        self.send(0, 0, None, 0, -1, 1)

    def spread(self, da):
        slot = 4 + 4 * self.order[da]
        self.send(da, 0, None, 1, 1, slot)
        self.send(da, 0, None, 1, -1, slot + 1)

    def forward_first(self):
        self.wait(-1, 0, None, 0)
        self.send(-1, 0, 0, 0, 1, 2)
        self.wait(1, 0, None, 1)
        self.send(1, 0, 1, 0, -1, 3)

    def forward_second(self, da):
        slot = 4 + 4 * self.order[da]
        self.wait(da, -1, None, slot)
        self.send(da, -1, 0, 1, 1, slot + 2)
        self.wait(da, 1, None, slot + 1)
        self.send(da, 1, 1, 1, -1, slot + 3)

    def wait_far_first(self):
        self.wait(2, 0, 0, 2)
        self.wait(2, 0, 1, 3)

    def wait_far_second(self, da):
        slot = 4 + 4 * self.order[da]
        self.wait(da, 2, 0, slot + 2)
        self.wait(da, 2, 1, slot + 3)

    def finish(self):
        for where in self.started:
            self.copy(*where).wait_send()


class PlaneReduce:
    order = {2: 0, 1: 1, -1: 2, 0: 3}

    def __init__(self, part, partial, buffers, send_sems, recv_sems, total):
        self.part, self.partial, self.total = part, partial, total
        self.far, self.near, self.summed, self.far_two, self.near_two = buffers
        self.send_sems, self.recv_sems = send_sems, recv_sems
        self.first, self.second = plane_coords(part)
        self.started = []

    def ref(self, da, db, half=None):
        index = plane_id(self.part, mod4(self.first + da), mod4(self.second + db))
        begin = self.part * HALF
        if half is None:
            return self.partial.at[index, pl.ds(begin, HALF)]
        return self.partial.at[index, pl.ds(begin + half * QUARTER, QUARTER)]

    def send(self, source, target, axis, step, slot):
        if axis == 0:
            to = plane_id(self.part, mod4(self.first + step), self.second)
        else:
            to = plane_id(self.part, self.first, mod4(self.second + step))
        sem = self.part * 20 + slot
        copy = plane_copy(source, target, self.send_sems.at[sem], self.recv_sems.at[sem], to)
        copy.start()
        self.started.append(copy)

    def wait(self, target, slot):
        sem = self.part * 20 + slot
        plane_copy(
            target, target, self.send_sems.at[sem], self.recv_sems.at[sem],
            plane_id(self.part, self.first, self.second),
        ).wait_recv()

    def add(self, target, source):
        target[...] = (target[...].astype(F32) + source[...].astype(F32)).astype(BF)

    def step_far(self, da):
        part, place = self.part, self.order[da]
        self.send(self.ref(da, 2, 0), self.far.at[part, place, 0], 1, 1, 4 * place)
        self.send(self.ref(da, 2, 1), self.far.at[part, place, 1], 1, -1, 4 * place + 1)

    def step_near(self, da):
        part, place = self.part, self.order[da]
        self.wait(self.far.at[part, place, 0], 4 * place)
        self.add(self.ref(da, 1, 0), self.far.at[part, place, 0])
        self.send(self.ref(da, 1), self.near.at[part, place, 0], 1, 1, 4 * place + 2)
        self.wait(self.far.at[part, place, 1], 4 * place + 1)
        self.add(self.ref(da, -1, 1), self.far.at[part, place, 1])
        self.send(self.ref(da, -1), self.near.at[part, place, 1], 1, -1, 4 * place + 3)

    def step_sum(self, da):
        part, place = self.part, self.order[da]
        self.wait(self.near.at[part, place, 0], 4 * place + 2)
        self.wait(self.near.at[part, place, 1], 4 * place + 3)
        value = (
            self.ref(da, 0)[...].astype(F32)
            + self.near[part, place, 0].astype(F32)
            + self.near[part, place, 1].astype(F32)
        )
        rows = pl.ds(part * HALF, HALF)
        if da == 0:
            self.total[rows] = value
            self.wait(self.near_two.at[part, 0], 18)
            self.wait(self.near_two.at[part, 1], 19)
            self.total[rows] += self.near_two[part, 0].astype(F32) + self.near_two[part, 1].astype(F32)
            return
        self.summed[part, place] = value.astype(BF)
        lower, upper = pl.ds(0, QUARTER), pl.ds(QUARTER, QUARTER)
        if da == 2:
            self.send(self.summed.at[part, 0, lower], self.far_two.at[part, 0], 0, 1, 16)
            self.send(self.summed.at[part, 0, upper], self.far_two.at[part, 1], 0, -1, 17)
        if da == 1:
            self.wait(self.far_two.at[part, 0], 16)
            self.add(self.summed.at[part, 1, lower], self.far_two.at[part, 0])
            self.send(self.summed.at[part, 1], self.near_two.at[part, 0], 0, 1, 18)
        if da == -1:
            self.wait(self.far_two.at[part, 1], 17)
            self.add(self.summed.at[part, 2, upper], self.far_two.at[part, 1])
            self.send(self.summed.at[part, 2], self.near_two.at[part, 1], 0, -1, 19)

    def finish(self):
        for copy in self.started:
            copy.wait_send()


def reduce_buffers():
    return [
        pltpu.VMEM((2, 4, 2, QUARTER, WIDTH), BF),
        pltpu.VMEM((2, 4, 2, HALF, WIDTH), BF),
        pltpu.VMEM((2, 3, HALF, WIDTH), BF),
        pltpu.VMEM((2, 2, QUARTER, WIDTH), BF),
        pltpu.VMEM((2, 2, HALF, WIDTH), BF),
    ]


class FlatRows:
    def __init__(self, ref, begin, lead, rows):
        self.ref, self.begin, self.lead, self.rows = ref, begin, lead, rows

    def slice(self, index):
        flat = 0
        for extent, place in zip(self.lead, index if isinstance(index, tuple) else (index,)):
            flat = flat * extent + place
        return pl.ds(self.begin + flat * self.rows, self.rows)

    @property
    def at(self):
        return FlatView(self)

    def __getitem__(self, index):
        return self.ref[self.slice(index), :]


class FlatView:
    def __init__(self, flat):
        self.flat = flat

    def __getitem__(self, index):
        return self.flat.ref.at[self.flat.slice(index)]


class RowRing:
    def __init__(self, summed, far, near, send_sems, recv_sems):
        self.summed, self.far, self.near = summed, far, near
        self.send_sems, self.recv_sems = send_sems, recv_sems
        self.me = lax.axis_index("seq")
        self.rows = (WIDTH + INNER) // 4
        self.started = []

    def piece(self, ref, shift, half=None):
        begin = mod4(self.me + shift) * self.rows
        if half is None:
            return ref.at[pl.ds(pl.multiple_of(begin, 16), self.rows)]
        return ref.at[pl.ds(pl.multiple_of(begin + half * (self.rows // 2), 16), self.rows // 2)]

    def copy(self, source, target, step, slot):
        return pltpu.make_async_remote_copy(
            src_ref=source,
            dst_ref=target,
            send_sem=self.send_sems.at[slot],
            recv_sem=self.recv_sems.at[slot],
            device_id={"seq": mod4(self.me + step)},
            device_id_type=MESH,
        )

    def send(self, source, target, step, slot):
        copy = self.copy(source, target, step, slot)
        copy.start()
        self.started.append(copy)

    def wait(self, target, slot):
        self.copy(target, target, 1, slot).wait_recv()

    def add(self, target, source):
        target[...] = (target[...].astype(F32) + source[...].astype(F32)).astype(BF)

    def step_far(self):
        self.send(self.piece(self.summed, 2, 0), self.far.at[0], 1, 0)
        self.send(self.piece(self.summed, 2, 1), self.far.at[1], -1, 1)

    def step_near(self):
        self.wait(self.far.at[0], 0)
        self.add(self.piece(self.summed, 1, 0), self.far.at[0])
        self.send(self.piece(self.summed, 1), self.near.at[0], 1, 2)
        self.wait(self.far.at[1], 1)
        self.add(self.piece(self.summed, -1, 1), self.far.at[1])
        self.send(self.piece(self.summed, -1), self.near.at[1], -1, 3)

    def step_sum(self):
        self.wait(self.near.at[0], 2)
        self.wait(self.near.at[1], 3)
        own = self.piece(self.summed, 0)
        own[...] = (
            own[...].astype(F32) + self.near[0].astype(F32) + self.near[1].astype(F32)
        ).astype(BF)

    def finish(self):
        for copy in self.started:
            copy.wait_send()


class RowSpread(RowRing):
    def __init__(self, own, total, send_sems, recv_sems, local_sem):
        super().__init__(total, None, None, send_sems, recv_sems)
        self.own, self.local_sem = own, local_sem

    def begin(self):
        target = self.piece(self.summed, 0)
        self.send(self.own, target, 1, 0)
        self.send(self.own, target, -1, 1)
        pltpu.make_async_copy(self.own, target, self.local_sem).start()

    def forward(self):
        self.wait(self.piece(self.summed, -1), 0)
        half = self.piece(self.summed, -1, 0)
        self.send(half, half, 1, 2)
        self.wait(self.piece(self.summed, 1), 1)
        half = self.piece(self.summed, 1, 1)
        self.send(half, half, -1, 3)

    def finish(self):
        self.wait(self.piece(self.summed, 2, 0), 2)
        self.wait(self.piece(self.summed, 2, 1), 3)
        pltpu.make_async_copy(self.own, self.piece(self.summed, 0), self.local_sem).wait()
        super().finish()


class CubeSum:
    def __init__(self, part, matrix, out, far, near, mid, low, send_sems, recv_sems):
        self.part, self.matrix, self.out = part, matrix, out
        self.far, self.near, self.mid, self.low = far, near, mid, low
        self.send_sems, self.recv_sems = send_sems, recv_sems
        line, plane = lax.axis_index("seq"), lax.axis_index("grp")
        coords = (line, plane // 4, lax.rem(plane, 4))
        self.coords = coords
        self.place = [coords[(part + level) % 3] for level in range(3)]
        self.started = []

    def device(self, level, step):
        axis = (self.part + level) % 3
        there = mod4(self.coords[axis] + step)
        if axis == 0:
            return {"seq": there}
        if axis == 1:
            return {"grp": there * 4 + self.coords[2]}
        return {"grp": self.coords[1] * 4 + there}

    def rows(self, level, shift):
        begin = 0
        for upper in range(level):
            begin = begin + self.place[upper] * (256 // 4**upper)
        return begin + mod4(self.place[level] + shift) * (256 // 4**level)

    def copy(self, source, target, level, step, slot):
        return pltpu.make_async_remote_copy(
            src_ref=source,
            dst_ref=target,
            send_sem=self.send_sems.at[self.part, slot],
            recv_sem=self.recv_sems.at[self.part, slot],
            device_id=self.device(level, step),
            device_id_type=MESH,
        )

    def send(self, source, target, level, step, slot):
        copy = self.copy(source, target, level, step, slot)
        copy.start()
        self.started.append(copy)

    def wait(self, target, slot):
        self.copy(target, target, 0, 0, slot).wait_recv()

    def add(self, target, *sources):
        value = target[...].astype(F32)
        for source in sources:
            value = value + source[...].astype(F32)
        target[...] = value.astype(BF)

    def step_far(self):
        begin = self.rows(0, 2)
        self.send(self.matrix.at[pl.ds(begin, 128)], self.far.at[0], 0, 1, 0)
        self.send(self.matrix.at[pl.ds(begin + 128, 128)], self.far.at[1], 0, -1, 1)

    def step_near(self):
        begin = self.rows(0, 1)
        self.wait(self.far.at[0], 0)
        self.add(self.matrix.at[pl.ds(begin, 128)], self.far.at[0])
        self.send(self.matrix.at[pl.ds(begin, 256)], self.near.at[0], 0, 1, 2)
        begin = self.rows(0, -1)
        self.wait(self.far.at[1], 1)
        self.add(self.matrix.at[pl.ds(begin + 128, 128)], self.far.at[1])
        self.send(self.matrix.at[pl.ds(begin, 256)], self.near.at[1], 0, -1, 3)

    def step_mid(self):
        self.wait(self.near.at[0], 2)
        self.wait(self.near.at[1], 3)
        self.add(self.matrix.at[pl.ds(self.rows(0, 0), 256)], self.near.at[0], self.near.at[1])
        for step in (1, 2, 3):
            self.send(
                self.matrix.at[pl.ds(self.rows(1, step), 64)], self.mid.at[step - 1], 1, step, 3 + step
            )

    def step_low(self):
        for step in (1, 2, 3):
            self.wait(self.mid.at[step - 1], 3 + step)
        self.add(
            self.matrix.at[pl.ds(self.rows(1, 0), 64)], self.mid.at[0], self.mid.at[1], self.mid.at[2]
        )
        for step in (1, 2, 3):
            self.send(
                self.matrix.at[pl.ds(self.rows(2, step), 16)], self.low.at[step - 1], 2, step, 6 + step
            )

    def step_done(self):
        for step in (1, 2, 3):
            self.wait(self.low.at[step - 1], 6 + step)
        own = self.rows(2, 0)
        value = self.matrix[pl.ds(own, 16), :].astype(F32)
        for step in (1, 2, 3):
            value = value + self.low[step - 1].astype(F32)
        self.out[pl.ds(own, 16), :] = value.astype(BF)
        ref = self.out.at[pl.ds(own, 16)]
        for step in (1, 2, 3):
            self.send(ref, ref, 2, step, 9 + step)

    def back_mid(self):
        for step in (1, 2, 3):
            self.wait(self.out.at[pl.ds(self.rows(2, -step), 16)], 9 + step)
        ref = self.out.at[pl.ds(self.rows(1, 0), 64)]
        for step in (1, 2, 3):
            self.send(ref, ref, 1, step, 12 + step)

    def back_near(self):
        for step in (1, 2, 3):
            self.wait(self.out.at[pl.ds(self.rows(1, -step), 64)], 12 + step)
        ref = self.out.at[pl.ds(self.rows(0, 0), 256)]
        self.send(ref, ref, 0, 1, 16)
        self.send(ref, ref, 0, -1, 17)
        self.share(0, 20)

    def back_far(self):
        begin = self.rows(0, -1)
        self.wait(self.out.at[pl.ds(begin, 256)], 16)
        ref = self.out.at[pl.ds(begin, 128)]
        self.send(ref, ref, 0, 1, 18)
        self.share(-1, 21)
        begin = self.rows(0, 1)
        self.wait(self.out.at[pl.ds(begin, 256)], 17)
        ref = self.out.at[pl.ds(begin + 128, 128)]
        self.send(ref, ref, 0, -1, 19)
        self.share(1, 22)

    def back_last(self):
        begin = self.rows(0, 2)
        self.wait(self.out.at[pl.ds(begin, 128)], 18)
        self.wait(self.out.at[pl.ds(begin + 128, 128)], 19)
        self.share(2, 23)

    def share_copy(self, shift, slot):
        ref = self.out.at[pl.ds(self.rows(0, shift), 256)]
        return pltpu.make_async_remote_copy(
            src_ref=ref,
            dst_ref=ref,
            send_sem=self.send_sems.at[self.part, slot],
            recv_sem=self.recv_sems.at[self.part, slot],
            device_id={"exp": 1 - lax.axis_index("exp")},
            device_id_type=MESH,
        )

    def share(self, shift, slot):
        copy = self.share_copy(shift, slot)
        copy.start()
        self.started.append(copy)

    def finish(self, other_out):
        for shift, slot in ((0, 20), (-1, 21), (1, 22), (2, 23)):
            ref = other_out.at[pl.ds(self.rows(0, shift), 256)]
            pltpu.make_async_remote_copy(
                src_ref=ref,
                dst_ref=ref,
                send_sem=self.send_sems.at[self.part, slot],
                recv_sem=self.recv_sems.at[self.part, slot],
                device_id={"exp": 1 - lax.axis_index("exp")},
                device_id_type=MESH,
            ).wait_recv()
        for copy in self.started:
            copy.wait_send()


SMALL_ROWS = 24


def total_kernel(
    mats_ref,
    small_ref,
    out_ref,
    small_out_ref,
    matrix,
    far,
    near,
    mid,
    low,
    arrived,
    small,
    small_first,
    send_sems,
    recv_sems,
    core_send,
    core_recv,
    small_send,
    small_recv,
):
    line, plane, core = lax.axis_index("seq"), lax.axis_index("grp"), lax.axis_index("exp")
    row, column = plane // 4, lax.rem(plane, 4)
    other = 1 - core
    places = (line, row, column)

    def neighbour(axis, step):
        if axis == 0:
            return {"seq": mod4(line + step)}
        if axis == 1:
            return {"grp": mod4(row + step) * 4 + column}
        return {"grp": row * 4 + mod4(column + step)}

    barrier = pltpu.get_barrier_semaphore()
    for axis in range(3):
        for step in (1, 2, 3):
            pl.semaphore_signal(
                barrier, inc=1, device_id=neighbour(axis, step), device_id_type=MESH
            )
    pl.semaphore_signal(barrier, inc=1, device_id={"exp": other}, device_id_type=MESH)
    pl.semaphore_wait(barrier, 10)

    def to_core(source, target, slot):
        return pltpu.make_async_remote_copy(
            src_ref=source,
            dst_ref=target,
            send_sem=core_send.at[slot],
            recv_sem=core_recv.at[slot],
            device_id={"exp": other},
            device_id_type=MESH,
        )

    own_small = pl.ds(core * SMALL_ROWS, SMALL_ROWS)
    core_copies = [to_core(mats_ref.at[other * 3 + part], arrived.at[part], part) for part in range(3)]
    core_copies.append(
        to_core(small_ref.at[pl.ds(other * SMALL_ROWS, SMALL_ROWS)], small_first, 3)
    )
    for copy in core_copies:
        copy.start()
    sums = [
        CubeSum(
            part,
            matrix.at[part],
            out_ref.at[core * 3 + part],
            far.at[part],
            near.at[part],
            mid.at[part],
            low.at[part],
            send_sems,
            recv_sems,
        )
        for part in range(3)
    ]
    for part in range(3):
        core_copies[part].wait()
        matrix[part] = (
            mats_ref[core * 3 + part].astype(F32) + arrived[part].astype(F32)
        ).astype(BF)
        sums[part].step_far()
    small_copies = []

    def small_step(axis):
        for step in (1, 2, 3):
            copy = pltpu.make_async_remote_copy(
                src_ref=small.at[axis, places[axis]],
                dst_ref=small.at[axis, places[axis]],
                send_sem=small_send.at[axis, step],
                recv_sem=small_recv.at[axis, step],
                device_id=neighbour(axis, step),
                device_id_type=MESH,
            )
            copy.start()
            small_copies.append(copy)

    def small_sum(axis):
        for step in (1, 2, 3):
            ref = small.at[axis, mod4(places[axis] - step)]
            pltpu.make_async_remote_copy(
                src_ref=ref,
                dst_ref=ref,
                send_sem=small_send.at[axis, step],
                recv_sem=small_recv.at[axis, step],
                device_id=neighbour(axis, step),
                device_id_type=MESH,
            ).wait_recv()
        return (small[axis, 0] + small[axis, 1]) + (small[axis, 2] + small[axis, 3])

    core_copies[3].wait()
    small[0, line] = small_ref[own_small, :] + small_first[...]
    small_step(0)
    for cube in sums:
        cube.step_near()
    small[1, row] = small_sum(0)
    small_step(1)
    for cube in sums:
        cube.step_mid()
    small[2, column] = small_sum(1)
    small_step(2)
    for cube in sums:
        cube.step_low()
    small_out_ref[own_small, :] = small_sum(2)
    small_last = to_core(small_out_ref.at[own_small], small_out_ref.at[own_small], 4)
    small_last.start()
    for cube in sums:
        cube.step_done()
    for cube in sums:
        cube.back_mid()
    for cube in sums:
        cube.back_near()
    for cube in sums:
        cube.back_far()
    for cube in sums:
        cube.back_last()
    for part in range(3):
        sums[part].finish(out_ref.at[other * 3 + part])
    small_last.wait_send()
    theirs = small_out_ref.at[pl.ds(other * SMALL_ROWS, SMALL_ROWS)]
    to_core(theirs, theirs, 4).wait_recv()
    for copy in small_copies:
        copy.wait_send()


def total_all(mats, small):
    dma = pltpu.SemaphoreType.DMA
    vmem = pl.BlockSpec(memory_space=pltpu.VMEM)
    return pl.pallas_call(
        total_kernel,
        out_shape=(
            jax.ShapeDtypeStruct((6, 1024, 512), BF),
            jax.ShapeDtypeStruct((2 * SMALL_ROWS, WIDTH), F32),
        ),
        in_specs=[vmem, vmem],
        out_specs=(vmem, vmem),
        scratch_shapes=[
            pltpu.VMEM((3, 1024, 512), BF),
            pltpu.VMEM((3, 2, 128, 512), BF),
            pltpu.VMEM((3, 2, 256, 512), BF),
            pltpu.VMEM((3, 3, 64, 512), BF),
            pltpu.VMEM((3, 3, 16, 512), BF),
            pltpu.VMEM((3, 1024, 512), BF),
            pltpu.VMEM((3, 4, SMALL_ROWS, WIDTH), F32),
            pltpu.VMEM((SMALL_ROWS, WIDTH), F32),
            dma((3, 24)),
            dma((3, 24)),
            dma((5,)),
            dma((5,)),
            dma((3, 4)),
            dma((3, 4)),
        ],
        compiler_params=pltpu.CompilerParams(
            collective_id=3, has_side_effects=True, vmem_limit_bytes=40 << 20
        ),
    )(mats, small)


def dot_tn(left, right):
    return lax.dot_general(left, right, (((0,), (0,)), ((), ())), preferred_element_type=F32)


def dot_nt(left, right):
    return lax.dot_general(left, right, (((1,), (1,)), ((), ())), preferred_element_type=F32)


def dot_nn(left, right):
    return lax.dot_general(left, right, (((1,), (0,)), ((), ())), preferred_element_type=F32)


def expert_kernel(
    rows_ref,
    meta_ref,
    cot_ref,
    w_in_ref,
    w_out_ref,
    sib_in_ref,
    sib_out_ref,
    row_total_ref,
    score_out_ref,
    moe_ref,
    grad_ref,
    blocks,
    meta_in,
    score_send,
    cots,
    weights,
    kept_rows,
    kept_grads,
    kept_hidden,
    kept_pairs,
    row_partial,
    moe_stage,
    picks,
    slot_cots,
    slot_res,
    slot_back,
    summed,
    from_pair,
    send_sems,
    recv_sems,
    rsend_sems,
    rrecv_sems,
    meta_send,
    meta_recv,
    score_ssem,
    score_rsem,
    local_sems,
    cot_sems,
    moe_sems,
    pair_send,
    pair_recv,
    ring_send,
    ring_recv,
    plane_ready,
    line_ready,
):
    me = lax.axis_index("grp")
    core = lax.axis_index("exp")
    line = lax.axis_index("seq")
    other = 1 - core
    row, column = me // 4, lax.rem(me, 4)
    barrier = pltpu.get_barrier_semaphore()
    for step in range(1, PLANE):
        pl.semaphore_signal(
            barrier, inc=1, device_id={"grp": lax.rem(me + step, PLANE)}, device_id_type=MESH
        )
    pl.semaphore_signal(barrier, inc=1, device_id={"exp": other}, device_id_type=MESH)
    for step in (1, -1):
        pl.semaphore_signal(
            barrier, inc=1, device_id={"seq": mod4(line + step)}, device_id_type=MESH
        )

    def weight_in(expert):
        return weights.at[pl.ds(expert * WIDTH, WIDTH)]

    def weight_out(expert):
        return weights.at[pl.ds(2 * WIDTH + expert * INNER, INNER)]

    loads = [
        pltpu.make_async_copy(source, target, local_sems.at[slot])
        for slot, (source, target) in enumerate(
            (
                (w_in_ref, weight_in(core)),
                (w_out_ref, weight_out(core)),
                (sib_in_ref, weight_in(other)),
                (sib_out_ref, weight_out(other)),
            )
        )
    ]
    for load in loads:
        load.start()
    blocks[pl.ds(pl.multiple_of(me * BLOCK, BLOCK), BLOCK), :] = rows_ref[...]
    meta_in[me] = meta_ref[me]

    def place_of(power, j):
        step = power * 4**j
        return (
            mod4(row + lax.rem(ROW_STEPS // step, 4)) * 4
            + mod4(column + lax.rem(COLUMN_STEPS // step, 4))
        )

    def cot_copy(index, parity, j):
        return pltpu.make_async_copy(cot_ref.at[index], cots.at[parity, j], cot_sems.at[parity, j])

    def moe_copy(j, index):
        return pltpu.make_async_copy(moe_stage.at[j], moe_ref.at[index], moe_sems.at[j])

    cot_copy(me, 1, 0).start()
    for j in range(GROUP):
        cot_copy(place_of(1, j), 0, j).start()
    pl.semaphore_wait(barrier, PLANE + 2)

    gathers = [PlaneGather(part, blocks, send_sems, recv_sems) for part in (0, 1)]
    for gather in gathers:
        gather.begin()
    for gather in gathers:
        gather.spread(0)
    meta_copies = []
    for step in range(1, PLANE):
        to = lax.rem(me + step, PLANE)
        copy = plane_copy(
            meta_ref.at[to], meta_in.at[me], meta_send.at[step], meta_recv.at[step], to
        )
        copy.start()
        meta_copies.append(copy)

    def process(indices, parity, base, first_wait):
        count = len(indices)
        slots = count * CAPACITY
        gates = ([], [])
        for j, index in enumerate(indices):
            slot_id = lax.broadcasted_iota(jnp.int32, (CAPACITY, BLOCK), 0).astype(F32)
            hits = [slot_id == meta_in[index, expert : expert + 1, :] for expert in range(2)]
            for expert in range(2):
                gate_row = meta_in[index, 2 + expert : 3 + expert, :]
                gates[expert].append(
                    jnp.sum(jnp.where(hits[expert], gate_row, 0.0), axis=1, keepdims=True)
                )
            pick = jnp.concatenate(
                [jnp.where(hit, 1.0, 0.0).astype(BF) for hit in hits], axis=0
            )
            picks[j] = pick
            rows = dot_nn(pick, blocks[pl.ds(pl.multiple_of(index * BLOCK, BLOCK), BLOCK), :])
            cot_rows = dot_nn(pick, cots[parity, j])
            for expert in range(2):
                here = pl.ds(pl.multiple_of(base + j * CAPACITY, 16), CAPACITY)
                part = slice(expert * CAPACITY, expert * CAPACITY + CAPACITY)
                kept_rows[expert, here, :] = rows[part].astype(BF)
                slot_cots[expert, pl.ds(j * CAPACITY, CAPACITY), :] = cot_rows[part].astype(BF)
                kept_grads[expert, here, :] = (
                    gates[expert][j] * (RESIDUAL_MULT * cot_rows[part])
                ).astype(BF)
        here = pl.ds(pl.multiple_of(base, 16), slots)
        local = pl.ds(0, slots)
        for expert in range(2):
            gate = jnp.concatenate(gates[expert], axis=0) if count > 1 else gates[expert][0]
            gate_up = dot_nn(kept_rows[expert, here, :], weight_in(expert)[...])
            gate_half, up_half = gate_up[:, :INNER], gate_up[:, INNER:]
            sigmoid = jax.nn.sigmoid(gate_half)
            activated = gate_half * sigmoid
            hidden = (activated * up_half).astype(BF)
            kept_hidden[expert, here, :] = hidden
            result = dot_nn(hidden, weight_out(expert)[...]).astype(BF).astype(F32)
            scored = RESIDUAL_MULT * jnp.sum(
                slot_cots[expert, local, :].astype(F32) * result, axis=1, keepdims=True
            )
            slot_res[expert, local, :] = (gate * result).astype(BF)
            hidden_grad = dot_nt(kept_grads[expert, here, :], weight_out(expert)[...])
            gate_part = hidden_grad * up_half * sigmoid * (1.0 + gate_half * (1.0 - sigmoid))
            up_part = hidden_grad * activated
            pair_grad = jnp.concatenate([gate_part.astype(BF), up_part.astype(BF)], axis=1)
            kept_pairs[expert, here, :] = pair_grad
            slot_back[expert, local, :] = dot_nt(pair_grad, weight_in(expert)[...]).astype(BF)
            for j, index in enumerate(indices):
                pick = picks[j, pl.ds(expert * CAPACITY, CAPACITY), :].astype(F32)
                score_send[index, expert : expert + 1, :] = jnp.sum(
                    pick * scored[j * CAPACITY : (j + 1) * CAPACITY], axis=0, keepdims=True
                )
        for j, index in enumerate(indices):
            local = pl.ds(j * CAPACITY, CAPACITY)
            pick = picks[j]
            first_wait(j, index)
            values = jnp.concatenate([slot_res[0, local, :], slot_res[1, local, :]], axis=0)
            moe_stage[j] = dot_tn(pick, values).astype(BF)
            moe_copy(j, index).start()
            values = jnp.concatenate([slot_back[0, local, :], slot_back[1, local, :]], axis=0)
            row_partial[index] = dot_tn(pick, values).astype(BF)

    for load in loads:
        load.wait()
    cot_copy(me, 1, 0).wait()
    process([me], 1, 0, lambda j, index: None)
    for gather in gathers:
        gather.forward_first()
        gather.spread(-1)
        gather.spread(1)
    for gather in gathers:
        gather.forward_second(0)
    for copy in meta_copies:
        copy.wait()

    def one_group(group, power):
        parity = lax.rem(group, 2)

        @pl.when(group == 1)
        def _():
            for gather in gathers:
                gather.wait_far_first()
                gather.spread(2)
            for gather in gathers:
                gather.wait_far_second(0)

        @pl.when(group == 2)
        def _():
            for gather in gathers:
                gather.forward_second(1)
                gather.forward_second(-1)

        @pl.when(group == 3)
        def _():
            for gather in gathers:
                gather.forward_second(2)
            for gather in gathers:
                gather.wait_far_second(1)
                gather.wait_far_second(-1)

        @pl.when(group == 4)
        def _():
            for gather in gathers:
                gather.wait_far_second(2)

        indices = [place_of(power, j) for j in range(GROUP)]

        @pl.when(group < 4)
        def _():
            for j in range(GROUP):
                cot_copy(place_of(power * 4**GROUP, j), 1 - parity, j).start()

        for j in range(GROUP):
            cot_copy(indices[j], parity, j).wait()

        def first_wait(j, index):
            if j == 0:
                moe_copy(j, index).wait()
            else:

                @pl.when(group > 0)
                def _():
                    moe_copy(j, index).wait()

        process(indices, parity, CAPACITY + group * (GROUP * CAPACITY), first_wait)
        return lax.select(group < 4, power * 4**GROUP, power)

    lax.fori_loop(0, 5, one_group, jnp.int32(1))

    for gather in gathers:
        gather.finish()
    for index in (
        mod4(row + 1) * 4 + column,
        mod4(row - 1) * 4 + column,
        row * 4 + mod4(column + 1),
        row * 4 + mod4(column - 1),
    ):
        pl.semaphore_signal(plane_ready, inc=1, device_id={"grp": index}, device_id_type=MESH)
    for step in (1, -1):
        pl.semaphore_signal(
            line_ready, inc=1, device_id={"seq": mod4(line + step)}, device_id_type=MESH
        )
    buffers = (
        FlatRows(blocks, 0, (2, 4, 2), QUARTER),
        FlatRows(blocks, 1024, (2, 4, 2), HALF),
        summed,
        FlatRows(blocks, 3072, (2, 2), QUARTER),
        FlatRows(blocks, 3328, (2, 2), HALF),
    )
    reducers = [
        PlaneReduce(part, row_partial, buffers, rsend_sems, rrecv_sems, row_total_ref)
        for part in (0, 1)
    ]
    pl.semaphore_wait(plane_ready, 4)
    for da in (2, 1, -1, 0):
        for reducer in reducers:
            reducer.step_far(da)
    score_out_ref[me] = score_send[me]
    score_copies = []
    for step in range(1, PLANE):
        to = lax.rem(me + step, PLANE)
        copy = plane_copy(
            score_send.at[to], score_out_ref.at[me], score_ssem.at[step], score_rsem.at[step], to
        )
        copy.start()
        score_copies.append(copy)

    def grad_tile(expert, tile):
        columns = pl.ds((tile % 4) * BLOCK, BLOCK)
        if tile < 4:
            return dot_tn(kept_rows[expert, :, columns], kept_pairs[expert])
        return dot_tn(kept_hidden[expert, :, columns], kept_grads[expert])

    def pair_copy(tile):
        return pltpu.make_async_remote_copy(
            src_ref=cots.at[tile // GROUP, tile % GROUP],
            dst_ref=from_pair.at[tile],
            send_sem=pair_send.at[tile],
            recv_sem=pair_recv.at[tile],
            device_id={"exp": other},
            device_id_type=MESH,
        )

    for tile in range(6):
        cots[tile // GROUP, tile % GROUP] = grad_tile(other, tile).astype(BF)
        pair_copy(tile).start()
        if tile == 3:
            for reducer in reducers:
                reducer.step_near(2)
    for reducer in reducers:
        reducer.step_near(1)
    for tile in range(6):
        value = grad_tile(core, tile)
        pair_copy(tile).wait()
        weights[pl.ds(tile * BLOCK, BLOCK), :] = (value + from_pair[tile].astype(F32)).astype(BF)
        if tile == 2:
            for reducer in reducers:
                reducer.step_near(-1)
    pl.semaphore_wait(line_ready, 2)
    ring = RowRing(
        weights.at[pl.ds(0, WIDTH + INNER)],
        FlatRows(weights, 1536, (2,), 192),
        FlatRows(weights, 1920, (2,), 384),
        ring_send,
        ring_recv,
    )
    ring.step_far()
    for reducer in reducers:
        reducer.step_near(0)
    for reducer in reducers:
        reducer.step_sum(2)
    ring.step_near()
    for da in (1, -1):
        for reducer in reducers:
            reducer.step_sum(da)
    ring.step_sum()
    store = pltpu.make_async_copy(ring.piece(ring.summed, 0), grad_ref, local_sems.at[0])
    store.start()
    for reducer in reducers:
        reducer.step_sum(0)
    for reducer in reducers:
        reducer.finish()
    for copy in score_copies:
        copy.wait()
    for j in range(GROUP):
        moe_copy(j, j).wait()
    ring.finish()
    store.wait()


def step_table(steps):
    return sum(step * 4**i for i, step in enumerate(steps))


ROW_STEPS = step_table((1, 3, 0, 0, 2, 0, 1, 1, 3, 3, 2, 2, 1, 3, 2))
COLUMN_STEPS = step_table((0, 0, 1, 3, 0, 2, 1, 3, 1, 3, 1, 3, 2, 2, 2))


def run_experts(rows, meta, cots, expert_in, expert_out, sib_in, sib_out):
    vmem = pl.BlockSpec(memory_space=pltpu.VMEM)
    hbm = pl.BlockSpec(memory_space=pl.ANY)
    dma = pltpu.SemaphoreType.DMA
    slots = GROUP * CAPACITY
    every = PLANE * CAPACITY
    return pl.pallas_call(
        expert_kernel,
        out_shape=(
            jax.ShapeDtypeStruct((BLOCK, WIDTH), F32),
            jax.ShapeDtypeStruct((PLANE, 8, BLOCK), F32),
            jax.ShapeDtypeStruct((PLANE, BLOCK, WIDTH), BF),
            jax.ShapeDtypeStruct(((WIDTH + INNER) // 4, WIDTH), BF),
        ),
        in_specs=[vmem, vmem, hbm, hbm, hbm, hbm, hbm],
        out_specs=(vmem, vmem, hbm, hbm),
        scratch_shapes=[
            pltpu.VMEM((PLANE * BLOCK, WIDTH), BF),
            pltpu.VMEM((PLANE, 8, BLOCK), F32),
            pltpu.VMEM((PLANE, 8, BLOCK), F32),
            pltpu.VMEM((2, GROUP, BLOCK, WIDTH), BF),
            pltpu.VMEM((2 * (WIDTH + INNER), WIDTH), BF),
            pltpu.VMEM((2, every, WIDTH), BF),
            pltpu.VMEM((2, every, WIDTH), BF),
            pltpu.VMEM((2, every, INNER), BF),
            pltpu.VMEM((2, every, 2 * INNER), BF),
            pltpu.VMEM((PLANE, BLOCK, WIDTH), BF),
            pltpu.VMEM((GROUP, BLOCK, WIDTH), BF),
            pltpu.VMEM((GROUP, 2 * CAPACITY, BLOCK), BF),
            pltpu.VMEM((2, slots, WIDTH), BF),
            pltpu.VMEM((2, slots, WIDTH), BF),
            pltpu.VMEM((2, slots, WIDTH), BF),
            pltpu.VMEM((2, 3, HALF, WIDTH), BF),
            pltpu.VMEM((6, BLOCK, WIDTH), BF),
        ]
        + [dma((40,))] * 4
        + [dma((PLANE,))] * 4
        + [dma((4,)), dma((2, GROUP)), dma((GROUP,))]
        + [dma((6,))] * 2
        + [dma((4,))] * 2
        + [pltpu.SemaphoreType.REGULAR] * 2,
        compiler_params=pltpu.CompilerParams(
            collective_id=2, has_side_effects=True, vmem_limit_bytes=VMEM_LIMIT
        ),
    )(rows, meta, cots, expert_in, expert_out, sib_in, sib_out)


VMEM_LIMIT = 63 << 20


def rope_lanes(values, cosine, sine):
    lane = lax.broadcasted_iota(jnp.int32, (1, 128), 1)
    lower = lax.rem(lane, 64) < 32
    chunks = []
    for begin in range(0, values.shape[1], 128):
        chunk = values[:, begin : begin + 128]
        partner = jnp.where(lower, pltpu.roll(chunk, 96, 1), pltpu.roll(chunk, 32, 1))
        chunks.append(chunk * cosine + partner * sine)
    return chunks


def norm_scale(values):
    return lax.rsqrt(jnp.mean(values * values, axis=1, keepdims=True) + EPSILON)


def slot_table(routes, ranks):
    routes, ranks = routes.astype(F32).T, ranks.astype(F32).T
    expert = lax.broadcasted_iota(jnp.int32, (BLOCK, 32), 1).astype(F32)
    rank_of = jnp.zeros((BLOCK, 32), F32)
    for k in range(8):
        rank_of = rank_of + jnp.where(
            routes[:, k : k + 1] == expert, ranks[:, k : k + 1] + 1.0, 0.0
        )
    chosen = rank_of > 0.0
    row = lax.broadcasted_iota(jnp.int32, (BLOCK, BLOCK), 0)
    lane = lax.broadcasted_iota(jnp.int32, (BLOCK, BLOCK), 1)
    source = lax.broadcasted_iota(jnp.int32, (32, BLOCK), 0)
    target = lax.broadcasted_iota(jnp.int32, (32, BLOCK), 1)
    repeat = jnp.where(lax.rem(target, 32) == source, 1.0, 0.0).astype(BF)
    rank_wide = dot_nn(rank_of.astype(BF), repeat)
    hit = rank_wide == (lane // 32 + 1).astype(F32)
    counts = jnp.where(hit, 1.0, 0.0)
    earlier = jnp.where(row > lane, 1.0, 0.0).astype(BF)
    before = dot_nn(earlier, counts.astype(BF))
    totals = jnp.sum(counts, axis=0, keepdims=True)
    lower = (lax.rem(row, 32) == lax.rem(lane, 32)) & (row // 32 < lane // 32)
    offsets = dot_nn(totals.astype(BF), jnp.where(lower, 1.0, 0.0).astype(BF))
    place = jnp.where(hit, before + offsets, 0.0)
    place = place[:, :128] + place[:, 128:]
    place = place + pltpu.roll(place, 64, 1)
    place = place + pltpu.roll(place, 32, 1)
    place = place[:, :32]
    return chosen, jnp.where(chosen & (place < CAPACITY), place, -1.0)


def attend_kernel(
    tokens_ref,
    seg_ref,
    routes_ref,
    ranks_ref,
    gain_one_ref,
    w_query_ref,
    w_key_ref,
    w_value_ref,
    w_output_ref,
    gain_two_ref,
    w_router_ref,
    table_ref,
    cot_ref,
    w_in_ref,
    w_out_ref,
    routed_ref,
    residual_ref,
    heads_ref,
    normed_ref,
    query_ref,
    kv_ref,
    lse_ref,
    bias_ref,
    gates_ref,
    meta_ref,
    cots_ref,
    sib_in_ref,
    sib_out_ref,
    cots,
    table,
    kv_relay,
    segs,
    top,
    acc,
    send_sems,
    recv_sems,
    kv_send,
    kv_recv,
    seg_send,
    seg_recv,
    weight_send,
    weight_recv,
    local_sems,
):
    line, plane, core = lax.axis_index("seq"), lax.axis_index("grp"), lax.axis_index("exp")
    block = 2 * line + core
    row, column = plane // 4, lax.rem(plane, 4)
    barrier = pltpu.get_barrier_semaphore()
    for index in (
        mod4(row + 1) * 4 + column,
        mod4(row - 1) * 4 + column,
        row * 4 + mod4(column + 1),
        row * 4 + mod4(column - 1),
    ):
        pl.semaphore_signal(barrier, inc=1, device_id={"grp": index}, device_id_type=MESH)
    for step in (1, 2, 3):
        pl.semaphore_signal(
            barrier, inc=1, device_id={"seq": mod4(line + step)}, device_id_type=MESH
        )
    pl.semaphore_signal(barrier, inc=1, device_id={"exp": 1 - core}, device_id_type=MESH)
    own_cot = pltpu.make_async_copy(
        cot_ref, cots.at[pl.ds(pl.multiple_of(plane * BLOCK, BLOCK), BLOCK)], local_sems.at[0]
    )
    own_cot.start()
    load_table = pltpu.make_async_copy(table_ref.at[block], table, local_sems.at[1])
    load_table.start()
    own_cot.wait()
    pl.semaphore_wait(barrier, 8)
    gathers = [PlaneGather(part, cots, send_sems, recv_sems) for part in (0, 1)]
    for gather in gathers:
        gather.begin()
    for gather in gathers:
        gather.spread(0)

    tokens = tokens_ref[...].astype(F32)
    normed = (tokens * norm_scale(tokens) * gain_one_ref[...]).astype(BF)
    normed_ref[...] = normed
    load_table.wait()
    cosine, sine = table[0], table[1]
    keys = dot_nn(normed, w_key_ref[...])
    values = dot_nn(normed, w_value_ref[...]).astype(BF)
    key_chunks = rope_lanes(keys, cosine, sine)
    for head in range(KV_HEADS):
        chunk = key_chunks[head // 2].astype(BF)
        key = chunk[:, (head % 2) * 64 : (head % 2) * 64 + 64]
        kv_ref[0, head] = jnp.concatenate([key, values[:, head * 64 : head * 64 + 64]], axis=1)
    seg_tile = jnp.broadcast_to(seg_ref[...].astype(F32), (8, BLOCK))
    segs[0] = seg_tile

    def kv_copies(source, target, device, slot):
        return [
            pltpu.make_async_remote_copy(
                src_ref=ref.at[source],
                dst_ref=ref.at[target],
                send_sem=sends.at[slot],
                recv_sem=recvs.at[target],
                device_id=device,
                device_id_type=MESH,
            )
            for ref, sends, recvs in ((kv_ref, kv_send, kv_recv), (segs, seg_send, seg_recv))
        ]

    def relay_copies(device, to_relay):
        pairs = (
            (kv_ref, kv_relay, 4, kv_send, kv_recv),
            (segs, segs.at[5], 4, seg_send, seg_recv),
        )
        copies = []
        for ref, held, slot, sends, recvs in pairs:
            source, target = (ref.at[0], held) if to_relay else (held, ref.at[slot])
            copies.append(
                pltpu.make_async_remote_copy(
                    src_ref=source,
                    dst_ref=target,
                    send_sem=sends.at[2 if to_relay else 5],
                    recv_sem=recvs.at[5 if to_relay else 4],
                    device_id=device,
                    device_id_type=MESH,
                )
            )
        return copies

    sibling = {"exp": 1 - core}
    to_near = kv_copies(0, 2, {"seq": mod4(line + 1)}, 1)
    to_relay = relay_copies({"seq": mod4(line - 1)}, True)
    from_relay = relay_copies({"seq": mod4(line - 1)}, False)
    to_sibling = kv_copies(0, 1, sibling, 0)
    forward_near = kv_copies(2, 3 - 2 * core, sibling, 3)
    forward_far = kv_copies(4, 3, sibling, 4)

    def begin(copies):
        for copy in copies:
            copy.start()

    def sent(copies):
        for copy in copies:
            copy.wait_send()

    @pl.when(line < 3)
    def _():
        begin(to_near)

    @pl.when(core == 0)
    def _():
        begin(to_sibling)

    @pl.when(line < 2)
    def _():
        begin(to_relay)

    for gather in gathers:
        gather.forward_first()
        gather.spread(-1)
        gather.spread(1)
    weight_copies = [
        pltpu.make_async_remote_copy(
            src_ref=source,
            dst_ref=target,
            send_sem=weight_send.at[slot],
            recv_sem=weight_recv.at[slot],
            device_id=sibling,
            device_id_type=MESH,
        )
        for slot, (source, target) in enumerate(((w_in_ref, sib_in_ref), (w_out_ref, sib_out_ref)))
    ]
    begin(weight_copies)

    lane = lax.broadcasted_iota(jnp.int32, (1, 128), 1)
    queries = dot_nn(normed, w_query_ref[...])
    for head, chunk in enumerate(rope_lanes(queries, cosine, sine)):
        chunk = (chunk.astype(BF).astype(F32) * ATTENTION_FACTOR)
        query_ref[head, :BLOCK, :] = jnp.where(lane < 64, chunk, 0.0).astype(BF)
        query_ref[head, BLOCK:, :] = jnp.where(lane < 64, pltpu.roll(chunk, 64, 1), 0.0).astype(BF)
    top[...] = jnp.full(top.shape, MASKED, F32)
    acc[...] = jnp.zeros(acc.shape, F32)

    def attend(slot):
        j = lax.broadcasted_iota(jnp.int32, (BLOCK, BLOCK), 0)
        i = lax.broadcasted_iota(jnp.int32, (BLOCK, BLOCK), 1)
        distance = slot * BLOCK + i - j
        same = segs[slot].T[:, :1] == seg_tile[:1, :]
        allowed = same & (distance >= 0) & (distance < WINDOW)
        bias_ref[slot] = jnp.where(allowed, 0.0, MASKED)

        @pl.loop(0, KV_HEADS, unroll=4)
        def _(head):
            pair = kv_ref[slot, head]
            one = bias_ref[slot]
            score = dot_nt(pair, query_ref[head]) + jnp.concatenate([one, one], axis=1)
            old = top[pl.ds(head, 1), :]
            new = jnp.maximum(old, jnp.max(score, axis=0, keepdims=True))
            weight = jnp.exp(score - new).astype(BF)
            fade = jnp.exp(old - new)
            summing = jnp.where(lane < 64, 1.0, pair.astype(F32)).astype(BF)
            acc[head] = acc[head] * fade + dot_tn(summing, weight)
            top[pl.ds(head, 1), :] = new

    def wait_block(slot):
        for ref, sends, recvs in ((kv_ref, kv_send, kv_recv), (segs, seg_send, seg_recv)):
            pltpu.make_async_remote_copy(
                src_ref=ref.at[slot],
                dst_ref=ref.at[slot],
                send_sem=sends.at[0],
                recv_sem=recvs.at[slot],
                device_id=sibling,
                device_id_type=MESH,
            ).wait_recv()

    attend(0)
    for gather in gathers:
        gather.forward_second(0)
    for gather in gathers:
        gather.wait_far_first()
        gather.spread(2)

    @pl.when((line == 0) | (line == 3))
    def _():
        for arrival, copy in zip(to_relay, from_relay):
            arrival.wait_recv()
            copy.start()

    chosen, kept = slot_table(routes_ref[...], ranks_ref[...])
    kept_rows = jnp.concatenate([kept, jnp.zeros((BLOCK, 96), F32)], axis=1).T
    for index in range(PLANE):
        meta_ref[index, 0:2, :] = kept_rows[2 * index : 2 * index + 2]
        meta_ref[index, 4:8, :] = jnp.zeros((4, BLOCK), F32)

    first = 2 - core

    @pl.when(block >= first)
    def _():
        wait_block(first)

        @pl.when(core == 0)
        def _():
            begin(forward_near)

        attend(first)

    for da in (-1, 1):
        for gather in gathers:
            gather.forward_second(da)
    second = 1 + core

    @pl.when(block >= second)
    def _():
        wait_block(second)

        @pl.when(core == 1)
        def _():
            begin(forward_near)

        attend(second)

    for gather in gathers:
        gather.forward_second(2)
    third = 4 - core

    @pl.when(block >= third)
    def _():
        wait_block(third)
        attend(third)

    fourth = 3 + core

    @pl.when(block >= fourth)
    def _():
        wait_block(fourth)

        @pl.when(core == 1)
        def _():
            begin(forward_far)

        attend(fourth)

    for head in range(KV_HEADS):
        both = acc[head]
        expsum = both[:1, :]
        pair = (both * (1.0 / expsum)).T
        heads_ref[:, head * 128 : head * 128 + 128] = jnp.where(
            lane < 64, pltpu.roll(pair[:BLOCK], 64, 1), pair[BLOCK:]
        ).astype(BF)
        lse_ref[head : head + 1, :] = top[head : head + 1, :] + jnp.log(expsum)
    branch = dot_nn(heads_ref[...], w_output_ref[...])
    residual = tokens_ref[...].astype(F32) + RESIDUAL_MULT * branch
    residual_ref[...] = residual
    routed = (residual * norm_scale(residual) * gain_two_ref[...]).astype(BF)
    routed_ref[...] = routed
    logits = dot_nt(routed, w_router_ref[...])
    logits = jnp.where(chosen, logits, MASKED)
    powers = jnp.exp(logits - jnp.max(logits, axis=1, keepdims=True))
    gates = jnp.where(chosen, powers / jnp.sum(powers, axis=1, keepdims=True), 0.0)
    gates_ref[...] = gates
    gate_rows = jnp.concatenate([gates, jnp.zeros((BLOCK, 96), F32)], axis=1).T
    for index in range(PLANE):
        meta_ref[index, 2:4, :] = gate_rows[2 * index : 2 * index + 2]

    for da in (0, -1, 1, 2):
        for gather in gathers:
            gather.wait_far_second(da)
    store_cots = pltpu.make_async_copy(cots, cots_ref, local_sems.at[0])
    store_cots.start()
    for gather in gathers:
        gather.finish()
    for copy in weight_copies:
        copy.wait()

    @pl.when(line < 3)
    def _():
        sent(to_near)

    @pl.when(core == 0)
    def _():
        sent(to_sibling)

    @pl.when(line < 2)
    def _():
        sent(to_relay)

    @pl.when((line == 0) | (line == 3))
    def _():
        sent(from_relay)

    @pl.when(line >= 1)
    def _():
        sent(forward_near)

    store_cots.wait()

    @pl.when((line >= 2) & (core == 1))
    def _():
        sent(forward_far)


def run_attention(
    tokens, seg_tile, routes, ranks, gain_one, w_query, w_key, w_value, w_output, gain_two,
    w_router, table, cot, expert_in, expert_out,
):
    vmem = pl.BlockSpec(memory_space=pltpu.VMEM)
    hbm = pl.BlockSpec(memory_space=pl.ANY)
    dma = pltpu.SemaphoreType.DMA
    shape = jax.ShapeDtypeStruct
    return pl.pallas_call(
        attend_kernel,
        out_shape=(
            shape((BLOCK, WIDTH), BF),
            shape((BLOCK, WIDTH), F32),
            shape((BLOCK, WIDTH), BF),
            shape((BLOCK, WIDTH), BF),
            shape((KV_HEADS, 2 * BLOCK, 128), BF),
            shape((5, KV_HEADS, BLOCK, 128), BF),
            shape((KV_HEADS, 2 * BLOCK), F32),
            shape((5, BLOCK, BLOCK), F32),
            shape((BLOCK, 32), F32),
            shape((PLANE, 8, BLOCK), F32),
            shape((PLANE * BLOCK, WIDTH), BF),
            shape((WIDTH, 2 * INNER), BF),
            shape((INNER, WIDTH), BF),
        ),
        in_specs=[vmem] * 11 + [hbm] * 4,
        out_specs=(vmem,) * 10 + (hbm,) * 3,
        scratch_shapes=[
            pltpu.VMEM((PLANE * BLOCK, WIDTH), BF),
            pltpu.VMEM((2, BLOCK, 128), F32),
            pltpu.VMEM((KV_HEADS, BLOCK, 128), BF),
            pltpu.VMEM((6, 8, BLOCK), F32),
            pltpu.VMEM((KV_HEADS, 2 * BLOCK), F32),
            pltpu.VMEM((KV_HEADS, 128, 2 * BLOCK), F32),
            dma((40,)),
            dma((40,)),
            dma((6,)),
            dma((6,)),
            dma((6,)),
            dma((6,)),
            dma((2,)),
            dma((2,)),
            dma((2,)),
        ],
        compiler_params=pltpu.CompilerParams(
            collective_id=0, has_side_effects=True, vmem_limit_bytes=58 << 20
        ),
    )(
        tokens, seg_tile, routes, ranks, gain_one, w_query, w_key, w_value, w_output, gain_two,
        w_router, table, cot, expert_in, expert_out,
    )


def backward_kernel(
    tokens_ref,
    cot_ref,
    residual_ref,
    row_total_ref,
    scores_ref,
    gates_ref,
    routed_ref,
    heads_ref,
    normed_ref,
    query_ref,
    kv_ref,
    bias_ref,
    w_query_ref,
    w_key_ref,
    w_value_ref,
    w_output_ref,
    w_router_ref,
    gain_one_ref,
    gain_two_ref,
    lse_ref,
    table_ref,
    partial_ref,
    grad_ref,
    output_ref,
    input_grad_ref,
    small_ref,
    mats_ref,
    grad_total_ref,
    table,
    partial,
    far,
    near,
    summed,
    far_two,
    near_two,
    moe_total,
    delta,
    head_grads,
    query_grads,
    own_grads,
    stage,
    from_pair,
    from_near,
    from_far,
    residual_grad,
    mats,
    send_sems,
    recv_sems,
    ring_send,
    ring_recv,
    kv_send,
    kv_recv,
    local_sems,
    mats_sems,
):
    line, plane, core = lax.axis_index("seq"), lax.axis_index("grp"), lax.axis_index("exp")
    block = 2 * line + core
    row, column = plane // 4, lax.rem(plane, 4)
    load = pltpu.make_async_copy(partial_ref, partial, local_sems.at[1])
    load_table = pltpu.make_async_copy(table_ref.at[block], table, local_sems.at[3])
    load_table.start()
    load.start()
    barrier = pltpu.get_barrier_semaphore()
    for index in (
        mod4(row + 1) * 4 + column,
        mod4(row - 1) * 4 + column,
        row * 4 + mod4(column + 1),
        row * 4 + mod4(column - 1),
    ):
        pl.semaphore_signal(barrier, inc=1, device_id={"grp": index}, device_id_type=MESH)
    for step in (1, 2, 3):
        pl.semaphore_signal(
            barrier, inc=1, device_id={"seq": mod4(line + step)}, device_id_type=MESH
        )
    pl.semaphore_signal(barrier, inc=1, device_id={"exp": 1 - core}, device_id_type=MESH)
    pl.semaphore_wait(barrier, 8)
    buffers = (far, near, summed, far_two, near_two)
    reducers = [
        PlaneReduce(part, partial, buffers, send_sems, recv_sems, moe_total) for part in (0, 1)
    ]
    spread = RowSpread(grad_ref, grad_total_ref, ring_send, ring_recv, local_sems.at[0])
    spread.begin()
    load.wait()
    for da in (2, 1, -1, 0):
        for reducer in reducers:
            reducer.step_far(da)

    lane = lax.broadcasted_iota(jnp.int32, (1, 128), 1)
    lower = lane < 64
    gate_grad = jnp.concatenate(
        [scores_ref[index, 0:2, :] for index in range(PLANE)] + [jnp.zeros((96, BLOCK), F32)], axis=0
    ).T[:, :32]
    gates = gates_ref[...]
    choice_grad = gates * (gate_grad - jnp.sum(gates * gate_grad, axis=1, keepdims=True))
    logit_grad = choice_grad.astype(BF)
    small_ref[0:32, :] = dot_tn(logit_grad, routed_ref[...])
    routed_grad = dot_nn(logit_grad, w_router_ref[...]) + row_total_ref[...]
    residual = residual_ref[...]
    scale_two = norm_scale(residual)
    small_ref[33:34, :] = jnp.sum(routed_grad * residual * scale_two, axis=0, keepdims=True)
    small_ref[34:48, :] = jnp.zeros((14, WIDTH), F32)
    weighted = routed_grad * gain_two_ref[...]
    shared = scale_two * scale_two * scale_two * jnp.mean(weighted * residual, axis=1, keepdims=True)
    grown = cot_ref[...].astype(F32) + scale_two * weighted - residual * shared
    residual_grad[...] = grown
    branch_grad = (RESIDUAL_MULT * grown).astype(BF)
    head_grad = dot_nt(branch_grad, w_output_ref[...]).astype(BF)
    for head in range(KV_HEADS):
        chunk = head_grad[:, head * 128 : head * 128 + 128].astype(F32)
        other = heads_ref[:, head * 128 : head * 128 + 128].astype(F32)
        head_grads[head, :BLOCK, :] = jnp.where(lower, 0.0, pltpu.roll(chunk, 64, 1)).astype(BF)
        head_grads[head, BLOCK:, :] = jnp.where(lower, 0.0, chunk).astype(BF)
        both = (chunk * other).T
        delta[head : head + 1, :BLOCK] = jnp.sum(both[:64], axis=0, keepdims=True)
        delta[head : head + 1, BLOCK:] = jnp.sum(both[64:], axis=0, keepdims=True)
    query_grads[...] = jnp.zeros(query_grads.shape, F32)

    def store_mats(slot, index):
        return pltpu.make_async_copy(mats.at[slot], mats_ref.at[index], mats_sems.at[slot])

    for slot in range(2):
        mats[slot] = dot_tn(heads_ref[...], branch_grad[:, slot * 512 : slot * 512 + 512]).astype(BF)
        store_mats(slot, 4 + slot).start()

    def attend_back(slot):
        @pl.loop(0, KV_HEADS, unroll=2)
        def _(head):
            pair, query, out_grad = kv_ref[slot, head], query_ref[head], head_grads[head]
            one = bias_ref[slot]
            score = dot_nt(pair, query) + jnp.concatenate([one, one], axis=1)
            prob = jnp.exp(score - lse_ref[pl.ds(head, 1), :])
            prob_grad = dot_nt(pair, out_grad)
            score_grad = (prob * (prob_grad - delta[pl.ds(head, 1), :])).astype(BF)
            query_grads[head] += dot_tn(pair, score_grad)
            pair_grad = dot_nn(score_grad, query) + dot_nn(prob.astype(BF), out_grad)
            own_grads[head] = pair_grad
            stage[slot, head] = pair_grad.astype(BF)

    sibling = {"exp": 1 - core}

    def kv_copy(source, target, device, slot):
        return pltpu.make_async_remote_copy(
            src_ref=source,
            dst_ref=target,
            send_sem=kv_send.at[slot],
            recv_sem=kv_recv.at[slot],
            device_id=device,
            device_id_type=MESH,
        )

    pair_three = kv_copy(stage.at[3], from_pair.at[core], sibling, 0)
    pair_one = kv_copy(stage.at[1], from_pair.at[2 + core], sibling, 1)
    to_near = kv_copy(stage.at[2], from_near, {"seq": mod4(line - 1)}, 2)
    to_far = kv_copy(stage.at[4], from_far, {"seq": mod4(line - 2)}, 3)

    def take_pair(three, slot):
        source = from_pair.at[(0 if three else 2) + 1 - core]
        kv_copy(source, source, sibling, 0 if three else 1).wait_recv()
        for head in range(KV_HEADS):
            stage[slot, head] = (
                stage[slot, head].astype(F32) + source[head].astype(F32)
            ).astype(BF)

    first, second, third, fourth = 3 + core, 4 - core, 1 + core, 2 - core

    @pl.when(block >= first)
    def _():
        attend_back(first)

    @pl.when((core == 0) & (line >= 2))
    def _():
        pair_three.start()

    for reducer in reducers:
        reducer.step_near(2)
        reducer.step_near(1)

    @pl.when((core == 1) & (line >= 2))
    def _():
        take_pair(True, 4)
        to_far.start()

    @pl.when(block >= second)
    def _():
        attend_back(second)

    @pl.when((core == 1) & (line >= 1))
    def _():
        pair_three.start()

    @pl.when((core == 0) & (line >= 2))
    def _():
        to_far.start()

    spread.forward()

    for reducer in reducers:
        reducer.step_near(-1)
        reducer.step_near(0)

    @pl.when(block >= third)
    def _():
        attend_back(third)

    @pl.when((core == 0) & (line >= 1))
    def _():
        pair_one.start()

    for reducer in reducers:
        reducer.step_sum(2)

    @pl.when((core == 1) & (line >= 1))
    def _():
        take_pair(False, 2)
        to_near.start()

    @pl.when(block >= fourth)
    def _():
        attend_back(fourth)

    @pl.when(core == 1)
    def _():
        pair_one.start()

    @pl.when((core == 0) & (line >= 1))
    def _():
        take_pair(True, 2)
        to_near.start()

    for reducer in reducers:
        reducer.step_sum(1)
        reducer.step_sum(-1)
    attend_back(0)

    load_table.wait()
    cosine, sine = table[0], table[1]
    normed = normed_ref[...]
    query_chunks = []
    for head in range(KV_HEADS):
        both = query_grads[head].T
        chunk = jnp.where(lower, both[:BLOCK], pltpu.roll(both[BLOCK:], 64, 1))
        query_chunks.append(chunk * ATTENTION_FACTOR)
    query_pre_grad = jnp.concatenate(
        rope_lanes(jnp.concatenate(query_chunks, axis=1), cosine, -sine), axis=1
    ).astype(BF)
    normed_grad = dot_nt(query_pre_grad, w_query_ref[...])
    for slot in range(2):
        store_mats(slot, 4 + slot).wait()
        mats[slot] = dot_tn(normed, query_pre_grad[:, slot * 512 : slot * 512 + 512]).astype(BF)
        store_mats(slot, slot).start()

    @pl.when(core == 0)
    def _():
        source = from_pair.at[3]
        kv_copy(source, source, sibling, 1).wait_recv()
        for head in range(KV_HEADS):
            own_grads[head] += source[head].astype(F32)

    @pl.when(line < 3)
    def _():
        kv_copy(from_near, from_near, sibling, 2).wait_recv()
        for head in range(KV_HEADS):
            own_grads[head] += from_near[head].astype(F32)

    @pl.when(line < 2)
    def _():
        kv_copy(from_far, from_far, sibling, 3).wait_recv()
        for head in range(KV_HEADS):
            own_grads[head] += from_far[head].astype(F32)

    key_chunks, value_chunks = [], []
    for head in range(0, KV_HEADS, 2):
        one, two = own_grads[head], own_grads[head + 1]
        key_chunks.append(jnp.where(lower, one, pltpu.roll(two, 64, 1)))
        value_chunks.append(jnp.where(lower, pltpu.roll(one, 64, 1), two))
    key_pre_grad = jnp.concatenate(
        rope_lanes(jnp.concatenate(key_chunks, axis=1), cosine, -sine), axis=1
    ).astype(BF)
    value_pre_grad = jnp.concatenate(value_chunks, axis=1).astype(BF)
    for slot, grad in enumerate((key_pre_grad, value_pre_grad)):
        store_mats(slot, slot).wait()
        mats[slot] = dot_tn(normed, grad).astype(BF)
        store_mats(slot, 2 + slot).start()
    normed_grad = (
        normed_grad
        + dot_nt(key_pre_grad, w_key_ref[...])
        + dot_nt(value_pre_grad, w_value_ref[...])
    )
    tokens = tokens_ref[...].astype(F32)
    scale_one = norm_scale(tokens)
    small_ref[32:33, :] = jnp.sum(normed_grad * tokens * scale_one, axis=0, keepdims=True)
    weighted = normed_grad * gain_one_ref[...]
    shared = scale_one * scale_one * scale_one * jnp.mean(weighted * tokens, axis=1, keepdims=True)
    input_grad_ref[...] = (residual_grad[...] + scale_one * weighted - tokens * shared).astype(BF)

    for reducer in reducers:
        reducer.step_sum(0)
    output_ref[...] = (residual_ref[...] + RESIDUAL_MULT * moe_total[...]).astype(BF)
    for reducer in reducers:
        reducer.finish()
    spread.finish()
    for slot in range(2):
        store_mats(slot, 2 + slot).wait()

    @pl.when(line >= 1 + (1 - core))
    def _():
        pair_three.wait_send()

    @pl.when((line >= 1) | (core == 1))
    def _():
        pair_one.wait_send()

    @pl.when(line >= 1)
    def _():
        to_near.wait_send()

    @pl.when(line >= 2)
    def _():
        to_far.wait_send()


def run_backward(*args):
    dma = pltpu.SemaphoreType.DMA
    rows = WIDTH + INNER
    vmem = pl.BlockSpec(memory_space=pltpu.VMEM)
    hbm = pl.BlockSpec(memory_space=pl.ANY)
    heads = (KV_HEADS, BLOCK, 128)
    shape = jax.ShapeDtypeStruct
    return pl.pallas_call(
        backward_kernel,
        out_shape=(
            shape((BLOCK, WIDTH), BF),
            shape((BLOCK, WIDTH), BF),
            shape((2 * SMALL_ROWS, WIDTH), F32),
            shape((6, WIDTH, 512), BF),
            shape((rows, WIDTH), BF),
        ),
        in_specs=[vmem] * 20 + [hbm] * 2 + [vmem],
        out_specs=(vmem, vmem, vmem, hbm, vmem),
        scratch_shapes=[pltpu.VMEM((2, BLOCK, 128), F32), pltpu.VMEM((PLANE, BLOCK, WIDTH), BF)]
        + reduce_buffers()
        + [
            pltpu.VMEM((BLOCK, WIDTH), F32),
            pltpu.VMEM((KV_HEADS, 2 * BLOCK), F32),
            pltpu.VMEM((KV_HEADS, 2 * BLOCK, 128), BF),
            pltpu.VMEM((KV_HEADS, 128, 2 * BLOCK), F32),
            pltpu.VMEM(heads, F32),
            pltpu.VMEM((5,) + heads, BF),
            pltpu.VMEM((4,) + heads, BF),
            pltpu.VMEM(heads, BF),
            pltpu.VMEM(heads, BF),
            pltpu.VMEM((BLOCK, WIDTH), F32),
            pltpu.VMEM((2, WIDTH, 512), BF),
            dma((40,)),
            dma((40,)),
            dma((4,)),
            dma((4,)),
            dma((4,)),
            dma((4,)),
            dma((4,)),
            dma((2,)),
        ],
        compiler_params=pltpu.CompilerParams(
            collective_id=1, has_side_effects=True, vmem_limit_bytes=VMEM_LIMIT
        ),
    )(*args)


def on_device(
    tokens,
    segments,
    routes,
    rank_order,
    attn_gain,
    w_query,
    w_key,
    w_value,
    w_output,
    ffn_gain,
    w_router,
    expert_in,
    expert_out,
    cotangent,
):
    tok_rows = tokens.shape[1]
    model_width = tokens.shape[2]
    table = jnp.asarray(rope_lane_table(8 * tok_rows)).reshape(8, 2, tok_rows, 128)
    router = w_router.T
    (
        routed_in, residual, heads_out, normed, query_heads, kv_heads_all, lse, bias, gates, meta,
        cots, sib_in, sib_out,
    ) = run_attention(
        tokens[0], segments, routes[0].T, rank_order[0].T, attn_gain[None], w_query, w_key, w_value,
        w_output, ffn_gain[None], router, table, cotangent[0], expert_in[0], expert_out[0],
    )
    expert_row_sum, scores, moe_partial, expert_grads = run_experts(
        routed_in, meta, cots.reshape(PLANE, BLOCK, WIDTH), expert_in[0], expert_out[0], sib_in, sib_out,
    )
    output, input_grad, small, mats, expert_total = run_backward(
        tokens[0], cotangent[0], residual, expert_row_sum, scores, gates, routed_in, heads_out,
        normed, query_heads, kv_heads_all, bias, w_query, w_key, w_value, w_output, router,
        attn_gain[None], ffn_gain[None], lse, table, moe_partial, expert_grads,
    )
    up_total = expert_total[None, :model_width].astype(jnp.float32)
    down_total = expert_total[None, model_width:].astype(jnp.float32)
    mats_total, small_total = total_all(mats, small)
    query_total = jnp.concatenate([mats_total[0], mats_total[1]], axis=1).astype(jnp.float32)
    key_total = mats_total[2].astype(jnp.float32)
    value_total = mats_total[3].astype(jnp.float32)
    out_total = jnp.concatenate([mats_total[4], mats_total[5]], axis=1).astype(jnp.float32)
    router_total = small_total[:32].T
    gain_one_total = small_total[32]
    gain_two_total = small_total[33]
    return (
        output[None],
        input_grad[None],
        gain_one_total,
        query_total,
        key_total,
        value_total,
        out_total,
        gain_two_total,
        router_total,
        up_total,
        down_total,
    )


def solution(mesh):
    placed = (
        P("grp", ("seq", "exp"), None),
        P("grp", ("seq", "exp")),
        P("grp", ("seq", "exp"), None),
        P("grp", ("seq", "exp"), None),
        P(),
        P(),
        P(),
        P(),
        P(),
        P(),
        P(),
        P(("grp", "exp"), None, None),
        P(("grp", "exp"), None, None),
        P("grp", ("seq", "exp"), None),
    )
    return jax.shard_map(
        on_device,
        mesh=mesh,
        in_specs=placed,
        out_specs=(
            P("grp", ("seq", "exp"), None),
            P("grp", ("seq", "exp"), None),
            P(),
            P(),
            P(),
            P(),
            P(),
            P(),
            P(),
            P(("grp", "exp"), None, None),
            P(("grp", "exp"), None, None),
        ),
        check_vma=False,
    )
```

```python
import math

import jax
import jax.numpy as jnp
import numpy as np
from jax import lax
from jax.experimental import pallas as pl
from jax.experimental.pallas import tpu as pltpu
from jax.sharding import PartitionSpec as P

HEADS = 16
KV_HEADS = 8
HEAD = 64
WINDOW = 1024


EPSILON = 1e-06
ATTENTION_FACTOR = 0.015625
RESIDUAL_MULT = 0.22
ROPE_BASE = 10000.0
MASKED = -1e30


def rope_lane_table(length):
    half_dim = HEAD // 2
    frequency = np.exp(
        np.arange(half_dim, dtype=np.float32) * np.float32(-2.0 * math.log(ROPE_BASE) / HEAD)
    ).astype(np.float32)
    angles = np.arange(length, dtype=np.float32)[:, None] * frequency[None, :]
    cosine, sine = np.cos(angles), np.sin(angles)
    tables = (np.tile(cosine, (1, 4)), np.tile(np.concatenate([-sine, sine], axis=1), (1, 2)))
    return np.stack([table.reshape(-1, BLOCK, 128) for table in tables], axis=1).astype(np.float32)


MESH = pl.DeviceIdType.MESH
CAPACITY = 80
BLOCK = 256
HALF = 128
QUARTER = 64
WIDTH = 1024
INNER = 512
PLANE = 16
GROUP = 3
BF = jnp.bfloat16
F32 = jnp.float32


def mod4(value):
    return lax.rem(value + 8, 4)


def plane_id(part, first, second):
    return first * 4 + second if part == 0 else second * 4 + first


def plane_coords(part):
    index = lax.axis_index("grp")
    row, column = index // 4, lax.rem(index, 4)
    return (row, column) if part == 0 else (column, row)


def plane_copy(source, target, send_sem, recv_sem, index):
    return pltpu.make_async_remote_copy(
        src_ref=source,
        dst_ref=target,
        send_sem=send_sem,
        recv_sem=recv_sem,
        device_id={"grp": index},
        device_id_type=MESH,
    )


class PlaneGather:
    order = {0: 0, -1: 1, 1: 2, 2: 3}

    def __init__(self, part, blocks, send_sems, recv_sems):
        self.part, self.blocks = part, blocks
        self.send_sems, self.recv_sems = send_sems, recv_sems
        self.first, self.second = plane_coords(part)
        self.started = []

    def ref(self, da, db, half=None):
        index = plane_id(self.part, mod4(self.first + da), mod4(self.second + db))
        begin = pl.multiple_of(index * BLOCK + self.part * HALF, HALF)
        if half is None:
            return self.blocks.at[pl.ds(begin, HALF)]
        return self.blocks.at[pl.ds(pl.multiple_of(begin + half * QUARTER, QUARTER), QUARTER)]

    def copy(self, da, db, half, axis, step, slot):
        if axis == 0:
            to = plane_id(self.part, mod4(self.first + step), self.second)
        else:
            to = plane_id(self.part, self.first, mod4(self.second + step))
        ref, sem = self.ref(da, db, half), self.part * 20 + slot
        return plane_copy(ref, ref, self.send_sems.at[sem], self.recv_sems.at[sem], to)

    def send(self, *where):
        self.copy(*where).start()
        self.started.append(where)

    def wait(self, da, db, half, slot):
        ref, sem = self.ref(da, db, half), self.part * 20 + slot
        plane_copy(
            ref, ref, self.send_sems.at[sem], self.recv_sems.at[sem],
            plane_id(self.part, self.first, self.second),
        ).wait_recv()

    def begin(self):
        self.send(0, 0, None, 0, 1, 0)
        self.send(0, 0, None, 0, -1, 1)

    def spread(self, da):
        slot = 4 + 4 * self.order[da]
        self.send(da, 0, None, 1, 1, slot)
        self.send(da, 0, None, 1, -1, slot + 1)

    def forward_first(self):
        self.wait(-1, 0, None, 0)
        self.send(-1, 0, 0, 0, 1, 2)
        self.wait(1, 0, None, 1)
        self.send(1, 0, 1, 0, -1, 3)

    def forward_second(self, da):
        slot = 4 + 4 * self.order[da]
        self.wait(da, -1, None, slot)
        self.send(da, -1, 0, 1, 1, slot + 2)
        self.wait(da, 1, None, slot + 1)
        self.send(da, 1, 1, 1, -1, slot + 3)

    def wait_far_first(self):
        self.wait(2, 0, 0, 2)
        self.wait(2, 0, 1, 3)

    def wait_far_second(self, da):
        slot = 4 + 4 * self.order[da]
        self.wait(da, 2, 0, slot + 2)
        self.wait(da, 2, 1, slot + 3)

    def finish(self):
        for where in self.started:
            self.copy(*where).wait_send()


class PlaneReduce:
    order = {2: 0, 1: 1, -1: 2, 0: 3}

    def __init__(self, part, partial, buffers, send_sems, recv_sems, total):
        self.part, self.partial, self.total = part, partial, total
        self.far, self.near, self.summed, self.far_two, self.near_two = buffers
        self.send_sems, self.recv_sems = send_sems, recv_sems
        self.first, self.second = plane_coords(part)
        self.started = []

    def ref(self, da, db, half=None):
        index = plane_id(self.part, mod4(self.first + da), mod4(self.second + db))
        begin = self.part * HALF
        if half is None:
            return self.partial.at[index, pl.ds(begin, HALF)]
        return self.partial.at[index, pl.ds(begin + half * QUARTER, QUARTER)]

    def send(self, source, target, axis, step, slot):
        if axis == 0:
            to = plane_id(self.part, mod4(self.first + step), self.second)
        else:
            to = plane_id(self.part, self.first, mod4(self.second + step))
        sem = self.part * 20 + slot
        copy = plane_copy(source, target, self.send_sems.at[sem], self.recv_sems.at[sem], to)
        copy.start()
        self.started.append(copy)

    def wait(self, target, slot):
        sem = self.part * 20 + slot
        plane_copy(
            target, target, self.send_sems.at[sem], self.recv_sems.at[sem],
            plane_id(self.part, self.first, self.second),
        ).wait_recv()

    def add(self, target, source):
        target[...] = (target[...].astype(F32) + source[...].astype(F32)).astype(BF)

    def step_far(self, da):
        part, place = self.part, self.order[da]
        self.send(self.ref(da, 2, 0), self.far.at[part, place, 0], 1, 1, 4 * place)
        self.send(self.ref(da, 2, 1), self.far.at[part, place, 1], 1, -1, 4 * place + 1)

    def step_near(self, da):
        part, place = self.part, self.order[da]
        self.wait(self.far.at[part, place, 0], 4 * place)
        self.add(self.ref(da, 1, 0), self.far.at[part, place, 0])
        self.send(self.ref(da, 1), self.near.at[part, place, 0], 1, 1, 4 * place + 2)
        self.wait(self.far.at[part, place, 1], 4 * place + 1)
        self.add(self.ref(da, -1, 1), self.far.at[part, place, 1])
        self.send(self.ref(da, -1), self.near.at[part, place, 1], 1, -1, 4 * place + 3)

    def step_sum(self, da):
        part, place = self.part, self.order[da]
        self.wait(self.near.at[part, place, 0], 4 * place + 2)
        self.wait(self.near.at[part, place, 1], 4 * place + 3)
        value = (
            self.ref(da, 0)[...].astype(F32)
            + self.near[part, place, 0].astype(F32)
            + self.near[part, place, 1].astype(F32)
        )
        rows = pl.ds(part * HALF, HALF)
        if da == 0:
            self.total[rows] = value
            self.wait(self.near_two.at[part, 0], 18)
            self.wait(self.near_two.at[part, 1], 19)
            self.total[rows] += self.near_two[part, 0].astype(F32) + self.near_two[part, 1].astype(F32)
            return
        self.summed[part, place] = value.astype(BF)
        lower, upper = pl.ds(0, QUARTER), pl.ds(QUARTER, QUARTER)
        if da == 2:
            self.send(self.summed.at[part, 0, lower], self.far_two.at[part, 0], 0, 1, 16)
            self.send(self.summed.at[part, 0, upper], self.far_two.at[part, 1], 0, -1, 17)
        if da == 1:
            self.wait(self.far_two.at[part, 0], 16)
            self.add(self.summed.at[part, 1, lower], self.far_two.at[part, 0])
            self.send(self.summed.at[part, 1], self.near_two.at[part, 0], 0, 1, 18)
        if da == -1:
            self.wait(self.far_two.at[part, 1], 17)
            self.add(self.summed.at[part, 2, upper], self.far_two.at[part, 1])
            self.send(self.summed.at[part, 2], self.near_two.at[part, 1], 0, -1, 19)

    def finish(self):
        for copy in self.started:
            copy.wait_send()


def reduce_buffers():
    return [
        pltpu.VMEM((2, 4, 2, QUARTER, WIDTH), BF),
        pltpu.VMEM((2, 4, 2, HALF, WIDTH), BF),
        pltpu.VMEM((2, 3, HALF, WIDTH), BF),
        pltpu.VMEM((2, 2, QUARTER, WIDTH), BF),
        pltpu.VMEM((2, 2, HALF, WIDTH), BF),
    ]


class FlatRows:
    def __init__(self, ref, begin, lead, rows):
        self.ref, self.begin, self.lead, self.rows = ref, begin, lead, rows

    def slice(self, index):
        flat = 0
        for extent, place in zip(self.lead, index if isinstance(index, tuple) else (index,)):
            flat = flat * extent + place
        return pl.ds(self.begin + flat * self.rows, self.rows)

    @property
    def at(self):
        return FlatView(self)

    def __getitem__(self, index):
        return self.ref[self.slice(index), :]


class FlatView:
    def __init__(self, flat):
        self.flat = flat

    def __getitem__(self, index):
        return self.flat.ref.at[self.flat.slice(index)]


class RowRing:
    def __init__(self, summed, far, near, send_sems, recv_sems):
        self.summed, self.far, self.near = summed, far, near
        self.send_sems, self.recv_sems = send_sems, recv_sems
        self.me = lax.axis_index("seq")
        self.rows = (WIDTH + INNER) // 4
        self.started = []

    def piece(self, ref, shift, half=None):
        begin = mod4(self.me + shift) * self.rows
        if half is None:
            return ref.at[pl.ds(pl.multiple_of(begin, 16), self.rows)]
        return ref.at[pl.ds(pl.multiple_of(begin + half * (self.rows // 2), 16), self.rows // 2)]

    def copy(self, source, target, step, slot):
        return pltpu.make_async_remote_copy(
            src_ref=source,
            dst_ref=target,
            send_sem=self.send_sems.at[slot],
            recv_sem=self.recv_sems.at[slot],
            device_id={"seq": mod4(self.me + step)},
            device_id_type=MESH,
        )

    def send(self, source, target, step, slot):
        copy = self.copy(source, target, step, slot)
        copy.start()
        self.started.append(copy)

    def wait(self, target, slot):
        self.copy(target, target, 1, slot).wait_recv()

    def add(self, target, source):
        target[...] = (target[...].astype(F32) + source[...].astype(F32)).astype(BF)

    def step_far(self):
        self.send(self.piece(self.summed, 2, 0), self.far.at[0], 1, 0)
        self.send(self.piece(self.summed, 2, 1), self.far.at[1], -1, 1)

    def step_near(self):
        self.wait(self.far.at[0], 0)
        self.add(self.piece(self.summed, 1, 0), self.far.at[0])
        self.send(self.piece(self.summed, 1), self.near.at[0], 1, 2)
        self.wait(self.far.at[1], 1)
        self.add(self.piece(self.summed, -1, 1), self.far.at[1])
        self.send(self.piece(self.summed, -1), self.near.at[1], -1, 3)

    def step_sum(self):
        self.wait(self.near.at[0], 2)
        self.wait(self.near.at[1], 3)
        own = self.piece(self.summed, 0)
        own[...] = (
            own[...].astype(F32) + self.near[0].astype(F32) + self.near[1].astype(F32)
        ).astype(BF)

    def finish(self):
        for copy in self.started:
            copy.wait_send()


class RowSpread(RowRing):
    def __init__(self, own, total, send_sems, recv_sems, local_sem):
        super().__init__(total, None, None, send_sems, recv_sems)
        self.own, self.local_sem = own, local_sem

    def begin(self):
        target = self.piece(self.summed, 0)
        self.send(self.own, target, 1, 0)
        self.send(self.own, target, -1, 1)
        pltpu.make_async_copy(self.own, target, self.local_sem).start()

    def forward(self):
        self.wait(self.piece(self.summed, -1), 0)
        half = self.piece(self.summed, -1, 0)
        self.send(half, half, 1, 2)
        self.wait(self.piece(self.summed, 1), 1)
        half = self.piece(self.summed, 1, 1)
        self.send(half, half, -1, 3)

    def finish(self):
        self.wait(self.piece(self.summed, 2, 0), 2)
        self.wait(self.piece(self.summed, 2, 1), 3)
        pltpu.make_async_copy(self.own, self.piece(self.summed, 0), self.local_sem).wait()
        super().finish()


class CubeSum:
    def __init__(self, part, matrix, out, column, other, buffers, send_sems, recv_sems):
        self.part, self.matrix, self.out = part, matrix, out
        self.width = matrix.shape[1]
        self.column = pl.multiple_of(column, 128)
        self.other = pl.multiple_of(other, 128)
        self.far, self.near, self.mid, self.low = buffers
        self.send_sems, self.recv_sems = send_sems, recv_sems
        line, plane = lax.axis_index("seq"), lax.axis_index("grp")
        coords = (line, plane // 4, lax.rem(plane, 4))
        self.coords = coords
        self.place = [coords[(part + level) % 3] for level in range(3)]
        self.started = []

    def device(self, level, step):
        axis = (self.part + level) % 3
        there = mod4(self.coords[axis] + step)
        if axis == 0:
            return {"seq": there}
        if axis == 1:
            return {"grp": there * 4 + self.coords[2]}
        return {"grp": self.coords[1] * 4 + there}

    def rows(self, level, shift):
        begin = 0
        for upper in range(level):
            begin = begin + self.place[upper] * (256 // 4**upper)
        return pl.multiple_of(begin + mod4(self.place[level] + shift) * (256 // 4**level), 16)

    def result(self, begin, count):
        return self.out.at[pl.ds(begin, count), pl.ds(self.column, self.width)]

    def copy(self, source, target, level, step, slot):
        return pltpu.make_async_remote_copy(
            src_ref=source,
            dst_ref=target,
            send_sem=self.send_sems.at[slot],
            recv_sem=self.recv_sems.at[slot],
            device_id=self.device(level, step),
            device_id_type=MESH,
        )

    def send(self, source, target, level, step, slot):
        copy = self.copy(source, target, level, step, slot)
        copy.start()
        self.started.append(copy)

    def wait(self, target, slot):
        self.copy(target, target, 0, 0, slot).wait_recv()

    def add(self, target, *sources):
        value = target[...].astype(F32)
        for source in sources:
            value = value + source[...].astype(F32)
        target[...] = value.astype(BF)

    def step_far(self):
        begin = self.rows(0, 2)
        self.send(self.matrix.at[pl.ds(begin, 128)], self.far.at[0], 0, 1, 0)
        self.send(self.matrix.at[pl.ds(begin + 128, 128)], self.far.at[1], 0, -1, 1)

    def step_near(self):
        begin = self.rows(0, 1)
        self.wait(self.far.at[0], 0)
        self.add(self.matrix.at[pl.ds(begin, 128)], self.far.at[0])
        self.send(self.matrix.at[pl.ds(begin, 256)], self.near.at[0], 0, 1, 2)
        begin = self.rows(0, -1)
        self.wait(self.far.at[1], 1)
        self.add(self.matrix.at[pl.ds(begin + 128, 128)], self.far.at[1])
        self.send(self.matrix.at[pl.ds(begin, 256)], self.near.at[1], 0, -1, 3)

    def step_mid(self):
        self.wait(self.near.at[0], 2)
        self.wait(self.near.at[1], 3)
        self.add(self.matrix.at[pl.ds(self.rows(0, 0), 256)], self.near.at[0], self.near.at[1])
        for step in (1, 2, 3):
            self.send(
                self.matrix.at[pl.ds(self.rows(1, step), 64)], self.mid.at[step - 1], 1, step, 3 + step
            )

    def step_low(self):
        for step in (1, 2, 3):
            self.wait(self.mid.at[step - 1], 3 + step)
        self.add(
            self.matrix.at[pl.ds(self.rows(1, 0), 64)], self.mid.at[0], self.mid.at[1], self.mid.at[2]
        )
        for step in (1, 2, 3):
            self.send(
                self.matrix.at[pl.ds(self.rows(2, step), 16)], self.low.at[step - 1], 2, step, 6 + step
            )

    def ring_far(self):
        self.wait(self.near.at[0], 2)
        self.wait(self.near.at[1], 3)
        self.add(self.matrix.at[pl.ds(self.rows(0, 0), 256)], self.near.at[0], self.near.at[1])
        begin = self.rows(1, 2)
        self.send(self.matrix.at[pl.ds(begin, 32)], self.mid.at[0, pl.ds(0, 32)], 1, 1, 4)
        self.send(self.matrix.at[pl.ds(begin + 32, 32)], self.mid.at[0, pl.ds(32, 32)], 1, -1, 5)

    def ring_near(self):
        begin = self.rows(1, 1)
        held = self.mid.at[0, pl.ds(0, 32)]
        self.wait(held, 4)
        self.add(self.matrix.at[pl.ds(begin, 32)], held)
        self.send(self.matrix.at[pl.ds(begin, 64)], self.mid.at[1], 1, 1, 6)
        begin = self.rows(1, -1)
        held = self.mid.at[0, pl.ds(32, 32)]
        self.wait(held, 5)
        self.add(self.matrix.at[pl.ds(begin + 32, 32)], held)
        self.send(self.matrix.at[pl.ds(begin, 64)], self.mid.at[2], 1, -1, 24)

    def ring_low(self):
        self.wait(self.mid.at[1], 6)
        self.wait(self.mid.at[2], 24)
        self.add(self.matrix.at[pl.ds(self.rows(1, 0), 64)], self.mid.at[1], self.mid.at[2])
        for step in (1, 2, 3):
            self.send(
                self.matrix.at[pl.ds(self.rows(2, step), 16)], self.low.at[step - 1], 2, step, 6 + step
            )

    def ring_back(self):
        for step in (1, 2, 3):
            self.wait(self.result(self.rows(2, -step), 16), 9 + step)
        ref = self.result(self.rows(1, 0), 64)
        self.send(ref, ref, 1, 1, 13)
        self.send(ref, ref, 1, -1, 14)

    def ring_forward(self):
        begin = self.rows(1, -1)
        self.wait(self.result(begin, 64), 13)
        ref = self.result(begin, 32)
        self.send(ref, ref, 1, 1, 15)
        begin = self.rows(1, 1)
        self.wait(self.result(begin, 64), 14)
        ref = self.result(begin + 32, 32)
        self.send(ref, ref, 1, -1, 25)

    def ring_last(self):
        begin = self.rows(1, 2)
        self.wait(self.result(begin, 32), 15)
        self.wait(self.result(begin + 32, 32), 25)
        self.spread_piece()

    def step_done(self):
        for step in (1, 2, 3):
            self.wait(self.low.at[step - 1], 6 + step)
        own = self.rows(2, 0)
        value = self.matrix[pl.ds(own, 16), :].astype(F32)
        for step in (1, 2, 3):
            value = value + self.low[step - 1].astype(F32)
        ref = self.result(own, 16)
        ref[...] = value.astype(BF)
        for step in (1, 2, 3):
            self.send(ref, ref, 2, step, 9 + step)

    def back_mid(self):
        for step in (1, 2, 3):
            self.wait(self.result(self.rows(2, -step), 16), 9 + step)
        ref = self.result(self.rows(1, 0), 64)
        for step in (1, 2, 3):
            self.send(ref, ref, 1, step, 12 + step)

    def back_near(self):
        for step in (1, 2, 3):
            self.wait(self.result(self.rows(1, -step), 64), 12 + step)
        self.spread_piece()

    def spread_piece(self):
        ref = self.result(self.rows(0, 0), 256)
        self.send(ref, ref, 0, 1, 16)
        self.send(ref, ref, 0, -1, 17)
        self.share(0, 20)

    def back_far(self):
        begin = self.rows(0, -1)
        self.wait(self.result(begin, 256), 16)
        ref = self.result(begin, 128)
        self.send(ref, ref, 0, 1, 18)
        self.share(-1, 21)
        begin = self.rows(0, 1)
        self.wait(self.result(begin, 256), 17)
        ref = self.result(begin + 128, 128)
        self.send(ref, ref, 0, -1, 19)
        self.share(1, 22)

    def back_last(self):
        begin = self.rows(0, 2)
        self.wait(self.result(begin, 128), 18)
        self.wait(self.result(begin + 128, 128), 19)
        self.share(2, 23)

    def share_copy(self, shift, slot):
        ref = self.result(self.rows(0, shift), 256)
        return pltpu.make_async_remote_copy(
            src_ref=ref,
            dst_ref=ref,
            send_sem=self.send_sems.at[slot],
            recv_sem=self.recv_sems.at[slot],
            device_id={"exp": 1 - lax.axis_index("exp")},
            device_id_type=MESH,
        )

    def share(self, shift, slot):
        copy = self.share_copy(shift, slot)
        copy.start()
        self.started.append(copy)

    def finish(self):
        for shift, slot in ((0, 20), (-1, 21), (1, 22), (2, 23)):
            ref = self.out.at[pl.ds(self.rows(0, shift), 256), pl.ds(self.other, self.width)]
            pltpu.make_async_remote_copy(
                src_ref=ref,
                dst_ref=ref,
                send_sem=self.send_sems.at[slot],
                recv_sem=self.recv_sems.at[slot],
                device_id={"exp": 1 - lax.axis_index("exp")},
                device_id_type=MESH,
            ).wait_recv()
        for copy in self.started:
            copy.wait_send()


SMALL_ROWS = 16


def dot_tn(left, right):
    return lax.dot_general(left, right, (((0,), (0,)), ((), ())), preferred_element_type=F32)


def dot_nt(left, right):
    return lax.dot_general(left, right, (((1,), (1,)), ((), ())), preferred_element_type=F32)


def dot_nn(left, right):
    return lax.dot_general(left, right, (((1,), (0,)), ((), ())), preferred_element_type=F32)


def expert_kernel(
    rows_ref,
    meta_ref,
    cot_ref,
    w_in_ref,
    w_out_ref,
    sib_in_ref,
    sib_out_ref,
    row_total_ref,
    score_out_ref,
    moe_ref,
    grad_ref,
    blocks,
    meta_in,
    score_send,
    cots,
    weights,
    kept_rows,
    kept_grads,
    kept_hidden,
    kept_pairs,
    row_partial,
    moe_stage,
    picks,
    slot_cots,
    slot_res,
    slot_back,
    summed,
    from_pair,
    send_sems,
    recv_sems,
    rsend_sems,
    rrecv_sems,
    meta_send,
    meta_recv,
    score_ssem,
    score_rsem,
    local_sems,
    cot_sems,
    moe_sems,
    pair_send,
    pair_recv,
    ring_send,
    ring_recv,
    plane_ready,
    line_ready,
):
    me = lax.axis_index("grp")
    core = lax.axis_index("exp")
    line = lax.axis_index("seq")
    other = 1 - core
    row, column = me // 4, lax.rem(me, 4)
    barrier = pltpu.get_barrier_semaphore()
    for step in range(1, PLANE):
        pl.semaphore_signal(
            barrier, inc=1, device_id={"grp": lax.rem(me + step, PLANE)}, device_id_type=MESH
        )
    pl.semaphore_signal(barrier, inc=1, device_id={"exp": other}, device_id_type=MESH)
    for step in (1, -1):
        pl.semaphore_signal(
            barrier, inc=1, device_id={"seq": mod4(line + step)}, device_id_type=MESH
        )

    def weight_in(expert):
        return weights.at[pl.ds(expert * WIDTH, WIDTH)]

    def weight_out(expert):
        return weights.at[pl.ds(2 * WIDTH + expert * INNER, INNER)]

    loads = [
        pltpu.make_async_copy(source, target, local_sems.at[slot])
        for slot, (source, target) in enumerate(
            (
                (w_in_ref, weight_in(core)),
                (w_out_ref, weight_out(core)),
                (sib_in_ref, weight_in(other)),
                (sib_out_ref, weight_out(other)),
            )
        )
    ]
    for load in loads:
        load.start()
    blocks[pl.ds(pl.multiple_of(me * BLOCK, BLOCK), BLOCK), :] = rows_ref[...]
    meta_in[me] = meta_ref[me]

    def place_of(power, j):
        step = power * 4**j
        return (
            mod4(row + lax.rem(ROW_STEPS // step, 4)) * 4
            + mod4(column + lax.rem(COLUMN_STEPS // step, 4))
        )

    def cot_copy(index, parity, j):
        return pltpu.make_async_copy(cot_ref.at[index], cots.at[parity, j], cot_sems.at[parity, j])

    def moe_copy(j, index):
        return pltpu.make_async_copy(moe_stage.at[j], moe_ref.at[index], moe_sems.at[j])

    cot_copy(me, 1, 0).start()
    for j in range(GROUP):
        cot_copy(place_of(1, j), 0, j).start()
    pl.semaphore_wait(barrier, PLANE + 2)

    gathers = [PlaneGather(part, blocks, send_sems, recv_sems) for part in (0, 1)]
    for gather in gathers:
        gather.begin()
    for gather in gathers:
        gather.spread(0)
    meta_copies = []
    for step in range(1, PLANE):
        to = lax.rem(me + step, PLANE)
        copy = plane_copy(
            meta_ref.at[to], meta_in.at[me], meta_send.at[step], meta_recv.at[step], to
        )
        copy.start()
        meta_copies.append(copy)

    def process(indices, parity, base, first_wait):
        count = len(indices)
        slots = count * CAPACITY
        gates = ([], [])
        for j, index in enumerate(indices):
            slot_id = lax.broadcasted_iota(jnp.int32, (CAPACITY, BLOCK), 0).astype(F32)
            hits = [slot_id == meta_in[index, expert : expert + 1, :] for expert in range(2)]
            for expert in range(2):
                gate_row = meta_in[index, 2 + expert : 3 + expert, :]
                gates[expert].append(
                    jnp.sum(jnp.where(hits[expert], gate_row, 0.0), axis=1, keepdims=True)
                )
            pick = jnp.concatenate(
                [jnp.where(hit, 1.0, 0.0).astype(BF) for hit in hits], axis=0
            )
            picks[j] = pick
            rows = dot_nn(pick, blocks[pl.ds(pl.multiple_of(index * BLOCK, BLOCK), BLOCK), :])
            cot_rows = dot_nn(pick, cots[parity, j])
            for expert in range(2):
                here = pl.ds(pl.multiple_of(base + j * CAPACITY, 16), CAPACITY)
                part = slice(expert * CAPACITY, expert * CAPACITY + CAPACITY)
                kept_rows[expert, here, :] = rows[part].astype(BF)
                slot_cots[expert, pl.ds(j * CAPACITY, CAPACITY), :] = cot_rows[part].astype(BF)
                kept_grads[expert, here, :] = (
                    gates[expert][j] * (RESIDUAL_MULT * cot_rows[part])
                ).astype(BF)
        here = pl.ds(pl.multiple_of(base, 16), slots)
        local = pl.ds(0, slots)
        for expert in range(2):
            gate = jnp.concatenate(gates[expert], axis=0) if count > 1 else gates[expert][0]
            gate_up = dot_nn(kept_rows[expert, here, :], weight_in(expert)[...])
            gate_half, up_half = gate_up[:, :INNER], gate_up[:, INNER:]
            sigmoid = jax.nn.sigmoid(gate_half)
            activated = gate_half * sigmoid
            hidden = (activated * up_half).astype(BF)
            kept_hidden[expert, here, :] = hidden
            result = dot_nn(hidden, weight_out(expert)[...]).astype(BF).astype(F32)
            scored = RESIDUAL_MULT * jnp.sum(
                slot_cots[expert, local, :].astype(F32) * result, axis=1, keepdims=True
            )
            slot_res[expert, local, :] = (gate * result).astype(BF)
            hidden_grad = dot_nt(kept_grads[expert, here, :], weight_out(expert)[...])
            gate_part = hidden_grad * up_half * sigmoid * (1.0 + gate_half * (1.0 - sigmoid))
            up_part = hidden_grad * activated
            pair_grad = jnp.concatenate([gate_part.astype(BF), up_part.astype(BF)], axis=1)
            kept_pairs[expert, here, :] = pair_grad
            slot_back[expert, local, :] = dot_nt(pair_grad, weight_in(expert)[...]).astype(BF)
            for j, index in enumerate(indices):
                pick = picks[j, pl.ds(expert * CAPACITY, CAPACITY), :].astype(F32)
                score_send[index, expert : expert + 1, :] = jnp.sum(
                    pick * scored[j * CAPACITY : (j + 1) * CAPACITY], axis=0, keepdims=True
                )
        for j, index in enumerate(indices):
            local = pl.ds(j * CAPACITY, CAPACITY)
            pick = picks[j]
            first_wait(j, index)
            values = jnp.concatenate([slot_res[0, local, :], slot_res[1, local, :]], axis=0)
            moe_stage[j] = dot_tn(pick, values).astype(BF)
            moe_copy(j, index).start()
            values = jnp.concatenate([slot_back[0, local, :], slot_back[1, local, :]], axis=0)
            row_partial[index] = dot_tn(pick, values).astype(BF)

    for load in loads:
        load.wait()
    cot_copy(me, 1, 0).wait()
    process([me], 1, 0, lambda j, index: None)
    for gather in gathers:
        gather.forward_first()
        gather.spread(-1)
        gather.spread(1)
    for gather in gathers:
        gather.forward_second(0)
    for copy in meta_copies:
        copy.wait()

    def one_group(group, power):
        parity = lax.rem(group, 2)

        @pl.when(group == 1)
        def _():
            for gather in gathers:
                gather.wait_far_first()
                gather.spread(2)
            for gather in gathers:
                gather.wait_far_second(0)

        @pl.when(group == 2)
        def _():
            for gather in gathers:
                gather.forward_second(1)
                gather.forward_second(-1)

        @pl.when(group == 3)
        def _():
            for gather in gathers:
                gather.forward_second(2)
            for gather in gathers:
                gather.wait_far_second(1)
                gather.wait_far_second(-1)

        @pl.when(group == 4)
        def _():
            for gather in gathers:
                gather.wait_far_second(2)

        indices = [place_of(power, j) for j in range(GROUP)]

        @pl.when(group < 4)
        def _():
            for j in range(GROUP):
                cot_copy(place_of(power * 4**GROUP, j), 1 - parity, j).start()

        for j in range(GROUP):
            cot_copy(indices[j], parity, j).wait()

        def first_wait(j, index):
            if j == 0:
                moe_copy(j, index).wait()
            else:

                @pl.when(group > 0)
                def _():
                    moe_copy(j, index).wait()

        process(indices, parity, CAPACITY + group * (GROUP * CAPACITY), first_wait)
        return lax.select(group < 4, power * 4**GROUP, power)

    lax.fori_loop(0, 5, one_group, jnp.int32(1))

    for gather in gathers:
        gather.finish()
    for index in (
        mod4(row + 1) * 4 + column,
        mod4(row - 1) * 4 + column,
        row * 4 + mod4(column + 1),
        row * 4 + mod4(column - 1),
    ):
        pl.semaphore_signal(plane_ready, inc=1, device_id={"grp": index}, device_id_type=MESH)
    for step in (1, -1):
        pl.semaphore_signal(
            line_ready, inc=1, device_id={"seq": mod4(line + step)}, device_id_type=MESH
        )
    buffers = (
        FlatRows(blocks, 0, (2, 4, 2), QUARTER),
        FlatRows(blocks, 1024, (2, 4, 2), HALF),
        summed,
        FlatRows(blocks, 3072, (2, 2), QUARTER),
        FlatRows(blocks, 3328, (2, 2), HALF),
    )
    reducers = [
        PlaneReduce(part, row_partial, buffers, rsend_sems, rrecv_sems, row_total_ref)
        for part in (0, 1)
    ]
    pl.semaphore_wait(plane_ready, 4)
    for da in (2, 1, -1, 0):
        for reducer in reducers:
            reducer.step_far(da)
    score_out_ref[me] = score_send[me]
    score_copies = []
    for step in range(1, PLANE):
        to = lax.rem(me + step, PLANE)
        copy = plane_copy(
            score_send.at[to], score_out_ref.at[me], score_ssem.at[step], score_rsem.at[step], to
        )
        copy.start()
        score_copies.append(copy)

    def grad_tile(expert, tile):
        columns = pl.ds((tile % 4) * BLOCK, BLOCK)
        if tile < 4:
            return dot_tn(kept_rows[expert, :, columns], kept_pairs[expert])
        return dot_tn(kept_hidden[expert, :, columns], kept_grads[expert])

    def pair_copy(tile):
        return pltpu.make_async_remote_copy(
            src_ref=cots.at[tile // GROUP, tile % GROUP],
            dst_ref=from_pair.at[tile],
            send_sem=pair_send.at[tile],
            recv_sem=pair_recv.at[tile],
            device_id={"exp": other},
            device_id_type=MESH,
        )

    for tile in range(6):
        cots[tile // GROUP, tile % GROUP] = grad_tile(other, tile).astype(BF)
        pair_copy(tile).start()
        if tile == 3:
            for reducer in reducers:
                reducer.step_near(2)
    for reducer in reducers:
        reducer.step_near(1)
    for tile in range(6):
        value = grad_tile(core, tile)
        pair_copy(tile).wait()
        weights[pl.ds(tile * BLOCK, BLOCK), :] = (value + from_pair[tile].astype(F32)).astype(BF)
        if tile == 2:
            for reducer in reducers:
                reducer.step_near(-1)
    pl.semaphore_wait(line_ready, 2)
    ring = RowRing(
        weights.at[pl.ds(0, WIDTH + INNER)],
        FlatRows(weights, 1536, (2,), 192),
        FlatRows(weights, 1920, (2,), 384),
        ring_send,
        ring_recv,
    )
    ring.step_far()
    for reducer in reducers:
        reducer.step_near(0)
    for reducer in reducers:
        reducer.step_sum(2)
    ring.step_near()
    for da in (1, -1):
        for reducer in reducers:
            reducer.step_sum(da)
    ring.step_sum()
    store = pltpu.make_async_copy(ring.piece(ring.summed, 0), grad_ref, local_sems.at[0])
    store.start()
    for reducer in reducers:
        reducer.step_sum(0)
    for reducer in reducers:
        reducer.finish()
    for copy in score_copies:
        copy.wait()
    for j in range(GROUP):
        moe_copy(j, j).wait()
    ring.finish()
    store.wait()


def step_table(steps):
    return sum(step * 4**i for i, step in enumerate(steps))


ROW_STEPS = step_table((1, 3, 0, 0, 2, 0, 1, 1, 3, 3, 2, 2, 1, 3, 2))
COLUMN_STEPS = step_table((0, 0, 1, 3, 0, 2, 1, 3, 1, 3, 1, 3, 2, 2, 2))


def run_experts(rows, meta, cots, expert_in, expert_out, sib_in, sib_out):
    vmem = pl.BlockSpec(memory_space=pltpu.VMEM)
    hbm = pl.BlockSpec(memory_space=pl.ANY)
    dma = pltpu.SemaphoreType.DMA
    slots = GROUP * CAPACITY
    every = PLANE * CAPACITY
    return pl.pallas_call(
        expert_kernel,
        out_shape=(
            jax.ShapeDtypeStruct((BLOCK, WIDTH), F32),
            jax.ShapeDtypeStruct((PLANE, 8, BLOCK), F32),
            jax.ShapeDtypeStruct((PLANE, BLOCK, WIDTH), BF),
            jax.ShapeDtypeStruct(((WIDTH + INNER) // 4, WIDTH), BF),
        ),
        in_specs=[vmem, vmem, hbm, hbm, hbm, hbm, hbm],
        out_specs=(vmem, vmem, hbm, hbm),
        scratch_shapes=[
            pltpu.VMEM((PLANE * BLOCK, WIDTH), BF),
            pltpu.VMEM((PLANE, 8, BLOCK), F32),
            pltpu.VMEM((PLANE, 8, BLOCK), F32),
            pltpu.VMEM((2, GROUP, BLOCK, WIDTH), BF),
            pltpu.VMEM((2 * (WIDTH + INNER), WIDTH), BF),
            pltpu.VMEM((2, every, WIDTH), BF),
            pltpu.VMEM((2, every, WIDTH), BF),
            pltpu.VMEM((2, every, INNER), BF),
            pltpu.VMEM((2, every, 2 * INNER), BF),
            pltpu.VMEM((PLANE, BLOCK, WIDTH), BF),
            pltpu.VMEM((GROUP, BLOCK, WIDTH), BF),
            pltpu.VMEM((GROUP, 2 * CAPACITY, BLOCK), BF),
            pltpu.VMEM((2, slots, WIDTH), BF),
            pltpu.VMEM((2, slots, WIDTH), BF),
            pltpu.VMEM((2, slots, WIDTH), BF),
            pltpu.VMEM((2, 3, HALF, WIDTH), BF),
            pltpu.VMEM((6, BLOCK, WIDTH), BF),
        ]
        + [dma((40,))] * 4
        + [dma((PLANE,))] * 4
        + [dma((4,)), dma((2, GROUP)), dma((GROUP,))]
        + [dma((6,))] * 2
        + [dma((4,))] * 2
        + [pltpu.SemaphoreType.REGULAR] * 2,
        compiler_params=pltpu.CompilerParams(
            collective_id=2, has_side_effects=True, vmem_limit_bytes=VMEM_LIMIT
        ),
    )(rows, meta, cots, expert_in, expert_out, sib_in, sib_out)


VMEM_LIMIT = 63 << 20


def rope_lanes(values, cosine, sine):
    lane = lax.broadcasted_iota(jnp.int32, (1, 128), 1)
    lower = lax.rem(lane, 64) < 32
    chunks = []
    for begin in range(0, values.shape[1], 128):
        chunk = values[:, begin : begin + 128]
        partner = jnp.where(lower, pltpu.roll(chunk, 96, 1), pltpu.roll(chunk, 32, 1))
        chunks.append(chunk * cosine + partner * sine)
    return chunks


def norm_scale(values):
    return lax.rsqrt(jnp.mean(values * values, axis=1, keepdims=True) + EPSILON)


def slot_table(routes, ranks):
    routes, ranks = routes.astype(F32).T, ranks.astype(F32).T
    expert = lax.broadcasted_iota(jnp.int32, (BLOCK, 32), 1).astype(F32)
    rank_of = jnp.zeros((BLOCK, 32), F32)
    for k in range(8):
        rank_of = rank_of + jnp.where(
            routes[:, k : k + 1] == expert, ranks[:, k : k + 1] + 1.0, 0.0
        )
    chosen = rank_of > 0.0
    row = lax.broadcasted_iota(jnp.int32, (BLOCK, BLOCK), 0)
    lane = lax.broadcasted_iota(jnp.int32, (BLOCK, BLOCK), 1)
    source = lax.broadcasted_iota(jnp.int32, (32, BLOCK), 0)
    target = lax.broadcasted_iota(jnp.int32, (32, BLOCK), 1)
    repeat = jnp.where(lax.rem(target, 32) == source, 1.0, 0.0).astype(BF)
    rank_wide = dot_nn(rank_of.astype(BF), repeat)
    hit = rank_wide == (lane // 32 + 1).astype(F32)
    counts = jnp.where(hit, 1.0, 0.0)
    earlier = jnp.where(row > lane, 1.0, 0.0).astype(BF)
    before = dot_nn(earlier, counts.astype(BF))
    totals = jnp.sum(counts, axis=0, keepdims=True)
    lower = (lax.rem(row, 32) == lax.rem(lane, 32)) & (row // 32 < lane // 32)
    offsets = dot_nn(totals.astype(BF), jnp.where(lower, 1.0, 0.0).astype(BF))
    place = jnp.where(hit, before + offsets, 0.0)
    place = place[:, :128] + place[:, 128:]
    place = place + pltpu.roll(place, 64, 1)
    place = place + pltpu.roll(place, 32, 1)
    place = place[:, :32]
    return chosen, jnp.where(chosen & (place < CAPACITY), place, -1.0)


def attend_kernel(
    tokens_ref,
    seg_ref,
    routes_ref,
    ranks_ref,
    gain_one_ref,
    w_query_ref,
    w_key_ref,
    w_value_ref,
    w_output_ref,
    gain_two_ref,
    w_router_ref,
    table_ref,
    cot_ref,
    w_in_ref,
    w_out_ref,
    routed_ref,
    residual_ref,
    heads_ref,
    normed_ref,
    query_ref,
    kv_ref,
    lse_ref,
    bias_ref,
    gates_ref,
    meta_ref,
    cots_ref,
    sib_in_ref,
    sib_out_ref,
    cots,
    table,
    kv_relay,
    segs,
    top,
    acc,
    send_sems,
    recv_sems,
    kv_send,
    kv_recv,
    seg_send,
    seg_recv,
    weight_send,
    weight_recv,
    local_sems,
):
    line, plane, core = lax.axis_index("seq"), lax.axis_index("grp"), lax.axis_index("exp")
    block = 2 * line + core
    row, column = plane // 4, lax.rem(plane, 4)
    barrier = pltpu.get_barrier_semaphore()
    for index in (
        mod4(row + 1) * 4 + column,
        mod4(row - 1) * 4 + column,
        row * 4 + mod4(column + 1),
        row * 4 + mod4(column - 1),
    ):
        pl.semaphore_signal(barrier, inc=1, device_id={"grp": index}, device_id_type=MESH)
    for step in (1, 2, 3):
        pl.semaphore_signal(
            barrier, inc=1, device_id={"seq": mod4(line + step)}, device_id_type=MESH
        )
    pl.semaphore_signal(barrier, inc=1, device_id={"exp": 1 - core}, device_id_type=MESH)
    own_cot = pltpu.make_async_copy(
        cot_ref, cots.at[pl.ds(pl.multiple_of(plane * BLOCK, BLOCK), BLOCK)], local_sems.at[0]
    )
    own_cot.start()
    load_table = pltpu.make_async_copy(table_ref.at[block], table, local_sems.at[1])
    load_table.start()
    own_cot.wait()
    pl.semaphore_wait(barrier, 8)
    gathers = [PlaneGather(part, cots, send_sems, recv_sems) for part in (0, 1)]
    for gather in gathers:
        gather.begin()
    for gather in gathers:
        gather.spread(0)

    tokens = tokens_ref[...].astype(F32)
    normed = (tokens * norm_scale(tokens) * gain_one_ref[...]).astype(BF)
    normed_ref[...] = normed
    load_table.wait()
    cosine, sine = table[0], table[1]
    keys = dot_nn(normed, w_key_ref[...])
    values = dot_nn(normed, w_value_ref[...]).astype(BF)
    key_chunks = rope_lanes(keys, cosine, sine)
    for head in range(KV_HEADS):
        chunk = key_chunks[head // 2].astype(BF)
        key = chunk[:, (head % 2) * 64 : (head % 2) * 64 + 64]
        kv_ref[0, head] = jnp.concatenate([key, values[:, head * 64 : head * 64 + 64]], axis=1)
    seg_tile = jnp.broadcast_to(seg_ref[...].astype(F32), (8, BLOCK))
    segs[0] = seg_tile

    def kv_copies(source, target, device, slot):
        return [
            pltpu.make_async_remote_copy(
                src_ref=ref.at[source],
                dst_ref=ref.at[target],
                send_sem=sends.at[slot],
                recv_sem=recvs.at[target],
                device_id=device,
                device_id_type=MESH,
            )
            for ref, sends, recvs in ((kv_ref, kv_send, kv_recv), (segs, seg_send, seg_recv))
        ]

    def relay_copies(device, to_relay):
        pairs = (
            (kv_ref, kv_relay, 4, kv_send, kv_recv),
            (segs, segs.at[5], 4, seg_send, seg_recv),
        )
        copies = []
        for ref, held, slot, sends, recvs in pairs:
            source, target = (ref.at[0], held) if to_relay else (held, ref.at[slot])
            copies.append(
                pltpu.make_async_remote_copy(
                    src_ref=source,
                    dst_ref=target,
                    send_sem=sends.at[2 if to_relay else 5],
                    recv_sem=recvs.at[5 if to_relay else 4],
                    device_id=device,
                    device_id_type=MESH,
                )
            )
        return copies

    sibling = {"exp": 1 - core}
    to_near = kv_copies(0, 2, {"seq": mod4(line + 1)}, 1)
    to_relay = relay_copies({"seq": mod4(line - 1)}, True)
    from_relay = relay_copies({"seq": mod4(line - 1)}, False)
    to_sibling = kv_copies(0, 1, sibling, 0)
    forward_near = kv_copies(2, 3 - 2 * core, sibling, 3)
    forward_far = kv_copies(4, 3, sibling, 4)

    def begin(copies):
        for copy in copies:
            copy.start()

    def sent(copies):
        for copy in copies:
            copy.wait_send()

    @pl.when(line < 3)
    def _():
        begin(to_near)

    @pl.when(core == 0)
    def _():
        begin(to_sibling)

    @pl.when(line < 2)
    def _():
        begin(to_relay)

    for gather in gathers:
        gather.forward_first()
        gather.spread(-1)
        gather.spread(1)
    weight_copies = [
        pltpu.make_async_remote_copy(
            src_ref=source,
            dst_ref=target,
            send_sem=weight_send.at[slot],
            recv_sem=weight_recv.at[slot],
            device_id=sibling,
            device_id_type=MESH,
        )
        for slot, (source, target) in enumerate(((w_in_ref, sib_in_ref), (w_out_ref, sib_out_ref)))
    ]
    begin(weight_copies)

    lane = lax.broadcasted_iota(jnp.int32, (1, 128), 1)
    queries = dot_nn(normed, w_query_ref[...])
    for head, chunk in enumerate(rope_lanes(queries, cosine, sine)):
        chunk = (chunk.astype(BF).astype(F32) * ATTENTION_FACTOR)
        query_ref[head, :BLOCK, :] = jnp.where(lane < 64, chunk, 0.0).astype(BF)
        query_ref[head, BLOCK:, :] = jnp.where(lane < 64, pltpu.roll(chunk, 64, 1), 0.0).astype(BF)
    top[...] = jnp.full(top.shape, MASKED, F32)
    acc[...] = jnp.zeros(acc.shape, F32)

    def attend(slot):
        j = lax.broadcasted_iota(jnp.int32, (BLOCK, BLOCK), 0)
        i = lax.broadcasted_iota(jnp.int32, (BLOCK, BLOCK), 1)
        distance = slot * BLOCK + i - j
        same = segs[slot].T[:, :1] == seg_tile[:1, :]
        allowed = same & (distance >= 0) & (distance < WINDOW)
        bias_ref[slot] = jnp.where(allowed, 0.0, MASKED).astype(BF)

        @pl.loop(0, KV_HEADS, unroll=4)
        def _(head):
            pair = kv_ref[slot, head]
            one = bias_ref[slot].astype(F32)
            score = dot_nt(pair, query_ref[head]) + jnp.concatenate([one, one], axis=1)
            old = top[pl.ds(head, 1), :]
            new = jnp.maximum(old, jnp.max(score, axis=0, keepdims=True))
            weight = jnp.exp(score - new).astype(BF)
            fade = jnp.exp(old - new)
            summing = jnp.where(lane < 64, 1.0, pair.astype(F32)).astype(BF)
            acc[head] = acc[head] * fade + dot_tn(summing, weight)
            top[pl.ds(head, 1), :] = new

    def wait_block(slot):
        for ref, sends, recvs in ((kv_ref, kv_send, kv_recv), (segs, seg_send, seg_recv)):
            pltpu.make_async_remote_copy(
                src_ref=ref.at[slot],
                dst_ref=ref.at[slot],
                send_sem=sends.at[0],
                recv_sem=recvs.at[slot],
                device_id=sibling,
                device_id_type=MESH,
            ).wait_recv()

    attend(0)
    for gather in gathers:
        gather.forward_second(0)
    for gather in gathers:
        gather.wait_far_first()
        gather.spread(2)

    @pl.when((line == 0) | (line == 3))
    def _():
        for arrival, copy in zip(to_relay, from_relay):
            arrival.wait_recv()
            copy.start()

    chosen, kept = slot_table(routes_ref[...], ranks_ref[...])
    kept_rows = jnp.concatenate([kept, jnp.zeros((BLOCK, 96), F32)], axis=1).T
    for index in range(PLANE):
        meta_ref[index, 0:2, :] = kept_rows[2 * index : 2 * index + 2]
        meta_ref[index, 4:8, :] = jnp.zeros((4, BLOCK), F32)

    first = 2 - core

    @pl.when(block >= first)
    def _():
        wait_block(first)

        @pl.when(core == 0)
        def _():
            begin(forward_near)

        attend(first)

    for da in (-1, 1):
        for gather in gathers:
            gather.forward_second(da)
    second = 1 + core

    @pl.when(block >= second)
    def _():
        wait_block(second)

        @pl.when(core == 1)
        def _():
            begin(forward_near)

        attend(second)

    for gather in gathers:
        gather.forward_second(2)
    third = 4 - core

    @pl.when(block >= third)
    def _():
        wait_block(third)
        attend(third)

    fourth = 3 + core

    @pl.when(block >= fourth)
    def _():
        wait_block(fourth)

        @pl.when(core == 1)
        def _():
            begin(forward_far)

        attend(fourth)

    for head in range(KV_HEADS):
        both = acc[head]
        expsum = both[:1, :]
        pair = (both * (1.0 / expsum)).T
        heads_ref[:, head * 128 : head * 128 + 128] = jnp.where(
            lane < 64, pltpu.roll(pair[:BLOCK], 64, 1), pair[BLOCK:]
        ).astype(BF)
        lse_ref[head : head + 1, :] = top[head : head + 1, :] + jnp.log(expsum)
    branch = dot_nn(heads_ref[...], w_output_ref[...])
    residual = tokens_ref[...].astype(F32) + RESIDUAL_MULT * branch
    residual_ref[...] = residual
    routed = (residual * norm_scale(residual) * gain_two_ref[...]).astype(BF)
    routed_ref[...] = routed
    logits = dot_nt(routed, w_router_ref[...])
    logits = jnp.where(chosen, logits, MASKED)
    powers = jnp.exp(logits - jnp.max(logits, axis=1, keepdims=True))
    gates = jnp.where(chosen, powers / jnp.sum(powers, axis=1, keepdims=True), 0.0)
    gates_ref[...] = gates
    gate_rows = jnp.concatenate([gates, jnp.zeros((BLOCK, 96), F32)], axis=1).T
    for index in range(PLANE):
        meta_ref[index, 2:4, :] = gate_rows[2 * index : 2 * index + 2]

    for da in (0, -1, 1, 2):
        for gather in gathers:
            gather.wait_far_second(da)
    store_cots = pltpu.make_async_copy(cots, cots_ref, local_sems.at[0])
    store_cots.start()
    for gather in gathers:
        gather.finish()
    for copy in weight_copies:
        copy.wait()

    @pl.when(line < 3)
    def _():
        sent(to_near)

    @pl.when(core == 0)
    def _():
        sent(to_sibling)

    @pl.when(line < 2)
    def _():
        sent(to_relay)

    @pl.when((line == 0) | (line == 3))
    def _():
        sent(from_relay)

    @pl.when(line >= 1)
    def _():
        sent(forward_near)

    store_cots.wait()

    @pl.when((line >= 2) & (core == 1))
    def _():
        sent(forward_far)


def run_attention(
    tokens, seg_tile, routes, ranks, gain_one, w_query, w_key, w_value, w_output, gain_two,
    w_router, table, cot, expert_in, expert_out,
):
    vmem = pl.BlockSpec(memory_space=pltpu.VMEM)
    hbm = pl.BlockSpec(memory_space=pl.ANY)
    dma = pltpu.SemaphoreType.DMA
    shape = jax.ShapeDtypeStruct
    return pl.pallas_call(
        attend_kernel,
        out_shape=(
            shape((BLOCK, WIDTH), BF),
            shape((BLOCK, WIDTH), F32),
            shape((BLOCK, WIDTH), BF),
            shape((BLOCK, WIDTH), BF),
            shape((KV_HEADS, 2 * BLOCK, 128), BF),
            shape((5, KV_HEADS, BLOCK, 128), BF),
            shape((KV_HEADS, 2 * BLOCK), F32),
            shape((5, BLOCK, BLOCK), BF),
            shape((BLOCK, 32), F32),
            shape((PLANE, 8, BLOCK), F32),
            shape((PLANE * BLOCK, WIDTH), BF),
            shape((WIDTH, 2 * INNER), BF),
            shape((INNER, WIDTH), BF),
        ),
        in_specs=[vmem] * 11 + [hbm] * 4,
        out_specs=(vmem,) * 10 + (hbm,) * 3,
        scratch_shapes=[
            pltpu.VMEM((PLANE * BLOCK, WIDTH), BF),
            pltpu.VMEM((2, BLOCK, 128), F32),
            pltpu.VMEM((KV_HEADS, BLOCK, 128), BF),
            pltpu.VMEM((6, 8, BLOCK), F32),
            pltpu.VMEM((KV_HEADS, 2 * BLOCK), F32),
            pltpu.VMEM((KV_HEADS, 128, 2 * BLOCK), F32),
            dma((40,)),
            dma((40,)),
            dma((6,)),
            dma((6,)),
            dma((6,)),
            dma((6,)),
            dma((2,)),
            dma((2,)),
            dma((2,)),
        ],
        compiler_params=pltpu.CompilerParams(
            collective_id=0, has_side_effects=True, vmem_limit_bytes=58 << 20
        ),
    )(
        tokens, seg_tile, routes, ranks, gain_one, w_query, w_key, w_value, w_output, gain_two,
        w_router, table, cot, expert_in, expert_out,
    )


def backward_kernel(
    tokens_ref,
    residual_ref,
    scores_ref,
    gates_ref,
    routed_ref,
    heads_ref,
    normed_ref,
    query_ref,
    kv_ref,
    bias_ref,
    w_key_ref,
    w_value_ref,
    w_router_ref,
    gain_one_ref,
    gain_two_ref,
    lse_ref,
    table_ref,
    partial_ref,
    grad_ref,
    row_total_ref,
    w_query_ref,
    w_output_ref,
    cot_ref,
    output_ref,
    input_grad_ref,
    trio_out_ref,
    output_w_ref,
    small_out_ref,
    gain_out_ref,
    grad_total_ref,
    table,
    partial,
    far,
    near,
    summed,
    far_two,
    near_two,
    moe_total,
    delta,
    head_grads,
    query_grads,
    own_grads,
    stage,
    from_pair,
    from_near,
    from_far,
    residual_grad,
    weight,
    wide,
    staged,
    arrived,
    mat_out,
    mat_one,
    mat_two,
    mat_three,
    cube_far,
    cube_near,
    cube_mid,
    cube_low,
    one_far,
    one_near,
    one_mid,
    one_low,
    two_far,
    two_near,
    two_mid,
    two_low,
    three_far,
    three_near,
    three_mid,
    three_low,
    small_own,
    small_first,
    small,
    gain_own,
    gain_first,
    gain,
    send_sems,
    recv_sems,
    ring_send,
    ring_recv,
    kv_send,
    kv_recv,
    local_sems,
    cube_send,
    cube_recv,
    core_send,
    core_recv,
    small_send,
    small_recv,
):
    line, plane, core = lax.axis_index("seq"), lax.axis_index("grp"), lax.axis_index("exp")
    block = 2 * line + core
    row, column = plane // 4, lax.rem(plane, 4)
    load = pltpu.make_async_copy(partial_ref, partial, local_sems.at[1])
    load_table = pltpu.make_async_copy(table_ref.at[block], table, local_sems.at[3])
    load_table.start()
    load.start()
    other = 1 - core
    places = (line, row, column)

    def neighbour(axis, step):
        if axis == 0:
            return {"seq": mod4(line + step)}
        if axis == 1:
            return {"grp": mod4(row + step) * 4 + column}
        return {"grp": row * 4 + mod4(column + step)}

    barrier = pltpu.get_barrier_semaphore()
    for axis in range(3):
        for step in (1, 2, 3):
            pl.semaphore_signal(
                barrier, inc=1, device_id=neighbour(axis, step), device_id_type=MESH
            )
    pl.semaphore_signal(barrier, inc=1, device_id={"exp": other}, device_id_type=MESH)
    load_rows = pltpu.make_async_copy(row_total_ref, moe_total, local_sems.at[2])
    load_rows.start()
    load_cot = pltpu.make_async_copy(cot_ref, wide, local_sems.at[5])
    load_cot.start()
    load_output = pltpu.make_async_copy(w_output_ref, weight, local_sems.at[4])
    load_output.start()
    load_query = pltpu.make_async_copy(w_query_ref, weight, local_sems.at[4])
    pl.semaphore_wait(barrier, 10)
    buffers = (far, near, summed, far_two, near_two)
    reducers = [
        PlaneReduce(part, partial, buffers, send_sems, recv_sems, moe_total) for part in (0, 1)
    ]
    spread = RowSpread(grad_ref, grad_total_ref, ring_send, ring_recv, local_sems.at[0])
    spread.begin()
    load.wait()
    for da in (2, 1, -1, 0):
        for reducer in reducers:
            reducer.step_far(da)

    def to_core(source, target, slot):
        return pltpu.make_async_remote_copy(
            src_ref=source,
            dst_ref=target,
            send_sem=core_send.at[slot],
            recv_sem=core_recv.at[slot],
            device_id={"exp": other},
            device_id_type=MESH,
        )

    cube_out = CubeSum(
        1, mat_out, output_w_ref, core * 512, other * 512, (cube_far, cube_near, cube_mid, cube_low),
        cube_send.at[0], cube_recv.at[0],
    )
    trio = [
        CubeSum(
            part, matrix, trio_out_ref, core * WIDTH + shift, other * WIDTH + shift, buffers,
            cube_send.at[1 + i], cube_recv.at[1 + i],
        )
        for i, (part, matrix, shift, buffers) in enumerate(
            (
                (0, mat_one, 0, (one_far, one_near, one_mid, one_low)),
                (1, mat_two, 384, (two_far, two_near, two_mid, two_low)),
                (2, mat_three, 768, (three_far, three_near, three_mid, three_low)),
            )
        )
    ]
    cubes = [cube_out] + trio

    def each(step):
        for cube in trio:
            getattr(cube, step)()

    own_small = pl.ds(pl.multiple_of(core * SMALL_ROWS, 16), SMALL_ROWS)
    other_small = pl.ds(pl.multiple_of(other * SMALL_ROWS, 16), SMALL_ROWS)
    share_out = to_core(weight.at[:, pl.ds(0, 512)], arrived.at[0], 0)
    share_query = to_core(staged, arrived.at[1], 1)
    share_pair = to_core(staged, arrived.at[2], 2)
    share_small = to_core(small_own.at[other_small], small_first, 3)
    share_total = to_core(small_out_ref.at[own_small], small_out_ref.at[own_small], 4)
    share_gain = to_core(gain_own, gain_first, 5)

    def axis_copy(held, base, axis, step):
        ref = held.at[axis, places[axis]]
        return pltpu.make_async_remote_copy(
            src_ref=ref,
            dst_ref=ref,
            send_sem=small_send.at[base + axis, step],
            recv_sem=small_recv.at[base + axis, step],
            device_id=neighbour(axis, step),
            device_id_type=MESH,
        )

    def axis_begin(held, base, axis):
        for step in (1, 2, 3):
            axis_copy(held, base, axis, step).start()

    def axis_sum(held, base, axis):
        for step in (1, 2, 3):
            ref = held.at[axis, mod4(places[axis] - step)]
            pltpu.make_async_remote_copy(
                src_ref=ref,
                dst_ref=ref,
                send_sem=small_send.at[base + axis, step],
                recv_sem=small_recv.at[base + axis, step],
                device_id=neighbour(axis, step),
                device_id_type=MESH,
            ).wait_recv()
        parts = [held[axis, i].astype(F32) for i in range(4)]
        return (parts[0] + parts[1]) + (parts[2] + parts[3])

    lane = lax.broadcasted_iota(jnp.int32, (1, 128), 1)
    lower = lane < 64
    gate_grad = jnp.concatenate(
        [scores_ref[index, 0:2, :] for index in range(PLANE)] + [jnp.zeros((96, BLOCK), F32)], axis=0
    ).T[:, :32]
    gates = gates_ref[...]
    choice_grad = gates * (gate_grad - jnp.sum(gates * gate_grad, axis=1, keepdims=True))
    logit_grad = choice_grad.astype(BF)
    small_own[...] = dot_tn(logit_grad, routed_ref[...]).astype(BF)
    share_small.start()
    gain_own[...] = jnp.zeros((8, WIDTH), F32)
    load_rows.wait()
    routed_grad = dot_nn(logit_grad, w_router_ref[...]) + moe_total[...]
    residual = residual_ref[...]
    scale_two = norm_scale(residual)
    gain_own[1:2, :] = jnp.sum(routed_grad * residual * scale_two, axis=0, keepdims=True)
    weighted = routed_grad * gain_two_ref[...]
    shared = scale_two * scale_two * scale_two * jnp.mean(weighted * residual, axis=1, keepdims=True)
    load_cot.wait()
    grown = wide[...].astype(F32) + scale_two * weighted - residual * shared
    residual_grad[...] = grown
    branch_grad = (RESIDUAL_MULT * grown).astype(BF)
    wide[...] = branch_grad
    load_output.wait()
    head_grad = dot_nt(branch_grad, weight[...]).astype(BF)
    for head in range(KV_HEADS):
        chunk = head_grad[:, head * 128 : head * 128 + 128].astype(F32)
        result = heads_ref[:, head * 128 : head * 128 + 128].astype(F32)
        head_grads[head, :BLOCK, :] = jnp.where(lower, 0.0, pltpu.roll(chunk, 64, 1)).astype(BF)
        head_grads[head, BLOCK:, :] = jnp.where(lower, 0.0, chunk).astype(BF)
        both = (chunk * result).T
        delta[head : head + 1, :BLOCK] = jnp.sum(both[:64], axis=0, keepdims=True)
        delta[head : head + 1, BLOCK:] = jnp.sum(both[64:], axis=0, keepdims=True)
    query_grads[...] = jnp.zeros(query_grads.shape, F32)

    for begin in (0, 256):
        columns = pl.ds(pl.multiple_of(core * 512 + begin, 256), 256)
        mat_out[:, begin : begin + 256] = dot_tn(heads_ref[...], wide[:, columns]).astype(BF)
    for begin in (0, 256):
        columns = pl.ds(pl.multiple_of(other * 512 + begin, 256), 256)
        weight[:, begin : begin + 256] = dot_tn(heads_ref[...], wide[:, columns]).astype(BF)
    share_out.start()

    def join(matrix, slot, place, begin, width):
        here = slice(place, place + width)
        matrix[:, here] = (
            matrix[:, here].astype(F32) + arrived[slot, :, begin : begin + width].astype(F32)
        ).astype(BF)

    own = 0

    def attend_back(slot):
        @pl.loop(0, KV_HEADS, unroll=2)
        def _(head):
            pair, query, out_grad = kv_ref[slot, head], query_ref[head], head_grads[head]
            one = bias_ref[slot].astype(F32)
            score = dot_nt(pair, query) + jnp.concatenate([one, one], axis=1)
            prob = jnp.exp(score - lse_ref[pl.ds(head, 1), :])
            prob_grad = dot_nt(pair, out_grad)
            score_grad = (prob * (prob_grad - delta[pl.ds(head, 1), :])).astype(BF)
            query_grads[head] += dot_tn(pair, score_grad)
            pair_grad = dot_nn(score_grad, query) + dot_nn(prob.astype(BF), out_grad)
            own_grads[head] = pair_grad
            if slot is not own:
                stage[slot - 1, head] = pair_grad.astype(BF)

    sibling = {"exp": 1 - core}

    def kv_copy(source, target, device, slot):
        return pltpu.make_async_remote_copy(
            src_ref=source,
            dst_ref=target,
            send_sem=kv_send.at[slot],
            recv_sem=kv_recv.at[slot],
            device_id=device,
            device_id_type=MESH,
        )

    pair_three = kv_copy(stage.at[2], from_pair.at[0], sibling, 0)
    pair_one = kv_copy(stage.at[0], from_pair.at[1], sibling, 1)
    to_near = kv_copy(stage.at[1], from_near, {"seq": mod4(line - 1)}, 2)
    to_far = kv_copy(stage.at[3], from_far, {"seq": mod4(line - 1)}, 3)

    def take_pair(three, slot):
        source = from_pair.at[0 if three else 1]
        kv_copy(source, source, sibling, 0 if three else 1).wait_recv()
        for head in range(KV_HEADS):
            stage[slot - 1, head] = (
                stage[slot - 1, head].astype(F32) + source[head].astype(F32)
            ).astype(BF)

    def take_far():
        @pl.when(line <= 2)
        def _():
            kv_copy(from_far, from_far, sibling, 3).wait_recv()
            for head in range(KV_HEADS):
                stage[1, head] = (
                    stage[1, head].astype(F32) + from_far[head].astype(F32)
                ).astype(BF)

    first, second, third, fourth = 3 + core, 4 - core, 1 + core, 2 - core

    @pl.when(block >= first)
    def _():
        attend_back(first)

    @pl.when((core == 0) & (line >= 2))
    def _():
        pair_three.start()

    for reducer in reducers:
        reducer.step_near(2)
        reducer.step_near(1)
    share_out.wait_recv()
    join(mat_out, 0, 0, 0, 512)
    cube_out.step_far()
    share_small.wait_recv()
    small[0, line] = (small_own[own_small, :].astype(F32) + small_first[...].astype(F32)).astype(BF)
    axis_begin(small, 0, 0)

    @pl.when((core == 1) & (line >= 2))
    def _():
        take_pair(True, 4)
        to_far.start()

    @pl.when(block >= second)
    def _():
        attend_back(second)

    @pl.when((core == 1) & (line >= 1))
    def _():
        pair_three.start()

    @pl.when((core == 0) & (line >= 2))
    def _():
        to_far.start()

    spread.forward()

    for reducer in reducers:
        reducer.step_near(-1)
        reducer.step_near(0)
    cube_out.step_near()

    @pl.when(block >= third)
    def _():
        attend_back(third)

    @pl.when((core == 0) & (line >= 1))
    def _():
        pair_one.start()

    for reducer in reducers:
        reducer.step_sum(2)
    small[1, row] = axis_sum(small, 0, 0).astype(BF)
    axis_begin(small, 0, 1)
    cube_out.ring_far()
    share_out.wait_send()
    load_query.start()

    @pl.when((core == 1) & (line >= 1))
    def _():
        take_pair(False, 2)
        take_far()
        to_near.start()

    @pl.when(block >= fourth)
    def _():
        attend_back(fourth)

    @pl.when(core == 1)
    def _():
        pair_one.start()

    @pl.when((core == 0) & (line >= 1))
    def _():
        take_pair(True, 2)
        take_far()
        to_near.start()

    for reducer in reducers:
        reducer.step_sum(1)
        reducer.step_sum(-1)
    small[2, column] = axis_sum(small, 0, 1).astype(BF)
    axis_begin(small, 0, 2)
    cube_out.ring_near()
    attend_back(own)

    load_table.wait()
    cosine, sine = table[0], table[1]
    normed = normed_ref[...]
    query_chunks = []
    for head in range(KV_HEADS):
        both = query_grads[head].T
        chunk = jnp.where(lower, both[:BLOCK], pltpu.roll(both[BLOCK:], 64, 1))
        query_chunks.append(chunk * ATTENTION_FACTOR)
    query_pre_grad = jnp.concatenate(
        rope_lanes(jnp.concatenate(query_chunks, axis=1), cosine, -sine), axis=1
    ).astype(BF)
    wide[...] = query_pre_grad
    for begin in (0, 256):
        columns = pl.ds(pl.multiple_of(other * 512 + begin, 256), 256)
        staged[:, begin : begin + 256] = dot_tn(normed, wide[:, columns]).astype(BF)
    share_query.start()
    for begin in (0, 256):
        columns = pl.ds(pl.multiple_of(core * 512 + begin, 256), 256)
        value = dot_tn(normed, wide[:, columns]).astype(BF)
        if begin == 0:
            mat_one[:, 0:256] = value
        else:
            mat_one[:, 256:384] = value[:, :128]
            mat_two[:, 0:128] = value[:, 128:]
    cube_out.ring_low()
    load_query.wait()
    normed_grad = dot_nt(query_pre_grad, weight[...])
    share_query.wait_recv()
    join(mat_one, 1, 0, 0, 384)
    join(mat_two, 1, 0, 384, 128)
    trio[0].step_far()

    @pl.when(core == 0)
    def _():
        source = from_pair.at[1]
        kv_copy(source, source, sibling, 1).wait_recv()
        for head in range(KV_HEADS):
            own_grads[head] += source[head].astype(F32)

    @pl.when(line < 3)
    def _():
        kv_copy(from_near, from_near, sibling, 2).wait_recv()
        for head in range(KV_HEADS):
            own_grads[head] += from_near[head].astype(F32)

    key_chunks, value_chunks = [], []
    for head in range(0, KV_HEADS, 2):
        one, two = own_grads[head], own_grads[head + 1]
        key_chunks.append(jnp.where(lower, one, pltpu.roll(two, 64, 1)))
        value_chunks.append(jnp.where(lower, pltpu.roll(one, 64, 1), two))
    key_pre_grad = jnp.concatenate(
        rope_lanes(jnp.concatenate(key_chunks, axis=1), cosine, -sine), axis=1
    ).astype(BF)
    value_pre_grad = jnp.concatenate(value_chunks, axis=1).astype(BF)
    wide[:, 0:512] = key_pre_grad
    wide[:, 512:1024] = value_pre_grad
    share_query.wait_send()
    for begin in (0, 256):
        columns = pl.ds(pl.multiple_of(other * 512 + begin, 256), 256)
        staged[:, begin : begin + 256] = dot_tn(normed, wide[:, columns]).astype(BF)
    share_pair.start()
    for begin in (0, 256):
        columns = pl.ds(pl.multiple_of(core * 512 + begin, 256), 256)
        value = dot_tn(normed, wide[:, columns]).astype(BF)
        if begin == 0:
            mat_two[:, 128:384] = value
        else:
            mat_three[...] = value
    cube_out.step_done()
    share_pair.wait_recv()
    join(mat_two, 2, 128, 0, 256)
    join(mat_three, 2, 0, 256, 256)
    trio[1].step_far()
    trio[2].step_far()
    small_out_ref[own_small, :] = axis_sum(small, 0, 2).astype(BF)
    share_total.start()
    normed_grad = (
        normed_grad
        + dot_nt(key_pre_grad, w_key_ref[...])
        + dot_nt(value_pre_grad, w_value_ref[...])
    )
    tokens = tokens_ref[...].astype(F32)
    scale_one = norm_scale(tokens)
    gain_own[0:1, :] = jnp.sum(normed_grad * tokens * scale_one, axis=0, keepdims=True)
    share_gain.start()
    weighted = normed_grad * gain_one_ref[...]
    shared = scale_one * scale_one * scale_one * jnp.mean(weighted * tokens, axis=1, keepdims=True)
    input_grad_ref[...] = (residual_grad[...] + scale_one * weighted - tokens * shared).astype(BF)

    each("step_near")
    cube_out.ring_back()
    share_gain.wait_recv()
    gain[0, line] = gain_own[...] + gain_first[...]
    axis_begin(gain, 3, 0)
    each("step_mid")
    cube_out.ring_forward()
    gain[1, row] = axis_sum(gain, 3, 0)
    axis_begin(gain, 3, 1)
    each("step_low")
    cube_out.ring_last()
    gain[2, column] = axis_sum(gain, 3, 1)
    axis_begin(gain, 3, 2)
    each("step_done")
    cube_out.back_far()
    gain_out_ref[...] = axis_sum(gain, 3, 2)
    each("back_mid")
    each("back_near")
    for reducer in reducers:
        reducer.step_sum(0)
    output_ref[...] = (residual_ref[...] + RESIDUAL_MULT * moe_total[...]).astype(BF)
    each("back_far")
    cube_out.back_last()
    each("back_last")
    for reducer in reducers:
        reducer.finish()
    spread.finish()
    for cube in cubes:
        cube.finish()
    for copy in (share_pair, share_small, share_gain, share_total):
        copy.wait_send()
    theirs = small_out_ref.at[other_small]
    to_core(theirs, theirs, 4).wait_recv()
    for base, held in ((0, small), (3, gain)):
        for axis in range(3):
            for step in (1, 2, 3):
                axis_copy(held, base, axis, step).wait_send()

    @pl.when(line >= 1 + (1 - core))
    def _():
        pair_three.wait_send()

    @pl.when((line >= 1) | (core == 1))
    def _():
        pair_one.wait_send()

    @pl.when(line >= 1)
    def _():
        to_near.wait_send()

    @pl.when(line >= 2)
    def _():
        to_far.wait_send()


def run_backward(*args):
    dma = pltpu.SemaphoreType.DMA
    rows = WIDTH + INNER
    vmem = pl.BlockSpec(memory_space=pltpu.VMEM)
    hbm = pl.BlockSpec(memory_space=pl.ANY)
    heads = (KV_HEADS, BLOCK, 128)
    shape = jax.ShapeDtypeStruct
    return pl.pallas_call(
        backward_kernel,
        out_shape=(
            shape((BLOCK, WIDTH), BF),
            shape((BLOCK, WIDTH), BF),
            shape((WIDTH, 2 * WIDTH), BF),
            shape((WIDTH, WIDTH), BF),
            shape((2 * SMALL_ROWS, WIDTH), BF),
            shape((8, WIDTH), F32),
            shape((rows, WIDTH), BF),
        ),
        in_specs=[vmem] * 16 + [hbm] * 7,
        out_specs=(vmem,) * 6 + (hbm,),
        scratch_shapes=[pltpu.VMEM((2, BLOCK, 128), F32), pltpu.VMEM((PLANE, BLOCK, WIDTH), BF)]
        + reduce_buffers()
        + [
            pltpu.VMEM((BLOCK, WIDTH), F32),
            pltpu.VMEM((KV_HEADS, 2 * BLOCK), F32),
            pltpu.VMEM((KV_HEADS, 2 * BLOCK, 128), BF),
            pltpu.VMEM((KV_HEADS, 128, 2 * BLOCK), F32),
            pltpu.VMEM(heads, F32),
            pltpu.VMEM((4,) + heads, BF),
            pltpu.VMEM((2,) + heads, BF),
            pltpu.VMEM(heads, BF),
            pltpu.VMEM(heads, BF),
            pltpu.VMEM((BLOCK, WIDTH), F32),
            pltpu.VMEM((WIDTH, WIDTH), BF),
            pltpu.VMEM((BLOCK, WIDTH), BF),
            pltpu.VMEM((WIDTH, 512), BF),
            pltpu.VMEM((3, WIDTH, 512), BF),
            pltpu.VMEM((WIDTH, 512), BF),
            pltpu.VMEM((WIDTH, 384), BF),
            pltpu.VMEM((WIDTH, 384), BF),
            pltpu.VMEM((WIDTH, 256), BF),
        ]
        + [
            pltpu.VMEM((count, extent, width), BF)
            for width in (512, 384, 384, 256)
            for count, extent in ((2, 128), (2, 256), (3, 64), (3, 16))
        ]
        + [
            pltpu.VMEM((2 * SMALL_ROWS, WIDTH), BF),
            pltpu.VMEM((SMALL_ROWS, WIDTH), BF),
            pltpu.VMEM((3, 4, SMALL_ROWS, WIDTH), BF),
            pltpu.VMEM((8, WIDTH), F32),
            pltpu.VMEM((8, WIDTH), F32),
            pltpu.VMEM((3, 4, 8, WIDTH), F32),
            dma((40,)),
            dma((40,)),
            dma((4,)),
            dma((4,)),
            dma((4,)),
            dma((4,)),
            dma((6,)),
            dma((4, 26)),
            dma((4, 26)),
            dma((6,)),
            dma((6,)),
            dma((6, 4)),
            dma((6, 4)),
        ],
        compiler_params=pltpu.CompilerParams(
            collective_id=1, has_side_effects=True, vmem_limit_bytes=VMEM_LIMIT
        ),
    )(*args)


def widen_kernel(
    up, down, output, query_one, query_two, key, value, up_out, down_out, output_out, query_out,
    key_out, value_out,
):
    for source, target in ((up, up_out), (down, down_out), (output, output_out), (key, key_out), (value, value_out)):
        target[...] = source[...].astype(F32)
    query_out[:, :512] = query_one[...].astype(F32)
    query_out[:, 512:] = query_two[...].astype(F32)


def widen_all(experts, output, trio):
    steps = 8
    in_rows, out_rows = WIDTH // steps, INNER // steps
    wide = pl.BlockSpec((in_rows, WIDTH), lambda i: (i, 0))
    low = pl.BlockSpec((out_rows, WIDTH), lambda i: (i, 0))
    narrow = pl.BlockSpec((in_rows, 512), lambda i: (i, 0))
    quarters = [pl.BlockSpec((in_rows, 512), lambda i, place=place: (i, place)) for place in range(4)]
    below = pl.BlockSpec((out_rows, WIDTH), lambda i: (WIDTH // out_rows + i, 0))
    shape = jax.ShapeDtypeStruct
    return pl.pallas_call(
        widen_kernel,
        grid=(steps,),
        out_shape=(
            shape((WIDTH, WIDTH), F32),
            shape((INNER, WIDTH), F32),
            shape((WIDTH, WIDTH), F32),
            shape((WIDTH, WIDTH), F32),
            shape((WIDTH, 512), F32),
            shape((WIDTH, 512), F32),
        ),
        in_specs=[wide, below, wide, quarters[0], quarters[2], quarters[1], quarters[3]],
        out_specs=(wide, low, wide, wide, narrow, narrow),
    )(experts, experts, output, trio, trio, trio, trio)


def on_device(
    tokens,
    segments,
    routes,
    rank_order,
    attn_gain,
    w_query,
    w_key,
    w_value,
    w_output,
    ffn_gain,
    w_router,
    expert_in,
    expert_out,
    cotangent,
):
    tok_rows = tokens.shape[1]
    table = jnp.asarray(rope_lane_table(8 * tok_rows)).reshape(8, 2, tok_rows, 128)
    router = w_router.T
    (
        routed_in, residual, heads_out, normed, query_heads, kv_heads_all, lse, bias, gates, meta,
        cots, sib_in, sib_out,
    ) = run_attention(
        tokens[0], segments, routes[0].T, rank_order[0].T, attn_gain[None], w_query, w_key, w_value,
        w_output, ffn_gain[None], router, table, cotangent[0], expert_in[0], expert_out[0],
    )
    expert_row_sum, scores, moe_partial, expert_grads = run_experts(
        routed_in, meta, cots.reshape(PLANE, BLOCK, WIDTH), expert_in[0], expert_out[0], sib_in, sib_out,
    )
    (
        output, input_grad, trio_sum, output_w_sum, small, gain_sum, expert_total,
    ) = run_backward(
        tokens[0], residual, scores, gates, routed_in, heads_out, normed, query_heads,
        kv_heads_all, bias, w_key, w_value, router, attn_gain[None], ffn_gain[None], lse, table,
        moe_partial, expert_grads, expert_row_sum, w_query, w_output, cotangent[0],
    )
    up_total, down_total, out_total, query_total, key_total, value_total = widen_all(
        expert_total, output_w_sum, trio_sum
    )
    router_total = small.T.astype(jnp.float32)
    gain_one_total = gain_sum[0]
    gain_two_total = gain_sum[1]
    return (
        output[None],
        input_grad[None],
        gain_one_total,
        query_total,
        key_total,
        value_total,
        out_total,
        gain_two_total,
        router_total,
        up_total[None],
        down_total[None],
    )


def solution(mesh):
    placed = (
        P("grp", ("seq", "exp"), None),
        P("grp", ("seq", "exp")),
        P("grp", ("seq", "exp"), None),
        P("grp", ("seq", "exp"), None),
        P(),
        P(),
        P(),
        P(),
        P(),
        P(),
        P(),
        P(("grp", "exp"), None, None),
        P(("grp", "exp"), None, None),
        P("grp", ("seq", "exp"), None),
    )
    return jax.shard_map(
        on_device,
        mesh=mesh,
        in_specs=placed,
        out_specs=(
            P("grp", ("seq", "exp"), None),
            P("grp", ("seq", "exp"), None),
            P(),
            P(),
            P(),
            P(),
            P(),
            P(),
            P(),
            P(("grp", "exp"), None, None),
            P(("grp", "exp"), None, None),
        ),
        check_vma=False,
    )
```

```python
import math

import jax
import jax.numpy as jnp
import numpy as np
from jax import lax
from jax.experimental import pallas as pl
from jax.experimental.pallas import tpu as pltpu
from jax.sharding import PartitionSpec as P

HEADS = 16
KV_HEADS = 8
HEAD = 64
WINDOW = 1024


EPSILON = 1e-06
ATTENTION_FACTOR = 0.015625
RESIDUAL_MULT = 0.22
ROPE_BASE = 10000.0
MASKED = -1e30


def rope_lane_table(length):
    half_dim = HEAD // 2
    frequency = np.exp(
        np.arange(half_dim, dtype=np.float32) * np.float32(-2.0 * math.log(ROPE_BASE) / HEAD)
    ).astype(np.float32)
    angles = np.arange(length, dtype=np.float32)[:, None] * frequency[None, :]
    cosine, sine = np.cos(angles), np.sin(angles)
    tables = (np.tile(cosine, (1, 4)), np.tile(np.concatenate([-sine, sine], axis=1), (1, 2)))
    return np.stack([table.reshape(-1, BLOCK, 128) for table in tables], axis=1).astype(np.float32)


MESH = pl.DeviceIdType.MESH
CAPACITY = 80
BLOCK = 256
HALF = 128
QUARTER = 64
WIDTH = 1024
INNER = 512
PLANE = 16
GROUP = 3
BF = jnp.bfloat16
F32 = jnp.float32


def mod4(value):
    return lax.rem(value + 8, 4)


def plane_id(part, first, second):
    return first * 4 + second if part == 0 else second * 4 + first


def plane_coords(part):
    index = lax.axis_index("grp")
    row, column = index // 4, lax.rem(index, 4)
    return (row, column) if part == 0 else (column, row)


def plane_copy(source, target, send_sem, recv_sem, index):
    return pltpu.make_async_remote_copy(
        src_ref=source,
        dst_ref=target,
        send_sem=send_sem,
        recv_sem=recv_sem,
        device_id={"grp": index},
        device_id_type=MESH,
    )


class PlaneGather:
    order = {0: 0, -1: 1, 1: 2, 2: 3}

    def __init__(self, part, blocks, send_sems, recv_sems):
        self.part, self.blocks = part, blocks
        self.send_sems, self.recv_sems = send_sems, recv_sems
        self.first, self.second = plane_coords(part)
        self.started = []

    def ref(self, da, db, half=None):
        index = plane_id(self.part, mod4(self.first + da), mod4(self.second + db))
        begin = pl.multiple_of(index * BLOCK + self.part * HALF, HALF)
        if half is None:
            return self.blocks.at[pl.ds(begin, HALF)]
        return self.blocks.at[pl.ds(pl.multiple_of(begin + half * QUARTER, QUARTER), QUARTER)]

    def copy(self, da, db, half, axis, step, slot):
        if axis == 0:
            to = plane_id(self.part, mod4(self.first + step), self.second)
        else:
            to = plane_id(self.part, self.first, mod4(self.second + step))
        ref, sem = self.ref(da, db, half), self.part * 20 + slot
        return plane_copy(ref, ref, self.send_sems.at[sem], self.recv_sems.at[sem], to)

    def send(self, *where):
        self.copy(*where).start()
        self.started.append(where)

    def wait(self, da, db, half, slot):
        ref, sem = self.ref(da, db, half), self.part * 20 + slot
        plane_copy(
            ref, ref, self.send_sems.at[sem], self.recv_sems.at[sem],
            plane_id(self.part, self.first, self.second),
        ).wait_recv()

    def begin(self):
        self.send(0, 0, None, 0, 1, 0)
        self.send(0, 0, None, 0, -1, 1)

    def spread(self, da):
        slot = 4 + 4 * self.order[da]
        self.send(da, 0, None, 1, 1, slot)
        self.send(da, 0, None, 1, -1, slot + 1)

    def forward_first(self):
        self.wait(-1, 0, None, 0)
        self.send(-1, 0, 0, 0, 1, 2)
        self.wait(1, 0, None, 1)
        self.send(1, 0, 1, 0, -1, 3)

    def forward_second(self, da):
        slot = 4 + 4 * self.order[da]
        self.wait(da, -1, None, slot)
        self.send(da, -1, 0, 1, 1, slot + 2)
        self.wait(da, 1, None, slot + 1)
        self.send(da, 1, 1, 1, -1, slot + 3)

    def wait_far_first(self):
        self.wait(2, 0, 0, 2)
        self.wait(2, 0, 1, 3)

    def wait_far_second(self, da):
        slot = 4 + 4 * self.order[da]
        self.wait(da, 2, 0, slot + 2)
        self.wait(da, 2, 1, slot + 3)

    def finish(self):
        for where in self.started:
            self.copy(*where).wait_send()


class PlaneReduce:
    order = {2: 0, 1: 1, -1: 2, 0: 3}

    def __init__(self, part, partial, buffers, send_sems, recv_sems, total):
        self.part, self.partial, self.total = part, partial, total
        self.far, self.near, self.summed, self.far_two, self.near_two = buffers
        self.send_sems, self.recv_sems = send_sems, recv_sems
        self.first, self.second = plane_coords(part)
        self.started = []

    def ref(self, da, db, half=None):
        index = plane_id(self.part, mod4(self.first + da), mod4(self.second + db))
        begin = self.part * HALF
        if half is None:
            return self.partial.at[index, pl.ds(begin, HALF)]
        return self.partial.at[index, pl.ds(begin + half * QUARTER, QUARTER)]

    def send(self, source, target, axis, step, slot):
        if axis == 0:
            to = plane_id(self.part, mod4(self.first + step), self.second)
        else:
            to = plane_id(self.part, self.first, mod4(self.second + step))
        sem = self.part * 20 + slot
        copy = plane_copy(source, target, self.send_sems.at[sem], self.recv_sems.at[sem], to)
        copy.start()
        self.started.append(copy)

    def wait(self, target, slot):
        sem = self.part * 20 + slot
        plane_copy(
            target, target, self.send_sems.at[sem], self.recv_sems.at[sem],
            plane_id(self.part, self.first, self.second),
        ).wait_recv()

    def add(self, target, source):
        target[...] = (target[...].astype(F32) + source[...].astype(F32)).astype(BF)

    def step_far(self, da):
        part, place = self.part, self.order[da]
        self.send(self.ref(da, 2, 0), self.far.at[part, place, 0], 1, 1, 4 * place)
        self.send(self.ref(da, 2, 1), self.far.at[part, place, 1], 1, -1, 4 * place + 1)

    def step_near(self, da):
        part, place = self.part, self.order[da]
        self.wait(self.far.at[part, place, 0], 4 * place)
        self.add(self.ref(da, 1, 0), self.far.at[part, place, 0])
        self.send(self.ref(da, 1), self.near.at[part, place, 0], 1, 1, 4 * place + 2)
        self.wait(self.far.at[part, place, 1], 4 * place + 1)
        self.add(self.ref(da, -1, 1), self.far.at[part, place, 1])
        self.send(self.ref(da, -1), self.near.at[part, place, 1], 1, -1, 4 * place + 3)

    def step_sum(self, da):
        part, place = self.part, self.order[da]
        self.wait(self.near.at[part, place, 0], 4 * place + 2)
        self.wait(self.near.at[part, place, 1], 4 * place + 3)
        value = (
            self.ref(da, 0)[...].astype(F32)
            + self.near[part, place, 0].astype(F32)
            + self.near[part, place, 1].astype(F32)
        )
        rows = pl.ds(part * HALF, HALF)
        if da == 0:
            self.total[rows] = value
            self.wait(self.near_two.at[part, 0], 18)
            self.wait(self.near_two.at[part, 1], 19)
            self.total[rows] += self.near_two[part, 0].astype(F32) + self.near_two[part, 1].astype(F32)
            return
        self.summed[part, place] = value.astype(BF)
        lower, upper = pl.ds(0, QUARTER), pl.ds(QUARTER, QUARTER)
        if da == 2:
            self.send(self.summed.at[part, 0, lower], self.far_two.at[part, 0], 0, 1, 16)
            self.send(self.summed.at[part, 0, upper], self.far_two.at[part, 1], 0, -1, 17)
        if da == 1:
            self.wait(self.far_two.at[part, 0], 16)
            self.add(self.summed.at[part, 1, lower], self.far_two.at[part, 0])
            self.send(self.summed.at[part, 1], self.near_two.at[part, 0], 0, 1, 18)
        if da == -1:
            self.wait(self.far_two.at[part, 1], 17)
            self.add(self.summed.at[part, 2, upper], self.far_two.at[part, 1])
            self.send(self.summed.at[part, 2], self.near_two.at[part, 1], 0, -1, 19)

    def finish(self):
        for copy in self.started:
            copy.wait_send()


def reduce_buffers():
    return [
        pltpu.VMEM((2, 4, 2, QUARTER, WIDTH), BF),
        pltpu.VMEM((2, 4, 2, HALF, WIDTH), BF),
        pltpu.VMEM((2, 3, HALF, WIDTH), BF),
        pltpu.VMEM((2, 2, QUARTER, WIDTH), BF),
        pltpu.VMEM((2, 2, HALF, WIDTH), BF),
    ]


class FlatRows:
    def __init__(self, ref, begin, lead, rows):
        self.ref, self.begin, self.lead, self.rows = ref, begin, lead, rows

    def slice(self, index):
        flat = 0
        for extent, place in zip(self.lead, index if isinstance(index, tuple) else (index,)):
            flat = flat * extent + place
        return pl.ds(self.begin + flat * self.rows, self.rows)

    @property
    def at(self):
        return FlatView(self)

    def __getitem__(self, index):
        return self.ref[self.slice(index), :]


class FlatView:
    def __init__(self, flat):
        self.flat = flat

    def __getitem__(self, index):
        return self.flat.ref.at[self.flat.slice(index)]


class RowRing:
    def __init__(self, summed, far, near, send_sems, recv_sems):
        self.summed, self.far, self.near = summed, far, near
        self.send_sems, self.recv_sems = send_sems, recv_sems
        self.me = lax.axis_index("seq")
        self.rows = (WIDTH + INNER) // 4
        self.started = []

    def piece(self, ref, shift, half=None):
        begin = mod4(self.me + shift) * self.rows
        if half is None:
            return ref.at[pl.ds(pl.multiple_of(begin, 16), self.rows)]
        return ref.at[pl.ds(pl.multiple_of(begin + half * (self.rows // 2), 16), self.rows // 2)]

    def copy(self, source, target, step, slot):
        return pltpu.make_async_remote_copy(
            src_ref=source,
            dst_ref=target,
            send_sem=self.send_sems.at[slot],
            recv_sem=self.recv_sems.at[slot],
            device_id={"seq": mod4(self.me + step)},
            device_id_type=MESH,
        )

    def send(self, source, target, step, slot):
        copy = self.copy(source, target, step, slot)
        copy.start()
        self.started.append(copy)

    def wait(self, target, slot):
        self.copy(target, target, 1, slot).wait_recv()

    def add(self, target, source):
        target[...] = (target[...].astype(F32) + source[...].astype(F32)).astype(BF)

    def step_far(self):
        self.send(self.piece(self.summed, 2, 0), self.far.at[0], 1, 0)
        self.send(self.piece(self.summed, 2, 1), self.far.at[1], -1, 1)

    def step_near(self):
        self.wait(self.far.at[0], 0)
        self.add(self.piece(self.summed, 1, 0), self.far.at[0])
        self.send(self.piece(self.summed, 1), self.near.at[0], 1, 2)
        self.wait(self.far.at[1], 1)
        self.add(self.piece(self.summed, -1, 1), self.far.at[1])
        self.send(self.piece(self.summed, -1), self.near.at[1], -1, 3)

    def step_sum(self):
        self.wait(self.near.at[0], 2)
        self.wait(self.near.at[1], 3)
        own = self.piece(self.summed, 0)
        own[...] = (
            own[...].astype(F32) + self.near[0].astype(F32) + self.near[1].astype(F32)
        ).astype(BF)

    def finish(self):
        for copy in self.started:
            copy.wait_send()


class RowSpread(RowRing):
    def __init__(self, own, total, send_sems, recv_sems, local_sem):
        super().__init__(total, None, None, send_sems, recv_sems)
        self.own, self.local_sem = own, local_sem

    def begin(self):
        target = self.piece(self.summed, 0)
        self.send(self.own, target, 1, 0)
        self.send(self.own, target, -1, 1)
        pltpu.make_async_copy(self.own, target, self.local_sem).start()

    def forward(self):
        self.wait(self.piece(self.summed, -1), 0)
        half = self.piece(self.summed, -1, 0)
        self.send(half, half, 1, 2)
        self.wait(self.piece(self.summed, 1), 1)
        half = self.piece(self.summed, 1, 1)
        self.send(half, half, -1, 3)

    def finish(self):
        self.wait(self.piece(self.summed, 2, 0), 2)
        self.wait(self.piece(self.summed, 2, 1), 3)
        pltpu.make_async_copy(self.own, self.piece(self.summed, 0), self.local_sem).wait()
        super().finish()


class CubeSum:
    def __init__(self, part, matrix, out, column, other, buffers, send_sems, recv_sems):
        self.part, self.matrix, self.out = part, matrix, out
        self.width = matrix.shape[1]
        self.column = pl.multiple_of(column, 128)
        self.other = pl.multiple_of(other, 128)
        self.far, self.near, self.mid, self.low = buffers
        self.send_sems, self.recv_sems = send_sems, recv_sems
        line, plane = lax.axis_index("seq"), lax.axis_index("grp")
        coords = (line, plane // 4, lax.rem(plane, 4))
        self.coords = coords
        self.place = [coords[(part + level) % 3] for level in range(3)]
        self.started = []

    def device(self, level, step):
        axis = (self.part + level) % 3
        there = mod4(self.coords[axis] + step)
        if axis == 0:
            return {"seq": there}
        if axis == 1:
            return {"grp": there * 4 + self.coords[2]}
        return {"grp": self.coords[1] * 4 + there}

    def rows(self, level, shift):
        begin = 0
        for upper in range(level):
            begin = begin + self.place[upper] * (256 // 4**upper)
        return pl.multiple_of(begin + mod4(self.place[level] + shift) * (256 // 4**level), 16)

    def result(self, begin, count):
        return self.out.at[pl.ds(begin, count), pl.ds(self.column, self.width)]

    def copy(self, source, target, level, step, slot):
        return pltpu.make_async_remote_copy(
            src_ref=source,
            dst_ref=target,
            send_sem=self.send_sems.at[slot],
            recv_sem=self.recv_sems.at[slot],
            device_id=self.device(level, step),
            device_id_type=MESH,
        )

    def send(self, source, target, level, step, slot):
        copy = self.copy(source, target, level, step, slot)
        copy.start()
        self.started.append(copy)

    def wait(self, target, slot):
        self.copy(target, target, 0, 0, slot).wait_recv()

    def add(self, target, *sources):
        value = target[...].astype(F32)
        for source in sources:
            value = value + source[...].astype(F32)
        target[...] = value.astype(BF)

    def step_far(self):
        begin = self.rows(0, 2)
        self.send(self.matrix.at[pl.ds(begin, 128)], self.far.at[0], 0, 1, 0)
        self.send(self.matrix.at[pl.ds(begin + 128, 128)], self.far.at[1], 0, -1, 1)

    def step_near(self):
        begin = self.rows(0, 1)
        self.wait(self.far.at[0], 0)
        self.add(self.matrix.at[pl.ds(begin, 128)], self.far.at[0])
        self.send(self.matrix.at[pl.ds(begin, 256)], self.near.at[0], 0, 1, 2)
        begin = self.rows(0, -1)
        self.wait(self.far.at[1], 1)
        self.add(self.matrix.at[pl.ds(begin + 128, 128)], self.far.at[1])
        self.send(self.matrix.at[pl.ds(begin, 256)], self.near.at[1], 0, -1, 3)

    def step_mid(self):
        self.wait(self.near.at[0], 2)
        self.wait(self.near.at[1], 3)
        self.add(self.matrix.at[pl.ds(self.rows(0, 0), 256)], self.near.at[0], self.near.at[1])
        for step in (1, 2, 3):
            self.send(
                self.matrix.at[pl.ds(self.rows(1, step), 64)], self.mid.at[step - 1], 1, step, 3 + step
            )

    def step_low(self):
        for step in (1, 2, 3):
            self.wait(self.mid.at[step - 1], 3 + step)
        self.add(
            self.matrix.at[pl.ds(self.rows(1, 0), 64)], self.mid.at[0], self.mid.at[1], self.mid.at[2]
        )
        for step in (1, 2, 3):
            self.send(
                self.matrix.at[pl.ds(self.rows(2, step), 16)], self.low.at[step - 1], 2, step, 6 + step
            )

    def ring_far(self):
        self.wait(self.near.at[0], 2)
        self.wait(self.near.at[1], 3)
        self.add(self.matrix.at[pl.ds(self.rows(0, 0), 256)], self.near.at[0], self.near.at[1])
        begin = self.rows(1, 2)
        self.send(self.matrix.at[pl.ds(begin, 32)], self.mid.at[0, pl.ds(0, 32)], 1, 1, 4)
        self.send(self.matrix.at[pl.ds(begin + 32, 32)], self.mid.at[0, pl.ds(32, 32)], 1, -1, 5)

    def ring_near(self):
        begin = self.rows(1, 1)
        held = self.mid.at[0, pl.ds(0, 32)]
        self.wait(held, 4)
        self.add(self.matrix.at[pl.ds(begin, 32)], held)
        self.send(self.matrix.at[pl.ds(begin, 64)], self.mid.at[1], 1, 1, 6)
        begin = self.rows(1, -1)
        held = self.mid.at[0, pl.ds(32, 32)]
        self.wait(held, 5)
        self.add(self.matrix.at[pl.ds(begin + 32, 32)], held)
        self.send(self.matrix.at[pl.ds(begin, 64)], self.mid.at[2], 1, -1, 24)

    def ring_low(self):
        self.wait(self.mid.at[1], 6)
        self.wait(self.mid.at[2], 24)
        self.add(self.matrix.at[pl.ds(self.rows(1, 0), 64)], self.mid.at[1], self.mid.at[2])
        for step in (1, 2, 3):
            self.send(
                self.matrix.at[pl.ds(self.rows(2, step), 16)], self.low.at[step - 1], 2, step, 6 + step
            )

    def ring_back(self):
        for step in (1, 2, 3):
            self.wait(self.result(self.rows(2, -step), 16), 9 + step)
        ref = self.result(self.rows(1, 0), 64)
        self.send(ref, ref, 1, 1, 13)
        self.send(ref, ref, 1, -1, 14)

    def ring_forward(self):
        begin = self.rows(1, -1)
        self.wait(self.result(begin, 64), 13)
        ref = self.result(begin, 32)
        self.send(ref, ref, 1, 1, 15)
        begin = self.rows(1, 1)
        self.wait(self.result(begin, 64), 14)
        ref = self.result(begin + 32, 32)
        self.send(ref, ref, 1, -1, 25)

    def ring_last(self):
        begin = self.rows(1, 2)
        self.wait(self.result(begin, 32), 15)
        self.wait(self.result(begin + 32, 32), 25)
        self.spread_piece()

    def step_done(self):
        for step in (1, 2, 3):
            self.wait(self.low.at[step - 1], 6 + step)
        own = self.rows(2, 0)
        value = self.matrix[pl.ds(own, 16), :].astype(F32)
        for step in (1, 2, 3):
            value = value + self.low[step - 1].astype(F32)
        ref = self.result(own, 16)
        ref[...] = value.astype(BF)
        for step in (1, 2, 3):
            self.send(ref, ref, 2, step, 9 + step)

    def back_mid(self):
        for step in (1, 2, 3):
            self.wait(self.result(self.rows(2, -step), 16), 9 + step)
        ref = self.result(self.rows(1, 0), 64)
        for step in (1, 2, 3):
            self.send(ref, ref, 1, step, 12 + step)

    def back_near(self):
        for step in (1, 2, 3):
            self.wait(self.result(self.rows(1, -step), 64), 12 + step)
        self.spread_piece()

    def spread_piece(self):
        ref = self.result(self.rows(0, 0), 256)
        self.send(ref, ref, 0, 1, 16)
        self.send(ref, ref, 0, -1, 17)
        self.share(0, 20)

    def back_far(self):
        begin = self.rows(0, -1)
        self.wait(self.result(begin, 256), 16)
        ref = self.result(begin, 128)
        self.send(ref, ref, 0, 1, 18)
        self.share(-1, 21)
        begin = self.rows(0, 1)
        self.wait(self.result(begin, 256), 17)
        ref = self.result(begin + 128, 128)
        self.send(ref, ref, 0, -1, 19)
        self.share(1, 22)

    def back_last(self):
        begin = self.rows(0, 2)
        self.wait(self.result(begin, 128), 18)
        self.wait(self.result(begin + 128, 128), 19)
        self.share(2, 23)

    def share_copy(self, shift, slot):
        ref = self.result(self.rows(0, shift), 256)
        return pltpu.make_async_remote_copy(
            src_ref=ref,
            dst_ref=ref,
            send_sem=self.send_sems.at[slot],
            recv_sem=self.recv_sems.at[slot],
            device_id={"exp": 1 - lax.axis_index("exp")},
            device_id_type=MESH,
        )

    def share(self, shift, slot):
        copy = self.share_copy(shift, slot)
        copy.start()
        self.started.append(copy)

    def finish(self):
        for shift, slot in ((0, 20), (-1, 21), (1, 22), (2, 23)):
            ref = self.out.at[pl.ds(self.rows(0, shift), 256), pl.ds(self.other, self.width)]
            pltpu.make_async_remote_copy(
                src_ref=ref,
                dst_ref=ref,
                send_sem=self.send_sems.at[slot],
                recv_sem=self.recv_sems.at[slot],
                device_id={"exp": 1 - lax.axis_index("exp")},
                device_id_type=MESH,
            ).wait_recv()
        for copy in self.started:
            copy.wait_send()


SMALL_ROWS = 16


def dot_tn(left, right):
    return lax.dot_general(left, right, (((0,), (0,)), ((), ())), preferred_element_type=F32)


def dot_nt(left, right):
    return lax.dot_general(left, right, (((1,), (1,)), ((), ())), preferred_element_type=F32)


def dot_nn(left, right):
    return lax.dot_general(left, right, (((1,), (0,)), ((), ())), preferred_element_type=F32)


def expert_kernel(
    rows_ref,
    meta_ref,
    cot_ref,
    w_in_ref,
    w_out_ref,
    sib_in_ref,
    sib_out_ref,
    row_total_ref,
    score_out_ref,
    moe_ref,
    grad_ref,
    blocks,
    meta_in,
    score_send,
    cots,
    weights,
    kept_rows,
    kept_grads,
    kept_hidden,
    kept_pairs,
    row_partial,
    moe_stage,
    picks,
    slot_cots,
    slot_both,
    summed,
    from_pair,
    send_sems,
    recv_sems,
    rsend_sems,
    rrecv_sems,
    meta_send,
    meta_recv,
    score_ssem,
    score_rsem,
    local_sems,
    cot_sems,
    moe_sems,
    pair_send,
    pair_recv,
    ring_send,
    ring_recv,
    plane_ready,
    line_ready,
):
    me = lax.axis_index("grp")
    core = lax.axis_index("exp")
    line = lax.axis_index("seq")
    other = 1 - core
    row, column = me // 4, lax.rem(me, 4)
    barrier = pltpu.get_barrier_semaphore()
    for step in range(1, PLANE):
        pl.semaphore_signal(
            barrier, inc=1, device_id={"grp": lax.rem(me + step, PLANE)}, device_id_type=MESH
        )
    pl.semaphore_signal(barrier, inc=1, device_id={"exp": other}, device_id_type=MESH)
    for step in (1, -1):
        pl.semaphore_signal(
            barrier, inc=1, device_id={"seq": mod4(line + step)}, device_id_type=MESH
        )

    def weight_in(expert):
        return weights.at[pl.ds(expert * WIDTH, WIDTH)]

    def weight_out(expert):
        return weights.at[pl.ds(2 * WIDTH + expert * INNER, INNER)]

    loads = [
        pltpu.make_async_copy(source, target, local_sems.at[slot])
        for slot, (source, target) in enumerate(
            (
                (w_in_ref, weight_in(core)),
                (w_out_ref, weight_out(core)),
                (sib_in_ref, weight_in(other)),
                (sib_out_ref, weight_out(other)),
            )
        )
    ]
    for load in loads:
        load.start()
    blocks[pl.ds(pl.multiple_of(me * BLOCK, BLOCK), BLOCK), :] = rows_ref[...]
    meta_in[me] = meta_ref[me]

    def place_of(power, j):
        step = power * 4**j
        return (
            mod4(row + lax.rem(ROW_STEPS // step, 4)) * 4
            + mod4(column + lax.rem(COLUMN_STEPS // step, 4))
        )

    def cot_copy(index, parity, j):
        return pltpu.make_async_copy(cot_ref.at[index], cots.at[parity, j], cot_sems.at[parity, j])

    def moe_copy(j, index):
        return pltpu.make_async_copy(moe_stage.at[j], moe_ref.at[index], moe_sems.at[j])

    cot_copy(me, 1, 0).start()
    for j in range(GROUP):
        cot_copy(place_of(1, j), 0, j).start()
    pl.semaphore_wait(barrier, PLANE + 2)

    gathers = [PlaneGather(part, blocks, send_sems, recv_sems) for part in (0, 1)]
    for gather in gathers:
        gather.begin()
    for gather in gathers:
        gather.spread(0)
    meta_copies = []
    for step in range(1, PLANE):
        to = lax.rem(me + step, PLANE)
        copy = plane_copy(
            meta_ref.at[to], meta_in.at[me], meta_send.at[step], meta_recv.at[step], to
        )
        copy.start()
        meta_copies.append(copy)

    def process(indices, parity, base, first_wait):
        count = len(indices)
        slots = count * CAPACITY
        gates = ([], [])
        for j, index in enumerate(indices):
            slot_id = lax.broadcasted_iota(jnp.int32, (CAPACITY, BLOCK), 0).astype(F32)
            hits = [slot_id == meta_in[index, expert : expert + 1, :] for expert in range(2)]
            for expert in range(2):
                gate_row = meta_in[index, 2 + expert : 3 + expert, :]
                gates[expert].append(
                    jnp.sum(jnp.where(hits[expert], gate_row, 0.0), axis=1, keepdims=True)
                )
            pick = jnp.concatenate(
                [jnp.where(hit, 1.0, 0.0).astype(BF) for hit in hits], axis=0
            )
            picks[j] = pick
            rows = dot_nn(pick, blocks[pl.ds(pl.multiple_of(index * BLOCK, BLOCK), BLOCK), :])
            cot_rows = dot_nn(pick, cots[parity, j])
            for expert in range(2):
                here = pl.ds(pl.multiple_of(base + j * CAPACITY, 16), CAPACITY)
                part = slice(expert * CAPACITY, expert * CAPACITY + CAPACITY)
                kept_rows[expert, here, :] = rows[part].astype(BF)
                slot_cots[expert, pl.ds(j * CAPACITY, CAPACITY), :] = cot_rows[part].astype(BF)
                kept_grads[expert, here, :] = (
                    gates[expert][j] * (RESIDUAL_MULT * cot_rows[part])
                ).astype(BF)
        here = pl.ds(pl.multiple_of(base, 16), slots)
        local = pl.ds(0, slots)
        for expert in range(2):
            gate = jnp.concatenate(gates[expert], axis=0) if count > 1 else gates[expert][0]
            gate_up = dot_nn(kept_rows[expert, here, :], weight_in(expert)[...])
            gate_half, up_half = gate_up[:, :INNER], gate_up[:, INNER:]
            sigmoid = jax.nn.sigmoid(gate_half)
            activated = gate_half * sigmoid
            hidden = (activated * up_half).astype(BF)
            kept_hidden[expert, here, :] = hidden
            result = dot_nn(hidden, weight_out(expert)[...]).astype(BF).astype(F32)
            scored = RESIDUAL_MULT * jnp.sum(
                slot_cots[expert, local, :].astype(F32) * result, axis=1, keepdims=True
            )
            weighted = (gate * result).astype(BF)
            hidden_grad = dot_nt(kept_grads[expert, here, :], weight_out(expert)[...])
            gate_part = hidden_grad * up_half * sigmoid * (1.0 + gate_half * (1.0 - sigmoid))
            up_part = hidden_grad * activated
            pair_grad = jnp.concatenate([gate_part.astype(BF), up_part.astype(BF)], axis=1)
            kept_pairs[expert, here, :] = pair_grad
            row_grad = dot_nt(pair_grad, weight_in(expert)[...]).astype(BF)
            for j in range(count):
                own, held = slice(j * CAPACITY, (j + 1) * CAPACITY), pl.ds(expert * CAPACITY, CAPACITY)
                slot_both[j, held, 0:WIDTH] = weighted[own]
                slot_both[j, held, WIDTH : 2 * WIDTH] = row_grad[own]
            for j, index in enumerate(indices):
                pick = picks[j, pl.ds(expert * CAPACITY, CAPACITY), :].astype(F32)
                score_send[index, expert : expert + 1, :] = jnp.sum(
                    pick * scored[j * CAPACITY : (j + 1) * CAPACITY], axis=0, keepdims=True
                )
        for j, index in enumerate(indices):
            both = dot_tn(picks[j], slot_both[j]).astype(BF)
            first_wait(j, index)
            moe_stage[j] = both[:, :WIDTH]
            moe_copy(j, index).start()
            row_partial[index] = both[:, WIDTH:]

    for load in loads:
        load.wait()
    cot_copy(me, 1, 0).wait()
    process([me], 1, 0, lambda j, index: None)
    for gather in gathers:
        gather.forward_first()
        gather.spread(-1)
        gather.spread(1)
    for gather in gathers:
        gather.forward_second(0)
    for copy in meta_copies:
        copy.wait()

    def one_group(group, power):
        parity = lax.rem(group, 2)

        @pl.when(group == 1)
        def _():
            for gather in gathers:
                gather.wait_far_first()
                gather.spread(2)
            for gather in gathers:
                gather.wait_far_second(0)

        @pl.when(group == 2)
        def _():
            for gather in gathers:
                gather.forward_second(1)
                gather.forward_second(-1)

        @pl.when(group == 3)
        def _():
            for gather in gathers:
                gather.forward_second(2)
            for gather in gathers:
                gather.wait_far_second(1)
                gather.wait_far_second(-1)

        @pl.when(group == 4)
        def _():
            for gather in gathers:
                gather.wait_far_second(2)

        indices = [place_of(power, j) for j in range(GROUP)]

        @pl.when(group < 4)
        def _():
            for j in range(GROUP):
                cot_copy(place_of(power * 4**GROUP, j), 1 - parity, j).start()

        for j in range(GROUP):
            cot_copy(indices[j], parity, j).wait()

        def first_wait(j, index):
            if j == 0:
                moe_copy(j, index).wait()
            else:

                @pl.when(group > 0)
                def _():
                    moe_copy(j, index).wait()

        process(indices, parity, CAPACITY + group * (GROUP * CAPACITY), first_wait)
        return lax.select(group < 4, power * 4**GROUP, power)

    lax.fori_loop(0, 5, one_group, jnp.int32(1))

    for gather in gathers:
        gather.finish()
    for index in (
        mod4(row + 1) * 4 + column,
        mod4(row - 1) * 4 + column,
        row * 4 + mod4(column + 1),
        row * 4 + mod4(column - 1),
    ):
        pl.semaphore_signal(plane_ready, inc=1, device_id={"grp": index}, device_id_type=MESH)
    for step in (1, -1):
        pl.semaphore_signal(
            line_ready, inc=1, device_id={"seq": mod4(line + step)}, device_id_type=MESH
        )
    buffers = (
        FlatRows(blocks, 0, (2, 4, 2), QUARTER),
        FlatRows(blocks, 1024, (2, 4, 2), HALF),
        summed,
        FlatRows(blocks, 3072, (2, 2), QUARTER),
        FlatRows(blocks, 3328, (2, 2), HALF),
    )
    reducers = [
        PlaneReduce(part, row_partial, buffers, rsend_sems, rrecv_sems, row_total_ref)
        for part in (0, 1)
    ]
    pl.semaphore_wait(plane_ready, 4)
    for da in (2, 1, -1, 0):
        for reducer in reducers:
            reducer.step_far(da)
    score_out_ref[me] = score_send[me]
    score_copies = []
    for step in range(1, PLANE):
        to = lax.rem(me + step, PLANE)
        copy = plane_copy(
            score_send.at[to], score_out_ref.at[me], score_ssem.at[step], score_rsem.at[step], to
        )
        copy.start()
        score_copies.append(copy)

    def grad_tile(expert, tile):
        columns = pl.ds((tile % 4) * BLOCK, BLOCK)
        if tile < 4:
            return dot_tn(kept_rows[expert, :, columns], kept_pairs[expert])
        return dot_tn(kept_hidden[expert, :, columns], kept_grads[expert])

    def pair_copy(tile):
        return pltpu.make_async_remote_copy(
            src_ref=cots.at[tile // GROUP, tile % GROUP],
            dst_ref=from_pair.at[tile],
            send_sem=pair_send.at[tile],
            recv_sem=pair_recv.at[tile],
            device_id={"exp": other},
            device_id_type=MESH,
        )

    for tile in range(6):
        cots[tile // GROUP, tile % GROUP] = grad_tile(other, tile).astype(BF)
        pair_copy(tile).start()
        if tile == 3:
            for reducer in reducers:
                reducer.step_near(2)
    for reducer in reducers:
        reducer.step_near(1)
    for tile in range(6):
        value = grad_tile(core, tile)
        pair_copy(tile).wait()
        weights[pl.ds(tile * BLOCK, BLOCK), :] = (value + from_pair[tile].astype(F32)).astype(BF)
        if tile == 2:
            for reducer in reducers:
                reducer.step_near(-1)
    pl.semaphore_wait(line_ready, 2)
    ring = RowRing(
        weights.at[pl.ds(0, WIDTH + INNER)],
        FlatRows(weights, 1536, (2,), 192),
        FlatRows(weights, 1920, (2,), 384),
        ring_send,
        ring_recv,
    )
    ring.step_far()
    for reducer in reducers:
        reducer.step_near(0)
    for reducer in reducers:
        reducer.step_sum(2)
    ring.step_near()
    for da in (1, -1):
        for reducer in reducers:
            reducer.step_sum(da)
    ring.step_sum()
    store = pltpu.make_async_copy(ring.piece(ring.summed, 0), grad_ref, local_sems.at[0])
    store.start()
    for reducer in reducers:
        reducer.step_sum(0)
    for reducer in reducers:
        reducer.finish()
    for copy in score_copies:
        copy.wait()
    for j in range(GROUP):
        moe_copy(j, j).wait()
    ring.finish()
    store.wait()


def step_table(steps):
    return sum(step * 4**i for i, step in enumerate(steps))


ROW_STEPS = step_table((1, 3, 0, 0, 2, 0, 1, 1, 3, 3, 2, 2, 1, 3, 2))
COLUMN_STEPS = step_table((0, 0, 1, 3, 0, 2, 1, 3, 1, 3, 1, 3, 2, 2, 2))


def run_experts(rows, meta, cots, expert_in, expert_out, sib_in, sib_out):
    vmem = pl.BlockSpec(memory_space=pltpu.VMEM)
    hbm = pl.BlockSpec(memory_space=pl.ANY)
    dma = pltpu.SemaphoreType.DMA
    slots = GROUP * CAPACITY
    every = PLANE * CAPACITY
    return pl.pallas_call(
        expert_kernel,
        out_shape=(
            jax.ShapeDtypeStruct((BLOCK, WIDTH), F32),
            jax.ShapeDtypeStruct((PLANE, 8, BLOCK), F32),
            jax.ShapeDtypeStruct((PLANE, BLOCK, WIDTH), BF),
            jax.ShapeDtypeStruct(((WIDTH + INNER) // 4, WIDTH), BF),
        ),
        in_specs=[vmem, vmem, hbm, hbm, hbm, hbm, hbm],
        out_specs=(vmem, vmem, hbm, hbm),
        scratch_shapes=[
            pltpu.VMEM((PLANE * BLOCK, WIDTH), BF),
            pltpu.VMEM((PLANE, 8, BLOCK), F32),
            pltpu.VMEM((PLANE, 8, BLOCK), F32),
            pltpu.VMEM((2, GROUP, BLOCK, WIDTH), BF),
            pltpu.VMEM((2 * (WIDTH + INNER), WIDTH), BF),
            pltpu.VMEM((2, every, WIDTH), BF),
            pltpu.VMEM((2, every, WIDTH), BF),
            pltpu.VMEM((2, every, INNER), BF),
            pltpu.VMEM((2, every, 2 * INNER), BF),
            pltpu.VMEM((PLANE, BLOCK, WIDTH), BF),
            pltpu.VMEM((GROUP, BLOCK, WIDTH), BF),
            pltpu.VMEM((GROUP, 2 * CAPACITY, BLOCK), BF),
            pltpu.VMEM((2, slots, WIDTH), BF),
            pltpu.VMEM((GROUP, 2 * CAPACITY, 2 * WIDTH), BF),
            pltpu.VMEM((2, 3, HALF, WIDTH), BF),
            pltpu.VMEM((6, BLOCK, WIDTH), BF),
        ]
        + [dma((40,))] * 4
        + [dma((PLANE,))] * 4
        + [dma((4,)), dma((2, GROUP)), dma((GROUP,))]
        + [dma((6,))] * 2
        + [dma((4,))] * 2
        + [pltpu.SemaphoreType.REGULAR] * 2,
        compiler_params=pltpu.CompilerParams(
            collective_id=2, has_side_effects=True, vmem_limit_bytes=VMEM_LIMIT
        ),
    )(rows, meta, cots, expert_in, expert_out, sib_in, sib_out)


VMEM_LIMIT = 63 << 20


def rope_lanes(values, cosine, sine):
    lane = lax.broadcasted_iota(jnp.int32, (1, 128), 1)
    lower = lax.rem(lane, 64) < 32
    chunks = []
    for begin in range(0, values.shape[1], 128):
        chunk = values[:, begin : begin + 128]
        partner = jnp.where(lower, pltpu.roll(chunk, 96, 1), pltpu.roll(chunk, 32, 1))
        chunks.append(chunk * cosine + partner * sine)
    return chunks


def norm_scale(values):
    return lax.rsqrt(jnp.mean(values * values, axis=1, keepdims=True) + EPSILON)


def slot_table(routes, ranks):
    routes, ranks = routes.astype(F32).T, ranks.astype(F32).T
    expert = lax.broadcasted_iota(jnp.int32, (BLOCK, 32), 1).astype(F32)
    rank_of = jnp.zeros((BLOCK, 32), F32)
    for k in range(8):
        rank_of = rank_of + jnp.where(
            routes[:, k : k + 1] == expert, ranks[:, k : k + 1] + 1.0, 0.0
        )
    chosen = rank_of > 0.0
    row = lax.broadcasted_iota(jnp.int32, (BLOCK, BLOCK), 0)
    lane = lax.broadcasted_iota(jnp.int32, (BLOCK, BLOCK), 1)
    source = lax.broadcasted_iota(jnp.int32, (32, BLOCK), 0)
    target = lax.broadcasted_iota(jnp.int32, (32, BLOCK), 1)
    repeat = jnp.where(lax.rem(target, 32) == source, 1.0, 0.0).astype(BF)
    rank_wide = dot_nn(rank_of.astype(BF), repeat)
    hit = rank_wide == (lane // 32 + 1).astype(F32)
    counts = jnp.where(hit, 1.0, 0.0)
    earlier = jnp.where(row > lane, 1.0, 0.0).astype(BF)
    before = dot_nn(earlier, counts.astype(BF))
    totals = jnp.sum(counts, axis=0, keepdims=True)
    lower = (lax.rem(row, 32) == lax.rem(lane, 32)) & (row // 32 < lane // 32)
    offsets = dot_nn(totals.astype(BF), jnp.where(lower, 1.0, 0.0).astype(BF))
    place = jnp.where(hit, before + offsets, 0.0)
    place = place[:, :128] + place[:, 128:]
    place = place + pltpu.roll(place, 64, 1)
    place = place + pltpu.roll(place, 32, 1)
    place = place[:, :32]
    return chosen, jnp.where(chosen & (place < CAPACITY), place, -1.0)


def attend_kernel(
    tokens_ref,
    seg_ref,
    routes_ref,
    ranks_ref,
    gain_one_ref,
    w_query_ref,
    w_key_ref,
    w_value_ref,
    w_output_ref,
    gain_two_ref,
    w_router_ref,
    table_ref,
    cot_ref,
    w_in_ref,
    w_out_ref,
    routed_ref,
    residual_ref,
    heads_ref,
    normed_ref,
    query_ref,
    kv_ref,
    lse_ref,
    bias_ref,
    gates_ref,
    meta_ref,
    cots_ref,
    sib_in_ref,
    sib_out_ref,
    cots,
    table,
    kv_relay,
    segs,
    top,
    acc,
    send_sems,
    recv_sems,
    kv_send,
    kv_recv,
    seg_send,
    seg_recv,
    weight_send,
    weight_recv,
    local_sems,
    store_sems,
):
    line, plane, core = lax.axis_index("seq"), lax.axis_index("grp"), lax.axis_index("exp")
    block = 2 * line + core
    row, column = plane // 4, lax.rem(plane, 4)
    barrier = pltpu.get_barrier_semaphore()
    for index in (
        mod4(row + 1) * 4 + column,
        mod4(row - 1) * 4 + column,
        row * 4 + mod4(column + 1),
        row * 4 + mod4(column - 1),
    ):
        pl.semaphore_signal(barrier, inc=1, device_id={"grp": index}, device_id_type=MESH)
    for step in (1, 2, 3):
        pl.semaphore_signal(
            barrier, inc=1, device_id={"seq": mod4(line + step)}, device_id_type=MESH
        )
    pl.semaphore_signal(barrier, inc=1, device_id={"exp": 1 - core}, device_id_type=MESH)
    own_cot = pltpu.make_async_copy(
        cot_ref, cots.at[pl.ds(pl.multiple_of(plane * BLOCK, BLOCK), BLOCK)], local_sems.at[0]
    )
    own_cot.start()
    load_table = pltpu.make_async_copy(table_ref.at[block], table, local_sems.at[1])
    load_table.start()
    own_cot.wait()
    pl.semaphore_wait(barrier, 8)
    gathers = [PlaneGather(part, cots, send_sems, recv_sems) for part in (0, 1)]
    for gather in gathers:
        gather.begin()
    for gather in gathers:
        gather.spread(0)

    tokens = tokens_ref[...].astype(F32)
    normed = (tokens * norm_scale(tokens) * gain_one_ref[...]).astype(BF)
    normed_ref[...] = normed
    load_table.wait()
    cosine, sine = table[0], table[1]
    keys = dot_nn(normed, w_key_ref[...])
    values = dot_nn(normed, w_value_ref[...]).astype(BF)
    key_chunks = rope_lanes(keys, cosine, sine)
    for head in range(KV_HEADS):
        chunk = key_chunks[head // 2].astype(BF)
        key = chunk[:, (head % 2) * 64 : (head % 2) * 64 + 64]
        kv_ref[0, head] = jnp.concatenate([key, values[:, head * 64 : head * 64 + 64]], axis=1)
    seg_tile = jnp.broadcast_to(seg_ref[...].astype(F32), (8, BLOCK))
    segs[0] = seg_tile

    def kv_copies(source, target, device, slot):
        return [
            pltpu.make_async_remote_copy(
                src_ref=ref.at[source],
                dst_ref=ref.at[target],
                send_sem=sends.at[slot],
                recv_sem=recvs.at[target],
                device_id=device,
                device_id_type=MESH,
            )
            for ref, sends, recvs in ((kv_ref, kv_send, kv_recv), (segs, seg_send, seg_recv))
        ]

    def relay_copies(device, to_relay):
        pairs = (
            (kv_ref, kv_relay, 4, kv_send, kv_recv),
            (segs, segs.at[5], 4, seg_send, seg_recv),
        )
        copies = []
        for ref, held, slot, sends, recvs in pairs:
            source, target = (ref.at[0], held) if to_relay else (held, ref.at[slot])
            copies.append(
                pltpu.make_async_remote_copy(
                    src_ref=source,
                    dst_ref=target,
                    send_sem=sends.at[2 if to_relay else 5],
                    recv_sem=recvs.at[5 if to_relay else 4],
                    device_id=device,
                    device_id_type=MESH,
                )
            )
        return copies

    sibling = {"exp": 1 - core}
    to_near = kv_copies(0, 2, {"seq": mod4(line + 1)}, 1)
    to_relay = relay_copies({"seq": mod4(line - 1)}, True)
    from_relay = relay_copies({"seq": mod4(line - 1)}, False)
    to_sibling = kv_copies(0, 1, sibling, 0)
    forward_near = kv_copies(2, 3 - 2 * core, sibling, 3)
    forward_far = kv_copies(4, 3, sibling, 4)

    def begin(copies):
        for copy in copies:
            copy.start()

    def sent(copies):
        for copy in copies:
            copy.wait_send()

    @pl.when(line < 3)
    def _():
        begin(to_near)

    @pl.when(core == 0)
    def _():
        begin(to_sibling)

    @pl.when(line < 2)
    def _():
        begin(to_relay)

    for gather in gathers:
        gather.forward_first()
        gather.spread(-1)
        gather.spread(1)
    weight_copies = [
        pltpu.make_async_remote_copy(
            src_ref=source,
            dst_ref=target,
            send_sem=weight_send.at[slot],
            recv_sem=weight_recv.at[slot],
            device_id=sibling,
            device_id_type=MESH,
        )
        for slot, (source, target) in enumerate(((w_in_ref, sib_in_ref), (w_out_ref, sib_out_ref)))
    ]
    begin(weight_copies)

    lane = lax.broadcasted_iota(jnp.int32, (1, 128), 1)
    queries = dot_nn(normed, w_query_ref[...])
    for head, chunk in enumerate(rope_lanes(queries, cosine, sine)):
        chunk = (chunk.astype(BF).astype(F32) * ATTENTION_FACTOR)
        query_ref[head, :BLOCK, :] = jnp.where(lane < 64, chunk, 0.0).astype(BF)
        query_ref[head, BLOCK:, :] = jnp.where(lane < 64, pltpu.roll(chunk, 64, 1), 0.0).astype(BF)
    top[...] = jnp.full(top.shape, MASKED, F32)
    acc[...] = jnp.zeros(acc.shape, F32)

    def attend(slot):
        j = lax.broadcasted_iota(jnp.int32, (BLOCK, BLOCK), 0)
        i = lax.broadcasted_iota(jnp.int32, (BLOCK, BLOCK), 1)
        distance = slot * BLOCK + i - j
        same = segs[slot].T[:, :1] == seg_tile[:1, :]
        allowed = same & (distance >= 0) & (distance < WINDOW)
        bias_ref[slot] = jnp.where(allowed, 0.0, MASKED).astype(BF)

        @pl.loop(0, KV_HEADS, unroll=4)
        def _(head):
            pair = kv_ref[slot, head]
            one = bias_ref[slot].astype(F32)
            score = dot_nt(pair, query_ref[head]) + jnp.concatenate([one, one], axis=1)
            old = top[pl.ds(head, 1), :]
            new = jnp.maximum(old, jnp.max(score, axis=0, keepdims=True))
            weight = jnp.exp(score - new).astype(BF)
            fade = jnp.exp(old - new)
            summing = jnp.where(lane < 64, 1.0, pair.astype(F32)).astype(BF)
            acc[head] = acc[head] * fade + dot_tn(summing, weight)
            top[pl.ds(head, 1), :] = new

    def wait_block(slot):
        for ref, sends, recvs in ((kv_ref, kv_send, kv_recv), (segs, seg_send, seg_recv)):
            pltpu.make_async_remote_copy(
                src_ref=ref.at[slot],
                dst_ref=ref.at[slot],
                send_sem=sends.at[0],
                recv_sem=recvs.at[slot],
                device_id=sibling,
                device_id_type=MESH,
            ).wait_recv()

    attend(0)
    for gather in gathers:
        gather.forward_second(0)
    for gather in gathers:
        gather.wait_far_first()
        gather.spread(2)

    @pl.when((line == 0) | (line == 3))
    def _():
        for arrival, copy in zip(to_relay, from_relay):
            arrival.wait_recv()
            copy.start()

    chosen, kept = slot_table(routes_ref[...], ranks_ref[...])
    kept_rows = jnp.concatenate([kept, jnp.zeros((BLOCK, 96), F32)], axis=1).T
    for index in range(PLANE):
        meta_ref[index, 0:2, :] = kept_rows[2 * index : 2 * index + 2]
        meta_ref[index, 4:8, :] = jnp.zeros((4, BLOCK), F32)

    first = 2 - core

    @pl.when(block >= first)
    def _():
        wait_block(first)

        @pl.when(core == 0)
        def _():
            begin(forward_near)

        attend(first)

    for da in (-1, 1):
        for gather in gathers:
            gather.forward_second(da)
    second = 1 + core

    @pl.when(block >= second)
    def _():
        wait_block(second)

        @pl.when(core == 1)
        def _():
            begin(forward_near)

        attend(second)

    for gather in gathers:
        gather.forward_second(2)
    third = 4 - core

    @pl.when(block >= third)
    def _():
        wait_block(third)
        attend(third)

    fourth = 3 + core

    @pl.when(block >= fourth)
    def _():
        wait_block(fourth)

        @pl.when(core == 1)
        def _():
            begin(forward_far)

        attend(fourth)

    def store_cots(part, da, db):
        gather = gathers[part]
        index = plane_id(part, mod4(gather.first + da), mod4(gather.second + db))
        begin = pl.ds(pl.multiple_of(index * BLOCK + part * HALF, HALF), HALF)
        return pltpu.make_async_copy(
            cots.at[begin], cots_ref.at[begin], store_sems.at[part, da % 4, db % 4]
        )

    for part in (0, 1):
        for da in (0, -1, 1, 2):
            for db in (0, -1, 1):
                store_cots(part, da, db).start()
    for head in range(KV_HEADS):
        both = acc[head]
        expsum = both[:1, :]
        pair = (both * (1.0 / expsum)).T
        heads_ref[:, head * 128 : head * 128 + 128] = jnp.where(
            lane < 64, pltpu.roll(pair[:BLOCK], 64, 1), pair[BLOCK:]
        ).astype(BF)
        lse_ref[head : head + 1, :] = top[head : head + 1, :] + jnp.log(expsum)
    branch = dot_nn(heads_ref[...], w_output_ref[...])
    residual = tokens_ref[...].astype(F32) + RESIDUAL_MULT * branch
    residual_ref[...] = residual
    routed = (residual * norm_scale(residual) * gain_two_ref[...]).astype(BF)
    routed_ref[...] = routed
    logits = dot_nt(routed, w_router_ref[...])
    logits = jnp.where(chosen, logits, MASKED)
    powers = jnp.exp(logits - jnp.max(logits, axis=1, keepdims=True))
    gates = jnp.where(chosen, powers / jnp.sum(powers, axis=1, keepdims=True), 0.0)
    gates_ref[...] = gates
    gate_rows = jnp.concatenate([gates, jnp.zeros((BLOCK, 96), F32)], axis=1).T
    for index in range(PLANE):
        meta_ref[index, 2:4, :] = gate_rows[2 * index : 2 * index + 2]

    for da in (0, -1, 1, 2):
        for gather in gathers:
            gather.wait_far_second(da)
    for da in (0, -1, 1, 2):
        for part in (0, 1):
            store_cots(part, da, 2).start()
    for gather in gathers:
        gather.finish()
    for copy in weight_copies:
        copy.wait()

    @pl.when(line < 3)
    def _():
        sent(to_near)

    @pl.when(core == 0)
    def _():
        sent(to_sibling)

    @pl.when(line < 2)
    def _():
        sent(to_relay)

    @pl.when((line == 0) | (line == 3))
    def _():
        sent(from_relay)

    @pl.when(line >= 1)
    def _():
        sent(forward_near)

    for part in (0, 1):
        for da in (0, -1, 1, 2):
            for db in (0, -1, 1, 2):
                store_cots(part, da, db).wait()

    @pl.when((line >= 2) & (core == 1))
    def _():
        sent(forward_far)


def run_attention(
    tokens, seg_tile, routes, ranks, gain_one, w_query, w_key, w_value, w_output, gain_two,
    w_router, table, cot, expert_in, expert_out,
):
    vmem = pl.BlockSpec(memory_space=pltpu.VMEM)
    hbm = pl.BlockSpec(memory_space=pl.ANY)
    dma = pltpu.SemaphoreType.DMA
    shape = jax.ShapeDtypeStruct
    return pl.pallas_call(
        attend_kernel,
        out_shape=(
            shape((BLOCK, WIDTH), BF),
            shape((BLOCK, WIDTH), F32),
            shape((BLOCK, WIDTH), BF),
            shape((BLOCK, WIDTH), BF),
            shape((KV_HEADS, 2 * BLOCK, 128), BF),
            shape((5, KV_HEADS, BLOCK, 128), BF),
            shape((KV_HEADS, 2 * BLOCK), F32),
            shape((5, BLOCK, BLOCK), BF),
            shape((BLOCK, 32), F32),
            shape((PLANE, 8, BLOCK), F32),
            shape((PLANE * BLOCK, WIDTH), BF),
            shape((WIDTH, 2 * INNER), BF),
            shape((INNER, WIDTH), BF),
        ),
        in_specs=[vmem] * 11 + [hbm] * 4,
        out_specs=(vmem,) * 10 + (hbm,) * 3,
        scratch_shapes=[
            pltpu.VMEM((PLANE * BLOCK, WIDTH), BF),
            pltpu.VMEM((2, BLOCK, 128), F32),
            pltpu.VMEM((KV_HEADS, BLOCK, 128), BF),
            pltpu.VMEM((6, 8, BLOCK), F32),
            pltpu.VMEM((KV_HEADS, 2 * BLOCK), F32),
            pltpu.VMEM((KV_HEADS, 128, 2 * BLOCK), F32),
            dma((40,)),
            dma((40,)),
            dma((6,)),
            dma((6,)),
            dma((6,)),
            dma((6,)),
            dma((2,)),
            dma((2,)),
            dma((2,)),
            dma((2, 4, 4)),
        ],
        compiler_params=pltpu.CompilerParams(
            collective_id=0, has_side_effects=True, vmem_limit_bytes=58 << 20
        ),
    )(
        tokens, seg_tile, routes, ranks, gain_one, w_query, w_key, w_value, w_output, gain_two,
        w_router, table, cot, expert_in, expert_out,
    )


def backward_kernel(
    tokens_ref,
    residual_ref,
    scores_ref,
    gates_ref,
    routed_ref,
    heads_ref,
    normed_ref,
    query_ref,
    kv_ref,
    bias_ref,
    w_key_ref,
    w_value_ref,
    w_router_ref,
    gain_one_ref,
    gain_two_ref,
    lse_ref,
    table_ref,
    partial_ref,
    grad_ref,
    row_total_ref,
    w_query_ref,
    w_output_ref,
    cot_ref,
    output_ref,
    input_grad_ref,
    trio_out_ref,
    output_w_ref,
    small_out_ref,
    gain_out_ref,
    grad_total_ref,
    table,
    partial,
    far,
    near,
    summed,
    far_two,
    near_two,
    moe_total,
    delta,
    head_grads,
    query_grads,
    own_grads,
    stage,
    from_pair,
    from_near,
    from_far,
    residual_grad,
    weight,
    wide,
    staged,
    arrived,
    mat_out,
    mat_one,
    mat_two,
    mat_three,
    cube_far,
    cube_near,
    cube_mid,
    cube_low,
    one_far,
    one_near,
    one_mid,
    one_low,
    two_far,
    two_near,
    two_mid,
    two_low,
    three_far,
    three_near,
    three_mid,
    three_low,
    small_own,
    small_first,
    small,
    gain_own,
    gain_first,
    gain,
    send_sems,
    recv_sems,
    ring_send,
    ring_recv,
    kv_send,
    kv_recv,
    local_sems,
    cube_send,
    cube_recv,
    core_send,
    core_recv,
    small_send,
    small_recv,
):
    line, plane, core = lax.axis_index("seq"), lax.axis_index("grp"), lax.axis_index("exp")
    block = 2 * line + core
    row, column = plane // 4, lax.rem(plane, 4)
    load = pltpu.make_async_copy(partial_ref, partial, local_sems.at[1])
    load_table = pltpu.make_async_copy(table_ref.at[block], table, local_sems.at[3])
    load_table.start()
    load.start()
    other = 1 - core
    places = (line, row, column)

    def neighbour(axis, step):
        if axis == 0:
            return {"seq": mod4(line + step)}
        if axis == 1:
            return {"grp": mod4(row + step) * 4 + column}
        return {"grp": row * 4 + mod4(column + step)}

    barrier = pltpu.get_barrier_semaphore()
    for axis in range(3):
        for step in (1, 2, 3):
            pl.semaphore_signal(
                barrier, inc=1, device_id=neighbour(axis, step), device_id_type=MESH
            )
    pl.semaphore_signal(barrier, inc=1, device_id={"exp": other}, device_id_type=MESH)
    load_rows = pltpu.make_async_copy(row_total_ref, moe_total, local_sems.at[2])
    load_rows.start()
    load_cot = pltpu.make_async_copy(cot_ref, wide, local_sems.at[5])
    load_cot.start()
    load_output = pltpu.make_async_copy(w_output_ref, weight, local_sems.at[4])
    load_output.start()
    load_query = pltpu.make_async_copy(w_query_ref, weight, local_sems.at[4])
    pl.semaphore_wait(barrier, 10)
    buffers = (far, near, summed, far_two, near_two)
    reducers = [
        PlaneReduce(part, partial, buffers, send_sems, recv_sems, moe_total) for part in (0, 1)
    ]
    spread = RowSpread(grad_ref, grad_total_ref, ring_send, ring_recv, local_sems.at[0])
    spread.begin()
    load.wait()
    for da in (2, 1, -1, 0):
        for reducer in reducers:
            reducer.step_far(da)

    def to_core(source, target, slot):
        return pltpu.make_async_remote_copy(
            src_ref=source,
            dst_ref=target,
            send_sem=core_send.at[slot],
            recv_sem=core_recv.at[slot],
            device_id={"exp": other},
            device_id_type=MESH,
        )

    cube_out = CubeSum(
        1, mat_out, output_w_ref, core * 512, other * 512, (cube_far, cube_near, cube_mid, cube_low),
        cube_send.at[0], cube_recv.at[0],
    )
    trio = [
        CubeSum(
            part, matrix, trio_out_ref, core * WIDTH + shift, other * WIDTH + shift, buffers,
            cube_send.at[1 + i], cube_recv.at[1 + i],
        )
        for i, (part, matrix, shift, buffers) in enumerate(
            (
                (0, mat_one, 0, (one_far, one_near, one_mid, one_low)),
                (1, mat_two, 384, (two_far, two_near, two_mid, two_low)),
                (2, mat_three, 768, (three_far, three_near, three_mid, three_low)),
            )
        )
    ]
    cubes = [cube_out] + trio

    def each(step):
        for cube in trio:
            getattr(cube, step)()

    own_small = pl.ds(pl.multiple_of(core * SMALL_ROWS, 16), SMALL_ROWS)
    other_small = pl.ds(pl.multiple_of(other * SMALL_ROWS, 16), SMALL_ROWS)
    share_out = to_core(weight.at[:, pl.ds(0, 512)], arrived.at[0], 0)
    share_query = to_core(staged, arrived.at[1], 1)
    share_pair = to_core(staged, arrived.at[2], 2)
    share_small = to_core(small_own.at[other_small], small_first, 3)
    share_total = to_core(small_out_ref.at[own_small], small_out_ref.at[own_small], 4)
    share_gain = to_core(gain_own, gain_first, 5)

    def axis_copy(held, base, axis, step):
        ref = held.at[axis, places[axis]]
        return pltpu.make_async_remote_copy(
            src_ref=ref,
            dst_ref=ref,
            send_sem=small_send.at[base + axis, step],
            recv_sem=small_recv.at[base + axis, step],
            device_id=neighbour(axis, step),
            device_id_type=MESH,
        )

    def axis_begin(held, base, axis):
        for step in (1, 2, 3):
            axis_copy(held, base, axis, step).start()

    def axis_sum(held, base, axis):
        for step in (1, 2, 3):
            ref = held.at[axis, mod4(places[axis] - step)]
            pltpu.make_async_remote_copy(
                src_ref=ref,
                dst_ref=ref,
                send_sem=small_send.at[base + axis, step],
                recv_sem=small_recv.at[base + axis, step],
                device_id=neighbour(axis, step),
                device_id_type=MESH,
            ).wait_recv()
        parts = [held[axis, i].astype(F32) for i in range(4)]
        return (parts[0] + parts[1]) + (parts[2] + parts[3])

    lane = lax.broadcasted_iota(jnp.int32, (1, 128), 1)
    lower = lane < 64
    gate_grad = jnp.concatenate(
        [scores_ref[index, 0:2, :] for index in range(PLANE)] + [jnp.zeros((96, BLOCK), F32)], axis=0
    ).T[:, :32]
    gates = gates_ref[...]
    choice_grad = gates * (gate_grad - jnp.sum(gates * gate_grad, axis=1, keepdims=True))
    logit_grad = choice_grad.astype(BF)
    small_own[...] = dot_tn(logit_grad, routed_ref[...]).astype(BF)
    share_small.start()
    gain_own[...] = jnp.zeros((8, WIDTH), F32)
    load_rows.wait()
    routed_grad = dot_nn(logit_grad, w_router_ref[...]) + moe_total[...]
    residual = residual_ref[...]
    scale_two = norm_scale(residual)
    gain_own[1:2, :] = jnp.sum(routed_grad * residual * scale_two, axis=0, keepdims=True)
    weighted = routed_grad * gain_two_ref[...]
    shared = scale_two * scale_two * scale_two * jnp.mean(weighted * residual, axis=1, keepdims=True)
    load_cot.wait()
    grown = wide[...].astype(F32) + scale_two * weighted - residual * shared
    residual_grad[...] = grown
    branch_grad = (RESIDUAL_MULT * grown).astype(BF)
    wide[...] = branch_grad
    load_output.wait()
    head_grad = dot_nt(branch_grad, weight[...]).astype(BF)
    for head in range(KV_HEADS):
        chunk = head_grad[:, head * 128 : head * 128 + 128].astype(F32)
        result = heads_ref[:, head * 128 : head * 128 + 128].astype(F32)
        head_grads[head, :BLOCK, :] = jnp.where(lower, 0.0, pltpu.roll(chunk, 64, 1)).astype(BF)
        head_grads[head, BLOCK:, :] = jnp.where(lower, 0.0, chunk).astype(BF)
        both = (chunk * result).T
        delta[head : head + 1, :BLOCK] = jnp.sum(both[:64], axis=0, keepdims=True)
        delta[head : head + 1, BLOCK:] = jnp.sum(both[64:], axis=0, keepdims=True)
    query_grads[...] = jnp.zeros(query_grads.shape, F32)

    for begin in (0, 256):
        columns = pl.ds(pl.multiple_of(core * 512 + begin, 256), 256)
        mat_out[:, begin : begin + 256] = dot_tn(heads_ref[...], wide[:, columns]).astype(BF)
    for begin in (0, 256):
        columns = pl.ds(pl.multiple_of(other * 512 + begin, 256), 256)
        weight[:, begin : begin + 256] = dot_tn(heads_ref[...], wide[:, columns]).astype(BF)
    share_out.start()

    def join(matrix, slot, place, begin, width):
        here = slice(place, place + width)
        matrix[:, here] = (
            matrix[:, here].astype(F32) + arrived[slot, :, begin : begin + width].astype(F32)
        ).astype(BF)

    own = 0

    def attend_back(slot):
        @pl.loop(0, KV_HEADS, unroll=2)
        def _(head):
            pair, query, out_grad = kv_ref[slot, head], query_ref[head], head_grads[head]
            one = bias_ref[slot].astype(F32)
            score = dot_nt(pair, query) + jnp.concatenate([one, one], axis=1)
            prob = jnp.exp(score - lse_ref[pl.ds(head, 1), :])
            prob_grad = dot_nt(pair, out_grad)
            score_grad = (prob * (prob_grad - delta[pl.ds(head, 1), :])).astype(BF)
            query_grads[head] += dot_tn(pair, score_grad)
            pair_grad = dot_nn(score_grad, query) + dot_nn(prob.astype(BF), out_grad)
            own_grads[head] = pair_grad
            if slot is not own:
                stage[slot - 1, head] = pair_grad.astype(BF)

    sibling = {"exp": 1 - core}

    def kv_copy(source, target, device, slot):
        return pltpu.make_async_remote_copy(
            src_ref=source,
            dst_ref=target,
            send_sem=kv_send.at[slot],
            recv_sem=kv_recv.at[slot],
            device_id=device,
            device_id_type=MESH,
        )

    pair_three = kv_copy(stage.at[2], from_pair.at[0], sibling, 0)
    pair_one = kv_copy(stage.at[0], from_pair.at[1], sibling, 1)
    to_near = kv_copy(stage.at[1], from_near, {"seq": mod4(line - 1)}, 2)
    to_far = kv_copy(stage.at[3], from_far, {"seq": mod4(line - 1)}, 3)

    def take_pair(three, slot):
        source = from_pair.at[0 if three else 1]
        kv_copy(source, source, sibling, 0 if three else 1).wait_recv()
        for head in range(KV_HEADS):
            stage[slot - 1, head] = (
                stage[slot - 1, head].astype(F32) + source[head].astype(F32)
            ).astype(BF)

    def take_far():
        @pl.when(line <= 2)
        def _():
            kv_copy(from_far, from_far, sibling, 3).wait_recv()
            for head in range(KV_HEADS):
                stage[1, head] = (
                    stage[1, head].astype(F32) + from_far[head].astype(F32)
                ).astype(BF)

    first, second, third, fourth = 3 + core, 4 - core, 1 + core, 2 - core

    @pl.when(block >= first)
    def _():
        attend_back(first)

    @pl.when((core == 0) & (line >= 2))
    def _():
        pair_three.start()

    for reducer in reducers:
        reducer.step_near(2)
        reducer.step_near(1)
    share_out.wait_recv()
    join(mat_out, 0, 0, 0, 512)
    cube_out.step_far()
    share_small.wait_recv()
    small[0, line] = (small_own[own_small, :].astype(F32) + small_first[...].astype(F32)).astype(BF)
    axis_begin(small, 0, 0)

    @pl.when((core == 1) & (line >= 2))
    def _():
        take_pair(True, 4)
        to_far.start()

    @pl.when(block >= second)
    def _():
        attend_back(second)

    @pl.when((core == 1) & (line >= 1))
    def _():
        pair_three.start()

    @pl.when((core == 0) & (line >= 2))
    def _():
        to_far.start()

    spread.forward()

    for reducer in reducers:
        reducer.step_near(-1)
        reducer.step_near(0)
    cube_out.step_near()

    @pl.when(block >= third)
    def _():
        attend_back(third)

    @pl.when((core == 0) & (line >= 1))
    def _():
        pair_one.start()

    for reducer in reducers:
        reducer.step_sum(2)
    small[1, row] = axis_sum(small, 0, 0).astype(BF)
    axis_begin(small, 0, 1)
    cube_out.ring_far()
    share_out.wait_send()
    load_query.start()

    @pl.when((core == 1) & (line >= 1))
    def _():
        take_pair(False, 2)
        take_far()
        to_near.start()

    @pl.when(block >= fourth)
    def _():
        attend_back(fourth)

    @pl.when(core == 1)
    def _():
        pair_one.start()

    @pl.when((core == 0) & (line >= 1))
    def _():
        take_pair(True, 2)
        take_far()
        to_near.start()

    for reducer in reducers:
        reducer.step_sum(1)
        reducer.step_sum(-1)
    small[2, column] = axis_sum(small, 0, 1).astype(BF)
    axis_begin(small, 0, 2)
    cube_out.ring_near()
    attend_back(own)

    load_table.wait()
    cosine, sine = table[0], table[1]
    normed = normed_ref[...]
    query_chunks = []
    for head in range(KV_HEADS):
        both = query_grads[head].T
        chunk = jnp.where(lower, both[:BLOCK], pltpu.roll(both[BLOCK:], 64, 1))
        query_chunks.append(chunk * ATTENTION_FACTOR)
    query_pre_grad = jnp.concatenate(
        rope_lanes(jnp.concatenate(query_chunks, axis=1), cosine, -sine), axis=1
    ).astype(BF)
    wide[...] = query_pre_grad
    for begin in (0, 256):
        columns = pl.ds(pl.multiple_of(other * 512 + begin, 256), 256)
        staged[:, begin : begin + 256] = dot_tn(normed, wide[:, columns]).astype(BF)
    share_query.start()
    for begin in (0, 256):
        columns = pl.ds(pl.multiple_of(core * 512 + begin, 256), 256)
        value = dot_tn(normed, wide[:, columns]).astype(BF)
        if begin == 0:
            mat_one[:, 0:256] = value
        else:
            mat_one[:, 256:384] = value[:, :128]
            mat_two[:, 0:128] = value[:, 128:]
    cube_out.ring_low()
    load_query.wait()
    normed_grad = dot_nt(query_pre_grad, weight[...])
    share_query.wait_recv()
    join(mat_one, 1, 0, 0, 384)
    join(mat_two, 1, 0, 384, 128)
    trio[0].step_far()

    @pl.when(core == 0)
    def _():
        source = from_pair.at[1]
        kv_copy(source, source, sibling, 1).wait_recv()
        for head in range(KV_HEADS):
            own_grads[head] += source[head].astype(F32)

    @pl.when(line < 3)
    def _():
        kv_copy(from_near, from_near, sibling, 2).wait_recv()
        for head in range(KV_HEADS):
            own_grads[head] += from_near[head].astype(F32)

    key_chunks, value_chunks = [], []
    for head in range(0, KV_HEADS, 2):
        one, two = own_grads[head], own_grads[head + 1]
        key_chunks.append(jnp.where(lower, one, pltpu.roll(two, 64, 1)))
        value_chunks.append(jnp.where(lower, pltpu.roll(one, 64, 1), two))
    key_pre_grad = jnp.concatenate(
        rope_lanes(jnp.concatenate(key_chunks, axis=1), cosine, -sine), axis=1
    ).astype(BF)
    value_pre_grad = jnp.concatenate(value_chunks, axis=1).astype(BF)
    wide[:, 0:512] = key_pre_grad
    wide[:, 512:1024] = value_pre_grad
    share_query.wait_send()
    for begin in (0, 256):
        columns = pl.ds(pl.multiple_of(other * 512 + begin, 256), 256)
        staged[:, begin : begin + 256] = dot_tn(normed, wide[:, columns]).astype(BF)
    share_pair.start()
    for begin in (0, 256):
        columns = pl.ds(pl.multiple_of(core * 512 + begin, 256), 256)
        value = dot_tn(normed, wide[:, columns]).astype(BF)
        if begin == 0:
            mat_two[:, 128:384] = value
        else:
            mat_three[...] = value
    cube_out.step_done()
    share_pair.wait_recv()
    join(mat_two, 2, 128, 0, 256)
    join(mat_three, 2, 0, 256, 256)
    trio[1].step_far()
    trio[2].step_far()
    small_out_ref[own_small, :] = axis_sum(small, 0, 2).astype(BF)
    share_total.start()
    normed_grad = (
        normed_grad
        + dot_nt(key_pre_grad, w_key_ref[...])
        + dot_nt(value_pre_grad, w_value_ref[...])
    )
    tokens = tokens_ref[...].astype(F32)
    scale_one = norm_scale(tokens)
    gain_own[0:1, :] = jnp.sum(normed_grad * tokens * scale_one, axis=0, keepdims=True)
    share_gain.start()
    weighted = normed_grad * gain_one_ref[...]
    shared = scale_one * scale_one * scale_one * jnp.mean(weighted * tokens, axis=1, keepdims=True)
    input_grad_ref[...] = (residual_grad[...] + scale_one * weighted - tokens * shared).astype(BF)

    each("step_near")
    cube_out.ring_back()
    share_gain.wait_recv()
    gain[0, line] = gain_own[...] + gain_first[...]
    axis_begin(gain, 3, 0)
    each("step_mid")
    cube_out.ring_forward()
    gain[1, row] = axis_sum(gain, 3, 0)
    axis_begin(gain, 3, 1)
    each("step_low")
    cube_out.ring_last()
    gain[2, column] = axis_sum(gain, 3, 1)
    axis_begin(gain, 3, 2)
    each("step_done")
    cube_out.back_far()
    gain_out_ref[...] = axis_sum(gain, 3, 2)
    each("back_mid")
    each("back_near")
    for reducer in reducers:
        reducer.step_sum(0)
    output_ref[...] = (residual_ref[...] + RESIDUAL_MULT * moe_total[...]).astype(BF)
    each("back_far")
    cube_out.back_last()
    each("back_last")
    for reducer in reducers:
        reducer.finish()
    spread.finish()
    for cube in cubes:
        cube.finish()
    for copy in (share_pair, share_small, share_gain, share_total):
        copy.wait_send()
    theirs = small_out_ref.at[other_small]
    to_core(theirs, theirs, 4).wait_recv()
    for base, held in ((0, small), (3, gain)):
        for axis in range(3):
            for step in (1, 2, 3):
                axis_copy(held, base, axis, step).wait_send()

    @pl.when(line >= 1 + (1 - core))
    def _():
        pair_three.wait_send()

    @pl.when((line >= 1) | (core == 1))
    def _():
        pair_one.wait_send()

    @pl.when(line >= 1)
    def _():
        to_near.wait_send()

    @pl.when(line >= 2)
    def _():
        to_far.wait_send()


def run_backward(*args):
    dma = pltpu.SemaphoreType.DMA
    rows = WIDTH + INNER
    vmem = pl.BlockSpec(memory_space=pltpu.VMEM)
    hbm = pl.BlockSpec(memory_space=pl.ANY)
    heads = (KV_HEADS, BLOCK, 128)
    shape = jax.ShapeDtypeStruct
    return pl.pallas_call(
        backward_kernel,
        out_shape=(
            shape((BLOCK, WIDTH), BF),
            shape((BLOCK, WIDTH), BF),
            shape((WIDTH, 2 * WIDTH), BF),
            shape((WIDTH, WIDTH), BF),
            shape((2 * SMALL_ROWS, WIDTH), BF),
            shape((8, WIDTH), F32),
            shape((rows, WIDTH), BF),
        ),
        in_specs=[vmem] * 16 + [hbm] * 7,
        out_specs=(vmem,) * 6 + (hbm,),
        scratch_shapes=[pltpu.VMEM((2, BLOCK, 128), F32), pltpu.VMEM((PLANE, BLOCK, WIDTH), BF)]
        + reduce_buffers()
        + [
            pltpu.VMEM((BLOCK, WIDTH), F32),
            pltpu.VMEM((KV_HEADS, 2 * BLOCK), F32),
            pltpu.VMEM((KV_HEADS, 2 * BLOCK, 128), BF),
            pltpu.VMEM((KV_HEADS, 128, 2 * BLOCK), F32),
            pltpu.VMEM(heads, F32),
            pltpu.VMEM((4,) + heads, BF),
            pltpu.VMEM((2,) + heads, BF),
            pltpu.VMEM(heads, BF),
            pltpu.VMEM(heads, BF),
            pltpu.VMEM((BLOCK, WIDTH), F32),
            pltpu.VMEM((WIDTH, WIDTH), BF),
            pltpu.VMEM((BLOCK, WIDTH), BF),
            pltpu.VMEM((WIDTH, 512), BF),
            pltpu.VMEM((3, WIDTH, 512), BF),
            pltpu.VMEM((WIDTH, 512), BF),
            pltpu.VMEM((WIDTH, 384), BF),
            pltpu.VMEM((WIDTH, 384), BF),
            pltpu.VMEM((WIDTH, 256), BF),
        ]
        + [
            pltpu.VMEM((count, extent, width), BF)
            for width in (512, 384, 384, 256)
            for count, extent in ((2, 128), (2, 256), (3, 64), (3, 16))
        ]
        + [
            pltpu.VMEM((2 * SMALL_ROWS, WIDTH), BF),
            pltpu.VMEM((SMALL_ROWS, WIDTH), BF),
            pltpu.VMEM((3, 4, SMALL_ROWS, WIDTH), BF),
            pltpu.VMEM((8, WIDTH), F32),
            pltpu.VMEM((8, WIDTH), F32),
            pltpu.VMEM((3, 4, 8, WIDTH), F32),
            dma((40,)),
            dma((40,)),
            dma((4,)),
            dma((4,)),
            dma((4,)),
            dma((4,)),
            dma((6,)),
            dma((4, 26)),
            dma((4, 26)),
            dma((6,)),
            dma((6,)),
            dma((6, 4)),
            dma((6, 4)),
        ],
        compiler_params=pltpu.CompilerParams(
            collective_id=1, has_side_effects=True, vmem_limit_bytes=VMEM_LIMIT
        ),
    )(*args)


def widen_kernel(
    up, down, output, query_one, query_two, key, value, router, result, grad, gains, up_out, down_out,
    output_out, query_out, key_out, value_out, router_out, result_out, grad_out,
    gain_one_out, gain_two_out,
):
    for source, target in ((up, up_out), (down, down_out), (output, output_out), (key, key_out), (value, value_out)):
        target[...] = source[...].astype(F32)
    query_out[:, :512] = query_one[...].astype(F32)
    query_out[:, 512:] = query_two[...].astype(F32)
    router_out[...] = router[...].astype(F32)
    result_out[...] = result[...]
    grad_out[...] = grad[...]
    gain_one_out[...] = gains[0, :]
    gain_two_out[...] = gains[1, :]


def widen_all(experts, output, trio, router, result, grad, gains):
    steps = 8
    in_rows, out_rows = WIDTH // steps, INNER // steps
    wide = pl.BlockSpec((in_rows, WIDTH), lambda i: (i, 0))
    low = pl.BlockSpec((out_rows, WIDTH), lambda i: (i, 0))
    narrow = pl.BlockSpec((in_rows, 512), lambda i: (i, 0))
    quarters = [pl.BlockSpec((in_rows, 512), lambda i, place=place: (i, place)) for place in range(4)]
    turned = pl.BlockSpec((32, in_rows), lambda i: (0, i))
    tokens = pl.BlockSpec((BLOCK // steps, WIDTH), lambda i: (i, 0))
    tile = pl.BlockSpec((8, WIDTH), lambda i: (0, 0))
    flat = pl.BlockSpec((WIDTH,), lambda i: (0,))
    below = pl.BlockSpec((out_rows, WIDTH), lambda i: (WIDTH // out_rows + i, 0))
    shape = jax.ShapeDtypeStruct
    return pl.pallas_call(
        widen_kernel,
        grid=(steps,),
        out_shape=(
            shape((WIDTH, WIDTH), F32),
            shape((INNER, WIDTH), F32),
            shape((WIDTH, WIDTH), F32),
            shape((WIDTH, WIDTH), F32),
            shape((WIDTH, 512), F32),
            shape((WIDTH, 512), F32),
            shape((32, WIDTH), F32),
            shape((BLOCK, WIDTH), BF),
            shape((BLOCK, WIDTH), BF),
            shape((WIDTH,), F32),
            shape((WIDTH,), F32),
        ),
        in_specs=[
            wide, below, wide, quarters[0], quarters[2], quarters[1], quarters[3], turned, tokens, tokens,
            tile,
        ],
        out_specs=(wide, low, wide, wide, narrow, narrow, turned, tokens, tokens, flat, flat),
        compiler_params=pltpu.CompilerParams(vmem_limit_bytes=VMEM_LIMIT),
    )(experts, experts, output, trio, trio, trio, trio, router, result, grad, gains)


def on_device(
    tokens,
    segments,
    routes,
    rank_order,
    attn_gain,
    w_query,
    w_key,
    w_value,
    w_output,
    ffn_gain,
    w_router,
    expert_in,
    expert_out,
    cotangent,
):
    tok_rows = tokens.shape[1]
    table = jnp.asarray(rope_lane_table(8 * tok_rows)).reshape(8, 2, tok_rows, 128)
    router = w_router.T
    (
        routed_in, residual, heads_out, normed, query_heads, kv_heads_all, lse, bias, gates, meta,
        cots, sib_in, sib_out,
    ) = run_attention(
        tokens[0], segments, routes[0].T, rank_order[0].T, attn_gain[None], w_query, w_key, w_value,
        w_output, ffn_gain[None], router, table, cotangent[0], expert_in[0], expert_out[0],
    )
    expert_row_sum, scores, moe_partial, expert_grads = run_experts(
        routed_in, meta, cots.reshape(PLANE, BLOCK, WIDTH), expert_in[0], expert_out[0], sib_in, sib_out,
    )
    (
        output, input_grad, trio_sum, output_w_sum, small, gain_sum, expert_total,
    ) = run_backward(
        tokens[0], residual, scores, gates, routed_in, heads_out, normed, query_heads,
        kv_heads_all, bias, w_key, w_value, router, attn_gain[None], ffn_gain[None], lse, table,
        moe_partial, expert_grads, expert_row_sum, w_query, w_output, cotangent[0],
    )
    (
        up_total, down_total, out_total, query_total, key_total, value_total, router_total, output,
        input_grad, gain_one_total, gain_two_total,
    ) = widen_all(expert_total, output_w_sum, trio_sum, small, output, input_grad, gain_sum)
    return (
        output[None],
        input_grad[None],
        gain_one_total,
        query_total,
        key_total,
        value_total,
        out_total,
        gain_two_total,
        router_total.T,
        up_total[None],
        down_total[None],
    )


def solution(mesh):
    placed = (
        P("grp", ("seq", "exp"), None),
        P("grp", ("seq", "exp")),
        P("grp", ("seq", "exp"), None),
        P("grp", ("seq", "exp"), None),
        P(),
        P(),
        P(),
        P(),
        P(),
        P(),
        P(),
        P(("grp", "exp"), None, None),
        P(("grp", "exp"), None, None),
        P("grp", ("seq", "exp"), None),
    )
    return jax.shard_map(
        on_device,
        mesh=mesh,
        in_specs=placed,
        out_specs=(
            P("grp", ("seq", "exp"), None),
            P("grp", ("seq", "exp"), None),
            P(),
            P(),
            P(),
            P(),
            P(),
            P(),
            P(),
            P(("grp", "exp"), None, None),
            P(("grp", "exp"), None, None),
        ),
        check_vma=False,
    )
```

```python
import math

import jax
import jax.numpy as jnp
import numpy as np
from jax import lax
from jax.experimental import pallas as pl
from jax.experimental.pallas import tpu as pltpu
from jax.sharding import PartitionSpec as P

HEADS = 16
KV_HEADS = 8
HEAD = 64
WINDOW = 1024


EPSILON = 1e-06
ATTENTION_FACTOR = 0.015625
RESIDUAL_MULT = 0.22
ROPE_BASE = 10000.0
MASKED = -1e30


def rope_lane_table(length):
    half_dim = HEAD // 2
    frequency = np.exp(
        np.arange(half_dim, dtype=np.float32) * np.float32(-2.0 * math.log(ROPE_BASE) / HEAD)
    ).astype(np.float32)
    angles = np.arange(length, dtype=np.float32)[:, None] * frequency[None, :]
    cosine, sine = np.cos(angles), np.sin(angles)
    tables = (np.tile(cosine, (1, 4)), np.tile(np.concatenate([-sine, sine], axis=1), (1, 2)))
    return np.stack([table.reshape(-1, BLOCK, 128) for table in tables], axis=1).astype(np.float32)


MESH = pl.DeviceIdType.MESH
CAPACITY = 80
BLOCK = 256
HALF = 128
QUARTER = 64
WIDTH = 1024
INNER = 512
PLANE = 16
GROUP = 3
BF = jnp.bfloat16
F32 = jnp.float32


def mod4(value):
    return lax.rem(value + 8, 4)


def plane_id(part, first, second):
    return first * 4 + second if part == 0 else second * 4 + first


def plane_coords(part):
    index = lax.axis_index("grp")
    row, column = index // 4, lax.rem(index, 4)
    return (row, column) if part == 0 else (column, row)


def plane_copy(source, target, send_sem, recv_sem, index):
    return pltpu.make_async_remote_copy(
        src_ref=source,
        dst_ref=target,
        send_sem=send_sem,
        recv_sem=recv_sem,
        device_id={"grp": index},
        device_id_type=MESH,
    )


class PlaneGather:
    order = {0: 0, -1: 1, 1: 2, 2: 3}

    def __init__(self, part, blocks, send_sems, recv_sems):
        self.part, self.blocks = part, blocks
        self.send_sems, self.recv_sems = send_sems, recv_sems
        self.first, self.second = plane_coords(part)
        self.started = []

    def ref(self, da, db, half=None):
        index = plane_id(self.part, mod4(self.first + da), mod4(self.second + db))
        begin = pl.multiple_of(index * BLOCK + self.part * HALF, HALF)
        if half is None:
            return self.blocks.at[pl.ds(begin, HALF)]
        return self.blocks.at[pl.ds(pl.multiple_of(begin + half * QUARTER, QUARTER), QUARTER)]

    def copy(self, da, db, half, axis, step, slot):
        if axis == 0:
            to = plane_id(self.part, mod4(self.first + step), self.second)
        else:
            to = plane_id(self.part, self.first, mod4(self.second + step))
        ref, sem = self.ref(da, db, half), self.part * 20 + slot
        return plane_copy(ref, ref, self.send_sems.at[sem], self.recv_sems.at[sem], to)

    def send(self, *where):
        self.copy(*where).start()
        self.started.append(where)

    def wait(self, da, db, half, slot):
        ref, sem = self.ref(da, db, half), self.part * 20 + slot
        plane_copy(
            ref, ref, self.send_sems.at[sem], self.recv_sems.at[sem],
            plane_id(self.part, self.first, self.second),
        ).wait_recv()

    def begin(self):
        self.send(0, 0, None, 0, 1, 0)
        self.send(0, 0, None, 0, -1, 1)

    def spread(self, da):
        slot = 4 + 4 * self.order[da]
        self.send(da, 0, None, 1, 1, slot)
        self.send(da, 0, None, 1, -1, slot + 1)

    def forward_first(self):
        self.wait(-1, 0, None, 0)
        self.send(-1, 0, 0, 0, 1, 2)
        self.wait(1, 0, None, 1)
        self.send(1, 0, 1, 0, -1, 3)

    def forward_second(self, da):
        slot = 4 + 4 * self.order[da]
        self.wait(da, -1, None, slot)
        self.send(da, -1, 0, 1, 1, slot + 2)
        self.wait(da, 1, None, slot + 1)
        self.send(da, 1, 1, 1, -1, slot + 3)

    def wait_far_first(self):
        self.wait(2, 0, 0, 2)
        self.wait(2, 0, 1, 3)

    def wait_far_second(self, da):
        slot = 4 + 4 * self.order[da]
        self.wait(da, 2, 0, slot + 2)
        self.wait(da, 2, 1, slot + 3)

    def finish(self):
        for where in self.started:
            self.copy(*where).wait_send()


class PlaneReduce:
    order = {2: 0, 1: 1, -1: 2, 0: 3}

    def __init__(self, part, partial, buffers, send_sems, recv_sems, total):
        self.part, self.partial, self.total = part, partial, total
        self.far, self.near, self.summed, self.far_two, self.near_two = buffers
        self.send_sems, self.recv_sems = send_sems, recv_sems
        self.first, self.second = plane_coords(part)
        self.started = []

    def ref(self, da, db, half=None):
        index = plane_id(self.part, mod4(self.first + da), mod4(self.second + db))
        begin = self.part * HALF
        if half is None:
            return self.partial.at[index, pl.ds(begin, HALF)]
        return self.partial.at[index, pl.ds(begin + half * QUARTER, QUARTER)]

    def send(self, source, target, axis, step, slot):
        if axis == 0:
            to = plane_id(self.part, mod4(self.first + step), self.second)
        else:
            to = plane_id(self.part, self.first, mod4(self.second + step))
        sem = self.part * 20 + slot
        copy = plane_copy(source, target, self.send_sems.at[sem], self.recv_sems.at[sem], to)
        copy.start()
        self.started.append(copy)

    def wait(self, target, slot):
        sem = self.part * 20 + slot
        plane_copy(
            target, target, self.send_sems.at[sem], self.recv_sems.at[sem],
            plane_id(self.part, self.first, self.second),
        ).wait_recv()

    def add(self, target, source):
        target[...] = (target[...].astype(F32) + source[...].astype(F32)).astype(BF)

    def step_far(self, da):
        part, place = self.part, self.order[da]
        self.send(self.ref(da, 2, 0), self.far.at[part, place, 0], 1, 1, 4 * place)
        self.send(self.ref(da, 2, 1), self.far.at[part, place, 1], 1, -1, 4 * place + 1)

    def step_near(self, da):
        part, place = self.part, self.order[da]
        self.wait(self.far.at[part, place, 0], 4 * place)
        self.add(self.ref(da, 1, 0), self.far.at[part, place, 0])
        self.send(self.ref(da, 1), self.near.at[part, place, 0], 1, 1, 4 * place + 2)
        self.wait(self.far.at[part, place, 1], 4 * place + 1)
        self.add(self.ref(da, -1, 1), self.far.at[part, place, 1])
        self.send(self.ref(da, -1), self.near.at[part, place, 1], 1, -1, 4 * place + 3)

    def step_sum(self, da):
        part, place = self.part, self.order[da]
        self.wait(self.near.at[part, place, 0], 4 * place + 2)
        self.wait(self.near.at[part, place, 1], 4 * place + 3)
        value = (
            self.ref(da, 0)[...].astype(F32)
            + self.near[part, place, 0].astype(F32)
            + self.near[part, place, 1].astype(F32)
        )
        rows = pl.ds(part * HALF, HALF)
        if da == 0:
            self.total[rows] = value
            self.wait(self.near_two.at[part, 0], 18)
            self.wait(self.near_two.at[part, 1], 19)
            self.total[rows] += self.near_two[part, 0].astype(F32) + self.near_two[part, 1].astype(F32)
            return
        self.summed[part, place] = value.astype(BF)
        lower, upper = pl.ds(0, QUARTER), pl.ds(QUARTER, QUARTER)
        if da == 2:
            self.send(self.summed.at[part, 0, lower], self.far_two.at[part, 0], 0, 1, 16)
            self.send(self.summed.at[part, 0, upper], self.far_two.at[part, 1], 0, -1, 17)
        if da == 1:
            self.wait(self.far_two.at[part, 0], 16)
            self.add(self.summed.at[part, 1, lower], self.far_two.at[part, 0])
            self.send(self.summed.at[part, 1], self.near_two.at[part, 0], 0, 1, 18)
        if da == -1:
            self.wait(self.far_two.at[part, 1], 17)
            self.add(self.summed.at[part, 2, upper], self.far_two.at[part, 1])
            self.send(self.summed.at[part, 2], self.near_two.at[part, 1], 0, -1, 19)

    def finish(self):
        for copy in self.started:
            copy.wait_send()


def reduce_buffers():
    return [
        pltpu.VMEM((2, 4, 2, QUARTER, WIDTH), BF),
        pltpu.VMEM((2, 4, 2, HALF, WIDTH), BF),
        pltpu.VMEM((2, 3, HALF, WIDTH), BF),
        pltpu.VMEM((2, 2, QUARTER, WIDTH), BF),
        pltpu.VMEM((2, 2, HALF, WIDTH), BF),
    ]


class FlatRows:
    def __init__(self, ref, begin, lead, rows):
        self.ref, self.begin, self.lead, self.rows = ref, begin, lead, rows

    def slice(self, index):
        flat = 0
        for extent, place in zip(self.lead, index if isinstance(index, tuple) else (index,)):
            flat = flat * extent + place
        return pl.ds(self.begin + flat * self.rows, self.rows)

    @property
    def at(self):
        return FlatView(self)

    def __getitem__(self, index):
        return self.ref[self.slice(index), :]


class FlatView:
    def __init__(self, flat):
        self.flat = flat

    def __getitem__(self, index):
        return self.flat.ref.at[self.flat.slice(index)]


class RowRing:
    def __init__(self, summed, far, near, send_sems, recv_sems):
        self.summed, self.far, self.near = summed, far, near
        self.send_sems, self.recv_sems = send_sems, recv_sems
        self.me = lax.axis_index("seq")
        self.rows = (WIDTH + INNER) // 4
        self.started = []

    def piece(self, ref, shift, half=None):
        begin = mod4(self.me + shift) * self.rows
        if half is None:
            return ref.at[pl.ds(pl.multiple_of(begin, 16), self.rows)]
        return ref.at[pl.ds(pl.multiple_of(begin + half * (self.rows // 2), 16), self.rows // 2)]

    def copy(self, source, target, step, slot):
        return pltpu.make_async_remote_copy(
            src_ref=source,
            dst_ref=target,
            send_sem=self.send_sems.at[slot],
            recv_sem=self.recv_sems.at[slot],
            device_id={"seq": mod4(self.me + step)},
            device_id_type=MESH,
        )

    def send(self, source, target, step, slot):
        copy = self.copy(source, target, step, slot)
        copy.start()
        self.started.append(copy)

    def wait(self, target, slot):
        self.copy(target, target, 1, slot).wait_recv()

    def add(self, target, source):
        target[...] = (target[...].astype(F32) + source[...].astype(F32)).astype(BF)

    def step_far(self):
        self.send(self.piece(self.summed, 2, 0), self.far.at[0], 1, 0)
        self.send(self.piece(self.summed, 2, 1), self.far.at[1], -1, 1)

    def step_near(self):
        self.wait(self.far.at[0], 0)
        self.add(self.piece(self.summed, 1, 0), self.far.at[0])
        self.send(self.piece(self.summed, 1), self.near.at[0], 1, 2)
        self.wait(self.far.at[1], 1)
        self.add(self.piece(self.summed, -1, 1), self.far.at[1])
        self.send(self.piece(self.summed, -1), self.near.at[1], -1, 3)

    def step_sum(self):
        self.wait(self.near.at[0], 2)
        self.wait(self.near.at[1], 3)
        own = self.piece(self.summed, 0)
        own[...] = (
            own[...].astype(F32) + self.near[0].astype(F32) + self.near[1].astype(F32)
        ).astype(BF)

    def finish(self):
        for copy in self.started:
            copy.wait_send()


class RowSpread(RowRing):
    def __init__(self, own, total, send_sems, recv_sems, local_sem):
        super().__init__(total, None, None, send_sems, recv_sems)
        self.own, self.local_sem = own, local_sem

    def begin(self):
        target = self.piece(self.summed, 0)
        self.send(self.own, target, 1, 0)
        self.send(self.own, target, -1, 1)
        pltpu.make_async_copy(self.own, target, self.local_sem).start()

    def forward(self):
        self.wait(self.piece(self.summed, -1), 0)
        half = self.piece(self.summed, -1, 0)
        self.send(half, half, 1, 2)
        self.wait(self.piece(self.summed, 1), 1)
        half = self.piece(self.summed, 1, 1)
        self.send(half, half, -1, 3)

    def finish(self):
        self.wait(self.piece(self.summed, 2, 0), 2)
        self.wait(self.piece(self.summed, 2, 1), 3)
        pltpu.make_async_copy(self.own, self.piece(self.summed, 0), self.local_sem).wait()
        super().finish()


class CubeSum:
    def __init__(self, part, matrix, out, column, other, buffers, send_sems, recv_sems):
        self.part, self.matrix, self.out = part, matrix, out
        self.width = matrix.shape[1]
        self.column = pl.multiple_of(column, 128)
        self.other = pl.multiple_of(other, 128)
        self.far, self.near, self.mid, self.low = buffers
        self.send_sems, self.recv_sems = send_sems, recv_sems
        line, plane = lax.axis_index("seq"), lax.axis_index("grp")
        coords = (line, plane // 4, lax.rem(plane, 4))
        self.coords = coords
        self.place = [coords[(part + level) % 3] for level in range(3)]
        self.started = []

    def device(self, level, step):
        axis = (self.part + level) % 3
        there = mod4(self.coords[axis] + step)
        if axis == 0:
            return {"seq": there}
        if axis == 1:
            return {"grp": there * 4 + self.coords[2]}
        return {"grp": self.coords[1] * 4 + there}

    def rows(self, level, shift):
        begin = 0
        for upper in range(level):
            begin = begin + self.place[upper] * (256 // 4**upper)
        return pl.multiple_of(begin + mod4(self.place[level] + shift) * (256 // 4**level), 16)

    def result(self, begin, count):
        return self.out.at[pl.ds(begin, count), pl.ds(self.column, self.width)]

    def copy(self, source, target, level, step, slot):
        return pltpu.make_async_remote_copy(
            src_ref=source,
            dst_ref=target,
            send_sem=self.send_sems.at[slot],
            recv_sem=self.recv_sems.at[slot],
            device_id=self.device(level, step),
            device_id_type=MESH,
        )

    def send(self, source, target, level, step, slot):
        copy = self.copy(source, target, level, step, slot)
        copy.start()
        self.started.append(copy)

    def wait(self, target, slot):
        self.copy(target, target, 0, 0, slot).wait_recv()

    def add(self, target, *sources):
        value = target[...].astype(F32)
        for source in sources:
            value = value + source[...].astype(F32)
        target[...] = value.astype(BF)

    def step_far(self):
        begin = self.rows(0, 2)
        self.send(self.matrix.at[pl.ds(begin, 128)], self.far.at[0], 0, 1, 0)
        self.send(self.matrix.at[pl.ds(begin + 128, 128)], self.far.at[1], 0, -1, 1)

    def step_near(self):
        begin = self.rows(0, 1)
        self.wait(self.far.at[0], 0)
        self.add(self.matrix.at[pl.ds(begin, 128)], self.far.at[0])
        self.send(self.matrix.at[pl.ds(begin, 256)], self.near.at[0], 0, 1, 2)
        begin = self.rows(0, -1)
        self.wait(self.far.at[1], 1)
        self.add(self.matrix.at[pl.ds(begin + 128, 128)], self.far.at[1])
        self.send(self.matrix.at[pl.ds(begin, 256)], self.near.at[1], 0, -1, 3)

    def step_mid(self):
        self.wait(self.near.at[0], 2)
        self.wait(self.near.at[1], 3)
        self.add(self.matrix.at[pl.ds(self.rows(0, 0), 256)], self.near.at[0], self.near.at[1])
        for step in (1, 2, 3):
            self.send(
                self.matrix.at[pl.ds(self.rows(1, step), 64)], self.mid.at[step - 1], 1, step, 3 + step
            )

    def step_low(self):
        for step in (1, 2, 3):
            self.wait(self.mid.at[step - 1], 3 + step)
        self.add(
            self.matrix.at[pl.ds(self.rows(1, 0), 64)], self.mid.at[0], self.mid.at[1], self.mid.at[2]
        )
        for step in (1, 2, 3):
            self.send(
                self.matrix.at[pl.ds(self.rows(2, step), 16)], self.low.at[step - 1], 2, step, 6 + step
            )

    def ring_far(self):
        self.wait(self.near.at[0], 2)
        self.wait(self.near.at[1], 3)
        self.add(self.matrix.at[pl.ds(self.rows(0, 0), 256)], self.near.at[0], self.near.at[1])
        begin = self.rows(1, 2)
        self.send(self.matrix.at[pl.ds(begin, 32)], self.mid.at[0, pl.ds(0, 32)], 1, 1, 4)
        self.send(self.matrix.at[pl.ds(begin + 32, 32)], self.mid.at[0, pl.ds(32, 32)], 1, -1, 5)

    def ring_near(self):
        begin = self.rows(1, 1)
        held = self.mid.at[0, pl.ds(0, 32)]
        self.wait(held, 4)
        self.add(self.matrix.at[pl.ds(begin, 32)], held)
        self.send(self.matrix.at[pl.ds(begin, 64)], self.mid.at[1], 1, 1, 6)
        begin = self.rows(1, -1)
        held = self.mid.at[0, pl.ds(32, 32)]
        self.wait(held, 5)
        self.add(self.matrix.at[pl.ds(begin + 32, 32)], held)
        self.send(self.matrix.at[pl.ds(begin, 64)], self.mid.at[2], 1, -1, 24)

    def ring_low(self):
        self.wait(self.mid.at[1], 6)
        self.wait(self.mid.at[2], 24)
        self.add(self.matrix.at[pl.ds(self.rows(1, 0), 64)], self.mid.at[1], self.mid.at[2])
        for step in (1, 2, 3):
            self.send(
                self.matrix.at[pl.ds(self.rows(2, step), 16)], self.low.at[step - 1], 2, step, 6 + step
            )

    def ring_back(self):
        for step in (1, 2, 3):
            self.wait(self.result(self.rows(2, -step), 16), 9 + step)
        ref = self.result(self.rows(1, 0), 64)
        self.send(ref, ref, 1, 1, 13)
        self.send(ref, ref, 1, -1, 14)

    def ring_forward(self):
        begin = self.rows(1, -1)
        self.wait(self.result(begin, 64), 13)
        ref = self.result(begin, 32)
        self.send(ref, ref, 1, 1, 15)
        begin = self.rows(1, 1)
        self.wait(self.result(begin, 64), 14)
        ref = self.result(begin + 32, 32)
        self.send(ref, ref, 1, -1, 25)

    def ring_last(self):
        begin = self.rows(1, 2)
        self.wait(self.result(begin, 32), 15)
        self.wait(self.result(begin + 32, 32), 25)
        self.spread_piece()

    def step_done(self):
        for step in (1, 2, 3):
            self.wait(self.low.at[step - 1], 6 + step)
        own = self.rows(2, 0)
        value = self.matrix[pl.ds(own, 16), :].astype(F32)
        for step in (1, 2, 3):
            value = value + self.low[step - 1].astype(F32)
        ref = self.result(own, 16)
        ref[...] = value.astype(BF)
        for step in (1, 2, 3):
            self.send(ref, ref, 2, step, 9 + step)

    def back_mid(self):
        for step in (1, 2, 3):
            self.wait(self.result(self.rows(2, -step), 16), 9 + step)
        ref = self.result(self.rows(1, 0), 64)
        for step in (1, 2, 3):
            self.send(ref, ref, 1, step, 12 + step)

    def back_near(self):
        for step in (1, 2, 3):
            self.wait(self.result(self.rows(1, -step), 64), 12 + step)
        self.spread_piece()

    def spread_piece(self):
        ref = self.result(self.rows(0, 0), 256)
        self.send(ref, ref, 0, 1, 16)
        self.send(ref, ref, 0, -1, 17)
        self.share(0, 20)

    def back_far(self):
        begin = self.rows(0, -1)
        self.wait(self.result(begin, 256), 16)
        ref = self.result(begin, 128)
        self.send(ref, ref, 0, 1, 18)
        self.share(-1, 21)
        begin = self.rows(0, 1)
        self.wait(self.result(begin, 256), 17)
        ref = self.result(begin + 128, 128)
        self.send(ref, ref, 0, -1, 19)
        self.share(1, 22)

    def back_last(self):
        begin = self.rows(0, 2)
        self.wait(self.result(begin, 128), 18)
        self.wait(self.result(begin + 128, 128), 19)
        self.share(2, 23)

    def share_copy(self, shift, slot):
        ref = self.result(self.rows(0, shift), 256)
        return pltpu.make_async_remote_copy(
            src_ref=ref,
            dst_ref=ref,
            send_sem=self.send_sems.at[slot],
            recv_sem=self.recv_sems.at[slot],
            device_id={"exp": 1 - lax.axis_index("exp")},
            device_id_type=MESH,
        )

    def share(self, shift, slot):
        copy = self.share_copy(shift, slot)
        copy.start()
        self.started.append(copy)

    def finish(self):
        for shift, slot in ((0, 20), (-1, 21), (1, 22), (2, 23)):
            ref = self.out.at[pl.ds(self.rows(0, shift), 256), pl.ds(self.other, self.width)]
            pltpu.make_async_remote_copy(
                src_ref=ref,
                dst_ref=ref,
                send_sem=self.send_sems.at[slot],
                recv_sem=self.recv_sems.at[slot],
                device_id={"exp": 1 - lax.axis_index("exp")},
                device_id_type=MESH,
            ).wait_recv()
        for copy in self.started:
            copy.wait_send()


SMALL_ROWS = 16


def dot_tn(left, right):
    return lax.dot_general(left, right, (((0,), (0,)), ((), ())), preferred_element_type=F32)


def dot_nt(left, right):
    return lax.dot_general(left, right, (((1,), (1,)), ((), ())), preferred_element_type=F32)


def dot_nn(left, right):
    return lax.dot_general(left, right, (((1,), (0,)), ((), ())), preferred_element_type=F32)


def expert_kernel(
    rows_ref,
    meta_ref,
    cot_ref,
    w_in_ref,
    w_out_ref,
    sib_in_ref,
    sib_out_ref,
    row_total_ref,
    score_out_ref,
    moe_ref,
    grad_ref,
    blocks,
    meta_in,
    score_send,
    cots,
    weights,
    kept_rows,
    kept_grads,
    kept_hidden,
    kept_pairs,
    row_partial,
    moe_stage,
    picks,
    slot_cots,
    slot_both,
    summed,
    from_pair,
    send_sems,
    recv_sems,
    rsend_sems,
    rrecv_sems,
    meta_send,
    meta_recv,
    score_ssem,
    score_rsem,
    local_sems,
    cot_sems,
    moe_sems,
    pair_send,
    pair_recv,
    ring_send,
    ring_recv,
    plane_ready,
    line_ready,
):
    me = lax.axis_index("grp")
    core = lax.axis_index("exp")
    line = lax.axis_index("seq")
    other = 1 - core
    row, column = me // 4, lax.rem(me, 4)
    barrier = pltpu.get_barrier_semaphore()
    for step in range(1, PLANE):
        pl.semaphore_signal(
            barrier, inc=1, device_id={"grp": lax.rem(me + step, PLANE)}, device_id_type=MESH
        )
    pl.semaphore_signal(barrier, inc=1, device_id={"exp": other}, device_id_type=MESH)
    for step in (1, -1):
        pl.semaphore_signal(
            barrier, inc=1, device_id={"seq": mod4(line + step)}, device_id_type=MESH
        )

    def weight_in(expert):
        return weights.at[pl.ds(expert * WIDTH, WIDTH)]

    def weight_out(expert):
        return weights.at[pl.ds(2 * WIDTH + expert * INNER, INNER)]

    loads = [
        pltpu.make_async_copy(source, target, local_sems.at[slot])
        for slot, (source, target) in enumerate(
            (
                (w_in_ref, weight_in(core)),
                (w_out_ref, weight_out(core)),
                (sib_in_ref, weight_in(other)),
                (sib_out_ref, weight_out(other)),
            )
        )
    ]
    for load in loads:
        load.start()
    blocks[pl.ds(pl.multiple_of(me * BLOCK, BLOCK), BLOCK), :] = rows_ref[...]
    meta_in[me] = meta_ref[me]

    def place_of(power, j):
        step = power * 4**j
        return (
            mod4(row + lax.rem(ROW_STEPS // step, 4)) * 4
            + mod4(column + lax.rem(COLUMN_STEPS // step, 4))
        )

    def cot_copy(index, parity, j):
        return pltpu.make_async_copy(cot_ref.at[index], cots.at[parity, j], cot_sems.at[parity, j])

    def moe_copy(j, index):
        return pltpu.make_async_copy(moe_stage.at[j], moe_ref.at[index], moe_sems.at[j])

    cot_copy(me, 1, 0).start()
    for j in range(GROUP):
        cot_copy(place_of(1, j), 0, j).start()
    pl.semaphore_wait(barrier, PLANE + 2)

    gathers = [PlaneGather(part, blocks, send_sems, recv_sems) for part in (0, 1)]
    for gather in gathers:
        gather.begin()
    for gather in gathers:
        gather.spread(0)
    meta_copies = []
    for step in range(1, PLANE):
        to = lax.rem(me + step, PLANE)
        copy = plane_copy(
            meta_ref.at[to], meta_in.at[me], meta_send.at[step], meta_recv.at[step], to
        )
        copy.start()
        meta_copies.append(copy)

    def process(indices, parity, base, first_wait):
        count = len(indices)
        slots = count * CAPACITY
        gates = ([], [])
        for j, index in enumerate(indices):
            slot_id = lax.broadcasted_iota(jnp.int32, (CAPACITY, BLOCK), 0).astype(F32)
            hits = [slot_id == meta_in[index, expert : expert + 1, :] for expert in range(2)]
            for expert in range(2):
                gate_row = meta_in[index, 2 + expert : 3 + expert, :]
                gates[expert].append(
                    jnp.sum(jnp.where(hits[expert], gate_row, 0.0), axis=1, keepdims=True)
                )
            pick = jnp.concatenate(
                [jnp.where(hit, 1.0, 0.0).astype(BF) for hit in hits], axis=0
            )
            picks[j] = pick
            rows = dot_nn(pick, blocks[pl.ds(pl.multiple_of(index * BLOCK, BLOCK), BLOCK), :])
            cot_rows = dot_nn(pick, cots[parity, j])
            for expert in range(2):
                here = pl.ds(pl.multiple_of(base + j * CAPACITY, 16), CAPACITY)
                part = slice(expert * CAPACITY, expert * CAPACITY + CAPACITY)
                kept_rows[expert, here, :] = rows[part].astype(BF)
                slot_cots[expert, pl.ds(j * CAPACITY, CAPACITY), :] = cot_rows[part].astype(BF)
                kept_grads[expert, here, :] = (
                    gates[expert][j] * (RESIDUAL_MULT * cot_rows[part])
                ).astype(BF)
        here = pl.ds(pl.multiple_of(base, 16), slots)
        local = pl.ds(0, slots)
        for expert in range(2):
            gate = jnp.concatenate(gates[expert], axis=0) if count > 1 else gates[expert][0]
            gate_up = dot_nn(kept_rows[expert, here, :], weight_in(expert)[...])
            gate_half, up_half = gate_up[:, :INNER], gate_up[:, INNER:]
            sigmoid = jax.nn.sigmoid(gate_half)
            activated = gate_half * sigmoid
            hidden = (activated * up_half).astype(BF)
            kept_hidden[expert, here, :] = hidden
            result = dot_nn(hidden, weight_out(expert)[...]).astype(BF).astype(F32)
            scored = RESIDUAL_MULT * jnp.sum(
                slot_cots[expert, local, :].astype(F32) * result, axis=1, keepdims=True
            )
            weighted = (gate * result).astype(BF)
            hidden_grad = dot_nt(kept_grads[expert, here, :], weight_out(expert)[...])
            gate_part = hidden_grad * up_half * sigmoid * (1.0 + gate_half * (1.0 - sigmoid))
            up_part = hidden_grad * activated
            pair_grad = jnp.concatenate([gate_part.astype(BF), up_part.astype(BF)], axis=1)
            kept_pairs[expert, here, :] = pair_grad
            row_grad = dot_nt(pair_grad, weight_in(expert)[...]).astype(BF)
            for j in range(count):
                own, held = slice(j * CAPACITY, (j + 1) * CAPACITY), pl.ds(expert * CAPACITY, CAPACITY)
                slot_both[j, held, 0:WIDTH] = weighted[own]
                slot_both[j, held, WIDTH : 2 * WIDTH] = row_grad[own]
            for j, index in enumerate(indices):
                pick = picks[j, pl.ds(expert * CAPACITY, CAPACITY), :].astype(F32)
                score_send[index, expert : expert + 1, :] = jnp.sum(
                    pick * scored[j * CAPACITY : (j + 1) * CAPACITY], axis=0, keepdims=True
                )
        for j, index in enumerate(indices):
            both = dot_tn(picks[j], slot_both[j]).astype(BF)
            first_wait(j, index)
            moe_stage[j] = both[:, :WIDTH]
            moe_copy(j, index).start()
            row_partial[index] = both[:, WIDTH:]

    for load in loads:
        load.wait()
    cot_copy(me, 1, 0).wait()
    process([me], 1, 0, lambda j, index: None)
    for gather in gathers:
        gather.forward_first()
        gather.spread(-1)
        gather.spread(1)
    for gather in gathers:
        gather.forward_second(0)
    for copy in meta_copies:
        copy.wait()

    def one_group(group, power):
        parity = lax.rem(group, 2)

        @pl.when(group == 1)
        def _():
            for gather in gathers:
                gather.wait_far_first()
                gather.spread(2)
            for gather in gathers:
                gather.wait_far_second(0)

        @pl.when(group == 2)
        def _():
            for gather in gathers:
                gather.forward_second(1)
                gather.forward_second(-1)

        @pl.when(group == 3)
        def _():
            for gather in gathers:
                gather.forward_second(2)
            for gather in gathers:
                gather.wait_far_second(1)
                gather.wait_far_second(-1)

        @pl.when(group == 4)
        def _():
            for gather in gathers:
                gather.wait_far_second(2)

        indices = [place_of(power, j) for j in range(GROUP)]

        @pl.when(group < 4)
        def _():
            for j in range(GROUP):
                cot_copy(place_of(power * 4**GROUP, j), 1 - parity, j).start()

        for j in range(GROUP):
            cot_copy(indices[j], parity, j).wait()

        def first_wait(j, index):
            if j == 0:
                moe_copy(j, index).wait()
            else:

                @pl.when(group > 0)
                def _():
                    moe_copy(j, index).wait()

        process(indices, parity, CAPACITY + group * (GROUP * CAPACITY), first_wait)
        return lax.select(group < 4, power * 4**GROUP, power)

    lax.fori_loop(0, 5, one_group, jnp.int32(1))

    for gather in gathers:
        gather.finish()
    for index in (
        mod4(row + 1) * 4 + column,
        mod4(row - 1) * 4 + column,
        row * 4 + mod4(column + 1),
        row * 4 + mod4(column - 1),
    ):
        pl.semaphore_signal(plane_ready, inc=1, device_id={"grp": index}, device_id_type=MESH)
    for step in (1, -1):
        pl.semaphore_signal(
            line_ready, inc=1, device_id={"seq": mod4(line + step)}, device_id_type=MESH
        )
    buffers = (
        FlatRows(blocks, 0, (2, 4, 2), QUARTER),
        FlatRows(blocks, 1024, (2, 4, 2), HALF),
        summed,
        FlatRows(blocks, 3072, (2, 2), QUARTER),
        FlatRows(blocks, 3328, (2, 2), HALF),
    )
    reducers = [
        PlaneReduce(part, row_partial, buffers, rsend_sems, rrecv_sems, row_total_ref)
        for part in (0, 1)
    ]
    pl.semaphore_wait(plane_ready, 4)
    for da in (2, 1, -1, 0):
        for reducer in reducers:
            reducer.step_far(da)
    score_out_ref[me] = score_send[me]
    score_copies = []
    for step in range(1, PLANE):
        to = lax.rem(me + step, PLANE)
        copy = plane_copy(
            score_send.at[to], score_out_ref.at[me], score_ssem.at[step], score_rsem.at[step], to
        )
        copy.start()
        score_copies.append(copy)

    def grad_tile(expert, tile):
        columns = pl.ds((tile % 4) * BLOCK, BLOCK)
        if tile < 4:
            return dot_tn(kept_rows[expert, :, columns], kept_pairs[expert])
        return dot_tn(kept_hidden[expert, :, columns], kept_grads[expert])

    def pair_copy(tile):
        return pltpu.make_async_remote_copy(
            src_ref=cots.at[tile // GROUP, tile % GROUP],
            dst_ref=from_pair.at[tile],
            send_sem=pair_send.at[tile],
            recv_sem=pair_recv.at[tile],
            device_id={"exp": other},
            device_id_type=MESH,
        )

    for tile in range(6):
        cots[tile // GROUP, tile % GROUP] = grad_tile(other, tile).astype(BF)
        pair_copy(tile).start()
        if tile == 3:
            for reducer in reducers:
                reducer.step_near(2)
    for reducer in reducers:
        reducer.step_near(1)
    for tile in range(6):
        value = grad_tile(core, tile)
        pair_copy(tile).wait()
        weights[pl.ds(tile * BLOCK, BLOCK), :] = (value + from_pair[tile].astype(F32)).astype(BF)
        if tile == 2:
            for reducer in reducers:
                reducer.step_near(-1)
    pl.semaphore_wait(line_ready, 2)
    ring = RowRing(
        weights.at[pl.ds(0, WIDTH + INNER)],
        FlatRows(weights, 1536, (2,), 192),
        FlatRows(weights, 1920, (2,), 384),
        ring_send,
        ring_recv,
    )
    ring.step_far()
    for reducer in reducers:
        reducer.step_near(0)
    for reducer in reducers:
        reducer.step_sum(2)
    ring.step_near()
    for da in (1, -1):
        for reducer in reducers:
            reducer.step_sum(da)
    ring.step_sum()
    store = pltpu.make_async_copy(ring.piece(ring.summed, 0), grad_ref, local_sems.at[0])
    store.start()
    for reducer in reducers:
        reducer.step_sum(0)
    for reducer in reducers:
        reducer.finish()
    for copy in score_copies:
        copy.wait()
    for j in range(GROUP):
        moe_copy(j, j).wait()
    ring.finish()
    store.wait()


def step_table(steps):
    return sum(step * 4**i for i, step in enumerate(steps))


ROW_STEPS = step_table((1, 3, 0, 0, 2, 0, 1, 1, 3, 3, 2, 2, 1, 3, 2))
COLUMN_STEPS = step_table((0, 0, 1, 3, 0, 2, 1, 3, 1, 3, 1, 3, 2, 2, 2))


def run_experts(rows, meta, cots, expert_in, expert_out, sib_in, sib_out):
    vmem = pl.BlockSpec(memory_space=pltpu.VMEM)
    hbm = pl.BlockSpec(memory_space=pl.ANY)
    dma = pltpu.SemaphoreType.DMA
    slots = GROUP * CAPACITY
    every = PLANE * CAPACITY
    return pl.pallas_call(
        expert_kernel,
        out_shape=(
            jax.ShapeDtypeStruct((BLOCK, WIDTH), F32),
            jax.ShapeDtypeStruct((PLANE, 8, BLOCK), F32),
            jax.ShapeDtypeStruct((PLANE, BLOCK, WIDTH), BF),
            jax.ShapeDtypeStruct(((WIDTH + INNER) // 4, WIDTH), BF),
        ),
        in_specs=[vmem, vmem, hbm, hbm, hbm, hbm, hbm],
        out_specs=(vmem, vmem, hbm, hbm),
        scratch_shapes=[
            pltpu.VMEM((PLANE * BLOCK, WIDTH), BF),
            pltpu.VMEM((PLANE, 8, BLOCK), F32),
            pltpu.VMEM((PLANE, 8, BLOCK), F32),
            pltpu.VMEM((2, GROUP, BLOCK, WIDTH), BF),
            pltpu.VMEM((2 * (WIDTH + INNER), WIDTH), BF),
            pltpu.VMEM((2, every, WIDTH), BF),
            pltpu.VMEM((2, every, WIDTH), BF),
            pltpu.VMEM((2, every, INNER), BF),
            pltpu.VMEM((2, every, 2 * INNER), BF),
            pltpu.VMEM((PLANE, BLOCK, WIDTH), BF),
            pltpu.VMEM((GROUP, BLOCK, WIDTH), BF),
            pltpu.VMEM((GROUP, 2 * CAPACITY, BLOCK), BF),
            pltpu.VMEM((2, slots, WIDTH), BF),
            pltpu.VMEM((GROUP, 2 * CAPACITY, 2 * WIDTH), BF),
            pltpu.VMEM((2, 3, HALF, WIDTH), BF),
            pltpu.VMEM((6, BLOCK, WIDTH), BF),
        ]
        + [dma((40,))] * 4
        + [dma((PLANE,))] * 4
        + [dma((4,)), dma((2, GROUP)), dma((GROUP,))]
        + [dma((6,))] * 2
        + [dma((4,))] * 2
        + [pltpu.SemaphoreType.REGULAR] * 2,
        compiler_params=pltpu.CompilerParams(
            collective_id=2, has_side_effects=True, vmem_limit_bytes=VMEM_LIMIT
        ),
    )(rows, meta, cots, expert_in, expert_out, sib_in, sib_out)


VMEM_LIMIT = 63 << 20


def rope_lanes(values, cosine, sine):
    lane = lax.broadcasted_iota(jnp.int32, (1, 128), 1)
    lower = lax.rem(lane, 64) < 32
    chunks = []
    for begin in range(0, values.shape[1], 128):
        chunk = values[:, begin : begin + 128]
        partner = jnp.where(lower, pltpu.roll(chunk, 96, 1), pltpu.roll(chunk, 32, 1))
        chunks.append(chunk * cosine + partner * sine)
    return chunks


def norm_scale(values):
    return lax.rsqrt(jnp.mean(values * values, axis=1, keepdims=True) + EPSILON)


def slot_table(routes, ranks):
    routes, ranks = routes.astype(F32).T, ranks.astype(F32).T
    expert = lax.broadcasted_iota(jnp.int32, (BLOCK, 32), 1).astype(F32)
    rank_of = jnp.zeros((BLOCK, 32), F32)
    for k in range(8):
        rank_of = rank_of + jnp.where(
            routes[:, k : k + 1] == expert, ranks[:, k : k + 1] + 1.0, 0.0
        )
    chosen = rank_of > 0.0
    row = lax.broadcasted_iota(jnp.int32, (BLOCK, BLOCK), 0)
    lane = lax.broadcasted_iota(jnp.int32, (BLOCK, BLOCK), 1)
    source = lax.broadcasted_iota(jnp.int32, (32, BLOCK), 0)
    target = lax.broadcasted_iota(jnp.int32, (32, BLOCK), 1)
    repeat = jnp.where(lax.rem(target, 32) == source, 1.0, 0.0).astype(BF)
    rank_wide = dot_nn(rank_of.astype(BF), repeat)
    hit = rank_wide == (lane // 32 + 1).astype(F32)
    counts = jnp.where(hit, 1.0, 0.0)
    earlier = jnp.where(row > lane, 1.0, 0.0).astype(BF)
    before = dot_nn(earlier, counts.astype(BF))
    totals = jnp.sum(counts, axis=0, keepdims=True)
    lower = (lax.rem(row, 32) == lax.rem(lane, 32)) & (row // 32 < lane // 32)
    offsets = dot_nn(totals.astype(BF), jnp.where(lower, 1.0, 0.0).astype(BF))
    place = jnp.where(hit, before + offsets, 0.0)
    place = place[:, :128] + place[:, 128:]
    place = place + pltpu.roll(place, 64, 1)
    place = place + pltpu.roll(place, 32, 1)
    place = place[:, :32]
    return chosen, jnp.where(chosen & (place < CAPACITY), place, -1.0)


def attend_kernel(
    tokens_ref,
    seg_ref,
    routes_ref,
    ranks_ref,
    gain_one_ref,
    w_query_far,
    w_key_far,
    w_value_far,
    w_output_far,
    gain_two_ref,
    w_router_ref,
    table_ref,
    cot_ref,
    w_in_ref,
    w_out_ref,
    routed_ref,
    residual_ref,
    heads_ref,
    normed_far,
    query_far,
    kv_far,
    lse_ref,
    bias_far,
    gates_ref,
    meta_ref,
    cots_ref,
    sib_in_ref,
    sib_out_ref,
    cots,
    table,
    kv_relay,
    segs,
    top,
    acc,
    send_sems,
    recv_sems,
    kv_send,
    kv_recv,
    seg_send,
    seg_recv,
    weight_send,
    weight_recv,
    local_sems,
    store_sems,
    w_query_ref,
    w_key_ref,
    w_value_ref,
    w_output_ref,
    normed_ref,
    query_ref,
    kv_ref,
    bias_ref,
    load_sems,
    out_sems,
):
    loads = [
        pltpu.make_async_copy(source, target, load_sems.at[i])
        for i, (source, target) in enumerate(
            (
                (w_key_far, w_key_ref),
                (w_value_far, w_value_ref),
                (w_query_far, w_query_ref),
                (w_output_far, w_output_ref),
            )
        )
    ]
    for load in loads:
        load.start()
    stores = [
        pltpu.make_async_copy(source, target, out_sems.at[i])
        for i, (source, target) in enumerate(
            (
                (normed_ref, normed_far),
                (query_ref, query_far),
                (kv_ref, kv_far),
                (bias_ref, bias_far),
            )
        )
    ]
    line, plane, core = lax.axis_index("seq"), lax.axis_index("grp"), lax.axis_index("exp")
    block = 2 * line + core
    row, column = plane // 4, lax.rem(plane, 4)
    barrier = pltpu.get_barrier_semaphore()
    for index in (
        mod4(row + 1) * 4 + column,
        mod4(row - 1) * 4 + column,
        row * 4 + mod4(column + 1),
        row * 4 + mod4(column - 1),
    ):
        pl.semaphore_signal(barrier, inc=1, device_id={"grp": index}, device_id_type=MESH)
    for step in (1, 2, 3):
        pl.semaphore_signal(
            barrier, inc=1, device_id={"seq": mod4(line + step)}, device_id_type=MESH
        )
    pl.semaphore_signal(barrier, inc=1, device_id={"exp": 1 - core}, device_id_type=MESH)
    own_cot = pltpu.make_async_copy(
        cot_ref, cots.at[pl.ds(pl.multiple_of(plane * BLOCK, BLOCK), BLOCK)], local_sems.at[0]
    )
    own_cot.start()
    load_table = pltpu.make_async_copy(table_ref.at[block], table, local_sems.at[1])
    load_table.start()
    own_cot.wait()
    pl.semaphore_wait(barrier, 8)
    gathers = [PlaneGather(part, cots, send_sems, recv_sems) for part in (0, 1)]
    for gather in gathers:
        gather.begin()
    for gather in gathers:
        gather.spread(0)

    tokens = tokens_ref[...].astype(F32)
    normed = (tokens * norm_scale(tokens) * gain_one_ref[...]).astype(BF)
    normed_ref[...] = normed
    stores[0].start()
    load_table.wait()
    cosine, sine = table[0], table[1]
    loads[0].wait()
    loads[1].wait()
    keys = dot_nn(normed, w_key_ref[...])
    values = dot_nn(normed, w_value_ref[...]).astype(BF)
    key_chunks = rope_lanes(keys, cosine, sine)
    for head in range(KV_HEADS):
        chunk = key_chunks[head // 2].astype(BF)
        key = chunk[:, (head % 2) * 64 : (head % 2) * 64 + 64]
        kv_ref[0, head] = jnp.concatenate([key, values[:, head * 64 : head * 64 + 64]], axis=1)
    seg_tile = jnp.broadcast_to(seg_ref[...].astype(F32), (8, BLOCK))
    segs[0] = seg_tile

    def kv_copies(source, target, device, slot):
        return [
            pltpu.make_async_remote_copy(
                src_ref=ref.at[source],
                dst_ref=ref.at[target],
                send_sem=sends.at[slot],
                recv_sem=recvs.at[target],
                device_id=device,
                device_id_type=MESH,
            )
            for ref, sends, recvs in ((kv_ref, kv_send, kv_recv), (segs, seg_send, seg_recv))
        ]

    def relay_copies(device, to_relay):
        pairs = (
            (kv_ref, kv_relay, 4, kv_send, kv_recv),
            (segs, segs.at[5], 4, seg_send, seg_recv),
        )
        copies = []
        for ref, held, slot, sends, recvs in pairs:
            source, target = (ref.at[0], held) if to_relay else (held, ref.at[slot])
            copies.append(
                pltpu.make_async_remote_copy(
                    src_ref=source,
                    dst_ref=target,
                    send_sem=sends.at[2 if to_relay else 5],
                    recv_sem=recvs.at[5 if to_relay else 4],
                    device_id=device,
                    device_id_type=MESH,
                )
            )
        return copies

    sibling = {"exp": 1 - core}
    to_near = kv_copies(0, 2, {"seq": mod4(line + 1)}, 1)
    to_relay = relay_copies({"seq": mod4(line - 1)}, True)
    from_relay = relay_copies({"seq": mod4(line - 1)}, False)
    to_sibling = kv_copies(0, 1, sibling, 0)
    forward_near = kv_copies(2, 3 - 2 * core, sibling, 3)
    forward_far = kv_copies(4, 3, sibling, 4)

    def begin(copies):
        for copy in copies:
            copy.start()

    def sent(copies):
        for copy in copies:
            copy.wait_send()

    @pl.when(line < 3)
    def _():
        begin(to_near)

    @pl.when(core == 0)
    def _():
        begin(to_sibling)

    @pl.when(line < 2)
    def _():
        begin(to_relay)

    for gather in gathers:
        gather.forward_first()
        gather.spread(-1)
        gather.spread(1)
    weight_copies = [
        pltpu.make_async_remote_copy(
            src_ref=source,
            dst_ref=target,
            send_sem=weight_send.at[slot],
            recv_sem=weight_recv.at[slot],
            device_id=sibling,
            device_id_type=MESH,
        )
        for slot, (source, target) in enumerate(((w_in_ref, sib_in_ref), (w_out_ref, sib_out_ref)))
    ]
    begin(weight_copies)

    lane = lax.broadcasted_iota(jnp.int32, (1, 128), 1)
    loads[2].wait()
    queries = dot_nn(normed, w_query_ref[...])
    for head, chunk in enumerate(rope_lanes(queries, cosine, sine)):
        chunk = (chunk.astype(BF).astype(F32) * ATTENTION_FACTOR)
        query_ref[head, :BLOCK, :] = jnp.where(lane < 64, chunk, 0.0).astype(BF)
        query_ref[head, BLOCK:, :] = jnp.where(lane < 64, pltpu.roll(chunk, 64, 1), 0.0).astype(BF)
    stores[1].start()
    top[...] = jnp.full(top.shape, MASKED, F32)
    acc[...] = jnp.zeros(acc.shape, F32)

    def attend(slot):
        j = lax.broadcasted_iota(jnp.int32, (BLOCK, BLOCK), 0)
        i = lax.broadcasted_iota(jnp.int32, (BLOCK, BLOCK), 1)
        distance = slot * BLOCK + i - j
        same = segs[slot].T[:, :1] == seg_tile[:1, :]
        allowed = same & (distance >= 0) & (distance < WINDOW)
        bias_ref[slot] = jnp.where(allowed, 0.0, MASKED).astype(BF)

        @pl.loop(0, KV_HEADS, unroll=4)
        def _(head):
            pair = kv_ref[slot, head]
            one = bias_ref[slot].astype(F32)
            score = dot_nt(pair, query_ref[head]) + jnp.concatenate([one, one], axis=1)
            old = top[pl.ds(head, 1), :]
            new = jnp.maximum(old, jnp.max(score, axis=0, keepdims=True))
            weight = jnp.exp(score - new).astype(BF)
            fade = jnp.exp(old - new)
            summing = jnp.where(lane < 64, 1.0, pair.astype(F32)).astype(BF)
            acc[head] = acc[head] * fade + dot_tn(summing, weight)
            top[pl.ds(head, 1), :] = new

    def wait_block(slot):
        for ref, sends, recvs in ((kv_ref, kv_send, kv_recv), (segs, seg_send, seg_recv)):
            pltpu.make_async_remote_copy(
                src_ref=ref.at[slot],
                dst_ref=ref.at[slot],
                send_sem=sends.at[0],
                recv_sem=recvs.at[slot],
                device_id=sibling,
                device_id_type=MESH,
            ).wait_recv()

    attend(0)
    for gather in gathers:
        gather.forward_second(0)
    for gather in gathers:
        gather.wait_far_first()
        gather.spread(2)

    @pl.when((line == 0) | (line == 3))
    def _():
        for arrival, copy in zip(to_relay, from_relay):
            arrival.wait_recv()
            copy.start()

    chosen, kept = slot_table(routes_ref[...], ranks_ref[...])
    kept_rows = jnp.concatenate([kept, jnp.zeros((BLOCK, 96), F32)], axis=1).T
    for index in range(PLANE):
        meta_ref[index, 0:2, :] = kept_rows[2 * index : 2 * index + 2]
        meta_ref[index, 4:8, :] = jnp.zeros((4, BLOCK), F32)

    first = 2 - core

    @pl.when(block >= first)
    def _():
        wait_block(first)

        @pl.when(core == 0)
        def _():
            begin(forward_near)

        attend(first)

    for da in (-1, 1):
        for gather in gathers:
            gather.forward_second(da)
    second = 1 + core

    @pl.when(block >= second)
    def _():
        wait_block(second)

        @pl.when(core == 1)
        def _():
            begin(forward_near)

        attend(second)

    for gather in gathers:
        gather.forward_second(2)
    third = 4 - core

    @pl.when(block >= third)
    def _():
        wait_block(third)
        attend(third)

    fourth = 3 + core

    @pl.when(block >= fourth)
    def _():
        wait_block(fourth)

        @pl.when(core == 1)
        def _():
            begin(forward_far)

        attend(fourth)

    stores[2].start()
    stores[3].start()
    loads[3].wait()

    def store_cots(part, da, db):
        gather = gathers[part]
        index = plane_id(part, mod4(gather.first + da), mod4(gather.second + db))
        begin = pl.ds(pl.multiple_of(index * BLOCK + part * HALF, HALF), HALF)
        return pltpu.make_async_copy(
            cots.at[begin], cots_ref.at[begin], store_sems.at[part, da % 4, db % 4]
        )

    for part in (0, 1):
        for da in (0, -1, 1, 2):
            for db in (0, -1, 1):
                store_cots(part, da, db).start()
    for head in range(KV_HEADS):
        both = acc[head]
        expsum = both[:1, :]
        pair = (both * (1.0 / expsum)).T
        heads_ref[:, head * 128 : head * 128 + 128] = jnp.where(
            lane < 64, pltpu.roll(pair[:BLOCK], 64, 1), pair[BLOCK:]
        ).astype(BF)
        lse_ref[head : head + 1, :] = top[head : head + 1, :] + jnp.log(expsum)
    branch = dot_nn(heads_ref[...], w_output_ref[...])
    residual = tokens_ref[...].astype(F32) + RESIDUAL_MULT * branch
    residual_ref[...] = residual
    routed = (residual * norm_scale(residual) * gain_two_ref[...]).astype(BF)
    routed_ref[...] = routed
    logits = dot_nt(routed, w_router_ref[...])
    logits = jnp.where(chosen, logits, MASKED)
    powers = jnp.exp(logits - jnp.max(logits, axis=1, keepdims=True))
    gates = jnp.where(chosen, powers / jnp.sum(powers, axis=1, keepdims=True), 0.0)
    gates_ref[...] = gates
    gate_rows = jnp.concatenate([gates, jnp.zeros((BLOCK, 96), F32)], axis=1).T
    for index in range(PLANE):
        meta_ref[index, 2:4, :] = gate_rows[2 * index : 2 * index + 2]

    for da in (0, -1, 1, 2):
        for gather in gathers:
            gather.wait_far_second(da)
    for da in (0, -1, 1, 2):
        for part in (0, 1):
            store_cots(part, da, 2).start()
    for gather in gathers:
        gather.finish()
    for copy in weight_copies:
        copy.wait()

    @pl.when(line < 3)
    def _():
        sent(to_near)

    @pl.when(core == 0)
    def _():
        sent(to_sibling)

    @pl.when(line < 2)
    def _():
        sent(to_relay)

    @pl.when((line == 0) | (line == 3))
    def _():
        sent(from_relay)

    @pl.when(line >= 1)
    def _():
        sent(forward_near)

    for store in stores:
        store.wait()
    for part in (0, 1):
        for da in (0, -1, 1, 2):
            for db in (0, -1, 1, 2):
                store_cots(part, da, db).wait()

    @pl.when((line >= 2) & (core == 1))
    def _():
        sent(forward_far)


def run_attention(
    tokens, seg_tile, routes, ranks, gain_one, w_query, w_key, w_value, w_output, gain_two,
    w_router, table, cot, expert_in, expert_out,
):
    vmem = pl.BlockSpec(memory_space=pltpu.VMEM)
    hbm = pl.BlockSpec(memory_space=pl.ANY)
    dma = pltpu.SemaphoreType.DMA
    shape = jax.ShapeDtypeStruct
    return pl.pallas_call(
        attend_kernel,
        out_shape=(
            shape((BLOCK, WIDTH), BF),
            shape((BLOCK, WIDTH), F32),
            shape((BLOCK, WIDTH), BF),
            shape((BLOCK, WIDTH), BF),
            shape((KV_HEADS, 2 * BLOCK, 128), BF),
            shape((5, KV_HEADS, BLOCK, 128), BF),
            shape((KV_HEADS, 2 * BLOCK), F32),
            shape((5, BLOCK, BLOCK), BF),
            shape((BLOCK, 32), F32),
            shape((PLANE, 8, BLOCK), F32),
            shape((PLANE * BLOCK, WIDTH), BF),
            shape((WIDTH, 2 * INNER), BF),
            shape((INNER, WIDTH), BF),
        ),
        in_specs=[vmem] * 5 + [hbm] * 4 + [vmem] * 2 + [hbm] * 4,
        out_specs=(vmem,) * 3 + (hbm,) * 3 + (vmem, hbm, vmem, vmem) + (hbm,) * 3,
        scratch_shapes=[
            pltpu.VMEM((PLANE * BLOCK, WIDTH), BF),
            pltpu.VMEM((2, BLOCK, 128), F32),
            pltpu.VMEM((KV_HEADS, BLOCK, 128), BF),
            pltpu.VMEM((6, 8, BLOCK), F32),
            pltpu.VMEM((KV_HEADS, 2 * BLOCK), F32),
            pltpu.VMEM((KV_HEADS, 128, 2 * BLOCK), F32),
            dma((40,)),
            dma((40,)),
            dma((6,)),
            dma((6,)),
            dma((6,)),
            dma((6,)),
            dma((2,)),
            dma((2,)),
            dma((2,)),
            dma((2, 4, 4)),
            pltpu.VMEM((WIDTH, WIDTH), BF),
            pltpu.VMEM((WIDTH, 512), BF),
            pltpu.VMEM((WIDTH, 512), BF),
            pltpu.VMEM((WIDTH, WIDTH), BF),
            pltpu.VMEM((BLOCK, WIDTH), BF),
            pltpu.VMEM((KV_HEADS, 2 * BLOCK, 128), BF),
            pltpu.VMEM((5, KV_HEADS, BLOCK, 128), BF),
            pltpu.VMEM((5, BLOCK, BLOCK), BF),
            dma((4,)),
            dma((4,)),
        ],
        compiler_params=pltpu.CompilerParams(
            collective_id=0, has_side_effects=True, vmem_limit_bytes=58 << 20
        ),
    )(
        tokens, seg_tile, routes, ranks, gain_one, w_query, w_key, w_value, w_output, gain_two,
        w_router, table, cot, expert_in, expert_out,
    )


def backward_kernel(
    tokens_far,
    residual_ref,
    scores_ref,
    gates_ref,
    routed_ref,
    heads_ref,
    normed_far,
    query_far,
    kv_far,
    bias_far,
    w_key_far,
    w_value_far,
    w_router_ref,
    gain_one_ref,
    gain_two_ref,
    lse_ref,
    table_ref,
    partial_ref,
    grad_ref,
    row_total_ref,
    w_query_ref,
    w_output_ref,
    cot_ref,
    output_ref,
    input_grad_ref,
    trio_out_ref,
    output_w_ref,
    small_out_ref,
    gain_out_ref,
    grad_total_ref,
    table,
    partial,
    far,
    near,
    summed,
    far_two,
    near_two,
    moe_total,
    delta,
    head_grads,
    query_grads,
    own_grads,
    stage,
    from_pair,
    from_near,
    from_far,
    residual_grad,
    weight,
    wide,
    staged,
    arrived,
    mat_out,
    mat_one,
    mat_two,
    mat_three,
    cube_far,
    cube_near,
    cube_mid,
    cube_low,
    one_far,
    one_near,
    one_mid,
    one_low,
    two_far,
    two_near,
    two_mid,
    two_low,
    three_far,
    three_near,
    three_mid,
    three_low,
    small_own,
    small_first,
    small,
    gain_own,
    gain_first,
    gain,
    send_sems,
    recv_sems,
    ring_send,
    ring_recv,
    kv_send,
    kv_recv,
    local_sems,
    cube_send,
    cube_recv,
    core_send,
    core_recv,
    small_send,
    small_recv,
    tokens_ref,
    normed_ref,
    query_ref,
    kv_ref,
    bias_ref,
    w_key_ref,
    w_value_ref,
    load_sems,
):
    loads = [
        pltpu.make_async_copy(source, target, load_sems.at[i])
        for i, (source, target) in enumerate(
            (
                (query_far, query_ref),
                (kv_far, kv_ref),
                (bias_far, bias_ref),
                (normed_far, normed_ref),
                (w_key_far, w_key_ref),
                (w_value_far, w_value_ref),
                (tokens_far, tokens_ref),
            )
        )
    ]
    line, plane, core = lax.axis_index("seq"), lax.axis_index("grp"), lax.axis_index("exp")
    block = 2 * line + core
    row, column = plane // 4, lax.rem(plane, 4)
    load = pltpu.make_async_copy(partial_ref, partial, local_sems.at[1])
    load_table = pltpu.make_async_copy(table_ref.at[block], table, local_sems.at[3])
    load_table.start()
    load.start()
    other = 1 - core
    places = (line, row, column)

    def neighbour(axis, step):
        if axis == 0:
            return {"seq": mod4(line + step)}
        if axis == 1:
            return {"grp": mod4(row + step) * 4 + column}
        return {"grp": row * 4 + mod4(column + step)}

    barrier = pltpu.get_barrier_semaphore()
    for axis in range(3):
        for step in (1, 2, 3):
            pl.semaphore_signal(
                barrier, inc=1, device_id=neighbour(axis, step), device_id_type=MESH
            )
    pl.semaphore_signal(barrier, inc=1, device_id={"exp": other}, device_id_type=MESH)
    load_rows = pltpu.make_async_copy(row_total_ref, moe_total, local_sems.at[2])
    load_rows.start()
    for later in loads:
        later.start()
    load_cot = pltpu.make_async_copy(cot_ref, wide, local_sems.at[5])
    load_cot.start()
    load_output = pltpu.make_async_copy(w_output_ref, weight, local_sems.at[4])
    load_output.start()
    load_query = pltpu.make_async_copy(w_query_ref, weight, local_sems.at[4])
    pl.semaphore_wait(barrier, 10)
    buffers = (far, near, summed, far_two, near_two)
    reducers = [
        PlaneReduce(part, partial, buffers, send_sems, recv_sems, moe_total) for part in (0, 1)
    ]
    spread = RowSpread(grad_ref, grad_total_ref, ring_send, ring_recv, local_sems.at[0])
    spread.begin()
    load.wait()
    for da in (2, 1, -1, 0):
        for reducer in reducers:
            reducer.step_far(da)

    def to_core(source, target, slot):
        return pltpu.make_async_remote_copy(
            src_ref=source,
            dst_ref=target,
            send_sem=core_send.at[slot],
            recv_sem=core_recv.at[slot],
            device_id={"exp": other},
            device_id_type=MESH,
        )

    cube_out = CubeSum(
        1, mat_out, output_w_ref, core * 512, other * 512, (cube_far, cube_near, cube_mid, cube_low),
        cube_send.at[0], cube_recv.at[0],
    )
    trio = [
        CubeSum(
            part, matrix, trio_out_ref, core * WIDTH + shift, other * WIDTH + shift, buffers,
            cube_send.at[1 + i], cube_recv.at[1 + i],
        )
        for i, (part, matrix, shift, buffers) in enumerate(
            (
                (0, mat_one, 0, (one_far, one_near, one_mid, one_low)),
                (1, mat_two, 384, (two_far, two_near, two_mid, two_low)),
                (2, mat_three, 768, (three_far, three_near, three_mid, three_low)),
            )
        )
    ]
    cubes = [cube_out] + trio

    def each(step):
        for cube in trio:
            getattr(cube, step)()

    own_small = pl.ds(pl.multiple_of(core * SMALL_ROWS, 16), SMALL_ROWS)
    other_small = pl.ds(pl.multiple_of(other * SMALL_ROWS, 16), SMALL_ROWS)
    share_out = to_core(weight.at[:, pl.ds(0, 512)], arrived.at[0], 0)
    share_query = to_core(staged, arrived.at[1], 1)
    share_pair = to_core(staged, arrived.at[2], 2)
    share_small = to_core(small_own.at[other_small], small_first, 3)
    share_total = to_core(small_out_ref.at[own_small], small_out_ref.at[own_small], 4)
    share_gain = to_core(gain_own, gain_first, 5)

    def axis_copy(held, base, axis, step):
        ref = held.at[axis, places[axis]]
        return pltpu.make_async_remote_copy(
            src_ref=ref,
            dst_ref=ref,
            send_sem=small_send.at[base + axis, step],
            recv_sem=small_recv.at[base + axis, step],
            device_id=neighbour(axis, step),
            device_id_type=MESH,
        )

    def axis_begin(held, base, axis):
        for step in (1, 2, 3):
            axis_copy(held, base, axis, step).start()

    def axis_sum(held, base, axis):
        for step in (1, 2, 3):
            ref = held.at[axis, mod4(places[axis] - step)]
            pltpu.make_async_remote_copy(
                src_ref=ref,
                dst_ref=ref,
                send_sem=small_send.at[base + axis, step],
                recv_sem=small_recv.at[base + axis, step],
                device_id=neighbour(axis, step),
                device_id_type=MESH,
            ).wait_recv()
        parts = [held[axis, i].astype(F32) for i in range(4)]
        return (parts[0] + parts[1]) + (parts[2] + parts[3])

    lane = lax.broadcasted_iota(jnp.int32, (1, 128), 1)
    lower = lane < 64
    gate_grad = jnp.concatenate(
        [scores_ref[index, 0:2, :] for index in range(PLANE)] + [jnp.zeros((96, BLOCK), F32)], axis=0
    ).T[:, :32]
    gates = gates_ref[...]
    choice_grad = gates * (gate_grad - jnp.sum(gates * gate_grad, axis=1, keepdims=True))
    logit_grad = choice_grad.astype(BF)
    small_own[...] = dot_tn(logit_grad, routed_ref[...]).astype(BF)
    share_small.start()
    gain_own[...] = jnp.zeros((8, WIDTH), F32)
    load_rows.wait()
    routed_grad = dot_nn(logit_grad, w_router_ref[...]) + moe_total[...]
    residual = residual_ref[...]
    scale_two = norm_scale(residual)
    gain_own[1:2, :] = jnp.sum(routed_grad * residual * scale_two, axis=0, keepdims=True)
    weighted = routed_grad * gain_two_ref[...]
    shared = scale_two * scale_two * scale_two * jnp.mean(weighted * residual, axis=1, keepdims=True)
    load_cot.wait()
    grown = wide[...].astype(F32) + scale_two * weighted - residual * shared
    residual_grad[...] = grown
    branch_grad = (RESIDUAL_MULT * grown).astype(BF)
    wide[...] = branch_grad
    load_output.wait()
    head_grad = dot_nt(branch_grad, weight[...]).astype(BF)
    for head in range(KV_HEADS):
        chunk = head_grad[:, head * 128 : head * 128 + 128].astype(F32)
        result = heads_ref[:, head * 128 : head * 128 + 128].astype(F32)
        head_grads[head, :BLOCK, :] = jnp.where(lower, 0.0, pltpu.roll(chunk, 64, 1)).astype(BF)
        head_grads[head, BLOCK:, :] = jnp.where(lower, 0.0, chunk).astype(BF)
        both = (chunk * result).T
        delta[head : head + 1, :BLOCK] = jnp.sum(both[:64], axis=0, keepdims=True)
        delta[head : head + 1, BLOCK:] = jnp.sum(both[64:], axis=0, keepdims=True)
    query_grads[...] = jnp.zeros(query_grads.shape, F32)

    for begin in (0, 256):
        columns = pl.ds(pl.multiple_of(core * 512 + begin, 256), 256)
        mat_out[:, begin : begin + 256] = dot_tn(heads_ref[...], wide[:, columns]).astype(BF)
    for begin in (0, 256):
        columns = pl.ds(pl.multiple_of(other * 512 + begin, 256), 256)
        weight[:, begin : begin + 256] = dot_tn(heads_ref[...], wide[:, columns]).astype(BF)
    share_out.start()

    def join(matrix, slot, place, begin, width):
        here = slice(place, place + width)
        matrix[:, here] = (
            matrix[:, here].astype(F32) + arrived[slot, :, begin : begin + width].astype(F32)
        ).astype(BF)

    own = 0

    def attend_back(slot):
        @pl.loop(0, KV_HEADS, unroll=2)
        def _(head):
            pair, query, out_grad = kv_ref[slot, head], query_ref[head], head_grads[head]
            one = bias_ref[slot].astype(F32)
            score = dot_nt(pair, query) + jnp.concatenate([one, one], axis=1)
            prob = jnp.exp(score - lse_ref[pl.ds(head, 1), :])
            prob_grad = dot_nt(pair, out_grad)
            score_grad = (prob * (prob_grad - delta[pl.ds(head, 1), :])).astype(BF)
            query_grads[head] += dot_tn(pair, score_grad)
            pair_grad = dot_nn(score_grad, query) + dot_nn(prob.astype(BF), out_grad)
            own_grads[head] = pair_grad
            if slot is not own:
                stage[slot - 1, head] = pair_grad.astype(BF)

    sibling = {"exp": 1 - core}

    def kv_copy(source, target, device, slot):
        return pltpu.make_async_remote_copy(
            src_ref=source,
            dst_ref=target,
            send_sem=kv_send.at[slot],
            recv_sem=kv_recv.at[slot],
            device_id=device,
            device_id_type=MESH,
        )

    pair_three = kv_copy(stage.at[2], from_pair.at[0], sibling, 0)
    pair_one = kv_copy(stage.at[0], from_pair.at[1], sibling, 1)
    to_near = kv_copy(stage.at[1], from_near, {"seq": mod4(line - 1)}, 2)
    to_far = kv_copy(stage.at[3], from_far, {"seq": mod4(line - 1)}, 3)

    def take_pair(three, slot):
        source = from_pair.at[0 if three else 1]
        kv_copy(source, source, sibling, 0 if three else 1).wait_recv()
        for head in range(KV_HEADS):
            stage[slot - 1, head] = (
                stage[slot - 1, head].astype(F32) + source[head].astype(F32)
            ).astype(BF)

    def take_far():
        @pl.when(line <= 2)
        def _():
            kv_copy(from_far, from_far, sibling, 3).wait_recv()
            for head in range(KV_HEADS):
                stage[1, head] = (
                    stage[1, head].astype(F32) + from_far[head].astype(F32)
                ).astype(BF)

    for later in loads[:3]:
        later.wait()
    first, second, third, fourth = 3 + core, 4 - core, 1 + core, 2 - core

    @pl.when(block >= first)
    def _():
        attend_back(first)

    @pl.when((core == 0) & (line >= 2))
    def _():
        pair_three.start()

    for reducer in reducers:
        reducer.step_near(2)
        reducer.step_near(1)
    share_out.wait_recv()
    join(mat_out, 0, 0, 0, 512)
    cube_out.step_far()
    share_small.wait_recv()
    small[0, line] = (small_own[own_small, :].astype(F32) + small_first[...].astype(F32)).astype(BF)
    axis_begin(small, 0, 0)

    @pl.when((core == 1) & (line >= 2))
    def _():
        take_pair(True, 4)
        to_far.start()

    @pl.when(block >= second)
    def _():
        attend_back(second)

    @pl.when((core == 1) & (line >= 1))
    def _():
        pair_three.start()

    @pl.when((core == 0) & (line >= 2))
    def _():
        to_far.start()

    spread.forward()

    for reducer in reducers:
        reducer.step_near(-1)
        reducer.step_near(0)
    cube_out.step_near()

    @pl.when(block >= third)
    def _():
        attend_back(third)

    @pl.when((core == 0) & (line >= 1))
    def _():
        pair_one.start()

    for reducer in reducers:
        reducer.step_sum(2)
    small[1, row] = axis_sum(small, 0, 0).astype(BF)
    axis_begin(small, 0, 1)
    cube_out.ring_far()
    share_out.wait_send()
    load_query.start()

    @pl.when((core == 1) & (line >= 1))
    def _():
        take_pair(False, 2)
        take_far()
        to_near.start()

    @pl.when(block >= fourth)
    def _():
        attend_back(fourth)

    @pl.when(core == 1)
    def _():
        pair_one.start()

    @pl.when((core == 0) & (line >= 1))
    def _():
        take_pair(True, 2)
        take_far()
        to_near.start()

    for reducer in reducers:
        reducer.step_sum(1)
        reducer.step_sum(-1)
    small[2, column] = axis_sum(small, 0, 1).astype(BF)
    axis_begin(small, 0, 2)
    cube_out.ring_near()
    attend_back(own)

    for later in loads[3:]:
        later.wait()
    load_table.wait()
    cosine, sine = table[0], table[1]
    normed = normed_ref[...]
    query_chunks = []
    for head in range(KV_HEADS):
        both = query_grads[head].T
        chunk = jnp.where(lower, both[:BLOCK], pltpu.roll(both[BLOCK:], 64, 1))
        query_chunks.append(chunk * ATTENTION_FACTOR)
    query_pre_grad = jnp.concatenate(
        rope_lanes(jnp.concatenate(query_chunks, axis=1), cosine, -sine), axis=1
    ).astype(BF)
    wide[...] = query_pre_grad
    for begin in (0, 256):
        columns = pl.ds(pl.multiple_of(other * 512 + begin, 256), 256)
        staged[:, begin : begin + 256] = dot_tn(normed, wide[:, columns]).astype(BF)
    share_query.start()
    for begin in (0, 256):
        columns = pl.ds(pl.multiple_of(core * 512 + begin, 256), 256)
        value = dot_tn(normed, wide[:, columns]).astype(BF)
        if begin == 0:
            mat_one[:, 0:256] = value
        else:
            mat_one[:, 256:384] = value[:, :128]
            mat_two[:, 0:128] = value[:, 128:]
    cube_out.ring_low()
    load_query.wait()
    normed_grad = dot_nt(query_pre_grad, weight[...])
    share_query.wait_recv()
    join(mat_one, 1, 0, 0, 384)
    join(mat_two, 1, 0, 384, 128)
    trio[0].step_far()

    @pl.when(core == 0)
    def _():
        source = from_pair.at[1]
        kv_copy(source, source, sibling, 1).wait_recv()
        for head in range(KV_HEADS):
            own_grads[head] += source[head].astype(F32)

    @pl.when(line < 3)
    def _():
        kv_copy(from_near, from_near, sibling, 2).wait_recv()
        for head in range(KV_HEADS):
            own_grads[head] += from_near[head].astype(F32)

    key_chunks, value_chunks = [], []
    for head in range(0, KV_HEADS, 2):
        one, two = own_grads[head], own_grads[head + 1]
        key_chunks.append(jnp.where(lower, one, pltpu.roll(two, 64, 1)))
        value_chunks.append(jnp.where(lower, pltpu.roll(one, 64, 1), two))
    key_pre_grad = jnp.concatenate(
        rope_lanes(jnp.concatenate(key_chunks, axis=1), cosine, -sine), axis=1
    ).astype(BF)
    value_pre_grad = jnp.concatenate(value_chunks, axis=1).astype(BF)
    wide[:, 0:512] = key_pre_grad
    wide[:, 512:1024] = value_pre_grad
    share_query.wait_send()
    for begin in (0, 256):
        columns = pl.ds(pl.multiple_of(other * 512 + begin, 256), 256)
        staged[:, begin : begin + 256] = dot_tn(normed, wide[:, columns]).astype(BF)
    share_pair.start()
    for begin in (0, 256):
        columns = pl.ds(pl.multiple_of(core * 512 + begin, 256), 256)
        value = dot_tn(normed, wide[:, columns]).astype(BF)
        if begin == 0:
            mat_two[:, 128:384] = value
        else:
            mat_three[...] = value
    cube_out.step_done()
    share_pair.wait_recv()
    join(mat_two, 2, 128, 0, 256)
    join(mat_three, 2, 0, 256, 256)
    trio[1].step_far()
    trio[2].step_far()
    small_out_ref[own_small, :] = axis_sum(small, 0, 2).astype(BF)
    share_total.start()
    normed_grad = (
        normed_grad
        + dot_nt(key_pre_grad, w_key_ref[...])
        + dot_nt(value_pre_grad, w_value_ref[...])
    )
    tokens = tokens_ref[...].astype(F32)
    scale_one = norm_scale(tokens)
    gain_own[0:1, :] = jnp.sum(normed_grad * tokens * scale_one, axis=0, keepdims=True)
    share_gain.start()
    weighted = normed_grad * gain_one_ref[...]
    shared = scale_one * scale_one * scale_one * jnp.mean(weighted * tokens, axis=1, keepdims=True)
    input_grad_ref[...] = (residual_grad[...] + scale_one * weighted - tokens * shared).astype(BF)

    each("step_near")
    cube_out.ring_back()
    share_gain.wait_recv()
    gain[0, line] = gain_own[...] + gain_first[...]
    axis_begin(gain, 3, 0)
    each("step_mid")
    cube_out.ring_forward()
    gain[1, row] = axis_sum(gain, 3, 0)
    axis_begin(gain, 3, 1)
    each("step_low")
    cube_out.ring_last()
    gain[2, column] = axis_sum(gain, 3, 1)
    axis_begin(gain, 3, 2)
    each("step_done")
    cube_out.back_far()
    gain_out_ref[...] = axis_sum(gain, 3, 2)
    each("back_mid")
    each("back_near")
    for reducer in reducers:
        reducer.step_sum(0)
    output_ref[...] = (residual_ref[...] + RESIDUAL_MULT * moe_total[...]).astype(BF)
    each("back_far")
    cube_out.back_last()
    each("back_last")
    for reducer in reducers:
        reducer.finish()
    spread.finish()
    for cube in cubes:
        cube.finish()
    for copy in (share_pair, share_small, share_gain, share_total):
        copy.wait_send()
    theirs = small_out_ref.at[other_small]
    to_core(theirs, theirs, 4).wait_recv()
    for base, held in ((0, small), (3, gain)):
        for axis in range(3):
            for step in (1, 2, 3):
                axis_copy(held, base, axis, step).wait_send()

    @pl.when(line >= 1 + (1 - core))
    def _():
        pair_three.wait_send()

    @pl.when((line >= 1) | (core == 1))
    def _():
        pair_one.wait_send()

    @pl.when(line >= 1)
    def _():
        to_near.wait_send()

    @pl.when(line >= 2)
    def _():
        to_far.wait_send()


def run_backward(*args):
    dma = pltpu.SemaphoreType.DMA
    rows = WIDTH + INNER
    vmem = pl.BlockSpec(memory_space=pltpu.VMEM)
    hbm = pl.BlockSpec(memory_space=pl.ANY)
    heads = (KV_HEADS, BLOCK, 128)
    shape = jax.ShapeDtypeStruct
    return pl.pallas_call(
        backward_kernel,
        out_shape=(
            shape((BLOCK, WIDTH), BF),
            shape((BLOCK, WIDTH), BF),
            shape((WIDTH, 2 * WIDTH), BF),
            shape((WIDTH, WIDTH), BF),
            shape((2 * SMALL_ROWS, WIDTH), BF),
            shape((8, WIDTH), F32),
            shape((rows, WIDTH), BF),
        ),
        in_specs=[hbm] + [vmem] * 5 + [hbm] * 6 + [vmem] * 4 + [hbm] * 7,
        out_specs=(vmem,) * 6 + (hbm,),
        scratch_shapes=[pltpu.VMEM((2, BLOCK, 128), F32), pltpu.VMEM((PLANE, BLOCK, WIDTH), BF)]
        + reduce_buffers()
        + [
            pltpu.VMEM((BLOCK, WIDTH), F32),
            pltpu.VMEM((KV_HEADS, 2 * BLOCK), F32),
            pltpu.VMEM((KV_HEADS, 2 * BLOCK, 128), BF),
            pltpu.VMEM((KV_HEADS, 128, 2 * BLOCK), F32),
            pltpu.VMEM(heads, F32),
            pltpu.VMEM((4,) + heads, BF),
            pltpu.VMEM((2,) + heads, BF),
            pltpu.VMEM(heads, BF),
            pltpu.VMEM(heads, BF),
            pltpu.VMEM((BLOCK, WIDTH), F32),
            pltpu.VMEM((WIDTH, WIDTH), BF),
            pltpu.VMEM((BLOCK, WIDTH), BF),
            pltpu.VMEM((WIDTH, 512), BF),
            pltpu.VMEM((3, WIDTH, 512), BF),
            pltpu.VMEM((WIDTH, 512), BF),
            pltpu.VMEM((WIDTH, 384), BF),
            pltpu.VMEM((WIDTH, 384), BF),
            pltpu.VMEM((WIDTH, 256), BF),
        ]
        + [
            pltpu.VMEM((count, extent, width), BF)
            for width in (512, 384, 384, 256)
            for count, extent in ((2, 128), (2, 256), (3, 64), (3, 16))
        ]
        + [
            pltpu.VMEM((2 * SMALL_ROWS, WIDTH), BF),
            pltpu.VMEM((SMALL_ROWS, WIDTH), BF),
            pltpu.VMEM((3, 4, SMALL_ROWS, WIDTH), BF),
            pltpu.VMEM((8, WIDTH), F32),
            pltpu.VMEM((8, WIDTH), F32),
            pltpu.VMEM((3, 4, 8, WIDTH), F32),
            dma((40,)),
            dma((40,)),
            dma((4,)),
            dma((4,)),
            dma((4,)),
            dma((4,)),
            dma((6,)),
            dma((4, 26)),
            dma((4, 26)),
            dma((6,)),
            dma((6,)),
            dma((6, 4)),
            dma((6, 4)),
            pltpu.VMEM((BLOCK, WIDTH), BF),
            pltpu.VMEM((BLOCK, WIDTH), BF),
            pltpu.VMEM((KV_HEADS, 2 * BLOCK, 128), BF),
            pltpu.VMEM((5,) + heads, BF),
            pltpu.VMEM((5, BLOCK, BLOCK), BF),
            pltpu.VMEM((WIDTH, 512), BF),
            pltpu.VMEM((WIDTH, 512), BF),
            dma((7,)),
        ],
        compiler_params=pltpu.CompilerParams(
            collective_id=1, has_side_effects=True, vmem_limit_bytes=VMEM_LIMIT
        ),
    )(*args)


def widen_kernel(
    up, down, output, query_one, query_two, key, value, router, result, grad, gains, up_out, down_out,
    output_out, query_out, key_out, value_out, router_out, result_out, grad_out,
    gain_one_out, gain_two_out,
):
    for source, target in ((up, up_out), (down, down_out), (output, output_out), (key, key_out), (value, value_out)):
        target[...] = source[...].astype(F32)
    query_out[:, :512] = query_one[...].astype(F32)
    query_out[:, 512:] = query_two[...].astype(F32)
    router_out[...] = router[...].astype(F32)
    result_out[...] = result[...]
    grad_out[...] = grad[...]
    gain_one_out[...] = gains[0, :]
    gain_two_out[...] = gains[1, :]


def widen_all(experts, output, trio, router, result, grad, gains):
    steps = 8
    in_rows, out_rows = WIDTH // steps, INNER // steps
    wide = pl.BlockSpec((in_rows, WIDTH), lambda i: (i, 0))
    low = pl.BlockSpec((out_rows, WIDTH), lambda i: (i, 0))
    narrow = pl.BlockSpec((in_rows, 512), lambda i: (i, 0))
    quarters = [pl.BlockSpec((in_rows, 512), lambda i, place=place: (i, place)) for place in range(4)]
    turned = pl.BlockSpec((32, in_rows), lambda i: (0, i))
    tokens = pl.BlockSpec((BLOCK // steps, WIDTH), lambda i: (i, 0))
    tile = pl.BlockSpec((8, WIDTH), lambda i: (0, 0))
    flat = pl.BlockSpec((WIDTH,), lambda i: (0,))
    below = pl.BlockSpec((out_rows, WIDTH), lambda i: (WIDTH // out_rows + i, 0))
    shape = jax.ShapeDtypeStruct
    return pl.pallas_call(
        widen_kernel,
        grid=(steps,),
        out_shape=(
            shape((WIDTH, WIDTH), F32),
            shape((INNER, WIDTH), F32),
            shape((WIDTH, WIDTH), F32),
            shape((WIDTH, WIDTH), F32),
            shape((WIDTH, 512), F32),
            shape((WIDTH, 512), F32),
            shape((32, WIDTH), F32),
            shape((BLOCK, WIDTH), BF),
            shape((BLOCK, WIDTH), BF),
            shape((WIDTH,), F32),
            shape((WIDTH,), F32),
        ),
        in_specs=[
            wide, below, wide, quarters[0], quarters[2], quarters[1], quarters[3], turned, tokens, tokens,
            tile,
        ],
        out_specs=(wide, low, wide, wide, narrow, narrow, turned, tokens, tokens, flat, flat),
        compiler_params=pltpu.CompilerParams(vmem_limit_bytes=VMEM_LIMIT),
    )(experts, experts, output, trio, trio, trio, trio, router, result, grad, gains)


def on_device(
    tokens,
    segments,
    routes,
    rank_order,
    attn_gain,
    w_query,
    w_key,
    w_value,
    w_output,
    ffn_gain,
    w_router,
    expert_in,
    expert_out,
    cotangent,
):
    tok_rows = tokens.shape[1]
    table = jnp.asarray(rope_lane_table(8 * tok_rows)).reshape(8, 2, tok_rows, 128)
    router = w_router.T
    (
        routed_in, residual, heads_out, normed, query_heads, kv_heads_all, lse, bias, gates, meta,
        cots, sib_in, sib_out,
    ) = run_attention(
        tokens[0], segments, routes[0].T, rank_order[0].T, attn_gain[None], w_query, w_key, w_value,
        w_output, ffn_gain[None], router, table, cotangent[0], expert_in[0], expert_out[0],
    )
    expert_row_sum, scores, moe_partial, expert_grads = run_experts(
        routed_in, meta, cots.reshape(PLANE, BLOCK, WIDTH), expert_in[0], expert_out[0], sib_in, sib_out,
    )
    (
        output, input_grad, trio_sum, output_w_sum, small, gain_sum, expert_total,
    ) = run_backward(
        tokens[0], residual, scores, gates, routed_in, heads_out, normed, query_heads,
        kv_heads_all, bias, w_key, w_value, router, attn_gain[None], ffn_gain[None], lse, table,
        moe_partial, expert_grads, expert_row_sum, w_query, w_output, cotangent[0],
    )
    (
        up_total, down_total, out_total, query_total, key_total, value_total, router_total, output,
        input_grad, gain_one_total, gain_two_total,
    ) = widen_all(expert_total, output_w_sum, trio_sum, small, output, input_grad, gain_sum)
    return (
        output[None],
        input_grad[None],
        gain_one_total,
        query_total,
        key_total,
        value_total,
        out_total,
        gain_two_total,
        router_total.T,
        up_total[None],
        down_total[None],
    )


def solution(mesh):
    placed = (
        P("grp", ("seq", "exp"), None),
        P("grp", ("seq", "exp")),
        P("grp", ("seq", "exp"), None),
        P("grp", ("seq", "exp"), None),
        P(),
        P(),
        P(),
        P(),
        P(),
        P(),
        P(),
        P(("grp", "exp"), None, None),
        P(("grp", "exp"), None, None),
        P("grp", ("seq", "exp"), None),
    )
    return jax.shard_map(
        on_device,
        mesh=mesh,
        in_specs=placed,
        out_specs=(
            P("grp", ("seq", "exp"), None),
            P("grp", ("seq", "exp"), None),
            P(),
            P(),
            P(),
            P(),
            P(),
            P(),
            P(),
            P(("grp", "exp"), None, None),
            P(("grp", "exp"), None, None),
        ),
        check_vma=False,
    )
```
